32 devices in a mesh: dp: 4 (over y, x), expert: 2 (over core), tensor: 4 (over z).
Axes of the slice: x: 2, y: 2, z: 4, core: 2. Of those that a mesh axis runs over, the one named last changes fastest.
Arguments:
- tokens: bfloat16 [4096, 2048], P(('dp', 'expert')), may hold values from -6 to 6
- cotangent: bfloat16 [4096, 2048], P(('dp', 'expert')), may hold values from -6 to 6
- route_ids: int32 [4096, 8], P(('dp', 'expert')), may hold values from 0 to 15, all different within a row; in each aligned block of 512 rows (0 to 511, 512 to 1023, ...) at most 320 rows name the same one
- route_weight: float32 [4096, 8], P(('dp', 'expert')), may hold values from 0.05 to 0.5
- lengths: int32 [8], P(('dp', 'expert')), may hold values from 128 to 512, as said below
- attention_norm: bfloat16 [2048], P(('dp', 'expert')), may hold values from 0.5 to 2
- query_weight: bfloat16 [2048, 4096], P(('dp', 'expert'), 'tensor'), may hold values from -0.125 to 0.125
- key_matrix: bfloat16 [2048, 512], P(('dp', 'expert'), 'tensor'), may hold values from -0.125 to 0.125
- value_matrix: bfloat16 [2048, 512], P(('dp', 'expert'), 'tensor'), may hold values from -0.125 to 0.125
- output_weight: bfloat16 [2048, 4096], P(('dp', 'expert'), 'tensor'), may hold values from -0.375 to 0.375
- query_norm: bfloat16 [128], P(('dp', 'expert')), may hold values from 0.5 to 2
- key_norm: bfloat16 [128], P(('dp', 'expert')), may hold values from 0.5 to 2
- experts_norm: bfloat16 [2048], P(('dp', 'expert')), may hold values from 0.5 to 2
- gate_weight: bfloat16 [16, 768, 2048], P('expert', 'tensor', 'dp'), may hold values from -0.125 to 0.125
- up_weight: bfloat16 [16, 768, 2048], P('expert', 'tensor', 'dp'), may hold values from -0.125 to 0.125
- down_weight: bfloat16 [16, 768, 2048], P('expert', 'tensor', 'dp'), may hold values from -0.4375 to 0.4375
Outputs:
- output: bfloat16 [4096, 2048], P(('dp', 'expert'))
- tokens_grad: float32 [4096, 2048], P(('dp', 'expert'))
- attention_norm_grad: float32 [2048], P(('dp', 'expert'))
- query_weight_grad: float32 [2048, 4096], P(('dp', 'expert'), 'tensor')
- key_weight_grad: float32 [2048, 512], P(('dp', 'expert'), 'tensor')
- value_weight_grad: float32 [2048, 512], P(('dp', 'expert'), 'tensor')
- output_weight_grad: float32 [2048, 4096], P(('dp', 'expert'), 'tensor')
- query_norm_grad: float32 [128], P(('dp', 'expert'))
- key_norm_grad: float32 [128], P(('dp', 'expert'))
- experts_norm_grad: float32 [2048], P(('dp', 'expert'))
- gate_weight_grad: float32 [16, 768, 2048], P('expert', 'tensor', 'dp')
- up_weight_grad: float32 [16, 768, 2048], P('expert', 'tensor', 'dp')
- down_weight_grad: float32 [16, 768, 2048], P('expert', 'tensor', 'dp')
The draws below stay inside these ranges and needn't reach their ends.
Inputs may be any that keep to these rules, and one draw needn't show every extreme that they name: `route_ids`: each row names 8 different experts. In each pack of 512 rows no expert is named by more than 320 rows, and in every draw some expert is named by exactly 320 rows of some pack. `lengths`: positions at or beyond a pack's length are padding whose keys no query reads; in every draw one pack is full.
All inputs are finite; a program needn't handle non-finite values.
Results may differ from the reference program's by a relative error of at most 0.03.
Values may be sent and summed in bfloat16 or wider, within the bound.
A program may use at most 384 MiB of HBM per device.

```python
import math
import jax
import jax.numpy as jnp
import numpy as np
from jax import lax

MODEL_WIDTH = 2048
QUERY_HEADS = 32
KEY_VALUE_HEADS = 4
HEAD_SIZE = 128
FFE = 768
TOP = 8
SLOT_POSITIONS = 512
EXPERTS = 16
PACKS = 8
TOKENS = 4096
CAP = 320
N_TENSOR = 4


def draw_lengths(key, part):
    first_key, second_key = jax.random.split(key)
    drawn = jax.random.randint(first_key, (PACKS,), SLOT_POSITIONS // 4, SLOT_POSITIONS + 1)
    full_pack = jax.random.randint(second_key, (1,), 0, PACKS)
    return jnp.where(jnp.arange(PACKS) == full_pack[0], SLOT_POSITIONS, drawn).astype(jnp.int32)


def levels(stream_key, shape, cuts, smallest, high):
    gain = 1.0
    for dim, shards_of in cuts:
        steps = jax.random.uniform(jax.random.fold_in(jax.random.fold_in(stream_key, 6), dim), (shards_of,), jnp.float32, smallest / len(cuts), high / len(cuts))
        gain = gain * jnp.repeat(jnp.exp(steps), shape[dim] // shards_of).reshape((-1,) + (1,) * (len(shape) - 1 - dim))
    return gain


def assign_block(key, own, number, rows, count, top, limit, skew):
    sequence = jax.random.permutation(key, count)
    packed, usual = load_shares(count, rows * top, limit, skew, True), load_shares(count, rows * top, limit, skew, False)
    places = jnp.arange(count)

    def named(sizes, offset_by):
        used = int((sizes > 0).sum())
        fixed = max(1, used // 4)
        moved = fixed + (places - fixed + offset_by * (used - fixed)) % max(1, count - fixed)
        return jnp.zeros((count,), jnp.int32).at[sequence[jnp.where(places < fixed, places, moved)]].set(jnp.asarray(sizes, jnp.int32))

    sizes = jnp.where(number % 4 == 0, named(packed, number // 4), named(usual, number - number // 4 - 1))
    mixed = jax.random.permutation(jax.random.fold_in(own, 3), count)
    donor, receiver = mixed[0:count // 2 * 2:2], mixed[1:count // 2 * 2:2]
    room = jnp.minimum(sizes[donor] - 1, limit - sizes[receiver]) // 2
    room = jnp.where((donor == sequence[0]) | (receiver == sequence[0]) | (sizes[receiver] == 0), 0, jnp.maximum(room, 0))
    moved = jax.random.randint(jax.random.fold_in(own, 4), (count // 2,), 0, 1 << 20) % (room + 1)
    sizes = sizes.at[donor].add(-moved).at[receiver].add(moved)
    items = jnp.searchsorted(jnp.cumsum(sizes), jnp.arange(rows * top), side="right").astype(jnp.int32)
    table = items.reshape(top, rows).T
    table = table[jax.random.permutation(jax.random.fold_in(own, 1), rows)]
    offset_by = jax.random.randint(jax.random.fold_in(own, 2), (rows, 1), 0, top)
    return jnp.take_along_axis(table, (jnp.arange(top)[None, :] + offset_by) % top, axis=1)


def load_shares(number_of, total, bound, slope, full):
    loads = [(1 << 20) // math.isqrt(rank ** slope) + 1 for rank in range(1, number_of + 1)]
    largest = bound if full else min(bound, max(-(-total // number_of), total * loads[0] // sum(loads)))
    least = 1 if total - largest >= number_of - 1 else 0
    given, spare = [largest] + [least] * (number_of - 1), total - largest - least * (number_of - 1)
    while spare > 0:
        free = [i for i in range(1, number_of) if given[i] < largest] or [i for i in range(1, number_of) if given[i] < bound]
        pool, remaining = sum([loads[i] for i in free]), spare
        for i in free:
            addition = min(bound - given[i], max(1, remaining * loads[i] // pool), spare)
            given[i] = given[i] + addition
            spare = spare - addition
    return np.array(given)


def scatter_about(stream_key, dims, scale, reach, cuts=(), kind=jnp.bfloat16):
    loudness = levels(stream_key, dims, cuts, -0.22, 0.18) if cuts else 1.0
    values = jax.random.normal(stream_key, dims, jnp.float32) * scale * loudness
    return jnp.minimum(jnp.maximum(values, -reach), reach).astype(kind)


def setup_inputs(seed: int = 0) -> dict:
    key_list = jax.random.split(jax.random.key(seed), 17)
    tokens = scatter_about(key_list[0], (TOKENS, MODEL_WIDTH), 1.0, 6.0, ((0, 8),))
    cotangent = scatter_about(key_list[1], (TOKENS, MODEL_WIDTH), 1.0, 6.0, ((0, 8),))
    route_ids_keys = jax.random.split(jax.random.fold_in(key_list[2], 1), TOKENS // SLOT_POSITIONS)
    route_ids_turns = jax.random.permutation(jax.random.fold_in(key_list[2], 3), TOKENS // SLOT_POSITIONS)
    route_ids = jax.vmap(lambda own, number: assign_block(jax.random.fold_in(key_list[2], 2), own, number, SLOT_POSITIONS, EXPERTS, TOP, CAP, 1))(route_ids_keys, route_ids_turns).reshape((TOKENS, TOP))
    route_weight = jnp.clip(jnp.exp(math.log(0.5) - 2.3025851 * jax.random.uniform(key_list[3], (TOKENS, TOP), jnp.float32) ** levels(key_list[3], (TOKENS, TOP), ((0, 8),), -0.2, 0.2)), 0.05, 0.5)
    lengths = draw_lengths(jax.random.fold_in(key_list[16], 71), 0)
    attention_norm = jnp.clip(jnp.exp(math.log(2.0) - 1.3862944 * jax.random.uniform(key_list[5], (MODEL_WIDTH,), jnp.float32) ** levels(key_list[5], (MODEL_WIDTH,), ((0, 8),), -0.2, 0.2)), 0.5, 2.0).astype(jnp.bfloat16)
    query_weight = scatter_about(key_list[6], (MODEL_WIDTH, QUERY_HEADS * HEAD_SIZE), MODEL_WIDTH ** -0.5, 0.125, ((0, 8), (1, 4)))
    key_matrix = scatter_about(key_list[7], (MODEL_WIDTH, KEY_VALUE_HEADS * HEAD_SIZE), MODEL_WIDTH ** -0.5, 0.125, ((0, 8), (1, 4)))
    value_matrix = scatter_about(key_list[8], (MODEL_WIDTH, KEY_VALUE_HEADS * HEAD_SIZE), MODEL_WIDTH ** -0.5, 0.125, ((0, 8), (1, 4)))
    output_weight = scatter_about(key_list[9], (MODEL_WIDTH, QUERY_HEADS * HEAD_SIZE), (QUERY_HEADS * HEAD_SIZE // 16) ** -0.5, 0.375, ((0, 8), (1, 4)))
    query_norm = jnp.clip(jnp.exp(math.log(2.0) - 1.3862944 * jax.random.uniform(key_list[10], (HEAD_SIZE,), jnp.float32) ** levels(key_list[10], (HEAD_SIZE,), ((0, 8),), -0.2, 0.2)), 0.5, 2.0).astype(jnp.bfloat16)
    key_norm = jnp.clip(jnp.exp(math.log(2.0) - 1.3862944 * jax.random.uniform(key_list[11], (HEAD_SIZE,), jnp.float32) ** levels(key_list[11], (HEAD_SIZE,), ((0, 8),), -0.2, 0.2)), 0.5, 2.0).astype(jnp.bfloat16)
    experts_norm = jnp.clip(jnp.exp(math.log(2.0) - 1.3862944 * jax.random.uniform(key_list[12], (MODEL_WIDTH,), jnp.float32) ** levels(key_list[12], (MODEL_WIDTH,), ((0, 8),), -0.2, 0.2)), 0.5, 2.0).astype(jnp.bfloat16)
    gate_weight = scatter_about(key_list[13], (EXPERTS, FFE, MODEL_WIDTH), MODEL_WIDTH ** -0.5, 0.125, ((0, 2), (1, 4), (2, 4)))
    up_weight = scatter_about(key_list[14], (EXPERTS, FFE, MODEL_WIDTH), MODEL_WIDTH ** -0.5, 0.125, ((0, 2), (1, 4), (2, 4)))
    down_weight = scatter_about(key_list[15], (EXPERTS, FFE, MODEL_WIDTH), (FFE // 4) ** -0.5, 0.4375, ((0, 2), (1, 4), (2, 4)))
    return dict(tokens=tokens, cotangent=cotangent, route_ids=route_ids, route_weight=route_weight, lengths=lengths, attention_norm=attention_norm, query_weight=query_weight, key_matrix=key_matrix, value_matrix=value_matrix, output_weight=output_weight, query_norm=query_norm, key_norm=key_norm, experts_norm=experts_norm, gate_weight=gate_weight, up_weight=up_weight, down_weight=down_weight)


@jax.custom_vjp
def reduced_precision(v):
    return lax.optimization_barrier(v.astype(jnp.bfloat16)).astype(jnp.float32)

@jax.custom_vjp
def reduced_backward(v):
    return v

def low_keep(v):
    return (reduced_precision(v), None)

def low_pass(kept, grad):
    return (grad,)

def back_keep(v):
    return (v, None)

def back_low(kept, grad):
    return (reduced_precision(grad),)
reduced_precision.defvjp(low_keep, low_pass)
reduced_backward.defvjp(back_keep, back_low)
highest_precision = lax.Precision.HIGHEST
epsilon = 1e-06

def rms_scale(values):
    return lax.rsqrt(lax.optimization_barrier(jnp.mean(values * values, axis=-1, keepdims=True)) + epsilon)

def rope_tables():
    half_dim = HEAD_SIZE // 2
    frequency = jnp.power(jnp.float32(1000000.0), -(jnp.arange(half_dim, dtype=jnp.float32) * (2.0 / HEAD_SIZE)))
    angles = jnp.arange(SLOT_POSITIONS, dtype=jnp.float32)[:, None] * frequency[None, :]
    return (jnp.cos(angles)[:, None, :], jnp.sin(angles)[:, None, :])

def rotate(values, cosine_table, sine_table):
    half_dim = values.shape[-1] // 2
    first_half = values[..., :half_dim]
    second_half = values[..., half_dim:]
    return jnp.concatenate([first_half * cosine_table - second_half * sine_table, second_half * cosine_table + first_half * sine_table], axis=-1)

def route_ranks(flat_ids, expert_count):
    route_count = flat_ids.shape[0]
    sorted_order = jnp.argsort(flat_ids, stable=True).astype(jnp.int32)
    matches = (flat_ids[:, None] == jnp.arange(expert_count, dtype=jnp.int32)[None, :]).astype(jnp.int32)
    counts = lax.optimization_barrier(jnp.sum(matches, axis=0)).astype(jnp.int32)
    starts = (jnp.cumsum(counts) - counts).astype(jnp.int32)
    ranked = jnp.arange(route_count, dtype=jnp.int32) - starts[flat_ids[sorted_order]]
    return jnp.zeros((route_count,), jnp.int32).at[sorted_order].set(ranked.astype(jnp.int32))

def pack_forward(tokens, flat_ids, weights, length, params):
    attention_norm, query_weight, key_matrix, value_matrix, output_weight, query_norm, key_norm, experts_norm, gate_weight, up_weight, down_weight = params
    cosine_table, sine_table = rope_tables()
    normed_one = tokens * rms_scale(tokens)
    first_hidden = reduced_precision(normed_one * attention_norm)
    queries = reduced_backward(jnp.dot(first_hidden, query_weight, precision=highest_precision)).reshape(SLOT_POSITIONS, QUERY_HEADS, HEAD_SIZE)
    unnormed_keys = reduced_backward(jnp.dot(first_hidden, key_matrix, precision=highest_precision)).reshape(SLOT_POSITIONS, KEY_VALUE_HEADS, HEAD_SIZE)
    unnormed_values = reduced_backward(reduced_precision(jnp.dot(first_hidden, value_matrix, precision=highest_precision))).reshape(SLOT_POSITIONS, KEY_VALUE_HEADS, HEAD_SIZE)
    rotated_query = reduced_precision(rotate(queries * rms_scale(queries) * query_norm, cosine_table, sine_table))
    key_rot = reduced_precision(rotate(unnormed_keys * rms_scale(unnormed_keys) * key_norm, cosine_table, sine_table))
    grouped_heads = rotated_query.reshape(SLOT_POSITIONS, KEY_VALUE_HEADS, QUERY_HEADS // KEY_VALUE_HEADS, HEAD_SIZE)
    scores = jnp.einsum('qkgd,skd->kgqs', grouped_heads, key_rot, precision=highest_precision) * HEAD_SIZE ** (-0.5)
    positions = jnp.arange(SLOT_POSITIONS, dtype=jnp.int32)
    allowed = (positions[None, :] <= positions[:, None]) & (positions[None, :] < length)
    scores = reduced_backward(jnp.where(allowed, scores, -1e+30))
    prob_low = reduced_precision(jax.nn.softmax(scores, axis=-1))
    attended = jnp.einsum('kgqs,skd->qkgd', prob_low, unnormed_values, precision=highest_precision).reshape(SLOT_POSITIONS, QUERY_HEADS * HEAD_SIZE)
    attended = reduced_backward(reduced_precision(attended))
    projected = reduced_backward(jnp.dot(attended, output_weight.T, precision=highest_precision))
    mixed_rows = tokens + projected
    normed_two = mixed_rows * rms_scale(mixed_rows)
    hidden_two = reduced_precision(normed_two * experts_norm)
    route_total = SLOT_POSITIONS * TOP
    route_rank = route_ranks(flat_ids, EXPERTS)
    places = flat_ids * CAP + route_rank
    route_of = jnp.full((EXPERTS * CAP,), route_total, jnp.int32).at[places].set(jnp.arange(route_total, dtype=jnp.int32))
    filled = (route_of < route_total).astype(jnp.float32)
    token_of = jnp.minimum(route_of // TOP, SLOT_POSITIONS - 1)
    slot_rows = (hidden_two[token_of] * filled[:, None]).reshape(EXPERTS, CAP, MODEL_WIDTH)
    width_part = FFE // N_TENSOR
    summed = jnp.zeros((EXPERTS, CAP, MODEL_WIDTH), jnp.float32)
    for quarter in range(N_TENSOR):
        lower_row = quarter * width_part
        gate_part = gate_weight[:, lower_row:lower_row + width_part, :]
        up_part = up_weight[:, lower_row:lower_row + width_part, :]
        down_part = down_weight[:, lower_row:lower_row + width_part, :]
        inputs = reduced_backward(slot_rows)
        gate_value = reduced_backward(jnp.einsum('ecd,efd->ecf', inputs, gate_part, precision=highest_precision))
        up_value = reduced_backward(jnp.einsum('ecd,efd->ecf', inputs, up_part, precision=highest_precision))
        activated = reduced_precision(jax.nn.silu(gate_value) * up_value)
        summed = summed + reduced_backward(reduced_precision(jnp.einsum('ecf,efd->ecd', activated, down_part, precision=highest_precision)))
    per_route = summed.reshape(EXPERTS * CAP, MODEL_WIDTH)[places].reshape(SLOT_POSITIONS, TOP, MODEL_WIDTH)
    return mixed_rows + lax.optimization_barrier(jnp.sum(per_route * weights[:, :, None], axis=1))

def reference(tokens, cotangent, route_ids, route_weight, lengths, attention_norm, query_weight, key_matrix, value_matrix, output_weight, query_norm, key_norm, experts_norm, gate_weight, up_weight, down_weight):
    params = tuple((element.astype(jnp.float32) for element in (attention_norm, query_weight, key_matrix, value_matrix, output_weight, query_norm, key_norm, experts_norm, gate_weight, up_weight, down_weight)))
    ids_packs = route_ids.reshape(PACKS, SLOT_POSITIONS * TOP).astype(jnp.int32)
    weight_packs = route_weight.astype(jnp.float32).reshape(PACKS, SLOT_POSITIONS, TOP)
    length_packs = lengths.astype(jnp.int32)
    checked = jax.checkpoint(pack_forward)

    def forward(token_packs, weights_all):

        def one_pack(unused_carry, element):
            pack_tokens, pack_ids, pack_weights, pack_length = element
            return (unused_carry, checked(pack_tokens, pack_ids, pack_weights, pack_length, weights_all))
        final_carry, results = lax.scan(one_pack, jnp.zeros((), jnp.float32), (token_packs, ids_packs, weight_packs, length_packs))
        return results
    results, pull_back = jax.vjp(forward, tokens.astype(jnp.float32).reshape(PACKS, SLOT_POSITIONS, MODEL_WIDTH), params)
    tokens_grad, param_grads = pull_back(cotangent.astype(jnp.float32).reshape(PACKS, SLOT_POSITIONS, MODEL_WIDTH))
    attention_norm_grad, query_weight_grad, key_weight_grad, value_weight_grad, output_weight_grad, query_norm_grad, key_norm_grad, experts_norm_grad, gate_weight_grad, up_weight_grad, down_weight_grad = param_grads
    return (results.reshape(TOKENS, MODEL_WIDTH).astype(jnp.bfloat16), tokens_grad.reshape(TOKENS, MODEL_WIDTH), attention_norm_grad, query_weight_grad, key_weight_grad, value_weight_grad, output_weight_grad, query_norm_grad, key_norm_grad, experts_norm_grad, gate_weight_grad, up_weight_grad, down_weight_grad)
```

```python
import jax
import jax.numpy as jnp
from jax import lax
from jax.sharding import PartitionSpec as P

HEAD_SIZE = 128
TOP = 8
epsilon = 1e-06
f32 = jnp.float32
bf16 = jnp.bfloat16


def rms_scale(values):
    return lax.rsqrt(jnp.mean(values * values, axis=-1, keepdims=True) + epsilon)


def rope_tables(rows):
    half_dim = HEAD_SIZE // 2
    frequency = jnp.power(f32(1000000.0), -(jnp.arange(half_dim, dtype=f32) * (2.0 / HEAD_SIZE)))
    angles = jnp.arange(rows, dtype=f32)[:, None] * frequency[None, :]
    return (jnp.cos(angles)[:, None, :], jnp.sin(angles)[:, None, :])


def rotate(values, cosine_table, sine_table):
    half_dim = values.shape[-1] // 2
    first_half = values[..., :half_dim]
    second_half = values[..., half_dim:]
    return jnp.concatenate(
        [
            first_half * cosine_table - second_half * sine_table,
            second_half * cosine_table + first_half * sine_table,
        ],
        axis=-1,
    )


def norm_back(grad_hidden, normed, scales, gains):
    grad_normed = grad_hidden * gains
    return scales * (grad_normed - normed * jnp.mean(grad_normed * normed, axis=-1, keepdims=True))


def flip(x, axis, bit):
    n = lax.axis_size(axis)
    return lax.ppermute(x, axis, [(i, i ^ bit) for i in range(n)])


def bits_of(n):
    return [1 << b for b in range(n.bit_length() - 1)]


def xor_gather(x, axis):
    pieces = [x]
    for bit in bits_of(lax.axis_size(axis)):
        pieces = pieces + [flip(p, axis, bit) for p in pieces]
    return pieces


def xor_scatter(parts, axis):
    for bit in reversed(bits_of(lax.axis_size(axis))):
        got = [flip(p, axis, bit) for p in parts[bit:]]
        parts = [
            (a.astype(f32) + r.astype(f32)).astype(a.dtype) for a, r in zip(parts[:bit], got)
        ]
    return parts[0]


def dp_gather(x, axis="dp"):
    n = lax.axis_size(axis)
    if n != 4:
        return xor_gather(x, axis)
    h = x.shape[0] // 2
    a, b = x[:h], x[h:]
    a1, b2 = flip(a, axis, 1), flip(b, axis, 2)
    a2, b1 = flip(a, axis, 2), flip(b, axis, 1)
    a3, b3 = flip(a1, axis, 2), flip(b2, axis, 1)
    cat = lambda p, q: jnp.concatenate([p, q], 0)
    return [cat(a, b), cat(a1, b1), cat(a2, b2), cat(a3, b3)]


def lane_order(x, axis, n, me):
    shape = x.shape
    axis = axis % x.ndim
    size = shape[axis] // n
    for bit in bits_of(n):
        parts = x.reshape(shape[:axis] + (n // (2 * bit), 2, bit * size) + shape[axis + 1 :])
        swapped = jnp.flip(parts, axis + 1).reshape(shape)
        x = jnp.where((me & bit) != 0, swapped, x)
    return x


def block_scores(query_block, key_rot, length):
    query_pos = jnp.arange(query_block.shape[0], dtype=jnp.int32)
    key_pos = jnp.arange(key_rot.shape[0], dtype=jnp.int32)
    allowed = (key_pos[None, :] <= query_pos[:, None]) & (key_pos[None, :] < length)
    scores = jnp.einsum(
        "qkgd,skd->kgqs", query_block, key_rot, preferred_element_type=f32
    ) * HEAD_SIZE ** (-0.5)
    return jnp.where(allowed, scores, -1e30)


def core_rows(pieces, axis="expert"):
    n = lax.axis_size(axis)
    own = jnp.stack(pieces, 0)
    if n == 2:
        other = flip(own, axis, 1)
        first = lax.axis_index(axis) == 0
        both = jnp.stack([jnp.where(first, own, other), jnp.where(first, other, own)], 1)
    else:
        both = lax.all_gather(own, axis, axis=1, tiled=False)
    return both.reshape((-1,) + own.shape[2:])


def dotf(a, b, dims):
    return lax.dot_general(a, b, (dims, ((), ())), preferred_element_type=f32)


def local(
    tokens,
    cotangent,
    route_ids,
    route_weight,
    lengths,
    attention_norm,
    query_weight,
    key_matrix,
    value_matrix,
    output_weight,
    query_norm,
    key_norm,
    experts_norm,
    gate_weight,
    up_weight,
    down_weight,
):
    n_dp = lax.axis_size("dp")
    n_ex = lax.axis_size("expert")
    me_dp = lax.axis_index("dp")
    me_ex = lax.axis_index("expert")
    rows, width = tokens.shape
    group, hidden, part = gate_weight.shape
    length = lengths[0]
    lane = lambda x, axis=-1: lane_order(x, axis, n_dp, me_dp)

    qkv_own = jnp.concatenate([query_weight, key_matrix, value_matrix], 1)
    qkv_pieces = dp_gather(qkv_own)
    wo_own, qkv_pieces = lax.optimization_barrier((output_weight, qkv_pieces))
    wo_pieces = dp_gather(wo_own)
    (gw, uw, dw), wo_pieces = lax.optimization_barrier(
        ((gate_weight, up_weight, down_weight), wo_pieces)
    )
    flat = group * hidden
    gate_up_own = jnp.concatenate([gw.reshape(flat, part), uw.reshape(flat, part)], 0)
    gate_up_pieces = dp_gather(gate_up_own)
    down_own, gate_up_pieces = lax.optimization_barrier((dw.reshape(flat, part), gate_up_pieces))
    down_pieces = dp_gather(down_own)

    gains = lax.all_gather(
        jnp.concatenate([attention_norm, experts_norm, query_norm, key_norm]),
        ("dp", "expert"),
        axis=0,
        tiled=False,
    ).astype(f32)
    na, nq = attention_norm.shape[0], query_norm.shape[0]
    gain_attention = lane(gains[:, :na].reshape(-1))
    gain_experts = lane(gains[:, na : 2 * na].reshape(-1))
    gain_query = gains[:, 2 * na : 2 * na + nq].reshape(-1)
    gain_key = gains[:, 2 * na + nq :].reshape(-1)

    experts = jnp.arange(group * n_ex, dtype=jnp.int32)
    table = jnp.zeros((rows, group * n_ex), f32)
    for c in range(route_ids.shape[1]):
        table = table + jnp.where(
            route_ids[:, c, None] == experts[None, :], route_weight[:, c, None], 0.0
        )
    table = jnp.concatenate(xor_gather(table, "expert"), 0)
    mine = lax.dynamic_slice_in_dim(table, me_ex * group, group, 1)
    unit_expert = jnp.arange(flat, dtype=jnp.int32) // hidden
    route_scale = jnp.zeros((table.shape[0], flat), f32)
    for j in range(group):
        route_scale = route_scale + jnp.where(unit_expert[None, :] == j, mine[:, j, None], 0.0)

    cosine_table, sine_table = rope_tables(rows)
    inputs = lane(tokens.astype(f32))
    scale_one = rms_scale(inputs)
    normed_one = inputs * scale_one
    first_hidden = (normed_one * gain_attention).astype(bf16)
    upstream_low = lane(cotangent)
    upstream_all = jnp.concatenate(xor_gather(upstream_low, "expert"), 0)

    full_qkv = core_rows(qkv_pieces)
    qkv = jnp.dot(first_hidden, full_qkv, preferred_element_type=f32)
    q_cols, k_cols = query_weight.shape[1], key_matrix.shape[1]
    heads_query, heads_key = q_cols // HEAD_SIZE, k_cols // HEAD_SIZE
    per_group = heads_query // heads_key
    query_raw = qkv[:, :q_cols].reshape(rows, heads_query, HEAD_SIZE)
    key_raw = qkv[:, q_cols : q_cols + k_cols].reshape(rows, heads_key, HEAD_SIZE)
    value_low = qkv[:, q_cols + k_cols :].astype(bf16).reshape(rows, heads_key, HEAD_SIZE)
    scale_query = rms_scale(query_raw)
    normed_query = query_raw * scale_query
    rotated_query = (
        rotate(normed_query * gain_query, cosine_table, sine_table)
        .astype(bf16)
        .reshape(rows, heads_key, per_group, HEAD_SIZE)
    )
    scale_key = rms_scale(key_raw)
    normed_key = key_raw * scale_key
    key_rot = rotate(normed_key * gain_key, cosine_table, sine_table).astype(bf16)
    scores = block_scores(rotated_query, key_rot, length)
    row_peak = jnp.max(scores, axis=-1, keepdims=True)
    shifted = jnp.exp(scores - row_peak)
    totals = jnp.sum(shifted, axis=-1, keepdims=True)
    probs = shifted / totals
    prob_low = probs.astype(bf16)
    attended_low = (
        jnp.einsum("kgqs,skd->qkgd", prob_low, value_low, preferred_element_type=f32)
        .reshape(rows, q_cols)
        .astype(bf16)
    )
    full_output = core_rows(wo_pieces)
    projected = dotf(attended_low, full_output, ((1,), (1,)))
    mixed_rows = inputs + lax.psum(projected.astype(bf16), "tensor").astype(f32)
    scale_two = rms_scale(mixed_rows)
    normed_two = mixed_rows * scale_two
    hidden_two = (normed_two * gain_experts).astype(bf16)

    hidden_all = jnp.concatenate(xor_gather(hidden_two, "expert"), 0)
    gate_up_full = jnp.concatenate(gate_up_pieces, 1)
    down_full = jnp.concatenate(down_pieces, 1)
    gate_up = dotf(hidden_all, gate_up_full, ((1,), (1,)))
    gate_value, up_value = gate_up[:, :flat], gate_up[:, flat:]
    grad_act = dotf(upstream_all, down_full, ((1,), (1,))) * route_scale
    sigmoid_gate = jax.nn.sigmoid(gate_value)
    scaled_act = (gate_value * sigmoid_gate * up_value * route_scale).astype(bf16)
    grad_up_low = (grad_act * gate_value * sigmoid_gate).astype(bf16)
    grad_gate_low = (
        grad_act * up_value * sigmoid_gate * (1.0 + gate_value * (1.0 - sigmoid_gate))
    ).astype(bf16)
    grad_gate_up = jnp.concatenate([grad_gate_low, grad_up_low], 1)
    grad_rows = jnp.dot(grad_gate_up, gate_up_full, preferred_element_type=f32).astype(bf16)
    grad_hidden_two = xor_scatter(jnp.split(grad_rows, n_ex, 0), "expert")
    grad_hidden_two = lax.psum(grad_hidden_two, "tensor").astype(f32)

    expert_out = jnp.dot(scaled_act, down_full, preferred_element_type=f32).astype(bf16)
    combined = xor_scatter(jnp.split(expert_out, n_ex, 0), "expert")
    output = (mixed_rows + lax.psum(combined, "tensor").astype(f32)).astype(bf16)
    output = lane(output)

    canonical_hidden = lane(hidden_all)
    canonical_up = lane(upstream_all)

    def expert_grad(low, acts):
        blocks = [
            dotf(low, acts[:, k * part : (k + 1) * part], ((0,), (0,))).astype(bf16)
            for k in range(n_dp)
        ]
        return lax.psum_scatter(
            jnp.stack(blocks, 0), "dp", scatter_dimension=0, tiled=False
        )

    down_shard = expert_grad(scaled_act, canonical_up)
    gate_shard = expert_grad(grad_gate_low, canonical_hidden)
    up_shard = expert_grad(grad_up_low, canonical_hidden)
    gate_shard, up_shard, down_shard = (
        s.astype(f32).reshape(group, hidden, part) for s in (gate_shard, up_shard, down_shard)
    )

    upstream = upstream_low.astype(f32)
    experts_gain_grad = jnp.sum(grad_hidden_two * normed_two, axis=0)
    grad_mixed = upstream + norm_back(grad_hidden_two, normed_two, scale_two, gain_experts)
    grad_proj_low = grad_mixed.astype(bf16)
    grad_att_low = (
        jnp.dot(grad_proj_low, full_output, preferred_element_type=f32)
        .astype(bf16)
        .reshape(rows, heads_key, per_group, HEAD_SIZE)
    )
    output_grad = dotf(lane(grad_proj_low), attended_low, ((0,), (0,)))
    grad_probs = jnp.einsum("qkgd,skd->kgqs", grad_att_low, value_low, preferred_element_type=f32)
    row_dot = jnp.sum(probs * grad_probs, axis=-1, keepdims=True)
    grad_scores = (probs * (grad_probs - row_dot)).astype(bf16)
    grad_value = jnp.einsum("kgqs,qkgd->skd", prob_low, grad_att_low, preferred_element_type=f32)
    grad_qrot = jnp.einsum(
        "kgqs,skd->qkgd", grad_scores, key_rot, preferred_element_type=f32
    ) * HEAD_SIZE ** (-0.5)
    grad_krot = jnp.einsum(
        "kgqs,qkgd->skd", grad_scores, rotated_query, preferred_element_type=f32
    ) * HEAD_SIZE ** (-0.5)
    grad_qrot = grad_qrot.reshape(rows, heads_query, HEAD_SIZE)
    grad_query_normed = rotate(grad_qrot, cosine_table, -sine_table)
    query_gain_grad = jnp.sum(grad_query_normed * normed_query, axis=(0, 1))
    grad_query_low = (
        norm_back(grad_query_normed, normed_query, scale_query, gain_query)
        .astype(bf16)
        .reshape(rows, q_cols)
    )
    grad_key_normed = rotate(grad_krot, cosine_table, -sine_table)
    key_gain_grad = jnp.sum(grad_key_normed * normed_key, axis=(0, 1))
    grad_key_low = (
        norm_back(grad_key_normed, normed_key, scale_key, gain_key).astype(bf16).reshape(rows, k_cols)
    )
    grad_value_low = grad_value.astype(bf16).reshape(rows, k_cols)
    grad_qkv_low = jnp.concatenate([grad_query_low, grad_key_low, grad_value_low], 1)
    grad_hidden_one = dotf(grad_qkv_low, full_qkv, ((1,), (1,)))
    grad_hidden_one = lax.psum(grad_hidden_one.astype(bf16), "tensor").astype(f32)
    qkv_grad = dotf(lane(first_hidden), grad_qkv_low, ((0,), (0,)))
    attention_grads = jnp.concatenate([qkv_grad.astype(bf16), output_grad.astype(bf16)], 1)
    attention_shard = lax.psum_scatter(
        attention_grads, ("dp", "expert"), scatter_dimension=0, tiled=True
    ).astype(f32)
    attention_gain_grad = jnp.sum(grad_hidden_one * normed_one, axis=0)
    tokens_grad = grad_mixed + norm_back(grad_hidden_one, normed_one, scale_one, gain_attention)
    tokens_grad = lane(tokens_grad)

    n_t = lax.axis_size("tensor")
    gain_grads = jnp.concatenate(
        [
            lane(attention_gain_grad) / n_t,
            lane(experts_gain_grad) / n_t,
            query_gain_grad,
            key_gain_grad,
        ]
    )
    gain_grads = lax.psum(gain_grads, ("dp", "expert", "tensor"))
    me = me_dp * n_ex + me_ex
    take = lambda start, size: lax.dynamic_slice_in_dim(gain_grads, start + me * size, size, 0)
    return (
        output,
        tokens_grad,
        take(0, na),
        attention_shard[:, :q_cols],
        attention_shard[:, q_cols : q_cols + k_cols],
        attention_shard[:, q_cols + k_cols : q_cols + 2 * k_cols],
        attention_shard[:, q_cols + 2 * k_cols :],
        take(2 * width, nq),
        take(2 * width + HEAD_SIZE, nq),
        take(width, na),
        gate_shard,
        up_shard,
        down_shard,
    )


def solution(mesh):
    both = ("dp", "expert")
    rows2, rows1, mats = P(both, None), P(both), P(both, "tensor")
    experts = P("expert", "tensor", "dp")
    return jax.shard_map(
        local,
        mesh=mesh,
        in_specs=(rows2, rows2, rows2, rows2, rows1, rows1, mats, mats, mats, mats, rows1, rows1, rows1)
        + (experts,) * 3,
        out_specs=(rows2, rows2, rows1, mats, mats, mats, mats, rows1, rows1, rows1) + (experts,) * 3,
        check_vma=False,
    )
```

```python
import jax
import jax.numpy as jnp
from jax import lax
from jax.experimental import pallas as pl
from jax.experimental.pallas import tpu as pltpu
from jax.sharding import PartitionSpec as P

HEAD_SIZE = 128
TOP = 8
epsilon = 1e-06
f32 = jnp.float32
bf16 = jnp.bfloat16
MESH = pl.DeviceIdType.MESH


def rms_scale(values):
    return lax.rsqrt(jnp.mean(values * values, axis=-1, keepdims=True) + epsilon)


def rope_tables(rows):
    half_dim = HEAD_SIZE // 2
    frequency = jnp.power(f32(1000000.0), -(jnp.arange(half_dim, dtype=f32) * (2.0 / HEAD_SIZE)))
    angles = jnp.arange(rows, dtype=f32)[:, None] * frequency[None, :]
    return (jnp.cos(angles)[:, None, :], jnp.sin(angles)[:, None, :])


def rotate(values, cosine_table, sine_table):
    half_dim = values.shape[-1] // 2
    first_half = values[..., :half_dim]
    second_half = values[..., half_dim:]
    return jnp.concatenate(
        [
            first_half * cosine_table - second_half * sine_table,
            second_half * cosine_table + first_half * sine_table,
        ],
        axis=-1,
    )


def norm_back(grad_hidden, normed, scales, gains):
    grad_normed = grad_hidden * gains
    return scales * (grad_normed - normed * jnp.mean(grad_normed * normed, axis=-1, keepdims=True))


def flip(x, axis, bit):
    n = lax.axis_size(axis)
    return lax.ppermute(x, axis, [(i, i ^ bit) for i in range(n)])


def bits_of(n):
    return [1 << b for b in range(n.bit_length() - 1)]


def xor_gather(x, axis):
    pieces = [x]
    for bit in bits_of(lax.axis_size(axis)):
        pieces = pieces + [flip(p, axis, bit) for p in pieces]
    return pieces


def xor_scatter(parts, axis):
    for bit in reversed(bits_of(lax.axis_size(axis))):
        got = [flip(p, axis, bit) for p in parts[bit:]]
        parts = [
            (a.astype(f32) + r.astype(f32)).astype(a.dtype) for a, r in zip(parts[:bit], got)
        ]
    return parts[0]


def dp_scatter(blocks, axis="dp"):
    n = len(blocks)
    if n != 4:
        return xor_scatter(blocks, axis).astype(f32)
    h = blocks[0].shape[0] // 2
    add = lambda p, q: p.astype(f32) + q.astype(f32)
    done = []
    for rows, first, second in ((slice(0, h), 1, 2), (slice(h, 2 * h), 2, 1)):
        b = [x[rows] for x in blocks]
        got = flip(jnp.concatenate([b[first], b[3]], 0), axis, first)
        on = add(b[second], got[h:]).astype(bf16)
        done.append(add(b[0], got[:h]) + flip(on, axis, second).astype(f32))
    return jnp.concatenate(done, 0)


def all_pieces(x, axis, me):
    got = jnp.stack(xor_gather(x, axis), 0)
    return lane_order(got, 0, got.shape[0], me)


def dp_gather(x, axis="dp"):
    n = lax.axis_size(axis)
    if n != 4:
        return xor_gather(x, axis)
    h = x.shape[0] // 2
    a, b = x[:h], x[h:]
    a1, b2 = flip(a, axis, 1), flip(b, axis, 2)
    a2, b1 = flip(a, axis, 2), flip(b, axis, 1)
    a3, b3 = flip(a1, axis, 2), flip(b2, axis, 1)
    cat = lambda p, q: jnp.concatenate([p, q], 0)
    return [cat(a, b), cat(a1, b1), cat(a2, b2), cat(a3, b3)]


def lane_block(x, axis, n, me, k):
    axis = axis % x.ndim
    size = x.shape[axis] // n
    return lax.dynamic_slice_in_dim(x, (me ^ k) * size, size, axis)


def lane_order(x, axis, n, me):
    return jnp.concatenate([lane_block(x, axis, n, me, k) for k in range(n)], axis)


def block_scores(query_block, key_rot, length):
    query_pos = jnp.arange(query_block.shape[0], dtype=jnp.int32)
    key_pos = jnp.arange(key_rot.shape[0], dtype=jnp.int32)
    allowed = (key_pos[None, :] <= query_pos[:, None]) & (key_pos[None, :] < length)
    scores = jnp.einsum(
        "qkgd,skd->kgqs", query_block, key_rot, preferred_element_type=f32
    ) * HEAD_SIZE ** (-0.5)
    return jnp.where(allowed, scores, -1e30)


def core_rows(pieces, axis="expert"):
    n = lax.axis_size(axis)
    own = jnp.stack(pieces, 0)
    if n == 2:
        other = flip(own, axis, 1)
        first = lax.axis_index(axis) == 0
        both = jnp.stack([jnp.where(first, own, other), jnp.where(first, other, own)], 1)
    else:
        both = lax.all_gather(own, axis, axis=1, tiled=False)
    return both.reshape((-1,) + own.shape[2:])


def dotf(a, b, dims):
    return lax.dot_general(a, b, (dims, ((), ())), preferred_element_type=f32)


def local_plain(
    tokens,
    cotangent,
    route_ids,
    route_weight,
    lengths,
    attention_norm,
    query_weight,
    key_matrix,
    value_matrix,
    output_weight,
    query_norm,
    key_norm,
    experts_norm,
    gate_weight,
    up_weight,
    down_weight,
):
    n_dp = lax.axis_size("dp")
    n_ex = lax.axis_size("expert")
    me_dp = lax.axis_index("dp")
    me_ex = lax.axis_index("expert")
    rows, width = tokens.shape
    group, hidden, part = gate_weight.shape
    length = lengths[0]
    lane = lambda x, axis=-1: lane_order(x, axis, n_dp, me_dp)

    qkv_own = jnp.concatenate([query_weight, key_matrix, value_matrix], 1)
    qkv_pieces = dp_gather(qkv_own)
    wo_own, qkv_pieces = lax.optimization_barrier((output_weight, qkv_pieces))
    wo_pieces = dp_gather(wo_own)
    (gw, uw, dw), wo_pieces = lax.optimization_barrier(
        ((gate_weight, up_weight, down_weight), wo_pieces)
    )
    flat = group * hidden
    gate_up_own = jnp.concatenate([gw.reshape(flat, part), uw.reshape(flat, part)], 0)
    gate_up_pieces = dp_gather(gate_up_own)
    down_own, gate_up_pieces = lax.optimization_barrier((dw.reshape(flat, part), gate_up_pieces))
    down_pieces = dp_gather(down_own)

    na, nq = attention_norm.shape[0], query_norm.shape[0]
    gains = jnp.concatenate([attention_norm, experts_norm, query_norm, key_norm])
    gains = jnp.pad(gains, (0, -gains.size % 128)).reshape(-1, 128)
    gains = all_pieces(all_pieces(gains, "expert", me_ex), "dp", me_dp)
    gains = gains.reshape(n_dp, n_ex, -1).astype(f32)
    gain_attention = lane(gains[:, :, :na].reshape(-1))
    gain_experts = lane(gains[:, :, na : 2 * na].reshape(-1))
    gain_query = gains[:, :, 2 * na : 2 * na + nq].reshape(-1)
    gain_key = gains[:, :, 2 * na + nq : 2 * na + 2 * nq].reshape(-1)

    experts = jnp.arange(group * n_ex, dtype=jnp.int32)
    table = jnp.zeros((rows, group * n_ex), f32)
    for c in range(route_ids.shape[1]):
        table = table + jnp.where(
            route_ids[:, c, None] == experts[None, :], route_weight[:, c, None], 0.0
        )
    table = jnp.concatenate(xor_gather(table, "expert"), 0)
    mine = lax.dynamic_slice_in_dim(table, me_ex * group, group, 1)
    unit_expert = jnp.arange(flat, dtype=jnp.int32) // hidden
    route_scale = jnp.zeros((table.shape[0], flat), f32)
    for j in range(group):
        route_scale = route_scale + jnp.where(unit_expert[None, :] == j, mine[:, j, None], 0.0)

    cosine_table, sine_table = rope_tables(rows)
    inputs = lane(tokens.astype(f32))
    scale_one = rms_scale(inputs)
    normed_one = inputs * scale_one
    first_hidden = (normed_one * gain_attention).astype(bf16)
    upstream_low = lane(cotangent)
    upstream_all = jnp.concatenate(xor_gather(upstream_low, "expert"), 0)

    full_qkv = core_rows(qkv_pieces)
    qkv = jnp.dot(first_hidden, full_qkv, preferred_element_type=f32)
    q_cols, k_cols = query_weight.shape[1], key_matrix.shape[1]
    heads_query, heads_key = q_cols // HEAD_SIZE, k_cols // HEAD_SIZE
    per_group = heads_query // heads_key
    query_raw = qkv[:, :q_cols].reshape(rows, heads_query, HEAD_SIZE)
    key_raw = qkv[:, q_cols : q_cols + k_cols].reshape(rows, heads_key, HEAD_SIZE)
    value_low = qkv[:, q_cols + k_cols :].astype(bf16).reshape(rows, heads_key, HEAD_SIZE)
    scale_query = rms_scale(query_raw)
    normed_query = query_raw * scale_query
    rotated_query = (
        rotate(normed_query * gain_query, cosine_table, sine_table)
        .astype(bf16)
        .reshape(rows, heads_key, per_group, HEAD_SIZE)
    )
    scale_key = rms_scale(key_raw)
    normed_key = key_raw * scale_key
    key_rot = rotate(normed_key * gain_key, cosine_table, sine_table).astype(bf16)
    scores = block_scores(rotated_query, key_rot, length)
    row_peak = jnp.max(scores, axis=-1, keepdims=True)
    shifted = jnp.exp(scores - row_peak)
    totals = jnp.sum(shifted, axis=-1, keepdims=True)
    probs = shifted / totals
    prob_low = probs.astype(bf16)
    attended_low = (
        jnp.einsum("kgqs,skd->qkgd", prob_low, value_low, preferred_element_type=f32)
        .reshape(rows, q_cols)
        .astype(bf16)
    )
    full_output = core_rows(wo_pieces)
    projected = dotf(attended_low, full_output, ((1,), (1,)))
    mixed_rows = inputs + lax.psum(projected.astype(bf16), "tensor").astype(f32)
    scale_two = rms_scale(mixed_rows)
    normed_two = mixed_rows * scale_two
    hidden_two = (normed_two * gain_experts).astype(bf16)

    hidden_all = jnp.concatenate(xor_gather(hidden_two, "expert"), 0)
    gate_up_full = jnp.concatenate(gate_up_pieces, 1)
    down_full = jnp.concatenate(down_pieces, 1)
    gate_up = dotf(hidden_all, gate_up_full, ((1,), (1,)))
    gate_value, up_value = gate_up[:, :flat], gate_up[:, flat:]
    grad_act = lax.optimization_barrier(dotf(upstream_all, down_full, ((1,), (1,)))) * route_scale
    sigmoid_gate = jax.nn.sigmoid(gate_value)
    scaled_act = (gate_value * sigmoid_gate * up_value * route_scale).astype(bf16)
    grad_up_low = (grad_act * gate_value * sigmoid_gate).astype(bf16)
    grad_gate_low = (
        grad_act * up_value * sigmoid_gate * (1.0 + gate_value * (1.0 - sigmoid_gate))
    ).astype(bf16)
    grad_gate_up = jnp.concatenate([grad_gate_low, grad_up_low], 1)
    grad_rows = jnp.dot(grad_gate_up, gate_up_full, preferred_element_type=f32).astype(bf16)
    grad_hidden_two = xor_scatter(jnp.split(grad_rows, n_ex, 0), "expert")
    grad_hidden_two = lax.psum(grad_hidden_two, "tensor")

    expert_out = jnp.dot(scaled_act, down_full, preferred_element_type=f32).astype(bf16)
    combined = xor_scatter(jnp.split(expert_out, n_ex, 0), "expert")
    def expert_grad(low, acts):
        return dotf(low, acts, ((0,), (0,))).astype(bf16)

    grads = [
        expert_grad(scaled_act, upstream_all),
        expert_grad(grad_gate_low, hidden_all),
        expert_grad(grad_up_low, hidden_all),
    ]
    grad_hidden_two, grads = lax.optimization_barrier((grad_hidden_two, grads))
    down_shard, gate_shard, up_shard = (
        dp_scatter(jnp.split(g, n_dp, 1)).reshape(group, hidden, part) for g in grads
    )
    combined, grad_hidden_two = lax.optimization_barrier((combined, grad_hidden_two))
    combined = lax.psum(combined, "tensor")
    output = lane((mixed_rows + combined.astype(f32)).astype(bf16))
    grad_hidden_two = grad_hidden_two.astype(f32)

    def attention_scatter(grad):
        grad = grad.reshape(n_dp, n_ex, width // (n_dp * n_ex), grad.shape[1])
        if n_ex == 2:
            away = lax.dynamic_index_in_dim(grad, 1 - me_ex, 1, keepdims=False)
            own = lax.dynamic_index_in_dim(grad, me_ex, 1, keepdims=False)
            grad = (own.astype(f32) + flip(away, "expert", 1).astype(f32)).astype(bf16)
        else:
            grad = lax.psum_scatter(grad, "expert", scatter_dimension=1, tiled=False)
        return dp_scatter(list(grad))

    upstream = upstream_low.astype(f32)
    experts_gain_grad = jnp.sum(grad_hidden_two * normed_two, axis=0)
    grad_mixed = upstream + norm_back(grad_hidden_two, normed_two, scale_two, gain_experts)
    grad_proj_low = grad_mixed.astype(bf16)
    grad_att_low = (
        jnp.dot(grad_proj_low, full_output, preferred_element_type=f32)
        .astype(bf16)
        .reshape(rows, heads_key, per_group, HEAD_SIZE)
    )
    output_grad = dotf(grad_proj_low, attended_low, ((0,), (0,))).astype(bf16)
    output_shard = attention_scatter(output_grad)
    grad_probs = jnp.einsum("qkgd,skd->kgqs", grad_att_low, value_low, preferred_element_type=f32)
    row_dot = jnp.sum(probs * grad_probs, axis=-1, keepdims=True)
    grad_scores = (probs * (grad_probs - row_dot)).astype(bf16)
    grad_value = jnp.einsum("kgqs,qkgd->skd", prob_low, grad_att_low, preferred_element_type=f32)
    grad_qrot = jnp.einsum(
        "kgqs,skd->qkgd", grad_scores, key_rot, preferred_element_type=f32
    ) * HEAD_SIZE ** (-0.5)
    grad_krot = jnp.einsum(
        "kgqs,qkgd->skd", grad_scores, rotated_query, preferred_element_type=f32
    ) * HEAD_SIZE ** (-0.5)
    grad_qrot = grad_qrot.reshape(rows, heads_query, HEAD_SIZE)
    grad_query_normed = rotate(grad_qrot, cosine_table, -sine_table)
    query_gain_grad = jnp.sum(grad_query_normed * normed_query, axis=(0, 1))
    grad_query_low = (
        norm_back(grad_query_normed, normed_query, scale_query, gain_query)
        .astype(bf16)
        .reshape(rows, q_cols)
    )
    grad_key_normed = rotate(grad_krot, cosine_table, -sine_table)
    key_gain_grad = jnp.sum(grad_key_normed * normed_key, axis=(0, 1))
    grad_key_low = (
        norm_back(grad_key_normed, normed_key, scale_key, gain_key).astype(bf16).reshape(rows, k_cols)
    )
    grad_value_low = grad_value.astype(bf16).reshape(rows, k_cols)
    grad_qkv_low = jnp.concatenate([grad_query_low, grad_key_low, grad_value_low], 1)
    grad_hidden_one = dotf(grad_qkv_low, full_qkv, ((1,), (1,)))
    head_gain_grads = jnp.stack([query_gain_grad, key_gain_grad]).astype(bf16)
    grad_hidden_one, head_gain_grads, _ = lax.optimization_barrier(
        (grad_hidden_one.astype(bf16), head_gain_grads, combined)
    )
    grad_hidden_one, head_gain_grads = lax.psum((grad_hidden_one, head_gain_grads), "tensor")
    grad_hidden_one = grad_hidden_one.astype(f32)
    qkv_grad = dotf(first_hidden, grad_qkv_low, ((0,), (0,))).astype(bf16)
    qkv_shard = attention_scatter(qkv_grad)
    attention_gain_grad = jnp.sum(grad_hidden_one * normed_one, axis=0)
    tokens_grad = grad_mixed + norm_back(grad_hidden_one, normed_one, scale_one, gain_attention)
    tokens_grad = lane(tokens_grad)

    blocks = lambda v: v.reshape(n_dp, n_ex, -1)
    gain_grads = jnp.concatenate(
        [
            blocks(attention_gain_grad),
            blocks(experts_gain_grad),
            lane(blocks(head_gain_grads[0].astype(f32)), 0),
            lane(blocks(head_gain_grads[1].astype(f32)), 0),
        ],
        2,
    )
    gain_grads = lane_order(gain_grads, 1, n_ex, me_ex)
    gain_grads = jnp.pad(gain_grads, ((0, 0), (0, 0), (0, -gain_grads.shape[2] % 128)))
    gain_grads = gain_grads.reshape(n_dp, n_ex, -1, 128)
    gain_grads = xor_scatter([gain_grads[:, k] for k in range(n_ex)], "expert")
    gain_grads = xor_scatter([gain_grads[k] for k in range(n_dp)], "dp").reshape(-1)
    take = lambda start, size: gain_grads[start : start + size]
    return (
        output,
        tokens_grad,
        take(0, na),
        qkv_shard[:, :q_cols],
        qkv_shard[:, q_cols : q_cols + k_cols],
        qkv_shard[:, q_cols + k_cols :],
        output_shard,
        take(2 * na, nq),
        take(2 * na + nq, nq),
        take(na, na),
        gate_shard,
        up_shard,
        down_shard,
    )


CHUNKS = 16


def line_roles(axis):
    p = lax.axis_index(axis)
    return p + 1 - 2 * (p % 2), 3 - p, (p + 1) // 2 == 1


def over(n, f, start=0):
    lax.fori_loop(start, n, lambda c, t: (f(c), t)[1], 0)


def line_sum_steps(x_ref, in_buf, mid_buf, part, out_ref, sems, axis, finish, lag=2):
    a_send, a_recv, b_send, b_recv, c_send, c_recv = sems
    side, mid, inner = line_roles(axis)
    step = x_ref.shape[0] // CHUNKS

    def rows(c):
        return pl.ds(pl.multiple_of(c * step, step), step)

    def copy(src, dst, c, send, recv, to):
        return pltpu.make_async_remote_copy(
            src.at[rows(c)], dst.at[rows(c)], send.at[c], recv.at[c], device_id={axis: to}, device_id_type=MESH
        )

    to_inner = lambda c: copy(x_ref, in_buf, c, a_send, a_recv, side)
    to_middle = lambda c: copy(part, mid_buf, c, b_send, b_recv, mid)
    to_outer = lambda c: copy(out_ref, out_ref, c, c_send, c_recv, side)

    @pl.when(jnp.logical_not(inner))
    def _():
        over(CHUNKS, lambda c: to_inner(c).start())

        def done(c):
            to_outer(c).wait_recv()
            finish(rows(c), c)
            to_inner(c).wait_send()

        over(CHUNKS, done)

    @pl.when(inner)
    def _():
        def first(c):
            to_inner(c).wait_recv()
            r = rows(c)
            part[r] = (x_ref[r].astype(f32) + in_buf[r].astype(f32)).astype(bf16)
            to_middle(c).start()

        def second(c):
            to_middle(c).wait_recv()
            r = rows(c)
            out_ref[r] = (part[r].astype(f32) + mid_buf[r].astype(f32)).astype(bf16)
            to_outer(c).start()
            finish(r, c)

        over(lag, first)
        over(CHUNKS - lag, lambda c: (first(c + lag), second(c))[0])
        over(CHUNKS, second, CHUNKS - lag)

        def done(c):
            to_middle(c).wait_send()
            to_outer(c).wait_send()

        over(CHUNKS, done)


def line_sems():
    return [pltpu.SemaphoreType.DMA((CHUNKS,))] * 6


def plane_partners():
    d, c = lax.axis_index("dp"), lax.axis_index("expert")
    ds = {0: d, 1: d + 1 - 2 * (d % 2), 2: d + 2 - 4 * (d // 2), 3: 3 - d}
    cs = {0: c, 1: 1 - c}
    return {(kd, kc): {"dp": ds[kd], "expert": cs[kc]} for kd in ds for kc in cs}


def remote(src, dst, send, recv, to):
    return pltpu.make_async_remote_copy(src, dst, send, recv, device_id=to, device_id_type=MESH)


def nt(a, b):
    return lax.dot_general(a, b, (((1,), (1,)), ((), ())), preferred_element_type=f32)


def nn(a, b):
    return lax.dot_general(a, b, (((1,), (0,)), ((), ())), preferred_element_type=f32)


def tn(a, b):
    return lax.dot_general(a, b, (((0,), (0,)), ((), ())), preferred_element_type=f32)


def forward_kernel(
    tokens, qkv_own, wo_own, gate_own, up_own, down_own, gains_own, cos, sin, key_ok,
    x2, h2, att, qrot, krot, value, raw, probs, gains, gate, up, down, qkv_out, wo_out,
    qkv, wo, h1, proj, in_buf, mid_buf, part, summed, gain_rows,
    w_send, w_recv, core_send, core_recv, g_send, g_recv, h_send, h_recv, own_sem, out_sem, *line,
):
    c = lax.axis_index("expert")
    to = plane_partners()
    side, mid, inner = line_roles("tensor")
    barrier = pltpu.get_barrier_semaphore()
    others = [k for k in to if k != (0, 0)]
    for k in others:
        pl.semaphore_signal(barrier, inc=1, device_id=to[k], device_id_type=MESH)
    pl.semaphore_signal(barrier, inc=1, device_id={"tensor": side}, device_id_type=MESH)

    @pl.when(inner)
    def _():
        pl.semaphore_signal(barrier, inc=1, device_id={"tensor": mid}, device_id_type=MESH)
        pl.semaphore_wait(barrier, len(others) + 2)

    @pl.when(jnp.logical_not(inner))
    def _():
        pl.semaphore_wait(barrier, len(others) + 1)

    rows, width = tokens.shape
    piece = qkv_own.shape[0]
    half = piece // 2
    tall = gate_own.shape[0] // 2
    wide = gate_own.shape[1]

    def small_slot(full):
        return lambda k, h: full.at[pl.ds(pl.multiple_of((k * 2 + c) * piece + h * half, half), half)]

    def big_slot(full):
        return lambda k, h: full.at[pl.ds(h * tall, tall), pl.ds(k * wide, wide)]

    mats = [
        (lambda h: qkv_own.at[pl.ds(h * half, half)], small_slot(qkv)),
        (lambda h: wo_own.at[pl.ds(h * half, half)], small_slot(wo)),
    ] + [
        (lambda h, own=own: own.at[pl.ds(h * tall, tall)], big_slot(full))
        for own, full in ((gate_own, gate), (up_own, up), (down_own, down))
    ]

    def move(m, i):
        own, slot = mats[m]
        src, dst, way = (
            (own(0), slot(1, 0), 1), (own(1), slot(2, 1), 2), (own(0), slot(2, 0), 2), (own(1), slot(1, 1), 1),
            (slot(1, 0), slot(3, 0), 2), (slot(2, 1), slot(3, 1), 1),
        )[i]
        return remote(src, dst, w_send.at[m, i], w_recv.at[m, i], to[way, 0])

    def begin(m):
        for i in range(4):
            move(m, i).start()

    def pass_on(m):
        for i in (0, 1):
            move(m, i).wait_recv()
            move(m, 4 + i).start()

    def arrived(m):
        for i in (2, 3, 4, 5):
            move(m, i).wait_recv()

    def core_move(m, k):
        full = (qkv, wo)[m]
        block = full.at[pl.ds(pl.multiple_of((k * 2 + c) * piece, piece), piece)]
        return remote(block, block, core_send.at[m, k], core_recv.at[m, k], to[0, 1])

    def gain_move(j):
        kd, kc = others[j]
        return remote(gains_own, gains.at[kd, c], g_send.at[j], g_recv.at[j], to[kd, kc])

    own_copies = [
        pltpu.make_async_copy(qkv_own, qkv.at[pl.ds(pl.multiple_of(c * piece, piece), piece)], own_sem.at[0]),
        pltpu.make_async_copy(wo_own, wo.at[pl.ds(pl.multiple_of(c * piece, piece), piece)], own_sem.at[1]),
    ] + [
        pltpu.make_async_copy(own, full.at[:, pl.ds(0, wide)], own_sem.at[2 + i])
        for i, (own, full) in enumerate(((gate_own, gate), (up_own, up), (down_own, down)))
    ]

    begin(0)
    for j in range(len(others)):
        gain_move(j).start()
    own_copies[0].start()
    own_copies[1].start()
    gains[pl.ds(0, 1), pl.ds(c, 1)] = gains_own[...].reshape(1, 1, 8, 128)
    own_copies[0].wait()
    core_move(0, 0).start()
    own_copies[1].wait()
    core_move(1, 0).start()
    for j in range(len(others)):
        gain_move(j).wait_recv()
    for kd in range(4):
        for kc in range(2):
            g = gains[kd, kc]
            for j in range(2):
                col = (kd * 2 + kc) * 256 + j * 128
                gain_rows[0:1, col : col + 128] = g[j : j + 1]
                gain_rows[1:2, col : col + 128] = g[2 + j : 3 + j]
    heads = jnp.sum(gains[...].reshape(8, 8, 128), axis=0)
    gain_query, gain_key = heads[4:5], heads[5:6]

    def hidden_one(i):
        r = pl.ds(pl.multiple_of(i * 64, 64), 64)
        x = tokens[r].astype(f32)
        scale = lax.rsqrt(jnp.mean(x * x, axis=-1, keepdims=True) + epsilon)
        h1[r] = (x * scale * gain_rows[0:1]).astype(bf16)

    over(rows // 64, hidden_one)

    pass_on(0)
    begin(1)
    for k, waits in ((1, (3,)), (2, (2,)), (3, (4, 5))):
        for i in waits:
            move(0, i).wait_recv()
        core_move(0, k).start()
    pass_on(1)
    for m in (2, 3, 4):
        begin(m)
        own_copies[m].start()
    for k in range(4):
        core_move(0, k).wait_recv()
    save_qkv = pltpu.make_async_copy(qkv, qkv_out, out_sem.at[0])
    save_qkv.start()

    def project(j):
        col = pl.ds(pl.multiple_of(j * 256, 256), 256)
        raw[:, col] = nn(h1[...], qkv[:, col])

    over(qkv.shape[1] // 256, project)
    q_cols = att.shape[1]

    def spin(u):
        return u * cos[...] + pltpu.roll(u, 64, 1) * sin[...]

    def unit(u):
        return u * lax.rsqrt(jnp.mean(u * u, axis=-1, keepdims=True) + epsilon)

    krot[...] = spin(unit(raw[:, pl.ds(q_cols, 128)]) * gain_key).astype(bf16)
    value[...] = raw[:, pl.ds(q_cols + 128, 128)].astype(bf16)
    block = rows // 2

    def head(h):
        col = pl.ds(pl.multiple_of(h * 128, 128), 128)
        qrot[:, col] = spin(unit(raw[:, col]) * gain_query).astype(bf16)
        for i in range(2):
            r, n = slice(i * block, (i + 1) * block), (i + 1) * block
            s = nt(qrot[r, col], krot[0:n]) * 128 ** (-0.5)
            row = lax.broadcasted_iota(jnp.int32, (block, n), 0) + i * block
            key = lax.broadcasted_iota(jnp.int32, (block, n), 1)
            s = jnp.where((key <= row) & (key_ok[:, 0:n] > 0), s, -1e30)
            e = jnp.exp(s - jnp.max(s, axis=-1, keepdims=True))
            p = (e / jnp.sum(e, axis=-1, keepdims=True)).astype(bf16)
            probs[h, r, 0:n] = p
            att[r, col] = nn(p, value[0:n]).astype(bf16)
        probs[h, 0:block, block:] = jnp.zeros((block, block), bf16)

    over(q_cols // 128, head)

    for k, waits in ((1, (3,)), (2, (2,)), (3, (4, 5))):
        for i in waits:
            move(1, i).wait_recv()
        core_move(1, k).start()
    for k in range(4):
        core_move(1, k).wait_recv()
    save_wo = pltpu.make_async_copy(wo, wo_out, out_sem.at[1])
    save_wo.start()

    def out_project(j):
        r = pl.ds(pl.multiple_of(j * 256, 256), 256)
        proj[:, r] = nt(att[...], wo[r]).astype(bf16)

    over(width // 256, out_project)
    pass_on(2)

    def give(i):
        n = rows // CHUNKS
        src = h2.at[pl.ds(pl.multiple_of(i * n, n), n)]
        dst = h2.at[pl.ds(pl.multiple_of(rows + i * n, n), n)]
        return remote(src, dst, h_send.at[i], h_recv.at[i], to[0, 1])

    def finish(r, i):
        mixed = tokens[r].astype(f32) + summed[r].astype(f32)
        x2[r] = mixed
        scale = lax.rsqrt(jnp.mean(mixed * mixed, axis=-1, keepdims=True) + epsilon)
        h2[r] = (mixed * scale * gain_rows[1:2]).astype(bf16)
        give(i).start()

    line_sum_steps(proj, in_buf, mid_buf, part, summed, line, "tensor", finish)
    pass_on(3)
    pass_on(4)
    over(CHUNKS, lambda i: give(i).wait())
    for m in (2, 3, 4):
        arrived(m)
        own_copies[m].wait()
    save_qkv.wait()
    save_wo.wait()
    for m in range(5):
        for i in range(6):
            move(m, i).wait_send()
    for m in range(2):
        for k in range(4):
            core_move(m, k).wait_send()
    for j in range(len(others)):
        gain_move(j).wait_send()


def forward_call(tokens, qkv_own, wo_own, gate_own, up_own, down_own, gains_own, cos, sin, key_ok):
    rows, width = tokens.shape
    qkv_cols, q_cols = qkv_own.shape[1], wo_own.shape[1]
    tall = gate_own.shape[0]
    vmem, anyspace = pl.BlockSpec(memory_space=pltpu.VMEM), pl.BlockSpec(memory_space=pl.ANY)
    shape = jax.ShapeDtypeStruct
    outs = [
        (shape((rows, width), f32), vmem),
        (shape((2 * rows, width), bf16), vmem),
        (shape((rows, q_cols), bf16), vmem),
        (shape((rows, q_cols), bf16), vmem),
        (shape((rows, 128), bf16), vmem),
        (shape((rows, 128), bf16), vmem),
        (shape((rows, qkv_cols), f32), vmem),
        (shape((q_cols // 128, rows, rows), bf16), vmem),
        (shape((4, 2, 8, 128), f32), vmem),
        (shape((tall, width), bf16), anyspace),
        (shape((tall, width), bf16), anyspace),
        (shape((tall, width), bf16), anyspace),
        (shape((width, qkv_cols), bf16), anyspace),
        (shape((width, q_cols), bf16), anyspace),
    ]
    dma = pltpu.SemaphoreType.DMA
    big = pltpu.VMEM((rows, width), bf16)
    return pl.pallas_call(
        forward_kernel,
        out_shape=[o[0] for o in outs],
        in_specs=[vmem] + [anyspace] * 5 + [vmem] * 4,
        out_specs=[o[1] for o in outs],
        scratch_shapes=[
            pltpu.VMEM((width, qkv_cols), bf16),
            pltpu.VMEM((width, q_cols), bf16),
            big, big, big, big, big, big,
            pltpu.VMEM((2, width), f32),
            dma((5, 6)), dma((5, 6)), dma((2, 4)), dma((2, 4)), dma((7,)), dma((7,)),
            dma((CHUNKS,)), dma((CHUNKS,)), dma((5,)), dma((2,)),
        ] + line_sems(),
        compiler_params=pltpu.CompilerParams(
            collective_id=1, has_side_effects=True, vmem_limit_bytes=60 * 2**20
        ),
        cost_estimate=pl.CostEstimate(flops=8 * 10**9, bytes_accessed=60 * 10**6, transcendentals=2 * 10**6),
        name="forward_to_experts",
    )(tokens, qkv_own, wo_own, gate_own, up_own, down_own, gains_own, cos, sin, key_ok)


def local_fast(
    tokens,
    cotangent,
    route_ids,
    route_weight,
    lengths,
    attention_norm,
    query_weight,
    key_matrix,
    value_matrix,
    output_weight,
    query_norm,
    key_norm,
    experts_norm,
    gate_weight,
    up_weight,
    down_weight,
):
    n_dp = lax.axis_size("dp")
    n_ex = lax.axis_size("expert")
    me_dp = lax.axis_index("dp")
    me_ex = lax.axis_index("expert")
    rows, width = tokens.shape
    group, hidden, part = gate_weight.shape
    length = lengths[0]
    lane = lambda x, axis=-1: lane_order(x, axis, n_dp, me_dp)

    flat = group * hidden
    na, nq = attention_norm.shape[0], query_norm.shape[0]
    q_cols, k_cols = query_weight.shape[1], key_matrix.shape[1]
    heads_query, heads_key = q_cols // HEAD_SIZE, k_cols // HEAD_SIZE
    per_group = heads_query // heads_key
    own_place = (me_dp * n_ex + me_ex) * nq
    placed = lambda v: lax.dynamic_update_slice(jnp.zeros((128,), f32), v.astype(f32), (own_place,))
    gains_own = jnp.concatenate(
        [
            attention_norm.astype(f32).reshape(-1, 128),
            experts_norm.astype(f32).reshape(-1, 128),
            placed(query_norm)[None],
            placed(key_norm)[None],
            jnp.zeros((2, 128), f32),
        ],
        0,
    )
    cosine_table, sine_table = rope_tables(rows)
    cos2 = jnp.concatenate([cosine_table[:, 0], cosine_table[:, 0]], 1)
    sin2 = jnp.concatenate([-sine_table[:, 0], sine_table[:, 0]], 1)
    key_ok = (jnp.arange(rows, dtype=jnp.int32) < length).astype(f32)[None]
    inputs_low = lane(tokens)
    inputs = inputs_low.astype(f32)
    (
        mixed_rows, hidden_all, attended_low, rotated_query, key_rot, value_low, raw, prob_low,
        gains, gate_full, up_full, down_full, full_qkv, full_output,
    ) = forward_call(
        inputs_low,
        jnp.concatenate([query_weight, key_matrix, value_matrix], 1),
        output_weight,
        gate_weight.reshape(flat, part),
        up_weight.reshape(flat, part),
        down_weight.reshape(flat, part),
        gains_own,
        cos2,
        sin2,
        key_ok,
    )
    gain_attention = gains[:, :, 0:2].reshape(-1)
    gain_experts = gains[:, :, 2:4].reshape(-1)
    gain_query = jnp.sum(gains[:, :, 4], (0, 1))
    gain_key = jnp.sum(gains[:, :, 5], (0, 1))

    experts = jnp.arange(group * n_ex, dtype=jnp.int32)
    table = jnp.zeros((rows, group * n_ex), f32)
    for c in range(route_ids.shape[1]):
        table = table + jnp.where(
            route_ids[:, c, None] == experts[None, :], route_weight[:, c, None], 0.0
        )
    table = jnp.concatenate(xor_gather(table, "expert"), 0)
    mine = lax.dynamic_slice_in_dim(table, me_ex * group, group, 1)
    unit_expert = jnp.arange(flat, dtype=jnp.int32) // hidden
    route_scale = jnp.zeros((table.shape[0], flat), f32)
    for j in range(group):
        route_scale = route_scale + jnp.where(unit_expert[None, :] == j, mine[:, j, None], 0.0)

    scale_one = rms_scale(inputs)
    normed_one = inputs * scale_one
    first_hidden = (normed_one * gain_attention).astype(bf16)
    upstream_low = lane(cotangent)
    upstream_all = jnp.concatenate(xor_gather(upstream_low, "expert"), 0)

    query_raw = raw[:, :q_cols].reshape(rows, heads_query, HEAD_SIZE)
    key_raw = raw[:, q_cols : q_cols + k_cols].reshape(rows, heads_key, HEAD_SIZE)
    value_low = value_low.reshape(rows, heads_key, HEAD_SIZE)
    rotated_query = rotated_query.reshape(rows, heads_key, per_group, HEAD_SIZE)
    key_rot = key_rot.reshape(rows, heads_key, HEAD_SIZE)
    prob_low = prob_low[None]
    probs = prob_low.astype(f32)
    scale_query = rms_scale(query_raw)
    normed_query = query_raw * scale_query
    scale_key = rms_scale(key_raw)
    normed_key = key_raw * scale_key
    scale_two = rms_scale(mixed_rows)
    normed_two = mixed_rows * scale_two

    gate_value = dotf(hidden_all, gate_full, ((1,), (1,)))
    up_value = dotf(hidden_all, up_full, ((1,), (1,)))
    grad_act = lax.optimization_barrier(dotf(upstream_all, down_full, ((1,), (1,)))) * route_scale
    sigmoid_gate = jax.nn.sigmoid(gate_value)
    scaled_act = (gate_value * sigmoid_gate * up_value * route_scale).astype(bf16)
    grad_up_low = (grad_act * gate_value * sigmoid_gate).astype(bf16)
    grad_gate_low = (
        grad_act * up_value * sigmoid_gate * (1.0 + gate_value * (1.0 - sigmoid_gate))
    ).astype(bf16)
    grad_rows = jnp.dot(grad_gate_low, gate_full, preferred_element_type=f32)
    grad_rows = (grad_rows + jnp.dot(grad_up_low, up_full, preferred_element_type=f32)).astype(bf16)
    grad_hidden_two = xor_scatter(jnp.split(grad_rows, n_ex, 0), "expert")
    grad_hidden_two = lax.psum(grad_hidden_two, "tensor")

    expert_out = jnp.dot(scaled_act, down_full, preferred_element_type=f32).astype(bf16)
    combined = xor_scatter(jnp.split(expert_out, n_ex, 0), "expert")
    def expert_grad(low, acts):
        return dotf(low, acts, ((0,), (0,))).astype(bf16)

    grads = [
        expert_grad(scaled_act, upstream_all),
        expert_grad(grad_gate_low, hidden_all),
        expert_grad(grad_up_low, hidden_all),
    ]
    grad_hidden_two, grads = lax.optimization_barrier((grad_hidden_two, grads))
    down_shard, gate_shard, up_shard = (
        dp_scatter(jnp.split(g, n_dp, 1)).reshape(group, hidden, part) for g in grads
    )
    combined, grad_hidden_two = lax.optimization_barrier((combined, grad_hidden_two))
    combined = lax.psum(combined, "tensor")
    output = lane((mixed_rows + combined.astype(f32)).astype(bf16))
    grad_hidden_two = grad_hidden_two.astype(f32)

    def attention_scatter(grad):
        grad = grad.reshape(n_dp, n_ex, width // (n_dp * n_ex), grad.shape[1])
        if n_ex == 2:
            away = lax.dynamic_index_in_dim(grad, 1 - me_ex, 1, keepdims=False)
            own = lax.dynamic_index_in_dim(grad, me_ex, 1, keepdims=False)
            grad = (own.astype(f32) + flip(away, "expert", 1).astype(f32)).astype(bf16)
        else:
            grad = lax.psum_scatter(grad, "expert", scatter_dimension=1, tiled=False)
        return dp_scatter(list(grad))

    upstream = upstream_low.astype(f32)
    experts_gain_grad = jnp.sum(grad_hidden_two * normed_two, axis=0)
    grad_mixed = upstream + norm_back(grad_hidden_two, normed_two, scale_two, gain_experts)
    grad_proj_low = grad_mixed.astype(bf16)
    grad_att_low = (
        jnp.dot(grad_proj_low, full_output, preferred_element_type=f32)
        .astype(bf16)
        .reshape(rows, heads_key, per_group, HEAD_SIZE)
    )
    output_grad = dotf(grad_proj_low, attended_low, ((0,), (0,))).astype(bf16)
    output_shard = attention_scatter(output_grad)
    grad_probs = jnp.einsum("qkgd,skd->kgqs", grad_att_low, value_low, preferred_element_type=f32)
    row_dot = jnp.sum(probs * grad_probs, axis=-1, keepdims=True)
    grad_scores = (probs * (grad_probs - row_dot)).astype(bf16)
    grad_value = jnp.einsum("kgqs,qkgd->skd", prob_low, grad_att_low, preferred_element_type=f32)
    grad_qrot = jnp.einsum(
        "kgqs,skd->qkgd", grad_scores, key_rot, preferred_element_type=f32
    ) * HEAD_SIZE ** (-0.5)
    grad_krot = jnp.einsum(
        "kgqs,qkgd->skd", grad_scores, rotated_query, preferred_element_type=f32
    ) * HEAD_SIZE ** (-0.5)
    grad_qrot = grad_qrot.reshape(rows, heads_query, HEAD_SIZE)
    grad_query_normed = rotate(grad_qrot, cosine_table, -sine_table)
    query_gain_grad = jnp.sum(grad_query_normed * normed_query, axis=(0, 1))
    grad_query_low = (
        norm_back(grad_query_normed, normed_query, scale_query, gain_query)
        .astype(bf16)
        .reshape(rows, q_cols)
    )
    grad_key_normed = rotate(grad_krot, cosine_table, -sine_table)
    key_gain_grad = jnp.sum(grad_key_normed * normed_key, axis=(0, 1))
    grad_key_low = (
        norm_back(grad_key_normed, normed_key, scale_key, gain_key).astype(bf16).reshape(rows, k_cols)
    )
    grad_value_low = grad_value.astype(bf16).reshape(rows, k_cols)
    grad_qkv_low = jnp.concatenate([grad_query_low, grad_key_low, grad_value_low], 1)
    grad_hidden_one = dotf(grad_qkv_low, full_qkv, ((1,), (1,)))
    head_gain_grads = jnp.stack([query_gain_grad, key_gain_grad]).astype(bf16)
    grad_hidden_one, head_gain_grads, _ = lax.optimization_barrier(
        (grad_hidden_one.astype(bf16), head_gain_grads, combined)
    )
    grad_hidden_one, head_gain_grads = lax.psum((grad_hidden_one, head_gain_grads), "tensor")
    grad_hidden_one = grad_hidden_one.astype(f32)
    qkv_grad = dotf(first_hidden, grad_qkv_low, ((0,), (0,))).astype(bf16)
    qkv_shard = attention_scatter(qkv_grad)
    attention_gain_grad = jnp.sum(grad_hidden_one * normed_one, axis=0)
    tokens_grad = grad_mixed + norm_back(grad_hidden_one, normed_one, scale_one, gain_attention)
    tokens_grad = lane(tokens_grad)

    blocks = lambda v: v.reshape(n_dp, n_ex, -1)
    gain_grads = jnp.concatenate(
        [
            blocks(attention_gain_grad),
            blocks(experts_gain_grad),
            lane(blocks(head_gain_grads[0].astype(f32)), 0),
            lane(blocks(head_gain_grads[1].astype(f32)), 0),
        ],
        2,
    )
    gain_grads = lane_order(gain_grads, 1, n_ex, me_ex)
    gain_grads = jnp.pad(gain_grads, ((0, 0), (0, 0), (0, -gain_grads.shape[2] % 128)))
    gain_grads = gain_grads.reshape(n_dp, n_ex, -1, 128)
    gain_grads = xor_scatter([gain_grads[:, k] for k in range(n_ex)], "expert")
    gain_grads = xor_scatter([gain_grads[k] for k in range(n_dp)], "dp").reshape(-1)
    take = lambda start, size: gain_grads[start : start + size]
    return (
        output,
        tokens_grad,
        take(0, na),
        qkv_shard[:, :q_cols],
        qkv_shard[:, q_cols : q_cols + k_cols],
        qkv_shard[:, q_cols + k_cols :],
        output_shard,
        take(2 * na, nq),
        take(2 * na + nq, nq),
        take(na, na),
        gate_shard,
        up_shard,
        down_shard,
    )


def local(*args):
    sizes = [lax.axis_size(a) for a in ("dp", "expert", "tensor")]
    return local_fast(*args) if sizes == [4, 2, 4] else local_plain(*args)


def solution(mesh):
    both = ("dp", "expert")
    rows2, rows1, mats = P(both, None), P(both), P(both, "tensor")
    experts = P("expert", "tensor", "dp")
    return jax.shard_map(
        local,
        mesh=mesh,
        in_specs=(rows2, rows2, rows2, rows2, rows1, rows1, mats, mats, mats, mats, rows1, rows1, rows1)
        + (experts,) * 3,
        out_specs=(rows2, rows2, rows1, mats, mats, mats, mats, rows1, rows1, rows1) + (experts,) * 3,
        check_vma=False,
    )
```

```python
import jax
import jax.numpy as jnp
from jax import lax
from jax.experimental import pallas as pl
from jax.experimental.pallas import tpu as pltpu
from jax.sharding import PartitionSpec as P

HEAD_SIZE = 128
TOP = 8
epsilon = 1e-06
f32 = jnp.float32
bf16 = jnp.bfloat16
MESH = pl.DeviceIdType.MESH


def rms_scale(values):
    return lax.rsqrt(jnp.mean(values * values, axis=-1, keepdims=True) + epsilon)


def rope_tables(rows):
    half_dim = HEAD_SIZE // 2
    frequency = jnp.power(f32(1000000.0), -(jnp.arange(half_dim, dtype=f32) * (2.0 / HEAD_SIZE)))
    angles = jnp.arange(rows, dtype=f32)[:, None] * frequency[None, :]
    return (jnp.cos(angles)[:, None, :], jnp.sin(angles)[:, None, :])


def rotate(values, cosine_table, sine_table):
    half_dim = values.shape[-1] // 2
    first_half = values[..., :half_dim]
    second_half = values[..., half_dim:]
    return jnp.concatenate(
        [
            first_half * cosine_table - second_half * sine_table,
            second_half * cosine_table + first_half * sine_table,
        ],
        axis=-1,
    )


def norm_back(grad_hidden, normed, scales, gains):
    grad_normed = grad_hidden * gains
    return scales * (grad_normed - normed * jnp.mean(grad_normed * normed, axis=-1, keepdims=True))


def flip(x, axis, bit):
    n = lax.axis_size(axis)
    return lax.ppermute(x, axis, [(i, i ^ bit) for i in range(n)])


def bits_of(n):
    return [1 << b for b in range(n.bit_length() - 1)]


def xor_gather(x, axis):
    pieces = [x]
    for bit in bits_of(lax.axis_size(axis)):
        pieces = pieces + [flip(p, axis, bit) for p in pieces]
    return pieces


def xor_scatter(parts, axis):
    for bit in reversed(bits_of(lax.axis_size(axis))):
        got = [flip(p, axis, bit) for p in parts[bit:]]
        parts = [
            (a.astype(f32) + r.astype(f32)).astype(a.dtype) for a, r in zip(parts[:bit], got)
        ]
    return parts[0]


def dp_scatter(blocks, axis="dp"):
    n = len(blocks)
    if n != 4:
        return xor_scatter(blocks, axis).astype(f32)
    h = blocks[0].shape[0] // 2
    add = lambda p, q: p.astype(f32) + q.astype(f32)
    done = []
    for rows, first, second in ((slice(0, h), 1, 2), (slice(h, 2 * h), 2, 1)):
        b = [x[rows] for x in blocks]
        got = flip(jnp.concatenate([b[first], b[3]], 0), axis, first)
        on = add(b[second], got[h:]).astype(bf16)
        done.append(add(b[0], got[:h]) + flip(on, axis, second).astype(f32))
    return jnp.concatenate(done, 0)


def all_pieces(x, axis, me):
    got = jnp.stack(xor_gather(x, axis), 0)
    return lane_order(got, 0, got.shape[0], me)


def dp_gather(x, axis="dp"):
    n = lax.axis_size(axis)
    if n != 4:
        return xor_gather(x, axis)
    h = x.shape[0] // 2
    a, b = x[:h], x[h:]
    a1, b2 = flip(a, axis, 1), flip(b, axis, 2)
    a2, b1 = flip(a, axis, 2), flip(b, axis, 1)
    a3, b3 = flip(a1, axis, 2), flip(b2, axis, 1)
    cat = lambda p, q: jnp.concatenate([p, q], 0)
    return [cat(a, b), cat(a1, b1), cat(a2, b2), cat(a3, b3)]


def lane_block(x, axis, n, me, k):
    axis = axis % x.ndim
    size = x.shape[axis] // n
    return lax.dynamic_slice_in_dim(x, (me ^ k) * size, size, axis)


def lane_order(x, axis, n, me):
    return jnp.concatenate([lane_block(x, axis, n, me, k) for k in range(n)], axis)


def block_scores(query_block, key_rot, length):
    query_pos = jnp.arange(query_block.shape[0], dtype=jnp.int32)
    key_pos = jnp.arange(key_rot.shape[0], dtype=jnp.int32)
    allowed = (key_pos[None, :] <= query_pos[:, None]) & (key_pos[None, :] < length)
    scores = jnp.einsum(
        "qkgd,skd->kgqs", query_block, key_rot, preferred_element_type=f32
    ) * HEAD_SIZE ** (-0.5)
    return jnp.where(allowed, scores, -1e30)


def core_rows(pieces, axis="expert"):
    n = lax.axis_size(axis)
    own = jnp.stack(pieces, 0)
    if n == 2:
        other = flip(own, axis, 1)
        first = lax.axis_index(axis) == 0
        both = jnp.stack([jnp.where(first, own, other), jnp.where(first, other, own)], 1)
    else:
        both = lax.all_gather(own, axis, axis=1, tiled=False)
    return both.reshape((-1,) + own.shape[2:])


def dotf(a, b, dims):
    return lax.dot_general(a, b, (dims, ((), ())), preferred_element_type=f32)


def local_plain(
    tokens,
    cotangent,
    route_ids,
    route_weight,
    lengths,
    attention_norm,
    query_weight,
    key_matrix,
    value_matrix,
    output_weight,
    query_norm,
    key_norm,
    experts_norm,
    gate_weight,
    up_weight,
    down_weight,
):
    n_dp = lax.axis_size("dp")
    n_ex = lax.axis_size("expert")
    me_dp = lax.axis_index("dp")
    me_ex = lax.axis_index("expert")
    rows, width = tokens.shape
    group, hidden, part = gate_weight.shape
    length = lengths[0]
    lane = lambda x, axis=-1: lane_order(x, axis, n_dp, me_dp)

    qkv_own = jnp.concatenate([query_weight, key_matrix, value_matrix], 1)
    qkv_pieces = dp_gather(qkv_own)
    wo_own, qkv_pieces = lax.optimization_barrier((output_weight, qkv_pieces))
    wo_pieces = dp_gather(wo_own)
    (gw, uw, dw), wo_pieces = lax.optimization_barrier(
        ((gate_weight, up_weight, down_weight), wo_pieces)
    )
    flat = group * hidden
    gate_up_own = jnp.concatenate([gw.reshape(flat, part), uw.reshape(flat, part)], 0)
    gate_up_pieces = dp_gather(gate_up_own)
    down_own, gate_up_pieces = lax.optimization_barrier((dw.reshape(flat, part), gate_up_pieces))
    down_pieces = dp_gather(down_own)

    na, nq = attention_norm.shape[0], query_norm.shape[0]
    gains = jnp.concatenate([attention_norm, experts_norm, query_norm, key_norm])
    gains = jnp.pad(gains, (0, -gains.size % 128)).reshape(-1, 128)
    gains = all_pieces(all_pieces(gains, "expert", me_ex), "dp", me_dp)
    gains = gains.reshape(n_dp, n_ex, -1).astype(f32)
    gain_attention = lane(gains[:, :, :na].reshape(-1))
    gain_experts = lane(gains[:, :, na : 2 * na].reshape(-1))
    gain_query = gains[:, :, 2 * na : 2 * na + nq].reshape(-1)
    gain_key = gains[:, :, 2 * na + nq : 2 * na + 2 * nq].reshape(-1)

    experts = jnp.arange(group * n_ex, dtype=jnp.int32)
    table = jnp.zeros((rows, group * n_ex), f32)
    for c in range(route_ids.shape[1]):
        table = table + jnp.where(
            route_ids[:, c, None] == experts[None, :], route_weight[:, c, None], 0.0
        )
    table = jnp.concatenate(xor_gather(table, "expert"), 0)
    mine = lax.dynamic_slice_in_dim(table, me_ex * group, group, 1)
    unit_expert = jnp.arange(flat, dtype=jnp.int32) // hidden
    route_scale = jnp.zeros((table.shape[0], flat), f32)
    for j in range(group):
        route_scale = route_scale + jnp.where(unit_expert[None, :] == j, mine[:, j, None], 0.0)

    cosine_table, sine_table = rope_tables(rows)
    inputs = lane(tokens.astype(f32))
    scale_one = rms_scale(inputs)
    normed_one = inputs * scale_one
    first_hidden = (normed_one * gain_attention).astype(bf16)
    upstream_low = lane(cotangent)
    upstream_all = jnp.concatenate(xor_gather(upstream_low, "expert"), 0)

    full_qkv = core_rows(qkv_pieces)
    qkv = jnp.dot(first_hidden, full_qkv, preferred_element_type=f32)
    q_cols, k_cols = query_weight.shape[1], key_matrix.shape[1]
    heads_query, heads_key = q_cols // HEAD_SIZE, k_cols // HEAD_SIZE
    per_group = heads_query // heads_key
    query_raw = qkv[:, :q_cols].reshape(rows, heads_query, HEAD_SIZE)
    key_raw = qkv[:, q_cols : q_cols + k_cols].reshape(rows, heads_key, HEAD_SIZE)
    value_low = qkv[:, q_cols + k_cols :].astype(bf16).reshape(rows, heads_key, HEAD_SIZE)
    scale_query = rms_scale(query_raw)
    normed_query = query_raw * scale_query
    rotated_query = (
        rotate(normed_query * gain_query, cosine_table, sine_table)
        .astype(bf16)
        .reshape(rows, heads_key, per_group, HEAD_SIZE)
    )
    scale_key = rms_scale(key_raw)
    normed_key = key_raw * scale_key
    key_rot = rotate(normed_key * gain_key, cosine_table, sine_table).astype(bf16)
    scores = block_scores(rotated_query, key_rot, length)
    row_peak = jnp.max(scores, axis=-1, keepdims=True)
    shifted = jnp.exp(scores - row_peak)
    totals = jnp.sum(shifted, axis=-1, keepdims=True)
    probs = shifted / totals
    prob_low = probs.astype(bf16)
    attended_low = (
        jnp.einsum("kgqs,skd->qkgd", prob_low, value_low, preferred_element_type=f32)
        .reshape(rows, q_cols)
        .astype(bf16)
    )
    full_output = core_rows(wo_pieces)
    projected = dotf(attended_low, full_output, ((1,), (1,)))
    mixed_rows = inputs + lax.psum(projected.astype(bf16), "tensor").astype(f32)
    scale_two = rms_scale(mixed_rows)
    normed_two = mixed_rows * scale_two
    hidden_two = (normed_two * gain_experts).astype(bf16)

    hidden_all = jnp.concatenate(xor_gather(hidden_two, "expert"), 0)
    gate_up_full = jnp.concatenate(gate_up_pieces, 1)
    down_full = jnp.concatenate(down_pieces, 1)
    gate_up = dotf(hidden_all, gate_up_full, ((1,), (1,)))
    gate_value, up_value = gate_up[:, :flat], gate_up[:, flat:]
    grad_act = lax.optimization_barrier(dotf(upstream_all, down_full, ((1,), (1,)))) * route_scale
    sigmoid_gate = jax.nn.sigmoid(gate_value)
    scaled_act = (gate_value * sigmoid_gate * up_value * route_scale).astype(bf16)
    grad_up_low = (grad_act * gate_value * sigmoid_gate).astype(bf16)
    grad_gate_low = (
        grad_act * up_value * sigmoid_gate * (1.0 + gate_value * (1.0 - sigmoid_gate))
    ).astype(bf16)
    grad_gate_up = jnp.concatenate([grad_gate_low, grad_up_low], 1)
    grad_rows = jnp.dot(grad_gate_up, gate_up_full, preferred_element_type=f32).astype(bf16)
    grad_hidden_two = xor_scatter(jnp.split(grad_rows, n_ex, 0), "expert")
    grad_hidden_two = lax.psum(grad_hidden_two, "tensor")

    expert_out = jnp.dot(scaled_act, down_full, preferred_element_type=f32).astype(bf16)
    combined = xor_scatter(jnp.split(expert_out, n_ex, 0), "expert")
    def expert_grad(low, acts):
        return dotf(low, acts, ((0,), (0,))).astype(bf16)

    grads = [
        expert_grad(scaled_act, upstream_all),
        expert_grad(grad_gate_low, hidden_all),
        expert_grad(grad_up_low, hidden_all),
    ]
    grad_hidden_two, grads = lax.optimization_barrier((grad_hidden_two, grads))
    down_shard, gate_shard, up_shard = (
        dp_scatter(jnp.split(g, n_dp, 1)).reshape(group, hidden, part) for g in grads
    )
    combined, grad_hidden_two = lax.optimization_barrier((combined, grad_hidden_two))
    combined = lax.psum(combined, "tensor")
    output = lane((mixed_rows + combined.astype(f32)).astype(bf16))
    grad_hidden_two = grad_hidden_two.astype(f32)

    def attention_scatter(grad):
        grad = grad.reshape(n_dp, n_ex, width // (n_dp * n_ex), grad.shape[1])
        if n_ex == 2:
            away = lax.dynamic_index_in_dim(grad, 1 - me_ex, 1, keepdims=False)
            own = lax.dynamic_index_in_dim(grad, me_ex, 1, keepdims=False)
            grad = (own.astype(f32) + flip(away, "expert", 1).astype(f32)).astype(bf16)
        else:
            grad = lax.psum_scatter(grad, "expert", scatter_dimension=1, tiled=False)
        return dp_scatter(list(grad))

    upstream = upstream_low.astype(f32)
    experts_gain_grad = jnp.sum(grad_hidden_two * normed_two, axis=0)
    grad_mixed = upstream + norm_back(grad_hidden_two, normed_two, scale_two, gain_experts)
    grad_proj_low = grad_mixed.astype(bf16)
    grad_att_low = (
        jnp.dot(grad_proj_low, full_output, preferred_element_type=f32)
        .astype(bf16)
        .reshape(rows, heads_key, per_group, HEAD_SIZE)
    )
    output_grad = dotf(grad_proj_low, attended_low, ((0,), (0,))).astype(bf16)
    output_shard = attention_scatter(output_grad)
    grad_probs = jnp.einsum("qkgd,skd->kgqs", grad_att_low, value_low, preferred_element_type=f32)
    row_dot = jnp.sum(probs * grad_probs, axis=-1, keepdims=True)
    grad_scores = (probs * (grad_probs - row_dot)).astype(bf16)
    grad_value = jnp.einsum("kgqs,qkgd->skd", prob_low, grad_att_low, preferred_element_type=f32)
    grad_qrot = jnp.einsum(
        "kgqs,skd->qkgd", grad_scores, key_rot, preferred_element_type=f32
    ) * HEAD_SIZE ** (-0.5)
    grad_krot = jnp.einsum(
        "kgqs,qkgd->skd", grad_scores, rotated_query, preferred_element_type=f32
    ) * HEAD_SIZE ** (-0.5)
    grad_qrot = grad_qrot.reshape(rows, heads_query, HEAD_SIZE)
    grad_query_normed = rotate(grad_qrot, cosine_table, -sine_table)
    query_gain_grad = jnp.sum(grad_query_normed * normed_query, axis=(0, 1))
    grad_query_low = (
        norm_back(grad_query_normed, normed_query, scale_query, gain_query)
        .astype(bf16)
        .reshape(rows, q_cols)
    )
    grad_key_normed = rotate(grad_krot, cosine_table, -sine_table)
    key_gain_grad = jnp.sum(grad_key_normed * normed_key, axis=(0, 1))
    grad_key_low = (
        norm_back(grad_key_normed, normed_key, scale_key, gain_key).astype(bf16).reshape(rows, k_cols)
    )
    grad_value_low = grad_value.astype(bf16).reshape(rows, k_cols)
    grad_qkv_low = jnp.concatenate([grad_query_low, grad_key_low, grad_value_low], 1)
    grad_hidden_one = dotf(grad_qkv_low, full_qkv, ((1,), (1,)))
    head_gain_grads = jnp.stack([query_gain_grad, key_gain_grad]).astype(bf16)
    grad_hidden_one, head_gain_grads, _ = lax.optimization_barrier(
        (grad_hidden_one.astype(bf16), head_gain_grads, combined)
    )
    grad_hidden_one, head_gain_grads = lax.psum((grad_hidden_one, head_gain_grads), "tensor")
    grad_hidden_one = grad_hidden_one.astype(f32)
    qkv_grad = dotf(first_hidden, grad_qkv_low, ((0,), (0,))).astype(bf16)
    qkv_shard = attention_scatter(qkv_grad)
    attention_gain_grad = jnp.sum(grad_hidden_one * normed_one, axis=0)
    tokens_grad = grad_mixed + norm_back(grad_hidden_one, normed_one, scale_one, gain_attention)
    tokens_grad = lane(tokens_grad)

    blocks = lambda v: v.reshape(n_dp, n_ex, -1)
    gain_grads = jnp.concatenate(
        [
            blocks(attention_gain_grad),
            blocks(experts_gain_grad),
            lane(blocks(head_gain_grads[0].astype(f32)), 0),
            lane(blocks(head_gain_grads[1].astype(f32)), 0),
        ],
        2,
    )
    gain_grads = lane_order(gain_grads, 1, n_ex, me_ex)
    gain_grads = jnp.pad(gain_grads, ((0, 0), (0, 0), (0, -gain_grads.shape[2] % 128)))
    gain_grads = gain_grads.reshape(n_dp, n_ex, -1, 128)
    gain_grads = xor_scatter([gain_grads[:, k] for k in range(n_ex)], "expert")
    gain_grads = xor_scatter([gain_grads[k] for k in range(n_dp)], "dp").reshape(-1)
    take = lambda start, size: gain_grads[start : start + size]
    return (
        output,
        tokens_grad,
        take(0, na),
        qkv_shard[:, :q_cols],
        qkv_shard[:, q_cols : q_cols + k_cols],
        qkv_shard[:, q_cols + k_cols :],
        output_shard,
        take(2 * na, nq),
        take(2 * na + nq, nq),
        take(na, na),
        gate_shard,
        up_shard,
        down_shard,
    )


CHUNKS = 16


def line_roles(axis):
    p = lax.axis_index(axis)
    return p + 1 - 2 * (p % 2), 3 - p, (p + 1) // 2 == 1


def over(n, f, start=0):
    lax.fori_loop(start, n, lambda c, t: (f(c), t)[1], 0)


def line_sum_steps(x_ref, in_buf, mid_buf, part, out_ref, sems, axis, finish, lag=2):
    a_send, a_recv, b_send, b_recv, c_send, c_recv = sems
    side, mid, inner = line_roles(axis)
    step = x_ref.shape[0] // CHUNKS

    def rows(c):
        return pl.ds(pl.multiple_of(c * step, step), step)

    def copy(src, dst, c, send, recv, to):
        return pltpu.make_async_remote_copy(
            src.at[rows(c)], dst.at[rows(c)], send.at[c], recv.at[c], device_id={axis: to}, device_id_type=MESH
        )

    to_inner = lambda c: copy(x_ref, in_buf, c, a_send, a_recv, side)
    to_middle = lambda c: copy(part, mid_buf, c, b_send, b_recv, mid)
    to_outer = lambda c: copy(out_ref, out_ref, c, c_send, c_recv, side)

    @pl.when(jnp.logical_not(inner))
    def _():
        over(CHUNKS, lambda c: to_inner(c).start())

        def done(c):
            to_outer(c).wait_recv()
            finish(rows(c), c)
            to_inner(c).wait_send()

        over(CHUNKS, done)

    @pl.when(inner)
    def _():
        def first(c):
            to_inner(c).wait_recv()
            r = rows(c)
            part[r] = (x_ref[r].astype(f32) + in_buf[r].astype(f32)).astype(bf16)
            to_middle(c).start()

        def second(c):
            to_middle(c).wait_recv()
            r = rows(c)
            out_ref[r] = (part[r].astype(f32) + mid_buf[r].astype(f32)).astype(bf16)
            to_outer(c).start()
            finish(r, c)

        over(lag, first)
        over(CHUNKS - lag, lambda c: (first(c + lag), second(c))[0])
        over(CHUNKS, second, CHUNKS - lag)

        def done(c):
            to_middle(c).wait_send()
            to_outer(c).wait_send()

        over(CHUNKS, done)


def line_sems():
    return [pltpu.SemaphoreType.DMA((CHUNKS,))] * 6


def plane_partners():
    d, c = lax.axis_index("dp"), lax.axis_index("expert")
    ds = {0: d, 1: d + 1 - 2 * (d % 2), 2: d + 2 - 4 * (d // 2), 3: 3 - d}
    cs = {0: c, 1: 1 - c}
    return {(kd, kc): {"dp": ds[kd], "expert": cs[kc]} for kd in ds for kc in cs}


def remote(src, dst, send, recv, to):
    return pltpu.make_async_remote_copy(src, dst, send, recv, device_id=to, device_id_type=MESH)


def nt(a, b):
    return lax.dot_general(a, b, (((1,), (1,)), ((), ())), preferred_element_type=f32)


def nn(a, b):
    return lax.dot_general(a, b, (((1,), (0,)), ((), ())), preferred_element_type=f32)


def tn(a, b):
    return lax.dot_general(a, b, (((0,), (0,)), ((), ())), preferred_element_type=f32)


def forward_kernel(
    tokens, qkv_own, wo_own, gate_own, up_own, down_own, gains_own, cos, sin, key_ok,
    x2, h2, att, qrot, krot, value, raw, probs, gains, gate, up, down, qkv_out, wo_out,
    qkv, wo, h1, proj, in_buf, mid_buf, part, summed, gain_rows,
    w_send, w_recv, core_send, core_recv, g_send, g_recv, h_send, h_recv, own_sem, out_sem, *line,
):
    c = lax.axis_index("expert")
    to = plane_partners()
    side, mid, inner = line_roles("tensor")
    barrier = pltpu.get_barrier_semaphore()
    others = [k for k in to if k != (0, 0)]
    for k in others:
        pl.semaphore_signal(barrier, inc=1, device_id=to[k], device_id_type=MESH)
    pl.semaphore_signal(barrier, inc=1, device_id={"tensor": side}, device_id_type=MESH)

    @pl.when(inner)
    def _():
        pl.semaphore_signal(barrier, inc=1, device_id={"tensor": mid}, device_id_type=MESH)
        pl.semaphore_wait(barrier, len(others) + 2)

    @pl.when(jnp.logical_not(inner))
    def _():
        pl.semaphore_wait(barrier, len(others) + 1)

    rows, width = tokens.shape
    piece = qkv_own.shape[0]
    half = piece // 2
    tall = gate_own.shape[0] // 2
    wide = gate_own.shape[1]

    def small_slot(full):
        return lambda k, h: full.at[pl.ds(pl.multiple_of((k * 2 + c) * piece + h * half, half), half)]

    def big_slot(full):
        return lambda k, h: full.at[pl.ds(h * tall, tall), pl.ds(k * wide, wide)]

    mats = [
        (lambda h: qkv_own.at[pl.ds(h * half, half)], small_slot(qkv)),
        (lambda h: wo_own.at[pl.ds(h * half, half)], small_slot(wo)),
    ] + [
        (lambda h, own=own: own.at[pl.ds(h * tall, tall)], big_slot(full))
        for own, full in ((gate_own, gate), (up_own, up), (down_own, down))
    ]

    def move(m, i):
        own, slot = mats[m]
        src, dst, way = (
            (own(0), slot(1, 0), 1), (own(1), slot(2, 1), 2), (own(0), slot(2, 0), 2), (own(1), slot(1, 1), 1),
            (slot(1, 0), slot(3, 0), 2), (slot(2, 1), slot(3, 1), 1),
        )[i]
        return remote(src, dst, w_send.at[m, i], w_recv.at[m, i], to[way, 0])

    def begin(m):
        for i in range(4):
            move(m, i).start()

    def pass_on(m):
        for i in (0, 1):
            move(m, i).wait_recv()
            move(m, 4 + i).start()

    def arrived(m):
        for i in (2, 3, 4, 5):
            move(m, i).wait_recv()

    def core_move(m, k):
        full = (qkv, wo)[m]
        block = full.at[pl.ds(pl.multiple_of((k * 2 + c) * piece, piece), piece)]
        return remote(block, block, core_send.at[m, k], core_recv.at[m, k], to[0, 1])

    def gain_move(j):
        kd, kc = others[j]
        return remote(gains_own, gains.at[kd, c], g_send.at[j], g_recv.at[j], to[kd, kc])

    own_copies = [
        pltpu.make_async_copy(qkv_own, qkv.at[pl.ds(pl.multiple_of(c * piece, piece), piece)], own_sem.at[0]),
        pltpu.make_async_copy(wo_own, wo.at[pl.ds(pl.multiple_of(c * piece, piece), piece)], own_sem.at[1]),
    ] + [
        pltpu.make_async_copy(own, full.at[:, pl.ds(0, wide)], own_sem.at[2 + i])
        for i, (own, full) in enumerate(((gate_own, gate), (up_own, up), (down_own, down)))
    ]

    begin(0)
    for j in range(len(others)):
        gain_move(j).start()
    own_copies[0].start()
    own_copies[1].start()
    gains[pl.ds(0, 1), pl.ds(c, 1)] = gains_own[...].reshape(1, 1, 8, 128)
    own_copies[0].wait()
    core_move(0, 0).start()
    own_copies[1].wait()
    core_move(1, 0).start()
    for j in range(len(others)):
        gain_move(j).wait_recv()
    for kd in range(4):
        for kc in range(2):
            g = gains[kd, kc]
            for j in range(2):
                col = (kd * 2 + kc) * 256 + j * 128
                gain_rows[0:1, col : col + 128] = g[j : j + 1]
                gain_rows[1:2, col : col + 128] = g[2 + j : 3 + j]
    heads = jnp.sum(gains[...].reshape(8, 8, 128), axis=0)
    gain_query, gain_key = heads[4:5], heads[5:6]

    def hidden_one(i):
        r = pl.ds(pl.multiple_of(i * 64, 64), 64)
        x = tokens[r].astype(f32)
        scale = lax.rsqrt(jnp.mean(x * x, axis=-1, keepdims=True) + epsilon)
        h1[r] = (x * scale * gain_rows[0:1]).astype(bf16)

    over(rows // 64, hidden_one)

    pass_on(0)
    begin(1)
    for k, waits in ((1, (3,)), (2, (2,)), (3, (4, 5))):
        for i in waits:
            move(0, i).wait_recv()
        core_move(0, k).start()
    pass_on(1)
    for m in (2, 3, 4):
        begin(m)
        own_copies[m].start()
    for k in range(4):
        core_move(0, k).wait_recv()
    save_qkv = pltpu.make_async_copy(qkv, qkv_out, out_sem.at[0])
    save_qkv.start()

    def project(j):
        col = pl.ds(pl.multiple_of(j * 256, 256), 256)
        raw[:, col] = nn(h1[...], qkv[:, col])

    over(qkv.shape[1] // 256, project)
    q_cols = att.shape[1]

    def spin(u):
        return u * cos[...] + pltpu.roll(u, 64, 1) * sin[...]

    def unit(u):
        return u * lax.rsqrt(jnp.mean(u * u, axis=-1, keepdims=True) + epsilon)

    krot[...] = spin(unit(raw[:, pl.ds(q_cols, 128)]) * gain_key).astype(bf16)
    value[...] = raw[:, pl.ds(q_cols + 128, 128)].astype(bf16)
    block = rows // 2

    def head(h):
        col = pl.ds(pl.multiple_of(h * 128, 128), 128)
        qrot[:, col] = spin(unit(raw[:, col]) * gain_query).astype(bf16)
        for i in range(2):
            r, n = slice(i * block, (i + 1) * block), (i + 1) * block
            s = nt(qrot[r, col], krot[0:n]) * 128 ** (-0.5)
            row = lax.broadcasted_iota(jnp.int32, (block, n), 0) + i * block
            key = lax.broadcasted_iota(jnp.int32, (block, n), 1)
            s = jnp.where((key <= row) & (key_ok[:, 0:n] > 0), s, -1e30)
            e = jnp.exp(s - jnp.max(s, axis=-1, keepdims=True))
            p = (e / jnp.sum(e, axis=-1, keepdims=True)).astype(bf16)
            probs[h, r, 0:n] = p
            att[r, col] = nn(p, value[0:n]).astype(bf16)
        probs[h, 0:block, block:] = jnp.zeros((block, block), bf16)

    over(q_cols // 128, head)

    for k, waits in ((1, (3,)), (2, (2,)), (3, (4, 5))):
        for i in waits:
            move(1, i).wait_recv()
        core_move(1, k).start()
    for k in range(4):
        core_move(1, k).wait_recv()
    save_wo = pltpu.make_async_copy(wo, wo_out, out_sem.at[1])
    save_wo.start()

    def out_project(j):
        r = pl.ds(pl.multiple_of(j * 256, 256), 256)
        proj[:, r] = nt(att[...], wo[r]).astype(bf16)

    over(width // 256, out_project)
    pass_on(2)

    def give(i):
        n = rows // CHUNKS
        src = h2.at[pl.ds(pl.multiple_of(i * n, n), n)]
        dst = h2.at[pl.ds(pl.multiple_of(rows + i * n, n), n)]
        return remote(src, dst, h_send.at[i], h_recv.at[i], to[0, 1])

    def finish(r, i):
        mixed = tokens[r].astype(f32) + summed[r].astype(f32)
        x2[r] = mixed
        scale = lax.rsqrt(jnp.mean(mixed * mixed, axis=-1, keepdims=True) + epsilon)
        h2[r] = (mixed * scale * gain_rows[1:2]).astype(bf16)
        give(i).start()

    line_sum_steps(proj, in_buf, mid_buf, part, summed, line, "tensor", finish)
    pass_on(3)
    pass_on(4)
    over(CHUNKS, lambda i: give(i).wait())
    for m in (2, 3, 4):
        arrived(m)
        own_copies[m].wait()
    save_qkv.wait()
    save_wo.wait()
    for m in range(5):
        for i in range(6):
            move(m, i).wait_send()
    for m in range(2):
        for k in range(4):
            core_move(m, k).wait_send()
    for j in range(len(others)):
        gain_move(j).wait_send()


def forward_call(tokens, qkv_own, wo_own, gate_own, up_own, down_own, gains_own, cos, sin, key_ok):
    rows, width = tokens.shape
    qkv_cols, q_cols = qkv_own.shape[1], wo_own.shape[1]
    tall = gate_own.shape[0]
    vmem, anyspace = pl.BlockSpec(memory_space=pltpu.VMEM), pl.BlockSpec(memory_space=pl.ANY)
    shape = jax.ShapeDtypeStruct
    outs = [
        (shape((rows, width), f32), vmem),
        (shape((2 * rows, width), bf16), vmem),
        (shape((rows, q_cols), bf16), vmem),
        (shape((rows, q_cols), bf16), vmem),
        (shape((rows, 128), bf16), vmem),
        (shape((rows, 128), bf16), vmem),
        (shape((rows, qkv_cols), f32), vmem),
        (shape((q_cols // 128, rows, rows), bf16), vmem),
        (shape((4, 2, 8, 128), f32), vmem),
        (shape((tall, width), bf16), anyspace),
        (shape((tall, width), bf16), anyspace),
        (shape((tall, width), bf16), anyspace),
        (shape((width, qkv_cols), bf16), anyspace),
        (shape((width, q_cols), bf16), anyspace),
    ]
    dma = pltpu.SemaphoreType.DMA
    big = pltpu.VMEM((rows, width), bf16)
    return pl.pallas_call(
        forward_kernel,
        out_shape=[o[0] for o in outs],
        in_specs=[vmem] + [anyspace] * 5 + [vmem] * 4,
        out_specs=[o[1] for o in outs],
        scratch_shapes=[
            pltpu.VMEM((width, qkv_cols), bf16),
            pltpu.VMEM((width, q_cols), bf16),
            big, big, big, big, big, big,
            pltpu.VMEM((2, width), f32),
            dma((5, 6)), dma((5, 6)), dma((2, 4)), dma((2, 4)), dma((7,)), dma((7,)),
            dma((CHUNKS,)), dma((CHUNKS,)), dma((5,)), dma((2,)),
        ] + line_sems(),
        compiler_params=pltpu.CompilerParams(
            collective_id=1, has_side_effects=True, vmem_limit_bytes=60 * 2**20
        ),
        cost_estimate=pl.CostEstimate(flops=8 * 10**9, bytes_accessed=60 * 10**6, transcendentals=2 * 10**6),
        name="forward_to_experts",
    )(tokens, qkv_own, wo_own, gate_own, up_own, down_own, gains_own, cos, sin, key_ok)


def expert_kernel(
    h2, g, mine, gate_in, up_in, down_in,
    grad_h2, out, grads, got,
    gate, up, down, acts, drow, rbuf, in_buf, mid_buf, stage,
    load_sem, x_send, x_recv, s_send, s_recv, keep_sem, out_sem, *line,
):
    to = plane_partners()
    side, mid, inner = line_roles("tensor")
    barrier = pltpu.get_barrier_semaphore()
    near = [(1, 0), (2, 0), (0, 1)]
    for k in near:
        pl.semaphore_signal(barrier, inc=1, device_id=to[k], device_id_type=MESH)
    pl.semaphore_signal(barrier, inc=1, device_id={"tensor": side}, device_id_type=MESH)

    @pl.when(inner)
    def _():
        pl.semaphore_signal(barrier, inc=1, device_id={"tensor": mid}, device_id_type=MESH)
        pl.semaphore_wait(barrier, len(near) + 2)

    @pl.when(jnp.logical_not(inner))
    def _():
        pl.semaphore_wait(barrier, len(near) + 1)

    tall, width = down.shape
    rows = drow.shape[0] // 2
    hidden = mine.shape[1]
    tiles = tall // 256
    wide = width // 4
    tile = lambda t: pl.ds(pl.multiple_of(t * 256, 256), 256)
    order = lambda i: i // 2 + (tiles // 2) * (i % 2)

    def load(t, j):
        src, dst = ((gate_in, gate), (up_in, up), (down_in, down))[j]
        return pltpu.make_async_copy(src.at[tile(t)], dst.at[tile(t)], load_sem.at[t, j])

    def start_loads(i):
        for j in range(3):
            load(order(i), j).start()

    over(tiles, start_loads)

    def keep(m, t, slot):
        return pltpu.make_async_copy(stage.at[slot], grads.at[m, tile(t)], keep_sem.at[slot])

    def send(m, t, j, way):
        src = grads.at[m, tile(t), pl.ds((3 if j else way) * wide, wide)]
        dst = got.at[m, tile(t), pl.ds(j * wide, wide)]
        return remote(src, dst, s_send.at[m, t, j], s_recv.at[m, t, j], to[way, 0])

    def send_tile(u):
        m, i = u // tiles, u % tiles
        t = order(i)
        keep(m, t, u % 2).wait()
        for way in (1, 2):

            @pl.when(i % 2 == way - 1)
            def _(way=way):
                for j in range(2):
                    send(m, t, j, way).start()

    def grad_tile(u, rhs):
        m, i = u // tiles, u % tiles
        t = order(i)
        low = acts[m, :, tile(t)]
        for k in range(4):
            cols = slice(k * wide, (k + 1) * wide)
            stage[u % 2, :, cols] = tn(low, rhs[:, cols]).astype(bf16)
        keep(m, t, u % 2).start()

        @pl.when(u > 0)
        def _():
            send_tile(u - 1)

    units = tall // 8

    def hidden_tile(i):
        t = order(i)
        for j in range(3):
            load(t, j).wait()
        first = (t * 256) // units
        edge = (first + 1) * units - t * 256
        lanes = lax.broadcasted_iota(jnp.int32, mine.shape, 1)
        pick = lambda e: jnp.sum(jnp.where(lanes == e, mine[...], 0.0), axis=1, keepdims=True)
        column = lax.broadcasted_iota(jnp.int32, (2 * rows, 256), 1)
        scale = jnp.where(column < edge, pick(first), pick(first + 1))
        gate_value = nt(h2[...], gate[tile(t)])
        up_value = nt(h2[...], up[tile(t)])
        grad_act = nt(g[...], down[tile(t)]) * scale
        sig = jax.nn.sigmoid(gate_value)
        silu = gate_value * sig
        acts[0, :, tile(t)] = (silu * up_value * scale).astype(bf16)
        acts[2, :, tile(t)] = (grad_act * silu).astype(bf16)
        acts[1, :, tile(t)] = (grad_act * up_value * sig * (1.0 + gate_value * (1.0 - sig))).astype(bf16)
        grad_tile(i, g)

    over(tiles, hidden_tile)

    step = rows // CHUNKS

    def give(i):
        src = drow.at[pl.ds(pl.multiple_of(rows + i * step, step), step)]
        dst = rbuf.at[pl.ds(pl.multiple_of(i * step, step), step)]
        return remote(src, dst, x_send.at[i], x_recv.at[i], to[0, 1])

    for part_rows in (slice(rows, 2 * rows), slice(0, rows)):

        def row_grads(j, part_rows=part_rows):
            col = pl.ds(pl.multiple_of(j * 256, 256), 256)
            drow[part_rows, col] = (
                nn(acts[1, part_rows, :], gate[:, col]) + nn(acts[2, part_rows, :], up[:, col])
            ).astype(bf16)

        over(width // 256, row_grads)
        if part_rows.start:
            over(CHUNKS, lambda i: give(i).start())

    def add_other(c):
        give(c).wait_recv()
        r = pl.ds(pl.multiple_of(c * step, step), step)
        drow[r] = (drow[r].astype(f32) + rbuf[r].astype(f32)).astype(bf16)

    def out_copy(j):
        col = pl.ds(pl.multiple_of(j * 256, 256), 256)
        return pltpu.make_async_copy(gate.at[pl.ds(0, 2 * rows), col], out.at[:, col], out_sem.at[j])

    def work(i):
        @pl.when(i < 2 * tiles)
        def _():
            grad_tile(tiles + i, h2)

        @pl.when(i == 2 * tiles)
        def _():
            send_tile(3 * tiles - 1)

        @pl.when(i >= 2 * tiles)
        def _():
            j = i - 2 * tiles
            col = pl.ds(pl.multiple_of(j * 256, 256), 256)
            gate[0 : 2 * rows, col] = nn(acts[0], down[:, col]).astype(bf16)
            out_copy(j).start()

    line_sum_work(
        drow, in_buf, mid_buf, drow, grad_h2, line, "tensor", rows, add_other, lambda r, c: None, work,
        2 * tiles + width // 256,
    )
    over(width // 256, lambda j: out_copy(j).wait())
    over(CHUNKS, lambda i: give(i).wait_send())

    def finish_tile(u):
        m, i = u // tiles, u % tiles
        for way in (1, 2):

            @pl.when(i % 2 == way - 1)
            def _(way=way):
                for j in range(2):
                    send(m, order(i), j, way).wait()

    over(3 * tiles, finish_tile)


def line_sum_work(x_ref, in_buf, mid_buf, part, out_ref, sems, axis, n_rows, ready, finish, work, n_work):
    a_send, a_recv, b_send, b_recv, c_send, c_recv = sems
    side, mid, inner = line_roles(axis)
    step = n_rows // CHUNKS
    steps = max(n_work, CHUNKS + 4)

    def rows(c):
        return pl.ds(pl.multiple_of(c * step, step), step)

    def copy(src, dst, c, send, recv, to):
        return pltpu.make_async_remote_copy(
            src.at[rows(c)], dst.at[rows(c)], send.at[c], recv.at[c], device_id={axis: to}, device_id_type=MESH
        )

    to_inner = lambda c: copy(x_ref, in_buf, c, a_send, a_recv, side)
    to_middle = lambda c: copy(part, mid_buf, c, b_send, b_recv, mid)
    to_outer = lambda c: copy(out_ref, out_ref, c, c_send, c_recv, side)

    @pl.when(jnp.logical_not(inner))
    def _():
        def begin(c):
            ready(c)
            to_inner(c).start()

        over(CHUNKS, begin)

        def one(i):
            @pl.when((i >= 4) & (i < CHUNKS + 4))
            def _():
                to_outer(i - 4).wait_recv()
                finish(rows(i - 4), i - 4)

            @pl.when(i < n_work)
            def _():
                work(i)

        over(steps, one)
        over(CHUNKS, lambda c: to_inner(c).wait_send())

    @pl.when(inner)
    def _():
        def first(c):
            ready(c)
            to_inner(c).wait_recv()
            r = rows(c)
            part[r] = (x_ref[r].astype(f32) + in_buf[r].astype(f32)).astype(bf16)
            to_middle(c).start()

        def second(c):
            to_middle(c).wait_recv()
            r = rows(c)
            out_ref[r] = (part[r].astype(f32) + mid_buf[r].astype(f32)).astype(bf16)
            to_outer(c).start()
            finish(r, c)

        def one(i):
            @pl.when(i < CHUNKS)
            def _():
                first(i)

            @pl.when((i >= 2) & (i < CHUNKS + 2))
            def _():
                second(i - 2)

            @pl.when(i < n_work)
            def _():
                work(i)

        over(steps, one)

        def done(c):
            to_middle(c).wait_send()
            to_outer(c).wait_send()

        over(CHUNKS, done)


def expert_call(h2, g, mine, gate, up, down):
    tall, width = down.shape
    rows = h2.shape[0] // 2
    vmem, anyspace = pl.BlockSpec(memory_space=pltpu.VMEM), pl.BlockSpec(memory_space=pl.ANY)
    shape = jax.ShapeDtypeStruct
    dma = pltpu.SemaphoreType.DMA
    tiles = tall // 256
    return pl.pallas_call(
        expert_kernel,
        out_shape=[
            shape((rows, width), bf16),
            shape((2 * rows, width), bf16),
            shape((3, tall, width), bf16),
            shape((3, tall, width // 2), bf16),
        ],
        in_specs=[vmem, vmem, vmem, anyspace, anyspace, anyspace],
        out_specs=[vmem, anyspace, anyspace, anyspace],
        scratch_shapes=[pltpu.VMEM((tall, width), bf16)] * 3
        + [
            pltpu.VMEM((3, 2 * rows, tall), bf16),
            pltpu.VMEM((2 * rows, width), bf16),
            pltpu.VMEM((rows, width), bf16),
            pltpu.VMEM((rows, width), bf16),
            pltpu.VMEM((rows, width), bf16),
            pltpu.VMEM((2, 256, width), bf16),
            dma((tiles, 3)), dma((CHUNKS,)), dma((CHUNKS,)), dma((3, tiles, 2)), dma((3, tiles, 2)),
            dma((2,)), dma((width // 256,)),
        ]
        + line_sems(),
        compiler_params=pltpu.CompilerParams(
            collective_id=2, has_side_effects=True, vmem_limit_bytes=62 * 2**20
        ),
        cost_estimate=pl.CostEstimate(flops=58 * 10**9, bytes_accessed=60 * 10**6, transcendentals=2 * 10**6),
        name="experts",
    )(h2, g, mine, gate, up, down)


def plane_barrier(to, z_others):
    barrier = pltpu.get_barrier_semaphore()
    others = [k for k in to if k != (0, 0)]
    for k in others:
        pl.semaphore_signal(barrier, inc=1, device_id=to[k], device_id_type=MESH)
    for z in z_others:
        pl.semaphore_signal(barrier, inc=1, device_id={"tensor": z}, device_id_type=MESH)
    pl.semaphore_wait(barrier, len(others) + len(z_others))
    return others


def z_partners():
    p = lax.axis_index("tensor")
    return [p + 1 - 2 * (p % 2), p + 2 - 4 * (p // 2), 3 - p]


def gain_vectors(gains, gain_rows):
    for kd in range(4):
        for kc in range(2):
            g = gains[kd, kc]
            for j in range(2):
                col = (kd * 2 + kc) * 256 + j * 128
                gain_rows[0:1, col : col + 128] = g[j : j + 1]
                gain_rows[1:2, col : col + 128] = g[2 + j : 3 + j]
    heads = jnp.sum(gains[...].reshape(8, 8, 128), axis=0)
    return heads[4:5], heads[5:6]


def attention_back_kernel(
    grad_h2, x2, cot, qrot, krot, value, raw, gains, cos, sin, probs, wo_in, qkv_in, out_part, grads, got,
    output, dx2, low, grad_qkv, grad_h1, gain_grads, got2,
    wo, qkv, own_out, rbuf, in_buf, mid_buf, summed, datt, pbuf, dk, dv, gain_rows, load_a, load_b, on_buf,
    w_sem, p_sem, l_sem, x_send, x_recv, s_send, s_recv, *line,
):
    to = plane_partners()
    plane_barrier(to, z_partners())
    places = [to[k, 0]["dp"] for k in range(4)]
    rows, width = x2.shape
    wide = width // 4
    tiles = grads.shape[1] // 256
    q_cols = qrot.shape[1]
    n_heads = q_cols // 128
    step = rows // CHUNKS
    rate = 128 ** (-0.5)
    order = lambda i: i // 2 + (tiles // 2) * (i % 2)
    tile = lambda t: pl.ds(pl.multiple_of(t * 256, 256), 256)

    def give(i):
        src = out_part.at[pl.ds(pl.multiple_of(rows + i * step, step), step)]
        dst = rbuf.at[pl.ds(pl.multiple_of(i * step, step), step)]
        return remote(src, dst, x_send.at[i], x_recv.at[i], to[0, 1])

    over(CHUNKS, lambda i: give(i).start())
    weights = [
        pltpu.make_async_copy(wo_in, wo, w_sem.at[0]),
        pltpu.make_async_copy(qkv_in, qkv, w_sem.at[1]),
        pltpu.make_async_copy(out_part.at[pl.ds(0, rows)], own_out, w_sem.at[2]),
    ]
    for w in weights:
        w.start()

    def load_probs(h):
        return pltpu.make_async_copy(probs.at[h], pbuf.at[h % 2], p_sem.at[h % 2])

    def loads(u, first):
        m, t = u // tiles, order(u % tiles)
        slot = u % 2
        return (
            pltpu.make_async_copy(
                grads.at[m, tile(t), pl.ds((3 - first) * wide, wide)], load_a.at[slot], l_sem.at[slot, 0]
            ),
            pltpu.make_async_copy(got.at[m, tile(t), pl.ds(wide, wide)], load_b.at[slot], l_sem.at[slot, 1]),
        )

    def by_half(u, f):
        for first in (1, 2):

            @pl.when((u % tiles) % 2 == first - 1)
            def _(first=first):
                f(first)

    def start_loads(u):
        by_half(u, lambda first: [x.start() for x in loads(u, first)])

    def pass_on(u, first):
        m, t = u // tiles, order(u % tiles)
        return remote(on_buf.at[u], got2.at[m, tile(t)], s_send.at[u], s_recv.at[u], to[3 - first, 0])

    def second_tile(u):
        def f(first):
            for x in loads(u, first):
                x.wait()
            on_buf[u] = (load_a[u % 2].astype(f32) + load_b[u % 2].astype(f32)).astype(bf16)
            pass_on(u, first).start()

        by_half(u, f)

        @pl.when(u + 2 < 3 * tiles)
        def _():
            start_loads(u + 2)

    start_loads(0)
    start_loads(1)
    load_probs(0).start()
    gain_query, gain_key = gain_vectors(gains, gain_rows)
    gain_grads[...] = jnp.zeros_like(gain_grads)
    dk[...] = jnp.zeros_like(dk)
    dv[...] = jnp.zeros_like(dv)

    def mixed_rows(i):
        r = pl.ds(pl.multiple_of(i * 64, 64), 64)
        x = x2[r]
        scale = lax.rsqrt(jnp.mean(x * x, axis=-1, keepdims=True) + epsilon)
        normed = x * scale
        grad = grad_h2[r].astype(f32)
        gain_grads[0:1, :] += jnp.sum(grad * normed, axis=0, keepdims=True)
        n = grad * gain_rows[1:2]
        d = cot[r].astype(f32) + scale * (n - normed * jnp.mean(n * normed, axis=-1, keepdims=True))
        dx2[r] = d
        low[r] = d.astype(bf16)

    def att_grads(j):
        col = pl.ds(pl.multiple_of(j * 256, 256), 256)
        datt[:, col] = nn(low[...], wo[:, col]).astype(bf16)

    def unspin(u):
        return u * cos[...] - pltpu.roll(u, 64, 1) * sin[...]

    def norm_grads(x, rotated, gain, row):
        scale = lax.rsqrt(jnp.mean(x * x, axis=-1, keepdims=True) + epsilon)
        normed = x * scale
        du = unspin(rotated)
        gain_grads[row : row + 1, 0:128] += jnp.sum(du * normed, axis=0, keepdims=True)
        n = du * gain
        return (scale * (n - normed * jnp.mean(n * normed, axis=-1, keepdims=True))).astype(bf16)

    block = rows // 2

    def head(h):
        load_probs(h).wait()

        @pl.when(h + 1 < n_heads)
        def _():
            load_probs(h + 1).start()

        col = pl.ds(pl.multiple_of(h * 128, 128), 128)
        dq = []
        for i in range(2):
            r, n = slice(i * block, (i + 1) * block), (i + 1) * block
            p_low = pbuf[h % 2, r, 0:n]
            p = p_low.astype(f32)
            dp = nt(datt[r, col], value[0:n])
            ds = (p * (dp - jnp.sum(p * dp, axis=-1, keepdims=True))).astype(bf16)
            dq.append(nn(ds, krot[0:n]) * rate)
            dk[0:n] += tn(ds, qrot[r, col])
            dv[0:n] += tn(p_low, datt[r, col])
        grad_qkv[:, col] = norm_grads(raw[:, col], jnp.concatenate(dq, 0), gain_query, 1)

    def key_value():
        grad_qkv[:, pl.ds(q_cols, 128)] = norm_grads(raw[:, pl.ds(q_cols, 128)], dk[...] * rate, gain_key, 2)
        grad_qkv[:, pl.ds(q_cols + 128, 128)] = dv[...].astype(bf16)

    def input_grads(j):
        r = pl.ds(pl.multiple_of(j * 256, 256), 256)
        grad_h1[:, r] = nt(grad_qkv[...], qkv[r]).astype(bf16)

    def work(i):
        @pl.when(i < 3 * tiles)
        def _():
            second_tile(i)

        @pl.when(i < 4)
        def _():
            mixed_rows(2 * i)
            mixed_rows(2 * i + 1)

        @pl.when(i == 4)
        def _():
            weights[0].wait()

        @pl.when((i >= 4) & (i < 6))
        def _():
            att_grads(2 * (i - 4))
            att_grads(2 * (i - 4) + 1)

        @pl.when((i >= 6) & (i < 6 + n_heads))
        def _():
            head(i - 6)

        @pl.when(i == 6 + n_heads)
        def _():
            key_value()
            weights[1].wait()

        @pl.when((i > 6 + n_heads) & (i <= 10 + n_heads))
        def _():
            j = 2 * (i - 7 - n_heads)
            input_grads(j)
            input_grads(j + 1)

    def ready(c):
        @pl.when(c == 0)
        def _():
            weights[2].wait()

        give(c).wait_recv()
        r = pl.ds(pl.multiple_of(c * step, step), step)
        own_out[r] = (own_out[r].astype(f32) + rbuf[r].astype(f32)).astype(bf16)

    def finish(r, c):
        done = (x2[r] + summed[r].astype(f32)).astype(bf16)
        for k in range(4):
            output[r, pl.ds(pl.multiple_of(places[k] * wide, wide), wide)] = done[:, k * wide : (k + 1) * wide]

    line_sum_work(
        own_out, in_buf, mid_buf, own_out, summed, line, "tensor", rows, ready, finish, work, 11 + n_heads
    )
    over(CHUNKS, lambda i: give(i).wait_send())
    over(3 * tiles, lambda u: by_half(u, lambda first: pass_on(u, first).wait()))


def attention_back_call(grad_h2, x2, cot, qrot, krot, value, raw, gains, cos, sin, probs, wo, qkv, out_part, grads, got):
    rows, width = x2.shape
    q_cols, qkv_cols = wo.shape[1], qkv.shape[1]
    tall = grads.shape[1]
    wide = width // 4
    vmem, anyspace = pl.BlockSpec(memory_space=pltpu.VMEM), pl.BlockSpec(memory_space=pl.ANY)
    shape = jax.ShapeDtypeStruct
    dma = pltpu.SemaphoreType.DMA
    tiles = tall // 256
    big = pltpu.VMEM((rows, width), bf16)
    return pl.pallas_call(
        attention_back_kernel,
        out_shape=[
            shape((rows, width), bf16),
            shape((rows, width), f32),
            shape((rows, width), bf16),
            shape((rows, qkv_cols), bf16),
            shape((rows, width), bf16),
            shape((8, width), f32),
            shape((3, tall, wide), bf16),
        ],
        in_specs=[vmem] * 10 + [anyspace] * 6,
        out_specs=[vmem] * 6 + [anyspace],
        scratch_shapes=[
            pltpu.VMEM((width, q_cols), bf16),
            pltpu.VMEM((width, qkv_cols), bf16),
            big, big, big, big, big,
            pltpu.VMEM((rows, q_cols), bf16),
            pltpu.VMEM((2, rows, rows), bf16),
            pltpu.VMEM((rows, 128), f32),
            pltpu.VMEM((rows, 128), f32),
            pltpu.VMEM((2, width), f32),
            pltpu.VMEM((2, 256, wide), bf16),
            pltpu.VMEM((2, 256, wide), bf16),
            pltpu.VMEM((3 * tiles, 256, wide), bf16),
            dma((3,)), dma((2,)), dma((2, 2)), dma((CHUNKS,)), dma((CHUNKS,)), dma((3 * tiles,)), dma((3 * tiles,)),
        ]
        + line_sems(),
        compiler_params=pltpu.CompilerParams(
            collective_id=3, has_side_effects=True, vmem_limit_bytes=62 * 2**20
        ),
        cost_estimate=pl.CostEstimate(flops=9 * 10**9, bytes_accessed=60 * 10**6, transcendentals=10**5),
        name="attention_backward",
    )(grad_h2, x2, cot, qrot, krot, value, raw, gains, cos, sin, probs, wo, qkv, out_part, grads, got)


def last_kernel(
    part, dx2, tokens, grad_qkv, low, att, gains, gain_grads,
    tokens_grad, qkv_shard, wo_shard, gain_sum,
    h1, in_buf, mid_buf, half_sum, summed, gain_rows, wo_all, qkv_all, wo_core, qkv_core, wo_one, qkv_one, wo_two, qkv_two,
    ga, z_got, g_out, g_got,
    z_send, z_recv, c_send, c_recv, f_send, f_recv, t_send, t_recv, g_send, g_recv, *line,
):
    c = lax.axis_index("expert")
    to = plane_partners()
    zs = z_partners()
    others = plane_barrier(to, zs)
    places = [to[k, 0]["dp"] for k in range(4)]
    rows, width = tokens.shape
    wide = width // 4
    piece = wide // 2
    half = piece // 2

    def z_move(j):
        return remote(gain_grads.at[pl.ds(0, 8), pl.ds(0, 128)], z_got.at[j], z_send.at[j], z_recv.at[j], {"tensor": zs[j]})

    for j in range(3):
        z_move(j).start()
    gain_vectors(gains, gain_rows)
    ga[...] = jnp.zeros_like(ga)

    def unit_rows(r):
        x = tokens[r].astype(f32)
        scale = lax.rsqrt(jnp.mean(x * x, axis=-1, keepdims=True) + epsilon)
        return x * scale, scale

    def hidden_one(i):
        r = pl.ds(pl.multiple_of(i * 64, 64), 64)
        h1[r] = (unit_rows(r)[0] * gain_rows[0:1]).astype(bf16)

    mats = [
        (low, att, wo_all, wo_core, wo_one, wo_two),
        (h1, grad_qkv, qkv_all, qkv_core, qkv_one, qkv_two),
    ]

    def block(k, core):
        return pl.ds(pl.multiple_of((k * 2 + core) * piece, piece), piece)

    def core_move(m, k):
        return remote(mats[m][2].at[block(k, 1 - c)], mats[m][3].at[k], c_send.at[m, k], c_recv.at[m, k], to[0, 1])

    def product(m, k, core):
        left, right, full = mats[m][:3]
        full[block(k, core)] = tn(left[:, block(k, core)], right[...]).astype(bf16)

    def away(k):
        for m in range(2):
            product(m, k, 1 - c)
            core_move(m, k).start()

    def home(k):
        for m in range(2):
            product(m, k, c)
            full, came = mats[m][2:4]
            core_move(m, k).wait_recv()
            full[block(k, c)] = (full[block(k, c)].astype(f32) + came[k].astype(f32)).astype(bf16)

    def slot(m, k, h):
        return mats[m][2].at[pl.ds(pl.multiple_of((k * 2 + c) * piece + h * half, half), half)]

    def first_move(m, h, j):
        way = 1 + h
        src = slot(m, 3 if j else way, h)
        return remote(src, mats[m][4].at[h, j], f_send.at[m, h, j], f_recv.at[m, h, j], to[way, 0])

    def second_move(m, h):
        return remote(slot(m, 2 - h, h), mats[m][5].at[h], t_send.at[m, h], t_recv.at[m, h], to[2 - h, 0])

    def add_first(m, h, j, k):
        full, one = mats[m][2], mats[m][4]
        r = pl.ds(pl.multiple_of((k * 2 + c) * piece + h * half, half), half)
        first_move(m, h, j).wait_recv()
        full[r] = (full[r].astype(f32) + one[h, j].astype(f32)).astype(bf16)

    def work(i):
        @pl.when(i == 0)
        def _():
            over(rows // 64, hidden_one)

        for n, k in enumerate((3, 1, 2, 0)):

            @pl.when(i == 1 + n)
            def _(k=k):
                away(k)

            @pl.when(i == 5 + n)
            def _(k=k, n=n):
                home(k)
                if n in (1, 2):
                    for m in range(2):
                        for j in range(2):
                            first_move(m, n - 1, j).start()

        for h in range(2):

            @pl.when(i == 17 + h)
            def _(h=h):
                for m in range(2):
                    add_first(m, h, 1, 2 - h)
                    second_move(m, h).start()

    def finish(r, i):
        grad = summed[r].astype(f32)
        normed, scale = unit_rows(r)
        ga[0:1, :] += jnp.sum(grad * normed, axis=0, keepdims=True)
        n = grad * gain_rows[0:1]
        d = dx2[r] + scale * (n - normed * jnp.mean(n * normed, axis=-1, keepdims=True))
        for k in range(4):
            tokens_grad[r, pl.ds(pl.multiple_of(places[k] * wide, wide), wide)] = d[:, k * wide : (k + 1) * wide]

    line_sum_work(part, in_buf, mid_buf, half_sum, summed, line, "tensor", rows, lambda k: None, finish, work, 20)

    head_rows = gain_grads[1:3, 0:128]
    for j in range(3):
        z_move(j).wait()
        head_rows += z_got[j, 1:3]
    for kd in range(4):
        for kc in range(2):
            for j in range(2):
                col = slice((kd * 2 + kc) * piece + j * 128, (kd * 2 + kc) * piece + (j + 1) * 128)
                g_out[kd, kc, j : j + 1] = ga[0:1, col]
                g_out[kd, kc, 2 + j : 3 + j] = gain_grads[0:1, col]
            g_out[kd, kc, 4:6] = head_rows

    def gain_move(j):
        kd, kc = others[j]
        core = c if kc == 0 else 1 - c
        return remote(g_out.at[kd, core], g_got.at[j], g_send.at[j], g_recv.at[j], to[kd, kc])

    for j in range(len(others)):
        gain_move(j).start()
    for m, shard in ((0, wo_shard), (1, qkv_shard)):
        full, two = mats[m][2], mats[m][5]
        for h in range(2):
            add_first(m, h, 0, 0)
            second_move(m, h).wait_recv()
            r = pl.ds(pl.multiple_of(c * piece + h * half, half), half)
            shard[h * half : (h + 1) * half] = full[r].astype(f32) + two[h].astype(f32)
    total = g_out[0, pl.ds(c, 1)].reshape(8, 128)
    for j in range(len(others)):
        gain_move(j).wait_recv()
        total += g_got[j]
    gain_sum[...] = total
    for m in range(2):
        for k in range(4):
            core_move(m, k).wait_send()
        for h in range(2):
            for j in range(2):
                first_move(m, h, j).wait_send()
            second_move(m, h).wait_send()
    for j in range(len(others)):
        gain_move(j).wait_send()


def last_call(part, dx2, tokens, grad_qkv, low, att, gains, gain_grads):
    rows, width = tokens.shape
    q_cols, qkv_cols = att.shape[1], grad_qkv.shape[1]
    piece = width // 8
    vmem = pl.BlockSpec(memory_space=pltpu.VMEM)
    shape = jax.ShapeDtypeStruct
    dma = pltpu.SemaphoreType.DMA
    big = pltpu.VMEM((rows, width), bf16)
    both = lambda *lead: [pltpu.VMEM(lead + (n,), bf16) for n in (q_cols, qkv_cols)]
    return pl.pallas_call(
        last_kernel,
        out_shape=[
            shape((rows, width), f32),
            shape((piece, qkv_cols), f32),
            shape((piece, q_cols), f32),
            shape((8, 128), f32),
        ],
        in_specs=[vmem] * 8,
        out_specs=[vmem] * 4,
        scratch_shapes=[big, big, big, big, big, pltpu.VMEM((2, width), f32)]
        + both(width)
        + both(4, piece)
        + both(2, 2, piece // 2)
        + both(2, piece // 2)
        + [
            pltpu.VMEM((8, width), f32),
            pltpu.VMEM((3, 8, 128), f32),
            pltpu.VMEM((4, 2, 8, 128), f32),
            pltpu.VMEM((7, 8, 128), f32),
            dma((3,)), dma((3,)), dma((2, 4)), dma((2, 4)), dma((2, 2, 2)), dma((2, 2, 2)), dma((2, 2)), dma((2, 2)),
            dma((7,)), dma((7,)),
        ]
        + line_sems(),
        compiler_params=pltpu.CompilerParams(
            collective_id=4, has_side_effects=True, vmem_limit_bytes=62 * 2**20
        ),
        cost_estimate=pl.CostEstimate(flops=5 * 10**9, bytes_accessed=40 * 10**6, transcendentals=10**5),
        name="input_gradients",
    )(part, dx2, tokens, grad_qkv, low, att, gains, gain_grads)


def local_fast(
    tokens,
    cotangent,
    route_ids,
    route_weight,
    lengths,
    attention_norm,
    query_weight,
    key_matrix,
    value_matrix,
    output_weight,
    query_norm,
    key_norm,
    experts_norm,
    gate_weight,
    up_weight,
    down_weight,
):
    n_dp = lax.axis_size("dp")
    n_ex = lax.axis_size("expert")
    me_dp = lax.axis_index("dp")
    me_ex = lax.axis_index("expert")
    rows, width = tokens.shape
    group, hidden, part = gate_weight.shape
    length = lengths[0]
    lane = lambda x, axis=-1: lane_order(x, axis, n_dp, me_dp)

    flat = group * hidden
    na, nq = attention_norm.shape[0], query_norm.shape[0]
    q_cols, k_cols = query_weight.shape[1], key_matrix.shape[1]
    heads_query, heads_key = q_cols // HEAD_SIZE, k_cols // HEAD_SIZE
    per_group = heads_query // heads_key
    own_place = (me_dp * n_ex + me_ex) * nq
    placed = lambda v: lax.dynamic_update_slice(jnp.zeros((128,), f32), v.astype(f32), (own_place,))
    gains_own = jnp.concatenate(
        [
            attention_norm.astype(f32).reshape(-1, 128),
            experts_norm.astype(f32).reshape(-1, 128),
            placed(query_norm)[None],
            placed(key_norm)[None],
            jnp.zeros((2, 128), f32),
        ],
        0,
    )
    cosine_table, sine_table = rope_tables(rows)
    cos2 = jnp.concatenate([cosine_table[:, 0], cosine_table[:, 0]], 1)
    sin2 = jnp.concatenate([-sine_table[:, 0], sine_table[:, 0]], 1)
    key_ok = (jnp.arange(rows, dtype=jnp.int32) < length).astype(f32)[None]
    inputs_low = lane(tokens)
    inputs = inputs_low.astype(f32)
    (
        mixed_rows, hidden_all, attended_low, rotated_query, key_rot, value_low, raw, prob_low,
        gains, gate_full, up_full, down_full, full_qkv, full_output,
    ) = forward_call(
        inputs_low,
        jnp.concatenate([query_weight, key_matrix, value_matrix], 1),
        output_weight,
        gate_weight.reshape(flat, part),
        up_weight.reshape(flat, part),
        down_weight.reshape(flat, part),
        gains_own,
        cos2,
        sin2,
        key_ok,
    )
    experts = jnp.arange(group * n_ex, dtype=jnp.int32)
    table = jnp.zeros((rows, group * n_ex), f32)
    for c in range(route_ids.shape[1]):
        table = table + jnp.where(
            route_ids[:, c, None] == experts[None, :], route_weight[:, c, None], 0.0
        )
    table = jnp.concatenate(xor_gather(table, "expert"), 0)
    mine = lax.dynamic_slice_in_dim(table, me_ex * group, group, 1)
    mine = jnp.pad(mine, ((0, 0), (0, 128 - group)))
    upstream_low = lane(cotangent)
    upstream_all = jnp.concatenate(xor_gather(upstream_low, "expert"), 0)

    grad_hidden_two, expert_out, grads, got = expert_call(
        hidden_all, upstream_all, mine, gate_full, up_full, down_full
    )
    output, grad_mixed, grad_proj_low, grad_qkv_low, grad_hidden_one, gain_grads, got2 = attention_back_call(
        grad_hidden_two, mixed_rows, upstream_low, rotated_query, key_rot, value_low, raw, gains, cos2, sin2,
        prob_low, full_output, full_qkv, expert_out, grads, got,
    )
    tokens_grad, qkv_shard, output_shard, gain_sum = last_call(
        grad_hidden_one, grad_mixed, inputs_low, grad_qkv_low, grad_proj_low, attended_low, gains, gain_grads
    )
    shards = grads[:, :, :part].astype(f32) + got[:, :, :part].astype(f32) + got2.astype(f32)
    down_shard, gate_shard, up_shard = (x.reshape(group, hidden, part) for x in shards)
    own_head = lambda row: lax.dynamic_slice_in_dim(gain_sum[row], own_place, nq, 0)
    return (
        output,
        tokens_grad,
        gain_sum[0:2].reshape(-1),
        qkv_shard[:, :q_cols],
        qkv_shard[:, q_cols : q_cols + k_cols],
        qkv_shard[:, q_cols + k_cols :],
        output_shard,
        own_head(4),
        own_head(5),
        gain_sum[2:4].reshape(-1),
        gate_shard,
        up_shard,
        down_shard,
    )


def local(*args):
    sizes = [lax.axis_size(a) for a in ("dp", "expert", "tensor")]
    return local_fast(*args) if sizes == [4, 2, 4] else local_plain(*args)


def solution(mesh):
    both = ("dp", "expert")
    rows2, rows1, mats = P(both, None), P(both), P(both, "tensor")
    experts = P("expert", "tensor", "dp")
    return jax.shard_map(
        local,
        mesh=mesh,
        in_specs=(rows2, rows2, rows2, rows2, rows1, rows1, mats, mats, mats, mats, rows1, rows1, rows1)
        + (experts,) * 3,
        out_specs=(rows2, rows2, rows1, mats, mats, mats, mats, rows1, rows1, rows1) + (experts,) * 3,
        check_vma=False,
    )
```

```python
import jax
import jax.numpy as jnp
from jax import lax
from jax.experimental import pallas as pl
from jax.experimental.pallas import tpu as pltpu
from jax.sharding import PartitionSpec as P

HEAD_SIZE = 128
TOP = 8
epsilon = 1e-06
f32 = jnp.float32
bf16 = jnp.bfloat16
MESH = pl.DeviceIdType.MESH


def rms_scale(values):
    return lax.rsqrt(jnp.mean(values * values, axis=-1, keepdims=True) + epsilon)


def rope_tables(rows):
    half_dim = HEAD_SIZE // 2
    frequency = jnp.power(f32(1000000.0), -(jnp.arange(half_dim, dtype=f32) * (2.0 / HEAD_SIZE)))
    angles = jnp.arange(rows, dtype=f32)[:, None] * frequency[None, :]
    return (jnp.cos(angles)[:, None, :], jnp.sin(angles)[:, None, :])


def rotate(values, cosine_table, sine_table):
    half_dim = values.shape[-1] // 2
    first_half = values[..., :half_dim]
    second_half = values[..., half_dim:]
    return jnp.concatenate(
        [
            first_half * cosine_table - second_half * sine_table,
            second_half * cosine_table + first_half * sine_table,
        ],
        axis=-1,
    )


def norm_back(grad_hidden, normed, scales, gains):
    grad_normed = grad_hidden * gains
    return scales * (grad_normed - normed * jnp.mean(grad_normed * normed, axis=-1, keepdims=True))


def flip(x, axis, bit):
    n = lax.axis_size(axis)
    return lax.ppermute(x, axis, [(i, i ^ bit) for i in range(n)])


def bits_of(n):
    return [1 << b for b in range(n.bit_length() - 1)]


def xor_gather(x, axis):
    pieces = [x]
    for bit in bits_of(lax.axis_size(axis)):
        pieces = pieces + [flip(p, axis, bit) for p in pieces]
    return pieces


def xor_scatter(parts, axis):
    for bit in reversed(bits_of(lax.axis_size(axis))):
        got = [flip(p, axis, bit) for p in parts[bit:]]
        parts = [
            (a.astype(f32) + r.astype(f32)).astype(a.dtype) for a, r in zip(parts[:bit], got)
        ]
    return parts[0]


def dp_scatter(blocks, axis="dp"):
    n = len(blocks)
    if n != 4:
        return xor_scatter(blocks, axis).astype(f32)
    h = blocks[0].shape[0] // 2
    add = lambda p, q: p.astype(f32) + q.astype(f32)
    done = []
    for rows, first, second in ((slice(0, h), 1, 2), (slice(h, 2 * h), 2, 1)):
        b = [x[rows] for x in blocks]
        got = flip(jnp.concatenate([b[first], b[3]], 0), axis, first)
        on = add(b[second], got[h:]).astype(bf16)
        done.append(add(b[0], got[:h]) + flip(on, axis, second).astype(f32))
    return jnp.concatenate(done, 0)


def all_pieces(x, axis, me):
    got = jnp.stack(xor_gather(x, axis), 0)
    return lane_order(got, 0, got.shape[0], me)


def dp_gather(x, axis="dp"):
    n = lax.axis_size(axis)
    if n != 4:
        return xor_gather(x, axis)
    h = x.shape[0] // 2
    a, b = x[:h], x[h:]
    a1, b2 = flip(a, axis, 1), flip(b, axis, 2)
    a2, b1 = flip(a, axis, 2), flip(b, axis, 1)
    a3, b3 = flip(a1, axis, 2), flip(b2, axis, 1)
    cat = lambda p, q: jnp.concatenate([p, q], 0)
    return [cat(a, b), cat(a1, b1), cat(a2, b2), cat(a3, b3)]


def lane_block(x, axis, n, me, k):
    axis = axis % x.ndim
    size = x.shape[axis] // n
    return lax.dynamic_slice_in_dim(x, (me ^ k) * size, size, axis)


def lane_order(x, axis, n, me):
    return jnp.concatenate([lane_block(x, axis, n, me, k) for k in range(n)], axis)


def block_scores(query_block, key_rot, length):
    query_pos = jnp.arange(query_block.shape[0], dtype=jnp.int32)
    key_pos = jnp.arange(key_rot.shape[0], dtype=jnp.int32)
    allowed = (key_pos[None, :] <= query_pos[:, None]) & (key_pos[None, :] < length)
    scores = jnp.einsum(
        "qkgd,skd->kgqs", query_block, key_rot, preferred_element_type=f32
    ) * HEAD_SIZE ** (-0.5)
    return jnp.where(allowed, scores, -1e30)


def core_rows(pieces, axis="expert"):
    n = lax.axis_size(axis)
    own = jnp.stack(pieces, 0)
    if n == 2:
        other = flip(own, axis, 1)
        first = lax.axis_index(axis) == 0
        both = jnp.stack([jnp.where(first, own, other), jnp.where(first, other, own)], 1)
    else:
        both = lax.all_gather(own, axis, axis=1, tiled=False)
    return both.reshape((-1,) + own.shape[2:])


def dotf(a, b, dims):
    return lax.dot_general(a, b, (dims, ((), ())), preferred_element_type=f32)


def local_plain(
    tokens,
    cotangent,
    route_ids,
    route_weight,
    lengths,
    attention_norm,
    query_weight,
    key_matrix,
    value_matrix,
    output_weight,
    query_norm,
    key_norm,
    experts_norm,
    gate_weight,
    up_weight,
    down_weight,
):
    n_dp = lax.axis_size("dp")
    n_ex = lax.axis_size("expert")
    me_dp = lax.axis_index("dp")
    me_ex = lax.axis_index("expert")
    rows, width = tokens.shape
    group, hidden, part = gate_weight.shape
    length = lengths[0]
    lane = lambda x, axis=-1: lane_order(x, axis, n_dp, me_dp)

    qkv_own = jnp.concatenate([query_weight, key_matrix, value_matrix], 1)
    qkv_pieces = dp_gather(qkv_own)
    wo_own, qkv_pieces = lax.optimization_barrier((output_weight, qkv_pieces))
    wo_pieces = dp_gather(wo_own)
    (gw, uw, dw), wo_pieces = lax.optimization_barrier(
        ((gate_weight, up_weight, down_weight), wo_pieces)
    )
    flat = group * hidden
    gate_up_own = jnp.concatenate([gw.reshape(flat, part), uw.reshape(flat, part)], 0)
    gate_up_pieces = dp_gather(gate_up_own)
    down_own, gate_up_pieces = lax.optimization_barrier((dw.reshape(flat, part), gate_up_pieces))
    down_pieces = dp_gather(down_own)

    na, nq = attention_norm.shape[0], query_norm.shape[0]
    gains = jnp.concatenate([attention_norm, experts_norm, query_norm, key_norm])
    gains = jnp.pad(gains, (0, -gains.size % 128)).reshape(-1, 128)
    gains = all_pieces(all_pieces(gains, "expert", me_ex), "dp", me_dp)
    gains = gains.reshape(n_dp, n_ex, -1).astype(f32)
    gain_attention = lane(gains[:, :, :na].reshape(-1))
    gain_experts = lane(gains[:, :, na : 2 * na].reshape(-1))
    gain_query = gains[:, :, 2 * na : 2 * na + nq].reshape(-1)
    gain_key = gains[:, :, 2 * na + nq : 2 * na + 2 * nq].reshape(-1)

    experts = jnp.arange(group * n_ex, dtype=jnp.int32)
    table = jnp.zeros((rows, group * n_ex), f32)
    for c in range(route_ids.shape[1]):
        table = table + jnp.where(
            route_ids[:, c, None] == experts[None, :], route_weight[:, c, None], 0.0
        )
    table = jnp.concatenate(xor_gather(table, "expert"), 0)
    mine = lax.dynamic_slice_in_dim(table, me_ex * group, group, 1)
    unit_expert = jnp.arange(flat, dtype=jnp.int32) // hidden
    route_scale = jnp.zeros((table.shape[0], flat), f32)
    for j in range(group):
        route_scale = route_scale + jnp.where(unit_expert[None, :] == j, mine[:, j, None], 0.0)

    cosine_table, sine_table = rope_tables(rows)
    inputs = lane(tokens.astype(f32))
    scale_one = rms_scale(inputs)
    normed_one = inputs * scale_one
    first_hidden = (normed_one * gain_attention).astype(bf16)
    upstream_low = lane(cotangent)
    upstream_all = jnp.concatenate(xor_gather(upstream_low, "expert"), 0)

    full_qkv = core_rows(qkv_pieces)
    qkv = jnp.dot(first_hidden, full_qkv, preferred_element_type=f32)
    q_cols, k_cols = query_weight.shape[1], key_matrix.shape[1]
    heads_query, heads_key = q_cols // HEAD_SIZE, k_cols // HEAD_SIZE
    per_group = heads_query // heads_key
    query_raw = qkv[:, :q_cols].reshape(rows, heads_query, HEAD_SIZE)
    key_raw = qkv[:, q_cols : q_cols + k_cols].reshape(rows, heads_key, HEAD_SIZE)
    value_low = qkv[:, q_cols + k_cols :].astype(bf16).reshape(rows, heads_key, HEAD_SIZE)
    scale_query = rms_scale(query_raw)
    normed_query = query_raw * scale_query
    rotated_query = (
        rotate(normed_query * gain_query, cosine_table, sine_table)
        .astype(bf16)
        .reshape(rows, heads_key, per_group, HEAD_SIZE)
    )
    scale_key = rms_scale(key_raw)
    normed_key = key_raw * scale_key
    key_rot = rotate(normed_key * gain_key, cosine_table, sine_table).astype(bf16)
    scores = block_scores(rotated_query, key_rot, length)
    row_peak = jnp.max(scores, axis=-1, keepdims=True)
    shifted = jnp.exp(scores - row_peak)
    totals = jnp.sum(shifted, axis=-1, keepdims=True)
    probs = shifted / totals
    prob_low = probs.astype(bf16)
    attended_low = (
        jnp.einsum("kgqs,skd->qkgd", prob_low, value_low, preferred_element_type=f32)
        .reshape(rows, q_cols)
        .astype(bf16)
    )
    full_output = core_rows(wo_pieces)
    projected = dotf(attended_low, full_output, ((1,), (1,)))
    mixed_rows = inputs + lax.psum(projected.astype(bf16), "tensor").astype(f32)
    scale_two = rms_scale(mixed_rows)
    normed_two = mixed_rows * scale_two
    hidden_two = (normed_two * gain_experts).astype(bf16)

    hidden_all = jnp.concatenate(xor_gather(hidden_two, "expert"), 0)
    gate_up_full = jnp.concatenate(gate_up_pieces, 1)
    down_full = jnp.concatenate(down_pieces, 1)
    gate_up = dotf(hidden_all, gate_up_full, ((1,), (1,)))
    gate_value, up_value = gate_up[:, :flat], gate_up[:, flat:]
    grad_act = lax.optimization_barrier(dotf(upstream_all, down_full, ((1,), (1,)))) * route_scale
    sigmoid_gate = jax.nn.sigmoid(gate_value)
    scaled_act = (gate_value * sigmoid_gate * up_value * route_scale).astype(bf16)
    grad_up_low = (grad_act * gate_value * sigmoid_gate).astype(bf16)
    grad_gate_low = (
        grad_act * up_value * sigmoid_gate * (1.0 + gate_value * (1.0 - sigmoid_gate))
    ).astype(bf16)
    grad_gate_up = jnp.concatenate([grad_gate_low, grad_up_low], 1)
    grad_rows = jnp.dot(grad_gate_up, gate_up_full, preferred_element_type=f32).astype(bf16)
    grad_hidden_two = xor_scatter(jnp.split(grad_rows, n_ex, 0), "expert")
    grad_hidden_two = lax.psum(grad_hidden_two, "tensor")

    expert_out = jnp.dot(scaled_act, down_full, preferred_element_type=f32).astype(bf16)
    combined = xor_scatter(jnp.split(expert_out, n_ex, 0), "expert")
    def expert_grad(low, acts):
        return dotf(low, acts, ((0,), (0,))).astype(bf16)

    grads = [
        expert_grad(scaled_act, upstream_all),
        expert_grad(grad_gate_low, hidden_all),
        expert_grad(grad_up_low, hidden_all),
    ]
    grad_hidden_two, grads = lax.optimization_barrier((grad_hidden_two, grads))
    down_shard, gate_shard, up_shard = (
        dp_scatter(jnp.split(g, n_dp, 1)).reshape(group, hidden, part) for g in grads
    )
    combined, grad_hidden_two = lax.optimization_barrier((combined, grad_hidden_two))
    combined = lax.psum(combined, "tensor")
    output = lane((mixed_rows + combined.astype(f32)).astype(bf16))
    grad_hidden_two = grad_hidden_two.astype(f32)

    def attention_scatter(grad):
        grad = grad.reshape(n_dp, n_ex, width // (n_dp * n_ex), grad.shape[1])
        if n_ex == 2:
            away = lax.dynamic_index_in_dim(grad, 1 - me_ex, 1, keepdims=False)
            own = lax.dynamic_index_in_dim(grad, me_ex, 1, keepdims=False)
            grad = (own.astype(f32) + flip(away, "expert", 1).astype(f32)).astype(bf16)
        else:
            grad = lax.psum_scatter(grad, "expert", scatter_dimension=1, tiled=False)
        return dp_scatter(list(grad))

    upstream = upstream_low.astype(f32)
    experts_gain_grad = jnp.sum(grad_hidden_two * normed_two, axis=0)
    grad_mixed = upstream + norm_back(grad_hidden_two, normed_two, scale_two, gain_experts)
    grad_proj_low = grad_mixed.astype(bf16)
    grad_att_low = (
        jnp.dot(grad_proj_low, full_output, preferred_element_type=f32)
        .astype(bf16)
        .reshape(rows, heads_key, per_group, HEAD_SIZE)
    )
    output_grad = dotf(grad_proj_low, attended_low, ((0,), (0,))).astype(bf16)
    output_shard = attention_scatter(output_grad)
    grad_probs = jnp.einsum("qkgd,skd->kgqs", grad_att_low, value_low, preferred_element_type=f32)
    row_dot = jnp.sum(probs * grad_probs, axis=-1, keepdims=True)
    grad_scores = (probs * (grad_probs - row_dot)).astype(bf16)
    grad_value = jnp.einsum("kgqs,qkgd->skd", prob_low, grad_att_low, preferred_element_type=f32)
    grad_qrot = jnp.einsum(
        "kgqs,skd->qkgd", grad_scores, key_rot, preferred_element_type=f32
    ) * HEAD_SIZE ** (-0.5)
    grad_krot = jnp.einsum(
        "kgqs,qkgd->skd", grad_scores, rotated_query, preferred_element_type=f32
    ) * HEAD_SIZE ** (-0.5)
    grad_qrot = grad_qrot.reshape(rows, heads_query, HEAD_SIZE)
    grad_query_normed = rotate(grad_qrot, cosine_table, -sine_table)
    query_gain_grad = jnp.sum(grad_query_normed * normed_query, axis=(0, 1))
    grad_query_low = (
        norm_back(grad_query_normed, normed_query, scale_query, gain_query)
        .astype(bf16)
        .reshape(rows, q_cols)
    )
    grad_key_normed = rotate(grad_krot, cosine_table, -sine_table)
    key_gain_grad = jnp.sum(grad_key_normed * normed_key, axis=(0, 1))
    grad_key_low = (
        norm_back(grad_key_normed, normed_key, scale_key, gain_key).astype(bf16).reshape(rows, k_cols)
    )
    grad_value_low = grad_value.astype(bf16).reshape(rows, k_cols)
    grad_qkv_low = jnp.concatenate([grad_query_low, grad_key_low, grad_value_low], 1)
    grad_hidden_one = dotf(grad_qkv_low, full_qkv, ((1,), (1,)))
    head_gain_grads = jnp.stack([query_gain_grad, key_gain_grad]).astype(bf16)
    grad_hidden_one, head_gain_grads, _ = lax.optimization_barrier(
        (grad_hidden_one.astype(bf16), head_gain_grads, combined)
    )
    grad_hidden_one, head_gain_grads = lax.psum((grad_hidden_one, head_gain_grads), "tensor")
    grad_hidden_one = grad_hidden_one.astype(f32)
    qkv_grad = dotf(first_hidden, grad_qkv_low, ((0,), (0,))).astype(bf16)
    qkv_shard = attention_scatter(qkv_grad)
    attention_gain_grad = jnp.sum(grad_hidden_one * normed_one, axis=0)
    tokens_grad = grad_mixed + norm_back(grad_hidden_one, normed_one, scale_one, gain_attention)
    tokens_grad = lane(tokens_grad)

    blocks = lambda v: v.reshape(n_dp, n_ex, -1)
    gain_grads = jnp.concatenate(
        [
            blocks(attention_gain_grad),
            blocks(experts_gain_grad),
            lane(blocks(head_gain_grads[0].astype(f32)), 0),
            lane(blocks(head_gain_grads[1].astype(f32)), 0),
        ],
        2,
    )
    gain_grads = lane_order(gain_grads, 1, n_ex, me_ex)
    gain_grads = jnp.pad(gain_grads, ((0, 0), (0, 0), (0, -gain_grads.shape[2] % 128)))
    gain_grads = gain_grads.reshape(n_dp, n_ex, -1, 128)
    gain_grads = xor_scatter([gain_grads[:, k] for k in range(n_ex)], "expert")
    gain_grads = xor_scatter([gain_grads[k] for k in range(n_dp)], "dp").reshape(-1)
    take = lambda start, size: gain_grads[start : start + size]
    return (
        output,
        tokens_grad,
        take(0, na),
        qkv_shard[:, :q_cols],
        qkv_shard[:, q_cols : q_cols + k_cols],
        qkv_shard[:, q_cols + k_cols :],
        output_shard,
        take(2 * na, nq),
        take(2 * na + nq, nq),
        take(na, na),
        gate_shard,
        up_shard,
        down_shard,
    )


CHUNKS = 16


def line_roles(axis):
    p = lax.axis_index(axis)
    return p + 1 - 2 * (p % 2), 3 - p, (p + 1) // 2 == 1


def over(n, f, start=0):
    lax.fori_loop(start, n, lambda c, t: (f(c), t)[1], 0)


def line_sum_steps(x_ref, in_buf, mid_buf, part, out_ref, sems, axis, finish, lag=2):
    a_send, a_recv, b_send, b_recv, c_send, c_recv = sems
    side, mid, inner = line_roles(axis)
    step = x_ref.shape[0] // CHUNKS

    def rows(c):
        return pl.ds(pl.multiple_of(c * step, step), step)

    def copy(src, dst, c, send, recv, to):
        return pltpu.make_async_remote_copy(
            src.at[rows(c)], dst.at[rows(c)], send.at[c], recv.at[c], device_id={axis: to}, device_id_type=MESH
        )

    to_inner = lambda c: copy(x_ref, in_buf, c, a_send, a_recv, side)
    to_middle = lambda c: copy(part, mid_buf, c, b_send, b_recv, mid)
    to_outer = lambda c: copy(out_ref, out_ref, c, c_send, c_recv, side)

    @pl.when(jnp.logical_not(inner))
    def _():
        over(CHUNKS, lambda c: to_inner(c).start())

        def done(c):
            to_outer(c).wait_recv()
            finish(rows(c), c)
            to_inner(c).wait_send()

        over(CHUNKS, done)

    @pl.when(inner)
    def _():
        def first(c):
            to_inner(c).wait_recv()
            r = rows(c)
            part[r] = (x_ref[r].astype(f32) + in_buf[r].astype(f32)).astype(bf16)
            to_middle(c).start()

        def second(c):
            to_middle(c).wait_recv()
            r = rows(c)
            out_ref[r] = (part[r].astype(f32) + mid_buf[r].astype(f32)).astype(bf16)
            to_outer(c).start()
            finish(r, c)

        over(lag, first)
        over(CHUNKS - lag, lambda c: (first(c + lag), second(c))[0])
        over(CHUNKS, second, CHUNKS - lag)

        def done(c):
            to_middle(c).wait_send()
            to_outer(c).wait_send()

        over(CHUNKS, done)


def line_sems():
    return [pltpu.SemaphoreType.DMA((CHUNKS,))] * 6


def plane_partners():
    d, c = lax.axis_index("dp"), lax.axis_index("expert")
    ds = {0: d, 1: d + 1 - 2 * (d % 2), 2: d + 2 - 4 * (d // 2), 3: 3 - d}
    cs = {0: c, 1: 1 - c}
    return {(kd, kc): {"dp": ds[kd], "expert": cs[kc]} for kd in ds for kc in cs}


def lane_copies(src, dst, sems, to):
    wide = src.shape[1] // 4
    places = [to[k, 0]["dp"] for k in range(4)]
    return [
        pltpu.make_async_copy(
            src.at[:, pl.ds(pl.multiple_of(places[k] * wide, wide), wide)], dst.at[:, pl.ds(k * wide, wide)], sems[k]
        )
        for k in range(4)
    ]


def remote(src, dst, send, recv, to):
    return pltpu.make_async_remote_copy(src, dst, send, recv, device_id=to, device_id_type=MESH)


def nt(a, b):
    return lax.dot_general(a, b, (((1,), (1,)), ((), ())), preferred_element_type=f32)


def nn(a, b):
    return lax.dot_general(a, b, (((1,), (0,)), ((), ())), preferred_element_type=f32)


def tn(a, b):
    return lax.dot_general(a, b, (((0,), (0,)), ((), ())), preferred_element_type=f32)


def forward_kernel(
    tokens_in, cot_in, ids, weight, q_own, k_own, v_own, wo_own, gate_own, up_own, down_own, gains_own, cos, sin, key_ok,
    tokens, cot, table, x2, h2, att, qrot, krot, value, raw, probs, gains, gate, up, down, qkv_out, wo_out,
    qkv, wo, h1, proj, in_buf, mid_buf, part, summed, gain_rows,
    w_send, w_recv, core_send, core_recv, g_send, g_recv, h_send, h_recv, own_sem, out_sem, r_send, r_recv, t_sem, *line,
):
    c = lax.axis_index("expert")
    to = plane_partners()
    side, mid, inner = line_roles("tensor")
    barrier = pltpu.get_barrier_semaphore()
    others = [k for k in to if k != (0, 0)]
    for k in others:
        pl.semaphore_signal(barrier, inc=1, device_id=to[k], device_id_type=MESH)
    pl.semaphore_signal(barrier, inc=1, device_id={"tensor": side}, device_id_type=MESH)

    @pl.when(inner)
    def _():
        pl.semaphore_signal(barrier, inc=1, device_id={"tensor": mid}, device_id_type=MESH)
        pl.semaphore_wait(barrier, len(others) + 2)

    @pl.when(jnp.logical_not(inner))
    def _():
        pl.semaphore_wait(barrier, len(others) + 1)

    rows, width = tokens.shape
    piece = wo_own.shape[0]
    half = piece // 2
    tall = gate_own.shape[0] // 2
    wide = gate_own.shape[1]
    q_cols, k_cols = q_own.shape[1], k_own.shape[1]
    places = [to[k, 0]["dp"] for k in range(4)]

    def lanes(k):
        return pl.ds(pl.multiple_of(places[k] * wide, wide), wide)

    fetch = lane_copies(tokens_in, tokens, [t_sem.at[k] for k in range(4)], to)

    def cot_away(k):
        dst = cot.at[:, pl.ds(k * wide, wide)]
        return remote(cot_in.at[:, lanes(k)], dst, r_send.at[k], r_recv.at[k], to[0, 1])

    def table_away():
        return remote(
            table.at[pl.ds(0, rows)], table.at[pl.ds(rows, rows)], r_send.at[4], r_recv.at[4], to[0, 1]
        )

    def small_slot(full):
        return lambda k, h: full.at[pl.ds(pl.multiple_of((k * 2 + c) * piece + h * half, half), half)]

    early = tall // 3 * 2

    def big_slot(full):
        return lambda k, h: full.at[pl.ds(h * tall, early), pl.ds(k * wide, wide)]

    mats = [
        (lambda h: small_slot(qkv)(0, h), small_slot(qkv)),
        (lambda h: wo_own.at[pl.ds(h * half, half)], small_slot(wo)),
    ] + [
        (lambda h, own=own: own.at[pl.ds(h * tall, early)], big_slot(full))
        for own, full in ((gate_own, gate), (up_own, up), (down_own, down))
    ]

    def move(m, i):
        own, slot = mats[m]
        src, dst, way = (
            (own(0), slot(1, 0), 1), (own(1), slot(2, 1), 2), (own(0), slot(2, 0), 2), (own(1), slot(1, 1), 1),
            (slot(1, 0), slot(3, 0), 2), (slot(2, 1), slot(3, 1), 1),
        )[i]
        return remote(src, dst, w_send.at[m, i], w_recv.at[m, i], to[way, 0])

    def begin(m):
        for i in range(4):
            move(m, i).start()

    def pass_on(m):
        for i in (0, 1):
            move(m, i).wait_recv()
            move(m, 4 + i).start()

    def arrived(m):
        for i in (2, 3, 4, 5):
            move(m, i).wait_recv()

    def core_move(m, k):
        full = (qkv, wo)[m]
        block = full.at[pl.ds(pl.multiple_of((k * 2 + c) * piece, piece), piece)]
        return remote(block, block, core_send.at[m, k], core_recv.at[m, k], to[0, 1])

    def gain_move(j):
        kd, kc = others[j]
        return remote(gains_own, gains.at[kd, c], g_send.at[j], g_recv.at[j], to[kd, kc])

    own_rows = pl.ds(pl.multiple_of(c * piece, piece), piece)
    own_qkv = [
        pltpu.make_async_copy(own, qkv.at[own_rows, pl.ds(col, own.shape[1])], own_sem.at[5 + i])
        for i, (own, col) in enumerate(((q_own, 0), (k_own, q_cols), (v_own, q_cols + k_cols)))
    ]
    own_copies = [
        None,
        pltpu.make_async_copy(wo_own, wo.at[pl.ds(pl.multiple_of(c * piece, piece), piece)], own_sem.at[1]),
    ]

    for x in own_qkv + [own_copies[1]] + fetch:
        x.start()
    for k in range(4):
        cot_away(k).start()
    for x in own_qkv:
        x.wait()
    begin(0)
    for j in range(len(others)):
        gain_move(j).start()
    gains[pl.ds(0, 1), pl.ds(c, 1)] = gains_own[...].reshape(1, 1, 8, 128)
    core_move(0, 0).start()
    lane_index = lax.broadcasted_iota(jnp.int32, (rows, 128), 1)
    routes = jnp.zeros((rows, 128), f32)
    for j in range(ids.shape[1]):
        routes += jnp.where(lane_index == ids[:, j : j + 1], weight[:, j : j + 1], 0.0)
    table[0:rows] = routes
    table_away().start()
    for k in range(4):
        fetch[k].wait()
    own_copies[1].wait()
    core_move(1, 0).start()
    for j in range(len(others)):
        gain_move(j).wait_recv()
    for kd in range(4):
        for kc in range(2):
            g = gains[kd, kc]
            for j in range(2):
                col = (kd * 2 + kc) * 256 + j * 128
                gain_rows[0:1, col : col + 128] = g[j : j + 1]
                gain_rows[1:2, col : col + 128] = g[2 + j : 3 + j]
    heads = jnp.sum(gains[...].reshape(8, 8, 128), axis=0)
    gain_query, gain_key = heads[4:5], heads[5:6]

    def hidden_one(i):
        r = pl.ds(pl.multiple_of(i * 64, 64), 64)
        x = tokens[r].astype(f32)
        scale = lax.rsqrt(jnp.mean(x * x, axis=-1, keepdims=True) + epsilon)
        h1[r] = (x * scale * gain_rows[0:1]).astype(bf16)

    over(rows // 64, hidden_one)

    pass_on(0)
    begin(1)
    for k, waits in ((1, (3,)), (2, (2,)), (3, (4, 5))):
        for i in waits:
            move(0, i).wait_recv()
        core_move(0, k).start()
    pass_on(1)
    for m in (2, 3, 4):
        begin(m)
    for k in range(4):
        core_move(0, k).wait_recv()
    save_qkv = pltpu.make_async_copy(qkv, qkv_out, out_sem.at[0])
    save_qkv.start()

    def project(j):
        col = pl.ds(pl.multiple_of(j * 256, 256), 256)
        raw[:, col] = nn(h1[...], qkv[:, col])

    over(qkv.shape[1] // 256, project)

    def spin(u):
        return u * cos[...] + pltpu.roll(u, 64, 1) * sin[...]

    def unit(u):
        return u * lax.rsqrt(jnp.mean(u * u, axis=-1, keepdims=True) + epsilon)

    krot[...] = spin(unit(raw[:, pl.ds(q_cols, 128)]) * gain_key).astype(bf16)
    value[...] = raw[:, pl.ds(q_cols + 128, 128)].astype(bf16)
    block = rows // 2

    def head(h):
        col = pl.ds(pl.multiple_of(h * 128, 128), 128)
        qrot[:, col] = spin(unit(raw[:, col]) * gain_query).astype(bf16)
        for i in range(2):
            r, n = slice(i * block, (i + 1) * block), (i + 1) * block
            s = nt(qrot[r, col], krot[0:n]) * 128 ** (-0.5)
            row = lax.broadcasted_iota(jnp.int32, (block, n), 0) + i * block
            key = lax.broadcasted_iota(jnp.int32, (block, n), 1)
            s = jnp.where((key <= row) & (key_ok[:, 0:n] > 0), s, -1e30)
            e = jnp.exp(s - jnp.max(s, axis=-1, keepdims=True))
            p = (e / jnp.sum(e, axis=-1, keepdims=True)).astype(bf16)
            probs[h, r, 0:n] = p
            att[r, col] = nn(p, value[0:n]).astype(bf16)
        probs[h, 0:block, block:] = jnp.zeros((block, block), bf16)

    over(q_cols // 128, head)
    for k, waits in ((1, (3,)), (2, (2,)), (3, (4, 5))):
        for i in waits:
            move(1, i).wait_recv()
        core_move(1, k).start()
    for k in range(4):
        core_move(1, k).wait_recv()
    save_wo = pltpu.make_async_copy(wo, wo_out, out_sem.at[1])
    save_wo.start()

    def out_project(j):
        r = pl.ds(pl.multiple_of(j * 256, 256), 256)
        proj[:, r] = nt(att[...], wo[r]).astype(bf16)

    over(width // 256, out_project)
    pass_on(2)

    def give(i):
        n = rows // CHUNKS
        src = h2.at[pl.ds(pl.multiple_of(i * n, n), n)]
        dst = h2.at[pl.ds(pl.multiple_of(rows + i * n, n), n)]
        return remote(src, dst, h_send.at[i], h_recv.at[i], to[0, 1])

    def finish(r, i):
        mixed = tokens[r].astype(f32) + summed[r].astype(f32)
        x2[r] = mixed
        scale = lax.rsqrt(jnp.mean(mixed * mixed, axis=-1, keepdims=True) + epsilon)
        h2[r] = (mixed * scale * gain_rows[1:2]).astype(bf16)
        give(i).start()

    line_sum_steps(proj, in_buf, mid_buf, part, summed, line, "tensor", finish)
    pass_on(3)
    pass_on(4)
    over(CHUNKS, lambda i: give(i).wait())
    for m in (2, 3, 4):
        arrived(m)
    save_qkv.wait()
    save_wo.wait()
    for k in range(4):
        cot_away(k).wait()
    table_away().wait()
    for m in range(5):
        for i in range(6):
            move(m, i).wait_send()
    for m in range(2):
        for k in range(4):
            core_move(m, k).wait_send()
    for j in range(len(others)):
        gain_move(j).wait_send()


def forward_call(tokens, cot, ids, weight, q_own, k_own, v_own, wo_own, gate_own, up_own, down_own, gains_own, cos, sin, key_ok):
    rows, width = tokens.shape
    q_cols = q_own.shape[1]
    qkv_cols = q_cols + k_own.shape[1] + v_own.shape[1]
    tall = gate_own.shape[0]
    vmem, anyspace = pl.BlockSpec(memory_space=pltpu.VMEM), pl.BlockSpec(memory_space=pl.ANY)
    shape = jax.ShapeDtypeStruct
    outs = [
        (shape((rows, width), bf16), vmem),
        (shape((rows, width), bf16), anyspace),
        (shape((2 * rows, 128), f32), vmem),
        (shape((rows, width), f32), vmem),
        (shape((2 * rows, width), bf16), vmem),
        (shape((rows, q_cols), bf16), vmem),
        (shape((rows, q_cols), bf16), vmem),
        (shape((rows, 128), bf16), vmem),
        (shape((rows, 128), bf16), vmem),
        (shape((rows, qkv_cols), f32), vmem),
        (shape((q_cols // 128, rows, rows), bf16), vmem),
        (shape((4, 2, 8, 128), f32), vmem),
        (shape((tall, width), bf16), anyspace),
        (shape((tall, width), bf16), anyspace),
        (shape((tall, width), bf16), anyspace),
        (shape((width, qkv_cols), bf16), anyspace),
        (shape((width, q_cols), bf16), anyspace),
    ]
    dma = pltpu.SemaphoreType.DMA
    big = pltpu.VMEM((rows, width), bf16)
    return pl.pallas_call(
        forward_kernel,
        out_shape=[o[0] for o in outs],
        in_specs=[anyspace] * 2 + [vmem] * 2 + [anyspace] * 7 + [vmem] * 4,
        out_specs=[o[1] for o in outs],
        scratch_shapes=[
            pltpu.VMEM((width, qkv_cols), bf16),
            pltpu.VMEM((width, q_cols), bf16),
            big, big, big, big, big, big,
            pltpu.VMEM((2, width), f32),
            dma((5, 6)), dma((5, 6)), dma((2, 4)), dma((2, 4)), dma((7,)), dma((7,)),
            dma((CHUNKS,)), dma((CHUNKS,)), dma((8,)), dma((2,)), dma((5,)), dma((5,)), dma((4,)),
        ] + line_sems(),
        compiler_params=pltpu.CompilerParams(
            collective_id=1, has_side_effects=True, vmem_limit_bytes=60 * 2**20
        ),
        cost_estimate=pl.CostEstimate(flops=8 * 10**9, bytes_accessed=60 * 10**6, transcendentals=2 * 10**6),
        name="forward_to_experts",
    )(tokens, cot, ids, weight, q_own, k_own, v_own, wo_own, gate_own, up_own, down_own, gains_own, cos, sin, key_ok)


def turn(i):
    return i // 2 + 3 * (i % 2)


def tile(t):
    return pl.ds(pl.multiple_of(t * 256, 256), 256)


def by_half(t, f):
    for first in (1, 2):

        @pl.when(t // 3 == first - 1)
        def _(first=first):
            f(first)


def first_exchange(m, t, j, first, grad, came, send, recv, to, wide):
    return remote(
        grad.at[m, tile(t), pl.ds((3 if j else first) * wide, wide)], came(t, pl.ds(j * wide, wide)), send, recv,
        to[first, 0],
    )


def second_exchange(count, grad_at, came_at, dst_at, load_a, load_b, on_buf, l_sem, s_send, s_recv, to, wide):
    def loads(u, first):
        slot = u % 2
        return (
            pltpu.make_async_copy(grad_at(u, pl.ds((3 - first) * wide, wide)), load_a.at[slot], l_sem.at[slot, 0]),
            pltpu.make_async_copy(came_at(u, pl.ds(wide, wide)), load_b.at[slot], l_sem.at[slot, 1]),
        )

    def pass_on(u, first):
        return remote(on_buf.at[u], dst_at(u), s_send.at[u], s_recv.at[u], to[3 - first, 0])

    def start(u):
        by_half(turn(u % 6), lambda first: [x.start() for x in loads(u, first)])

    def step(u):
        def f(first):
            for x in loads(u, first):
                x.wait()
            on_buf[u] = (load_a[u % 2].astype(f32) + load_b[u % 2].astype(f32)).astype(bf16)
            pass_on(u, first).start()

        by_half(turn(u % 6), f)

        @pl.when(u + 2 < count)
        def _():
            start(u + 2)

    def finish():
        over(count, lambda u: by_half(turn(u % 6), lambda first: pass_on(u, first).wait()))

    return start, step, finish


def expert_kernel(
    h2, g_own, g_other, mine, gate_own, up_own, down_own, gate_in, up_in, down_in,
    grad_h2, out, grads, got,
    g, g_sem, gate, up, down, acts, drow, rbuf, in_buf, mid_buf, stage,
    load_sem, rest_sem, w_send, w_recv, x_send, x_recv, s_send, s_recv, keep_sem, out_sem, *line,
):
    to = plane_partners()
    side, mid, inner = line_roles("tensor")
    barrier = pltpu.get_barrier_semaphore()
    near = [(1, 0), (2, 0), (0, 1)]
    for k in near:
        pl.semaphore_signal(barrier, inc=1, device_id=to[k], device_id_type=MESH)
    pl.semaphore_signal(barrier, inc=1, device_id={"tensor": side}, device_id_type=MESH)

    @pl.when(inner)
    def _():
        pl.semaphore_signal(barrier, inc=1, device_id={"tensor": mid}, device_id_type=MESH)
        pl.semaphore_wait(barrier, len(near) + 2)

    @pl.when(jnp.logical_not(inner))
    def _():
        pl.semaphore_wait(barrier, len(near) + 1)

    tall, width = down.shape
    rows = drow.shape[0] // 2
    first_expert = 8 * lax.axis_index("expert")
    wide = width // 4
    units = tall // 8
    late = 4 * 256
    mats = ((gate_own, gate_in, gate), (up_own, up_in, up), (down_own, down_in, down))

    def shard_move(j, n):
        shard, _, full = mats[j]
        own = lambda i: shard.at[tile(turn(i))]
        slot = lambda k, i: full.at[tile(i), pl.ds(k * wide, wide)]
        a, b = 4, 5
        src, dst, way = (
            (own(a), slot(1, a), 1), (own(b), slot(2, b), 2), (own(a), slot(2, a), 2), (own(b), slot(1, b), 1),
            (slot(1, a), slot(3, a), 2), (slot(2, b), slot(3, b), 1),
        )[n]
        return remote(src, dst, w_send.at[j, n], w_recv.at[j, n], to[way, 0])

    for j in range(3):
        for n in range(4):
            shard_move(j, n).start()

    def load_own(i, j):
        return pltpu.make_async_copy(
            mats[j][0].at[tile(turn(i))], mats[j][2].at[tile(i), pl.ds(0, wide)], load_sem.at[i, j]
        )

    def load_rest(i, j):
        cols = pl.ds(wide, 3 * wide)
        return pltpu.make_async_copy(
            mats[j][1].at[tile(turn(i)), cols], mats[j][2].at[tile(i), cols], rest_sem.at[i, j]
        )

    load_g = lane_copies(g_own, g.at[pl.ds(0, rows)], [g_sem.at[k] for k in range(4)], to) + [
        pltpu.make_async_copy(g_other, g.at[pl.ds(rows, rows)], g_sem.at[4])
    ]
    for x in load_g:
        x.start()
    over(4, lambda i: [x(i, j).start() for x in (load_own, load_rest) for j in range(3)])
    for i in (4, 5):
        for j in range(3):
            load_own(i, j).start()
    for x in load_g:
        x.wait()

    def hidden_tile(i):
        t = turn(i)
        first = (t * 256) // units
        edge = (first + 1) * units - t * 256
        lanes = lax.broadcasted_iota(jnp.int32, mine.shape, 1)
        pick = lambda e: jnp.sum(jnp.where(lanes == e + first_expert, mine[...], 0.0), axis=1, keepdims=True)
        column = lax.broadcasted_iota(jnp.int32, (2 * rows, 256), 1)
        scale = jnp.where(column < edge, pick(first), pick(first + 1))
        gate_value = nt(h2[...], gate[tile(i)])
        up_value = nt(h2[...], up[tile(i)])
        grad_act = nt(g[...], down[tile(i)]) * scale
        sig = jax.nn.sigmoid(gate_value)
        silu = gate_value * sig
        acts[0, :, tile(i)] = (silu * up_value * scale).astype(bf16)
        acts[2, :, tile(i)] = (grad_act * silu).astype(bf16)
        acts[1, :, tile(i)] = (grad_act * up_value * sig * (1.0 + gate_value * (1.0 - sig))).astype(bf16)

    def parts(v):
        return v // 6, (v % 6) // 2, 1 - v % 2

    def keep(v, ab):
        m, q, s = parts(v)
        cols = pl.ds(pl.multiple_of(s * 2 * wide, 2 * wide), 2 * wide)
        return pltpu.make_async_copy(
            stage.at[v % 2, pl.ds(ab * 256, 256)], grads.at[m, tile(q + 3 * ab), cols], keep_sem.at[v % 2, ab]
        )

    def send(m, t, j, first):
        came = lambda t, cols: got.at[m, tile(t), cols]
        return first_exchange(m, t, j, first, grads, came, s_send.at[m, t, j], s_recv.at[m, t, j], to, wide)

    def flush(v):
        m, q, s = parts(v)
        for ab in range(2):
            keep(v, ab).wait()

        @pl.when((m < 2) & (s == 1))
        def _():
            send(m, q, 1, 1).start()
            send(m, q + 3, 0, 2).start()
            send(m, q + 3, 1, 2).start()

        @pl.when((m < 2) & (s == 0))
        def _():
            send(m, q, 0, 1).start()

    def grad_unit(v, rhs):
        m, q, s = parts(v)
        low = acts[m, :, pl.ds(pl.multiple_of(q * 512, 512), 512)]
        for n in range(2):
            cols = pl.ds(pl.multiple_of((2 * s + n) * wide, wide), wide)
            stage[v % 2, :, n * wide : (n + 1) * wide] = tn(low, rhs[:, cols]).astype(bf16)
        for ab in range(2):
            keep(v, ab).start()

        @pl.when(v > 0)
        def _():
            flush(v - 1)

    def early_tile(i):
        for x in (load_own, load_rest):
            for j in range(3):
                x(i, j).wait()
        hidden_tile(i)

    over(4, early_tile)

    def early_rows(j):
        col = pl.ds(pl.multiple_of(j * 256, 256), 256)
        drow[:, col] = (nn(acts[1, :, 0:late], gate[0:late, col]) + nn(acts[2, :, 0:late], up[0:late, col])).astype(bf16)

    over(width // 256, early_rows)
    over(2, lambda v: grad_unit(v, g))
    for j in range(3):
        for n in (0, 1):
            shard_move(j, n).wait_recv()
            shard_move(j, 4 + n).start()
    over(4, lambda v: grad_unit(v, g), 2)
    for i in (4, 5):
        for j in range(3):
            load_own(i, j).wait()
    for j in range(3):
        for n in (2, 3, 4, 5):
            shard_move(j, n).wait_recv()
    over(6, hidden_tile, 4)

    step = rows // CHUNKS

    def give(i):
        src = drow.at[pl.ds(pl.multiple_of(rows + i * step, step), step)]
        dst = rbuf.at[pl.ds(pl.multiple_of(i * step, step), step)]
        return remote(src, dst, x_send.at[i], x_recv.at[i], to[0, 1])

    for some in (slice(rows, 2 * rows), slice(0, rows)):

        def late_rows(j, some=some):
            col = pl.ds(pl.multiple_of(j * 256, 256), 256)
            more = nn(acts[1, some, late:], gate[late:, col]) + nn(acts[2, some, late:], up[late:, col])
            drow[some, col] = (drow[some, col].astype(f32) + more).astype(bf16)

        over(width // 256, late_rows)
        if some.start:
            over(CHUNKS, lambda i: give(i).start())

    def add_other(c):
        give(c).wait_recv()
        r = pl.ds(pl.multiple_of(c * step, step), step)
        drow[r] = (drow[r].astype(f32) + rbuf[r].astype(f32)).astype(bf16)

    def out_copy(j):
        col = pl.ds(pl.multiple_of(j * 256, 256), 256)
        return pltpu.make_async_copy(gate.at[pl.ds(0, 2 * rows), col], out.at[:, col], out_sem.at[j])

    def work(i):
        @pl.when(i < 2)
        def _():
            grad_unit(4 + i, g)

        @pl.when((i >= 2) & (i < 14))
        def _():
            grad_unit(4 + i, h2)

        @pl.when(i == 14)
        def _():
            flush(17)

        @pl.when(i >= 14)
        def _():
            j = i - 14
            col = pl.ds(pl.multiple_of(j * 256, 256), 256)
            gate[0 : 2 * rows, col] = nn(acts[0], down[:, col]).astype(bf16)
            out_copy(j).start()

    line_sum_work(
        drow, in_buf, mid_buf, drow, grad_h2, line, "tensor", rows, add_other, lambda r, c: None, work,
        14 + width // 256,
    )
    over(width // 256, lambda j: out_copy(j).wait())
    over(CHUNKS, lambda i: give(i).wait_send())
    for j in range(3):
        for n in range(6):
            shard_move(j, n).wait_send()
    for m in range(2):
        for t in range(6):
            for j in range(2):
                send(m, t, j, 1 + t // 3).wait()


def line_sum_work(x_ref, in_buf, mid_buf, part, out_ref, sems, axis, n_rows, ready, finish, work, n_work):
    a_send, a_recv, b_send, b_recv, c_send, c_recv = sems
    side, mid, inner = line_roles(axis)
    step = n_rows // CHUNKS
    steps = max(n_work, CHUNKS + 4)

    def rows(c):
        return pl.ds(pl.multiple_of(c * step, step), step)

    def copy(src, dst, c, send, recv, to):
        return pltpu.make_async_remote_copy(
            src.at[rows(c)], dst.at[rows(c)], send.at[c], recv.at[c], device_id={axis: to}, device_id_type=MESH
        )

    to_inner = lambda c: copy(x_ref, in_buf, c, a_send, a_recv, side)
    to_middle = lambda c: copy(part, mid_buf, c, b_send, b_recv, mid)
    to_outer = lambda c: copy(out_ref, out_ref, c, c_send, c_recv, side)

    @pl.when(jnp.logical_not(inner))
    def _():
        def begin(c):
            ready(c)
            to_inner(c).start()

        over(CHUNKS, begin)

        def one(i):
            @pl.when((i >= 4) & (i < CHUNKS + 4))
            def _():
                to_outer(i - 4).wait_recv()
                finish(rows(i - 4), i - 4)

            @pl.when(i < n_work)
            def _():
                work(i)

        over(steps, one)
        over(CHUNKS, lambda c: to_inner(c).wait_send())

    @pl.when(inner)
    def _():
        def first(c):
            ready(c)
            to_inner(c).wait_recv()
            r = rows(c)
            part[r] = (x_ref[r].astype(f32) + in_buf[r].astype(f32)).astype(bf16)
            to_middle(c).start()

        def second(c):
            to_middle(c).wait_recv()
            r = rows(c)
            out_ref[r] = (part[r].astype(f32) + mid_buf[r].astype(f32)).astype(bf16)
            to_outer(c).start()
            finish(r, c)

        def one(i):
            @pl.when(i < CHUNKS)
            def _():
                first(i)

            @pl.when((i >= 2) & (i < CHUNKS + 2))
            def _():
                second(i - 2)

            @pl.when(i < n_work)
            def _():
                work(i)

        over(steps, one)

        def done(c):
            to_middle(c).wait_send()
            to_outer(c).wait_send()

        over(CHUNKS, done)


def expert_call(h2, g_own, g_other, mine, gate_own, up_own, down_own, gate, up, down):
    tall, width = down.shape
    rows = h2.shape[0] // 2
    vmem, anyspace = pl.BlockSpec(memory_space=pltpu.VMEM), pl.BlockSpec(memory_space=pl.ANY)
    shape = jax.ShapeDtypeStruct
    dma = pltpu.SemaphoreType.DMA
    return pl.pallas_call(
        expert_kernel,
        out_shape=[
            shape((rows, width), bf16),
            shape((2 * rows, width), bf16),
            shape((3, tall, width), bf16),
            shape((2, tall, width // 2), bf16),
        ],
        in_specs=[vmem, anyspace, anyspace, vmem] + [anyspace] * 6,
        out_specs=[vmem, anyspace, anyspace, anyspace],
        scratch_shapes=[pltpu.VMEM((2 * rows, width), bf16), dma((5,))]
        + [pltpu.VMEM((tall, width), bf16)] * 3
        + [
            pltpu.VMEM((3, 2 * rows, tall), bf16),
            pltpu.VMEM((2 * rows, width), bf16),
            pltpu.VMEM((rows, width), bf16),
            pltpu.VMEM((rows, width), bf16),
            pltpu.VMEM((rows, width), bf16),
            pltpu.VMEM((2, 512, width // 2), bf16),
            dma((6, 3)), dma((4, 3)), dma((3, 6)), dma((3, 6)), dma((CHUNKS,)), dma((CHUNKS,)), dma((2, 6, 2)), dma((2, 6, 2)),
            dma((2, 2)), dma((width // 256,)),
        ]
        + line_sems(),
        compiler_params=pltpu.CompilerParams(
            collective_id=2, has_side_effects=True, vmem_limit_bytes=62 * 2**20
        ),
        cost_estimate=pl.CostEstimate(flops=58 * 10**9, bytes_accessed=60 * 10**6, transcendentals=2 * 10**6),
        name="experts",
    )(h2, g_own, g_other, mine, gate_own, up_own, down_own, gate, up, down)


def plane_barrier(to, z_others):
    barrier = pltpu.get_barrier_semaphore()
    others = [k for k in to if k != (0, 0)]
    for k in others:
        pl.semaphore_signal(barrier, inc=1, device_id=to[k], device_id_type=MESH)
    for z in z_others:
        pl.semaphore_signal(barrier, inc=1, device_id={"tensor": z}, device_id_type=MESH)
    pl.semaphore_wait(barrier, len(others) + len(z_others))
    return others


def z_partners():
    p = lax.axis_index("tensor")
    return [p + 1 - 2 * (p % 2), p + 2 - 4 * (p // 2), 3 - p]


def gain_vectors(gains, gain_rows):
    for kd in range(4):
        for kc in range(2):
            g = gains[kd, kc]
            for j in range(2):
                col = (kd * 2 + kc) * 256 + j * 128
                gain_rows[0:1, col : col + 128] = g[j : j + 1]
                gain_rows[1:2, col : col + 128] = g[2 + j : 3 + j]
    heads = jnp.sum(gains[...].reshape(8, 8, 128), axis=0)
    return heads[4:5], heads[5:6]


def attention_back_kernel(
    gains, cos, sin, grad_h2_in, x2_in, cot_in, qrot_in, krot_in, value_in, raw_in, probs, wo_in, qkv_in, out_part,
    grads, got,
    output, dx2, low, grad_qkv, grad_h1, gain_grads, got2, got_up,
    grad_h2, x2, cot, qrot, krot, value, raw, f_sem, wo, qkv, own_out, rbuf, in_buf, mid_buf, summed, datt, pbuf, dk, dv, gain_rows, load_a, load_b, on_buf,
    w_sem, p_sem, l_sem, x_send, x_recv, s_send, s_recv, u_send, u_recv, *line,
):
    to = plane_partners()
    fetch = [
        pltpu.make_async_copy(src, dst, f_sem.at[i])
        for i, (src, dst) in enumerate(
            ((x2_in, x2), (grad_h2_in, grad_h2), (qrot_in, qrot), (krot_in, krot), (value_in, value), (raw_in, raw))
        )
    ]
    early = fetch[:2] + lane_copies(cot_in, cot, [f_sem.at[6 + k] for k in range(4)], to)
    plane_barrier(to, z_partners())
    places = [to[k, 0]["dp"] for k in range(4)]
    rows, width = x2.shape
    wide = width // 4
    q_cols = qrot.shape[1]
    n_heads = q_cols // 128
    step = rows // CHUNKS
    rate = 128 ** (-0.5)

    def give(i):
        src = out_part.at[pl.ds(pl.multiple_of(rows + i * step, step), step)]
        dst = rbuf.at[pl.ds(pl.multiple_of(i * step, step), step)]
        return remote(src, dst, x_send.at[i], x_recv.at[i], to[0, 1])

    over(CHUNKS, lambda i: give(i).start())
    weights = [
        pltpu.make_async_copy(wo_in, wo, w_sem.at[0]),
        pltpu.make_async_copy(qkv_in, qkv, w_sem.at[1]),
        pltpu.make_async_copy(out_part.at[pl.ds(0, rows)], own_out, w_sem.at[2]),
    ]
    for w in [weights[2]] + early + [weights[0]] + fetch[2:] + [weights[1]]:
        w.start()

    def load_probs(h):
        return pltpu.make_async_copy(probs.at[h], pbuf.at[h % 2], p_sem.at[h % 2])

    def up_move(t, j, first):
        came = lambda t, cols: got_up.at[tile(t), cols]
        return first_exchange(2, t, j, first, grads, came, u_send.at[t, j], u_recv.at[t, j], to, wide)

    def up_moves(i, f):
        t = turn(i)
        by_half(t, lambda first: [f(up_move(t, j, first)) for j in range(2)])

    over(6, lambda i: up_moves(i, lambda x: x.start()))
    at = lambda ref: lambda u, cols=pl.ds(0, wide): ref.at[u // 6, tile(turn(u % 6)), cols]
    start, second_tile, second_done = second_exchange(
        12, at(grads), at(got), at(got2), load_a, load_b, on_buf, l_sem, s_send, s_recv, to, wide
    )
    start(0)
    start(1)
    load_probs(0).start()
    gain_query, gain_key = gain_vectors(gains, gain_rows)
    gain_grads[...] = jnp.zeros_like(gain_grads)
    dk[...] = jnp.zeros_like(dk)
    dv[...] = jnp.zeros_like(dv)

    def mixed_rows(i):
        r = pl.ds(pl.multiple_of(i * 64, 64), 64)
        x = x2[r]
        scale = lax.rsqrt(jnp.mean(x * x, axis=-1, keepdims=True) + epsilon)
        normed = x * scale
        grad = grad_h2[r].astype(f32)
        gain_grads[0:1, :] += jnp.sum(grad * normed, axis=0, keepdims=True)
        n = grad * gain_rows[1:2]
        d = cot[r].astype(f32) + scale * (n - normed * jnp.mean(n * normed, axis=-1, keepdims=True))
        dx2[r] = d
        low[r] = d.astype(bf16)

    def att_grads(j):
        col = pl.ds(pl.multiple_of(j * 256, 256), 256)
        datt[:, col] = nn(low[...], wo[:, col]).astype(bf16)

    def unspin(u):
        return u * cos[...] - pltpu.roll(u, 64, 1) * sin[...]

    def norm_grads(x, rotated, gain, row):
        scale = lax.rsqrt(jnp.mean(x * x, axis=-1, keepdims=True) + epsilon)
        normed = x * scale
        du = unspin(rotated)
        gain_grads[row : row + 1, 0:128] += jnp.sum(du * normed, axis=0, keepdims=True)
        n = du * gain
        return (scale * (n - normed * jnp.mean(n * normed, axis=-1, keepdims=True))).astype(bf16)

    block = rows // 2

    def head(h):
        load_probs(h).wait()

        @pl.when(h + 1 < n_heads)
        def _():
            load_probs(h + 1).start()

        col = pl.ds(pl.multiple_of(h * 128, 128), 128)
        dq = []
        for i in range(2):
            r, n = slice(i * block, (i + 1) * block), (i + 1) * block
            p_low = pbuf[h % 2, r, 0:n]
            p = p_low.astype(f32)
            dp = nt(datt[r, col], value[0:n])
            ds = (p * (dp - jnp.sum(p * dp, axis=-1, keepdims=True))).astype(bf16)
            dq.append(nn(ds, krot[0:n]) * rate)
            dk[0:n] += tn(ds, qrot[r, col])
            dv[0:n] += tn(p_low, datt[r, col])
        grad_qkv[:, col] = norm_grads(raw[:, col], jnp.concatenate(dq, 0), gain_query, 1)

    def key_value():
        grad_qkv[:, pl.ds(q_cols, 128)] = norm_grads(raw[:, pl.ds(q_cols, 128)], dk[...] * rate, gain_key, 2)
        grad_qkv[:, pl.ds(q_cols + 128, 128)] = dv[...].astype(bf16)

    def input_grads(j):
        r = pl.ds(pl.multiple_of(j * 256, 256), 256)
        grad_h1[:, r] = nt(grad_qkv[...], qkv[r]).astype(bf16)

    def work(i):
        @pl.when(i < 12)
        def _():
            second_tile(i)

        @pl.when(i == 0)
        def _():
            for x in early:
                x.wait()

        @pl.when(i < 4)
        def _():
            mixed_rows(2 * i)
            mixed_rows(2 * i + 1)

        @pl.when(i == 4)
        def _():
            weights[0].wait()
            for x in fetch[2:]:
                x.wait()

        @pl.when((i >= 4) & (i < 6))
        def _():
            att_grads(2 * (i - 4))
            att_grads(2 * (i - 4) + 1)

        @pl.when((i >= 6) & (i < 6 + n_heads))
        def _():
            head(i - 6)

        @pl.when(i == 6 + n_heads)
        def _():
            key_value()
            weights[1].wait()

        @pl.when((i > 6 + n_heads) & (i <= 10 + n_heads))
        def _():
            j = 2 * (i - 7 - n_heads)
            input_grads(j)
            input_grads(j + 1)

    def ready(c):
        @pl.when(c == 0)
        def _():
            weights[2].wait()

        give(c).wait_recv()
        r = pl.ds(pl.multiple_of(c * step, step), step)
        own_out[r] = (own_out[r].astype(f32) + rbuf[r].astype(f32)).astype(bf16)

    def finish(r, c):
        done = (x2[r] + summed[r].astype(f32)).astype(bf16)
        for k in range(4):
            output[r, pl.ds(pl.multiple_of(places[k] * wide, wide), wide)] = done[:, k * wide : (k + 1) * wide]

    line_sum_work(
        own_out, in_buf, mid_buf, own_out, summed, line, "tensor", rows, ready, finish, work, 11 + n_heads
    )
    over(CHUNKS, lambda i: give(i).wait_send())
    second_done()
    over(6, lambda i: up_moves(i, lambda x: x.wait()))


def attention_back_call(grad_h2, x2, cot, qrot, krot, value, raw, gains, cos, sin, probs, wo, qkv, out_part, grads, got):
    rows, width = x2.shape
    q_cols, qkv_cols = wo.shape[1], qkv.shape[1]
    tall = grads.shape[1]
    wide = width // 4
    vmem, anyspace = pl.BlockSpec(memory_space=pltpu.VMEM), pl.BlockSpec(memory_space=pl.ANY)
    shape = jax.ShapeDtypeStruct
    dma = pltpu.SemaphoreType.DMA
    big = pltpu.VMEM((rows, width), bf16)
    return pl.pallas_call(
        attention_back_kernel,
        out_shape=[
            shape((rows, width), bf16),
            shape((rows, width), f32),
            shape((rows, width), bf16),
            shape((rows, qkv_cols), bf16),
            shape((rows, width), bf16),
            shape((8, width), f32),
            shape((2, tall, wide), bf16),
            shape((tall, 2 * wide), bf16),
        ],
        in_specs=[vmem] * 3 + [anyspace] * 13,
        out_specs=[vmem] * 6 + [anyspace] * 2,
        scratch_shapes=[
            big,
            pltpu.VMEM((rows, width), f32),
            big,
            pltpu.VMEM((rows, q_cols), bf16),
            pltpu.VMEM((rows, 128), bf16),
            pltpu.VMEM((rows, 128), bf16),
            pltpu.VMEM((rows, qkv_cols), f32),
            dma((10,)),
            pltpu.VMEM((width, q_cols), bf16),
            pltpu.VMEM((width, qkv_cols), bf16),
            big, big, big, big, big,
            pltpu.VMEM((rows, q_cols), bf16),
            pltpu.VMEM((2, rows, rows), bf16),
            pltpu.VMEM((rows, 128), f32),
            pltpu.VMEM((rows, 128), f32),
            pltpu.VMEM((2, width), f32),
            pltpu.VMEM((2, 256, wide), bf16),
            pltpu.VMEM((2, 256, wide), bf16),
            pltpu.VMEM((12, 256, wide), bf16),
            dma((3,)), dma((2,)), dma((2, 2)), dma((CHUNKS,)), dma((CHUNKS,)), dma((12,)), dma((12,)),
            dma((6, 2)), dma((6, 2)),
        ]
        + line_sems(),
        compiler_params=pltpu.CompilerParams(
            collective_id=3, has_side_effects=True, vmem_limit_bytes=62 * 2**20
        ),
        cost_estimate=pl.CostEstimate(flops=9 * 10**9, bytes_accessed=60 * 10**6, transcendentals=10**5),
        name="attention_backward",
    )(gains, cos, sin, grad_h2, x2, cot, qrot, krot, value, raw, probs, wo, qkv, out_part, grads, got)


def last_kernel(
    gains, gain_grads, part_in, dx2_in, tokens_in, grad_qkv_in, low_in, att_in, grads, got_up,
    tokens_grad, q_shard, k_shard, v_shard, wo_shard, gain_sum, got2_up,
    part, dx2, tokens, grad_qkv, low, att, f_sem, h1, in_buf, mid_buf, half_sum, summed, gain_rows, wo_all, qkv_all, wo_core, qkv_core, wo_one, qkv_one, wo_two, qkv_two,
    ga, z_got, g_out, g_got, load_a, load_b, on_buf, l_sem, s_send, s_recv,
    z_send, z_recv, c_send, c_recv, f_send, f_recv, t_send, t_recv, g_send, g_recv, *line,
):
    fetch = [
        pltpu.make_async_copy(src, dst, f_sem.at[i])
        for i, (src, dst) in enumerate(
            (
                (part_in, part), (tokens_in, tokens), (low_in, low), (att_in, att), (grad_qkv_in, grad_qkv),
                (dx2_in, dx2),
            )
        )
    ]
    for x in fetch:
        x.start()
    c = lax.axis_index("expert")
    to = plane_partners()
    zs = z_partners()
    others = plane_barrier(to, zs)
    places = [to[k, 0]["dp"] for k in range(4)]
    rows, width = tokens.shape
    wide = width // 4
    piece = wide // 2
    half = piece // 2

    def z_move(j):
        return remote(gain_grads.at[pl.ds(0, 8), pl.ds(0, 128)], z_got.at[j], z_send.at[j], z_recv.at[j], {"tensor": zs[j]})

    for j in range(3):
        z_move(j).start()
    up_at = lambda ref: lambda u, cols=pl.ds(0, wide): ref.at[tile(turn(u)), cols]
    start, second_tile, second_done = second_exchange(
        6, lambda u, cols: grads.at[2, tile(turn(u)), cols], up_at(got_up), up_at(got2_up),
        load_a, load_b, on_buf, l_sem, s_send, s_recv, to, wide,
    )
    start(0)
    start(1)
    gain_vectors(gains, gain_rows)
    ga[...] = jnp.zeros_like(ga)

    def unit_rows(r):
        x = tokens[r].astype(f32)
        scale = lax.rsqrt(jnp.mean(x * x, axis=-1, keepdims=True) + epsilon)
        return x * scale, scale

    def hidden_one(i):
        r = pl.ds(pl.multiple_of(i * 64, 64), 64)
        h1[r] = (unit_rows(r)[0] * gain_rows[0:1]).astype(bf16)

    mats = [
        (low, att, wo_all, wo_core, wo_one, wo_two),
        (h1, grad_qkv, qkv_all, qkv_core, qkv_one, qkv_two),
    ]

    def block(k, core):
        return pl.ds(pl.multiple_of((k * 2 + core) * piece, piece), piece)

    def core_move(m, k):
        return remote(mats[m][2].at[block(k, 1 - c)], mats[m][3].at[k], c_send.at[m, k], c_recv.at[m, k], to[0, 1])

    def product(m, k, core):
        left, right, full = mats[m][:3]
        full[block(k, core)] = tn(left[:, block(k, core)], right[...]).astype(bf16)

    def away(k):
        for m in range(2):
            product(m, k, 1 - c)
            core_move(m, k).start()

    def home(k):
        for m in range(2):
            product(m, k, c)
            full, came = mats[m][2:4]
            core_move(m, k).wait_recv()
            full[block(k, c)] = (full[block(k, c)].astype(f32) + came[k].astype(f32)).astype(bf16)

    def slot(m, k, h):
        return mats[m][2].at[pl.ds(pl.multiple_of((k * 2 + c) * piece + h * half, half), half)]

    def first_move(m, h, j):
        way = 1 + h
        src = slot(m, 3 if j else way, h)
        return remote(src, mats[m][4].at[h, j], f_send.at[m, h, j], f_recv.at[m, h, j], to[way, 0])

    def second_move(m, h):
        return remote(slot(m, 2 - h, h), mats[m][5].at[h], t_send.at[m, h], t_recv.at[m, h], to[2 - h, 0])

    def add_first(m, h, j, k):
        full, one = mats[m][2], mats[m][4]
        r = pl.ds(pl.multiple_of((k * 2 + c) * piece + h * half, half), half)
        first_move(m, h, j).wait_recv()
        full[r] = (full[r].astype(f32) + one[h, j].astype(f32)).astype(bf16)

    def work(i):
        @pl.when(i == 0)
        def _():
            for x in fetch[1:]:
                x.wait()
            over(rows // 64, hidden_one)

        @pl.when(i < 6)
        def _():
            second_tile(i)

        for n, k in enumerate((3, 1, 2, 0)):

            @pl.when(i == 1 + n)
            def _(k=k):
                away(k)

            @pl.when(i == 5 + n)
            def _(k=k, n=n):
                home(k)
                if n in (1, 2):
                    for m in range(2):
                        for j in range(2):
                            first_move(m, n - 1, j).start()

        for h in range(2):

            @pl.when(i == 17 + h)
            def _(h=h):
                for m in range(2):
                    add_first(m, h, 1, 2 - h)
                    second_move(m, h).start()

    def finish(r, i):
        grad = summed[r].astype(f32)
        normed, scale = unit_rows(r)
        ga[0:1, :] += jnp.sum(grad * normed, axis=0, keepdims=True)
        n = grad * gain_rows[0:1]
        d = dx2[r] + scale * (n - normed * jnp.mean(n * normed, axis=-1, keepdims=True))
        for k in range(4):
            tokens_grad[r, pl.ds(pl.multiple_of(places[k] * wide, wide), wide)] = d[:, k * wide : (k + 1) * wide]

    fetch[0].wait()
    line_sum_work(part, in_buf, mid_buf, half_sum, summed, line, "tensor", rows, lambda k: None, finish, work, 20)

    head_rows = gain_grads[1:3, 0:128]
    for j in range(3):
        z_move(j).wait()
        head_rows += z_got[j, 1:3]
    for kd in range(4):
        for kc in range(2):
            for j in range(2):
                col = slice((kd * 2 + kc) * piece + j * 128, (kd * 2 + kc) * piece + (j + 1) * 128)
                g_out[kd, kc, j : j + 1] = ga[0:1, col]
                g_out[kd, kc, 2 + j : 3 + j] = gain_grads[0:1, col]
            g_out[kd, kc, 4:6] = head_rows

    def gain_move(j):
        kd, kc = others[j]
        core = c if kc == 0 else 1 - c
        return remote(g_out.at[kd, core], g_got.at[j], g_send.at[j], g_recv.at[j], to[kd, kc])

    for j in range(len(others)):
        gain_move(j).start()
    q_cols, k_cols = q_shard.shape[1], k_shard.shape[1]
    shards = (
        ((wo_shard, 0),),
        ((q_shard, 0), (k_shard, q_cols), (v_shard, q_cols + k_cols)),
    )
    for m in range(2):
        full, two = mats[m][2], mats[m][5]
        for h in range(2):
            add_first(m, h, 0, 0)
            second_move(m, h).wait_recv()
            r = pl.ds(pl.multiple_of(c * piece + h * half, half), half)
            for shard, col in shards[m]:
                cols = pl.ds(col, shard.shape[1])
                shard[h * half : (h + 1) * half] = full[r, cols].astype(f32) + two[h, :, cols].astype(f32)
    total = g_out[0, pl.ds(c, 1)].reshape(8, 128)
    for j in range(len(others)):
        gain_move(j).wait_recv()
        total += g_got[j]
    gain_sum[...] = total
    second_done()
    for m in range(2):
        for k in range(4):
            core_move(m, k).wait_send()
        for h in range(2):
            for j in range(2):
                first_move(m, h, j).wait_send()
            second_move(m, h).wait_send()
    for j in range(len(others)):
        gain_move(j).wait_send()


def last_call(part, dx2, tokens, grad_qkv, low, att, gains, gain_grads, grads, got_up):
    rows, width = tokens.shape
    q_cols, qkv_cols = att.shape[1], grad_qkv.shape[1]
    piece = width // 8
    vmem = pl.BlockSpec(memory_space=pltpu.VMEM)
    shape = jax.ShapeDtypeStruct
    dma = pltpu.SemaphoreType.DMA
    big = pltpu.VMEM((rows, width), bf16)
    both = lambda *lead: [pltpu.VMEM(lead + (n,), bf16) for n in (q_cols, qkv_cols)]
    return pl.pallas_call(
        last_kernel,
        out_shape=[
            shape((rows, width), f32),
            shape((piece, q_cols), f32),
            shape((piece, (qkv_cols - q_cols) // 2), f32),
            shape((piece, (qkv_cols - q_cols) // 2), f32),
            shape((piece, q_cols), f32),
            shape((8, 128), f32),
            shape((got_up.shape[0], width // 4), bf16),
        ],
        in_specs=[vmem] * 2 + [pl.BlockSpec(memory_space=pl.ANY)] * 8,
        out_specs=[vmem] * 6 + [pl.BlockSpec(memory_space=pl.ANY)],
        scratch_shapes=[
            big,
            pltpu.VMEM((rows, width), f32),
            big,
            pltpu.VMEM((rows, qkv_cols), bf16),
            big,
            pltpu.VMEM((rows, q_cols), bf16),
            dma((6,)),
        ]
        + [big, big, big, big, big, pltpu.VMEM((2, width), f32)]
        + both(width)
        + both(4, piece)
        + both(2, 2, piece // 2)
        + both(2, piece // 2)
        + [
            pltpu.VMEM((8, width), f32),
            pltpu.VMEM((3, 8, 128), f32),
            pltpu.VMEM((4, 2, 8, 128), f32),
            pltpu.VMEM((7, 8, 128), f32),
            pltpu.VMEM((2, 256, width // 4), bf16),
            pltpu.VMEM((2, 256, width // 4), bf16),
            pltpu.VMEM((6, 256, width // 4), bf16),
            dma((2, 2)), dma((6,)), dma((6,)),
            dma((3,)), dma((3,)), dma((2, 4)), dma((2, 4)), dma((2, 2, 2)), dma((2, 2, 2)), dma((2, 2)), dma((2, 2)),
            dma((7,)), dma((7,)),
        ]
        + line_sems(),
        compiler_params=pltpu.CompilerParams(
            collective_id=4, has_side_effects=True, vmem_limit_bytes=62 * 2**20
        ),
        cost_estimate=pl.CostEstimate(flops=5 * 10**9, bytes_accessed=40 * 10**6, transcendentals=10**5),
        name="input_gradients",
    )(gains, gain_grads, part, dx2, tokens, grad_qkv, low, att, grads, got_up)


def local_fast(
    tokens,
    cotangent,
    route_ids,
    route_weight,
    lengths,
    attention_norm,
    query_weight,
    key_matrix,
    value_matrix,
    output_weight,
    query_norm,
    key_norm,
    experts_norm,
    gate_weight,
    up_weight,
    down_weight,
):
    n_dp = lax.axis_size("dp")
    n_ex = lax.axis_size("expert")
    me_dp = lax.axis_index("dp")
    me_ex = lax.axis_index("expert")
    rows, width = tokens.shape
    group, hidden, part = gate_weight.shape
    length = lengths[0]
    lane = lambda x, axis=-1: lane_order(x, axis, n_dp, me_dp)

    flat = group * hidden
    na, nq = attention_norm.shape[0], query_norm.shape[0]
    q_cols, k_cols = query_weight.shape[1], key_matrix.shape[1]
    heads_query, heads_key = q_cols // HEAD_SIZE, k_cols // HEAD_SIZE
    per_group = heads_query // heads_key
    own_place = (me_dp * n_ex + me_ex) * nq
    placed = lambda v: lax.dynamic_update_slice(jnp.zeros((128,), f32), v.astype(f32), (own_place,))
    gains_own = jnp.concatenate(
        [
            attention_norm.astype(f32).reshape(-1, 128),
            experts_norm.astype(f32).reshape(-1, 128),
            placed(query_norm)[None],
            placed(key_norm)[None],
            jnp.zeros((2, 128), f32),
        ],
        0,
    )
    cosine_table, sine_table = rope_tables(rows)
    cos2 = jnp.concatenate([cosine_table[:, 0], cosine_table[:, 0]], 1)
    sin2 = jnp.concatenate([-sine_table[:, 0], sine_table[:, 0]], 1)
    key_ok = (jnp.arange(rows, dtype=jnp.int32) < length).astype(f32)[None]
    own_experts = [w.reshape(flat, part) for w in (gate_weight, up_weight, down_weight)]
    (
        inputs_low, upstream_other, table, mixed_rows, hidden_all, attended_low, rotated_query, key_rot, value_low, raw,
        prob_low, gains, gate_full, up_full, down_full, full_qkv, full_output,
    ) = forward_call(
        tokens,
        cotangent,
        route_ids,
        route_weight,
        query_weight,
        key_matrix,
        value_matrix,
        output_weight,
        *own_experts,
        gains_own,
        cos2,
        sin2,
        key_ok,
    )
    grad_hidden_two, expert_out, grads, got = expert_call(
        hidden_all, cotangent, upstream_other, table, *own_experts, gate_full, up_full, down_full
    )
    output, grad_mixed, grad_proj_low, grad_qkv_low, grad_hidden_one, gain_grads, got2, got_up = attention_back_call(
        grad_hidden_two, mixed_rows, cotangent, rotated_query, key_rot, value_low, raw, gains, cos2, sin2,
        prob_low, full_output, full_qkv, expert_out, grads, got,
    )
    tokens_grad, query_shard, key_shard, value_shard, output_shard, gain_sum, got2_up = last_call(
        grad_hidden_one, grad_mixed, inputs_low, grad_qkv_low, grad_proj_low, attended_low, gains, gain_grads,
        grads, got_up,
    )
    down_shard, gate_shard, up_shard = (
        (grads[m, :, :part].astype(f32) + first[:, :part].astype(f32) + second.astype(f32)).reshape(
            group, hidden, part
        )
        for m, (first, second) in enumerate(((got[0], got2[0]), (got[1], got2[1]), (got_up, got2_up)))
    )
    own_head = lambda row: lax.dynamic_slice_in_dim(gain_sum[row], own_place, nq, 0)
    return (
        output,
        tokens_grad,
        gain_sum[0:2].reshape(-1),
        query_shard,
        key_shard,
        value_shard,
        output_shard,
        own_head(4),
        own_head(5),
        gain_sum[2:4].reshape(-1),
        gate_shard,
        up_shard,
        down_shard,
    )


def local(*args):
    sizes = [lax.axis_size(a) for a in ("dp", "expert", "tensor")]
    return local_fast(*args) if sizes == [4, 2, 4] else local_plain(*args)


def solution(mesh):
    both = ("dp", "expert")
    rows2, rows1, mats = P(both, None), P(both), P(both, "tensor")
    experts = P("expert", "tensor", "dp")
    return jax.shard_map(
        local,
        mesh=mesh,
        in_specs=(rows2, rows2, rows2, rows2, rows1, rows1, mats, mats, mats, mats, rows1, rows1, rows1)
        + (experts,) * 3,
        out_specs=(rows2, rows2, rows1, mats, mats, mats, mats, rows1, rows1, rows1) + (experts,) * 3,
        check_vma=False,
    )
```

```python
import jax
import jax.numpy as jnp
import numpy as np
from jax import lax
from jax.experimental import pallas as pl
from jax.experimental.pallas import tpu as pltpu
from jax.sharding import PartitionSpec as P

HEAD_SIZE = 128
TOP = 8
epsilon = 1e-06
f32 = jnp.float32
bf16 = jnp.bfloat16
MESH = pl.DeviceIdType.MESH


def rms_scale(values):
    return lax.rsqrt(jnp.mean(values * values, axis=-1, keepdims=True) + epsilon)


def rope_lanes(rows):
    half = HEAD_SIZE // 2
    frequency = np.power(np.float32(1000000.0), -(np.arange(half, dtype=np.float32) * np.float32(2.0 / HEAD_SIZE)))
    angles = np.arange(rows, dtype=np.float32)[:, None] * frequency[None, :]
    cos, sin = np.cos(angles), np.sin(angles)
    return np.concatenate([cos, cos], 1), np.concatenate([-sin, sin], 1)


def rope_tables(rows):
    half_dim = HEAD_SIZE // 2
    frequency = jnp.power(f32(1000000.0), -(jnp.arange(half_dim, dtype=f32) * (2.0 / HEAD_SIZE)))
    angles = jnp.arange(rows, dtype=f32)[:, None] * frequency[None, :]
    return (jnp.cos(angles)[:, None, :], jnp.sin(angles)[:, None, :])


def rotate(values, cosine_table, sine_table):
    half_dim = values.shape[-1] // 2
    first_half = values[..., :half_dim]
    second_half = values[..., half_dim:]
    return jnp.concatenate(
        [
            first_half * cosine_table - second_half * sine_table,
            second_half * cosine_table + first_half * sine_table,
        ],
        axis=-1,
    )


def norm_back(grad_hidden, normed, scales, gains):
    grad_normed = grad_hidden * gains
    return scales * (grad_normed - normed * jnp.mean(grad_normed * normed, axis=-1, keepdims=True))


def flip(x, axis, bit):
    n = lax.axis_size(axis)
    return lax.ppermute(x, axis, [(i, i ^ bit) for i in range(n)])


def bits_of(n):
    return [1 << b for b in range(n.bit_length() - 1)]


def xor_gather(x, axis):
    pieces = [x]
    for bit in bits_of(lax.axis_size(axis)):
        pieces = pieces + [flip(p, axis, bit) for p in pieces]
    return pieces


def xor_scatter(parts, axis):
    for bit in reversed(bits_of(lax.axis_size(axis))):
        got = [flip(p, axis, bit) for p in parts[bit:]]
        parts = [
            (a.astype(f32) + r.astype(f32)).astype(a.dtype) for a, r in zip(parts[:bit], got)
        ]
    return parts[0]


def dp_scatter(blocks, axis="dp"):
    n = len(blocks)
    if n != 4:
        return xor_scatter(blocks, axis).astype(f32)
    h = blocks[0].shape[0] // 2
    add = lambda p, q: p.astype(f32) + q.astype(f32)
    done = []
    for rows, first, second in ((slice(0, h), 1, 2), (slice(h, 2 * h), 2, 1)):
        b = [x[rows] for x in blocks]
        got = flip(jnp.concatenate([b[first], b[3]], 0), axis, first)
        on = add(b[second], got[h:]).astype(bf16)
        done.append(add(b[0], got[:h]) + flip(on, axis, second).astype(f32))
    return jnp.concatenate(done, 0)


def all_pieces(x, axis, me):
    got = jnp.stack(xor_gather(x, axis), 0)
    return lane_order(got, 0, got.shape[0], me)


def dp_gather(x, axis="dp"):
    n = lax.axis_size(axis)
    if n != 4:
        return xor_gather(x, axis)
    h = x.shape[0] // 2
    a, b = x[:h], x[h:]
    a1, b2 = flip(a, axis, 1), flip(b, axis, 2)
    a2, b1 = flip(a, axis, 2), flip(b, axis, 1)
    a3, b3 = flip(a1, axis, 2), flip(b2, axis, 1)
    cat = lambda p, q: jnp.concatenate([p, q], 0)
    return [cat(a, b), cat(a1, b1), cat(a2, b2), cat(a3, b3)]


def lane_block(x, axis, n, me, k):
    axis = axis % x.ndim
    size = x.shape[axis] // n
    return lax.dynamic_slice_in_dim(x, (me ^ k) * size, size, axis)


def lane_order(x, axis, n, me):
    return jnp.concatenate([lane_block(x, axis, n, me, k) for k in range(n)], axis)


def block_scores(query_block, key_rot, length):
    query_pos = jnp.arange(query_block.shape[0], dtype=jnp.int32)
    key_pos = jnp.arange(key_rot.shape[0], dtype=jnp.int32)
    allowed = (key_pos[None, :] <= query_pos[:, None]) & (key_pos[None, :] < length)
    scores = jnp.einsum(
        "qkgd,skd->kgqs", query_block, key_rot, preferred_element_type=f32
    ) * HEAD_SIZE ** (-0.5)
    return jnp.where(allowed, scores, -1e30)


def core_rows(pieces, axis="expert"):
    n = lax.axis_size(axis)
    own = jnp.stack(pieces, 0)
    if n == 2:
        other = flip(own, axis, 1)
        first = lax.axis_index(axis) == 0
        both = jnp.stack([jnp.where(first, own, other), jnp.where(first, other, own)], 1)
    else:
        both = lax.all_gather(own, axis, axis=1, tiled=False)
    return both.reshape((-1,) + own.shape[2:])


def dotf(a, b, dims):
    return lax.dot_general(a, b, (dims, ((), ())), preferred_element_type=f32)


def local_plain(
    tokens,
    cotangent,
    route_ids,
    route_weight,
    lengths,
    attention_norm,
    query_weight,
    key_matrix,
    value_matrix,
    output_weight,
    query_norm,
    key_norm,
    experts_norm,
    gate_weight,
    up_weight,
    down_weight,
):
    n_dp = lax.axis_size("dp")
    n_ex = lax.axis_size("expert")
    me_dp = lax.axis_index("dp")
    me_ex = lax.axis_index("expert")
    rows, width = tokens.shape
    group, hidden, part = gate_weight.shape
    length = lengths[0]
    lane = lambda x, axis=-1: lane_order(x, axis, n_dp, me_dp)

    qkv_own = jnp.concatenate([query_weight, key_matrix, value_matrix], 1)
    qkv_pieces = dp_gather(qkv_own)
    wo_own, qkv_pieces = lax.optimization_barrier((output_weight, qkv_pieces))
    wo_pieces = dp_gather(wo_own)
    (gw, uw, dw), wo_pieces = lax.optimization_barrier(
        ((gate_weight, up_weight, down_weight), wo_pieces)
    )
    flat = group * hidden
    gate_up_own = jnp.concatenate([gw.reshape(flat, part), uw.reshape(flat, part)], 0)
    gate_up_pieces = dp_gather(gate_up_own)
    down_own, gate_up_pieces = lax.optimization_barrier((dw.reshape(flat, part), gate_up_pieces))
    down_pieces = dp_gather(down_own)

    na, nq = attention_norm.shape[0], query_norm.shape[0]
    gains = jnp.concatenate([attention_norm, experts_norm, query_norm, key_norm])
    gains = jnp.pad(gains, (0, -gains.size % 128)).reshape(-1, 128)
    gains = all_pieces(all_pieces(gains, "expert", me_ex), "dp", me_dp)
    gains = gains.reshape(n_dp, n_ex, -1).astype(f32)
    gain_attention = lane(gains[:, :, :na].reshape(-1))
    gain_experts = lane(gains[:, :, na : 2 * na].reshape(-1))
    gain_query = gains[:, :, 2 * na : 2 * na + nq].reshape(-1)
    gain_key = gains[:, :, 2 * na + nq : 2 * na + 2 * nq].reshape(-1)

    experts = jnp.arange(group * n_ex, dtype=jnp.int32)
    table = jnp.zeros((rows, group * n_ex), f32)
    for c in range(route_ids.shape[1]):
        table = table + jnp.where(
            route_ids[:, c, None] == experts[None, :], route_weight[:, c, None], 0.0
        )
    table = jnp.concatenate(xor_gather(table, "expert"), 0)
    mine = lax.dynamic_slice_in_dim(table, me_ex * group, group, 1)
    unit_expert = jnp.arange(flat, dtype=jnp.int32) // hidden
    route_scale = jnp.zeros((table.shape[0], flat), f32)
    for j in range(group):
        route_scale = route_scale + jnp.where(unit_expert[None, :] == j, mine[:, j, None], 0.0)

    cosine_table, sine_table = rope_tables(rows)
    inputs = lane(tokens.astype(f32))
    scale_one = rms_scale(inputs)
    normed_one = inputs * scale_one
    first_hidden = (normed_one * gain_attention).astype(bf16)
    upstream_low = lane(cotangent)
    upstream_all = jnp.concatenate(xor_gather(upstream_low, "expert"), 0)

    full_qkv = core_rows(qkv_pieces)
    qkv = jnp.dot(first_hidden, full_qkv, preferred_element_type=f32)
    q_cols, k_cols = query_weight.shape[1], key_matrix.shape[1]
    heads_query, heads_key = q_cols // HEAD_SIZE, k_cols // HEAD_SIZE
    per_group = heads_query // heads_key
    query_raw = qkv[:, :q_cols].reshape(rows, heads_query, HEAD_SIZE)
    key_raw = qkv[:, q_cols : q_cols + k_cols].reshape(rows, heads_key, HEAD_SIZE)
    value_low = qkv[:, q_cols + k_cols :].astype(bf16).reshape(rows, heads_key, HEAD_SIZE)
    scale_query = rms_scale(query_raw)
    normed_query = query_raw * scale_query
    rotated_query = (
        rotate(normed_query * gain_query, cosine_table, sine_table)
        .astype(bf16)
        .reshape(rows, heads_key, per_group, HEAD_SIZE)
    )
    scale_key = rms_scale(key_raw)
    normed_key = key_raw * scale_key
    key_rot = rotate(normed_key * gain_key, cosine_table, sine_table).astype(bf16)
    scores = block_scores(rotated_query, key_rot, length)
    row_peak = jnp.max(scores, axis=-1, keepdims=True)
    shifted = jnp.exp(scores - row_peak)
    totals = jnp.sum(shifted, axis=-1, keepdims=True)
    probs = shifted / totals
    prob_low = probs.astype(bf16)
    attended_low = (
        jnp.einsum("kgqs,skd->qkgd", prob_low, value_low, preferred_element_type=f32)
        .reshape(rows, q_cols)
        .astype(bf16)
    )
    full_output = core_rows(wo_pieces)
    projected = dotf(attended_low, full_output, ((1,), (1,)))
    mixed_rows = inputs + lax.psum(projected.astype(bf16), "tensor").astype(f32)
    scale_two = rms_scale(mixed_rows)
    normed_two = mixed_rows * scale_two
    hidden_two = (normed_two * gain_experts).astype(bf16)

    hidden_all = jnp.concatenate(xor_gather(hidden_two, "expert"), 0)
    gate_up_full = jnp.concatenate(gate_up_pieces, 1)
    down_full = jnp.concatenate(down_pieces, 1)
    gate_up = dotf(hidden_all, gate_up_full, ((1,), (1,)))
    gate_value, up_value = gate_up[:, :flat], gate_up[:, flat:]
    grad_act = lax.optimization_barrier(dotf(upstream_all, down_full, ((1,), (1,)))) * route_scale
    sigmoid_gate = jax.nn.sigmoid(gate_value)
    scaled_act = (gate_value * sigmoid_gate * up_value * route_scale).astype(bf16)
    grad_up_low = (grad_act * gate_value * sigmoid_gate).astype(bf16)
    grad_gate_low = (
        grad_act * up_value * sigmoid_gate * (1.0 + gate_value * (1.0 - sigmoid_gate))
    ).astype(bf16)
    grad_gate_up = jnp.concatenate([grad_gate_low, grad_up_low], 1)
    grad_rows = jnp.dot(grad_gate_up, gate_up_full, preferred_element_type=f32).astype(bf16)
    grad_hidden_two = xor_scatter(jnp.split(grad_rows, n_ex, 0), "expert")
    grad_hidden_two = lax.psum(grad_hidden_two, "tensor")

    expert_out = jnp.dot(scaled_act, down_full, preferred_element_type=f32).astype(bf16)
    combined = xor_scatter(jnp.split(expert_out, n_ex, 0), "expert")
    def expert_grad(low, acts):
        return dotf(low, acts, ((0,), (0,))).astype(bf16)

    grads = [
        expert_grad(scaled_act, upstream_all),
        expert_grad(grad_gate_low, hidden_all),
        expert_grad(grad_up_low, hidden_all),
    ]
    grad_hidden_two, grads = lax.optimization_barrier((grad_hidden_two, grads))
    down_shard, gate_shard, up_shard = (
        dp_scatter(jnp.split(g, n_dp, 1)).reshape(group, hidden, part) for g in grads
    )
    combined, grad_hidden_two = lax.optimization_barrier((combined, grad_hidden_two))
    combined = lax.psum(combined, "tensor")
    output = lane((mixed_rows + combined.astype(f32)).astype(bf16))
    grad_hidden_two = grad_hidden_two.astype(f32)

    def attention_scatter(grad):
        grad = grad.reshape(n_dp, n_ex, width // (n_dp * n_ex), grad.shape[1])
        if n_ex == 2:
            away = lax.dynamic_index_in_dim(grad, 1 - me_ex, 1, keepdims=False)
            own = lax.dynamic_index_in_dim(grad, me_ex, 1, keepdims=False)
            grad = (own.astype(f32) + flip(away, "expert", 1).astype(f32)).astype(bf16)
        else:
            grad = lax.psum_scatter(grad, "expert", scatter_dimension=1, tiled=False)
        return dp_scatter(list(grad))

    upstream = upstream_low.astype(f32)
    experts_gain_grad = jnp.sum(grad_hidden_two * normed_two, axis=0)
    grad_mixed = upstream + norm_back(grad_hidden_two, normed_two, scale_two, gain_experts)
    grad_proj_low = grad_mixed.astype(bf16)
    grad_att_low = (
        jnp.dot(grad_proj_low, full_output, preferred_element_type=f32)
        .astype(bf16)
        .reshape(rows, heads_key, per_group, HEAD_SIZE)
    )
    output_grad = dotf(grad_proj_low, attended_low, ((0,), (0,))).astype(bf16)
    output_shard = attention_scatter(output_grad)
    grad_probs = jnp.einsum("qkgd,skd->kgqs", grad_att_low, value_low, preferred_element_type=f32)
    row_dot = jnp.sum(probs * grad_probs, axis=-1, keepdims=True)
    grad_scores = (probs * (grad_probs - row_dot)).astype(bf16)
    grad_value = jnp.einsum("kgqs,qkgd->skd", prob_low, grad_att_low, preferred_element_type=f32)
    grad_qrot = jnp.einsum(
        "kgqs,skd->qkgd", grad_scores, key_rot, preferred_element_type=f32
    ) * HEAD_SIZE ** (-0.5)
    grad_krot = jnp.einsum(
        "kgqs,qkgd->skd", grad_scores, rotated_query, preferred_element_type=f32
    ) * HEAD_SIZE ** (-0.5)
    grad_qrot = grad_qrot.reshape(rows, heads_query, HEAD_SIZE)
    grad_query_normed = rotate(grad_qrot, cosine_table, -sine_table)
    query_gain_grad = jnp.sum(grad_query_normed * normed_query, axis=(0, 1))
    grad_query_low = (
        norm_back(grad_query_normed, normed_query, scale_query, gain_query)
        .astype(bf16)
        .reshape(rows, q_cols)
    )
    grad_key_normed = rotate(grad_krot, cosine_table, -sine_table)
    key_gain_grad = jnp.sum(grad_key_normed * normed_key, axis=(0, 1))
    grad_key_low = (
        norm_back(grad_key_normed, normed_key, scale_key, gain_key).astype(bf16).reshape(rows, k_cols)
    )
    grad_value_low = grad_value.astype(bf16).reshape(rows, k_cols)
    grad_qkv_low = jnp.concatenate([grad_query_low, grad_key_low, grad_value_low], 1)
    grad_hidden_one = dotf(grad_qkv_low, full_qkv, ((1,), (1,)))
    head_gain_grads = jnp.stack([query_gain_grad, key_gain_grad]).astype(bf16)
    grad_hidden_one, head_gain_grads, _ = lax.optimization_barrier(
        (grad_hidden_one.astype(bf16), head_gain_grads, combined)
    )
    grad_hidden_one, head_gain_grads = lax.psum((grad_hidden_one, head_gain_grads), "tensor")
    grad_hidden_one = grad_hidden_one.astype(f32)
    qkv_grad = dotf(first_hidden, grad_qkv_low, ((0,), (0,))).astype(bf16)
    qkv_shard = attention_scatter(qkv_grad)
    attention_gain_grad = jnp.sum(grad_hidden_one * normed_one, axis=0)
    tokens_grad = grad_mixed + norm_back(grad_hidden_one, normed_one, scale_one, gain_attention)
    tokens_grad = lane(tokens_grad)

    blocks = lambda v: v.reshape(n_dp, n_ex, -1)
    gain_grads = jnp.concatenate(
        [
            blocks(attention_gain_grad),
            blocks(experts_gain_grad),
            lane(blocks(head_gain_grads[0].astype(f32)), 0),
            lane(blocks(head_gain_grads[1].astype(f32)), 0),
        ],
        2,
    )
    gain_grads = lane_order(gain_grads, 1, n_ex, me_ex)
    gain_grads = jnp.pad(gain_grads, ((0, 0), (0, 0), (0, -gain_grads.shape[2] % 128)))
    gain_grads = gain_grads.reshape(n_dp, n_ex, -1, 128)
    gain_grads = xor_scatter([gain_grads[:, k] for k in range(n_ex)], "expert")
    gain_grads = xor_scatter([gain_grads[k] for k in range(n_dp)], "dp").reshape(-1)
    take = lambda start, size: gain_grads[start : start + size]
    return (
        output,
        tokens_grad,
        take(0, na),
        qkv_shard[:, :q_cols],
        qkv_shard[:, q_cols : q_cols + k_cols],
        qkv_shard[:, q_cols + k_cols :],
        output_shard,
        take(2 * na, nq),
        take(2 * na + nq, nq),
        take(na, na),
        gate_shard,
        up_shard,
        down_shard,
    )


CHUNKS = 16
SECOND = (12, 18)


def line_roles(axis):
    p = lax.axis_index(axis)
    return p + 1 - 2 * (p % 2), 3 - p, (p + 1) // 2 == 1


def over(n, f, start=0):
    lax.fori_loop(start, n, lambda c, t: (f(c), t)[1], 0)


def line_sum_steps(x_ref, in_buf, mid_buf, part, out_ref, sems, axis, finish, lag=2):
    a_send, a_recv, b_send, b_recv, c_send, c_recv = sems
    side, mid, inner = line_roles(axis)
    step = x_ref.shape[0] // CHUNKS

    def rows(c):
        return pl.ds(pl.multiple_of(c * step, step), step)

    def copy(src, dst, c, send, recv, to):
        return pltpu.make_async_remote_copy(
            src.at[rows(c)], dst.at[rows(c)], send.at[c], recv.at[c], device_id={axis: to}, device_id_type=MESH
        )

    to_inner = lambda c: copy(x_ref, in_buf, c, a_send, a_recv, side)
    to_middle = lambda c: copy(part, mid_buf, c, b_send, b_recv, mid)
    to_outer = lambda c: copy(out_ref, out_ref, c, c_send, c_recv, side)

    @pl.when(jnp.logical_not(inner))
    def _():
        over(CHUNKS, lambda c: to_inner(c).start())

        def done(c):
            to_outer(c).wait_recv()
            finish(rows(c), c)
            to_inner(c).wait_send()

        over(CHUNKS, done)

    @pl.when(inner)
    def _():
        def first(c):
            to_inner(c).wait_recv()
            r = rows(c)
            part[r] = (x_ref[r].astype(f32) + in_buf[r].astype(f32)).astype(bf16)
            to_middle(c).start()

        def second(c):
            to_middle(c).wait_recv()
            r = rows(c)
            out_ref[r] = (part[r].astype(f32) + mid_buf[r].astype(f32)).astype(bf16)
            to_outer(c).start()
            finish(r, c)

        over(lag, first)
        over(CHUNKS - lag, lambda c: (first(c + lag), second(c))[0])
        over(CHUNKS, second, CHUNKS - lag)

        def done(c):
            to_middle(c).wait_send()
            to_outer(c).wait_send()

        over(CHUNKS, done)


def line_sems():
    return [pltpu.SemaphoreType.DMA((CHUNKS,))] * 6


def plane_partners():
    d, c = lax.axis_index("dp"), lax.axis_index("expert")
    ds = {0: d, 1: d + 1 - 2 * (d % 2), 2: d + 2 - 4 * (d // 2), 3: 3 - d}
    cs = {0: c, 1: 1 - c}
    return {(kd, kc): {"dp": ds[kd], "expert": cs[kc]} for kd in ds for kc in cs}


def lane_copies(src, dst, sems, to):
    wide = src.shape[1] // 4
    places = [to[k, 0]["dp"] for k in range(4)]
    return [
        pltpu.make_async_copy(
            src.at[:, pl.ds(pl.multiple_of(places[k] * wide, wide), wide)], dst.at[:, pl.ds(k * wide, wide)], sems[k]
        )
        for k in range(4)
    ]


def remote(src, dst, send, recv, to):
    return pltpu.make_async_remote_copy(src, dst, send, recv, device_id=to, device_id_type=MESH)


def nt(a, b):
    return lax.dot_general(a, b, (((1,), (1,)), ((), ())), preferred_element_type=f32)


def nn(a, b):
    return lax.dot_general(a, b, (((1,), (0,)), ((), ())), preferred_element_type=f32)


def tn(a, b):
    return lax.dot_general(a, b, (((0,), (0,)), ((), ())), preferred_element_type=f32)


def forward_kernel(
    tokens_in, cot_in, ids, weight, lengths, q_own, k_own, v_own, wo_own, gate_own, up_own, down_own, gains_in, cos, sin,
    tokens, cot, table, x2, h2, att, qrot, krot, value, raw, probs, gains, gate, up, down, qkv_out, wo_out,
    qkv, wo, h1, proj, in_buf, mid_buf, part, summed, gain_rows, gains_own,
    w_send, w_recv, core_send, core_recv, g_send, g_recv, h_send, h_recv, own_sem, out_sem, r_send, r_recv, t_sem, *line,
):
    c = lax.axis_index("expert")
    to = plane_partners()
    side, mid, inner = line_roles("tensor")
    barrier = pltpu.get_barrier_semaphore()
    others = [k for k in to if k != (0, 0)]
    for k in others:
        pl.semaphore_signal(barrier, inc=1, device_id=to[k], device_id_type=MESH)
    pl.semaphore_signal(barrier, inc=1, device_id={"tensor": side}, device_id_type=MESH)

    @pl.when(inner)
    def _():
        pl.semaphore_signal(barrier, inc=1, device_id={"tensor": mid}, device_id_type=MESH)
        pl.semaphore_wait(barrier, len(others) + 2)

    @pl.when(jnp.logical_not(inner))
    def _():
        pl.semaphore_wait(barrier, len(others) + 1)

    rows, width = tokens.shape
    piece = wo_own.shape[0]
    half = piece // 2
    tall = gate_own.shape[0] // 2
    wide = gate_own.shape[1]
    q_cols, k_cols = q_own.shape[1], k_own.shape[1]
    places = [to[k, 0]["dp"] for k in range(4)]

    def lanes(k):
        return pl.ds(pl.multiple_of(places[k] * wide, wide), wide)

    fetch = lane_copies(tokens_in, tokens, [t_sem.at[k] for k in range(4)], to)

    def cot_away(k):
        dst = cot.at[:, pl.ds(k * wide, wide)]
        return remote(cot_in.at[:, lanes(k)], dst, r_send.at[k], r_recv.at[k], to[0, 1])

    def table_away():
        return remote(
            table.at[pl.ds(0, rows)], table.at[pl.ds(rows, rows)], r_send.at[4], r_recv.at[4], to[0, 1]
        )

    def small_slot(full):
        return lambda k, h: full.at[pl.ds(pl.multiple_of((k * 2 + c) * piece + h * half, half), half)]

    early = tall // 3 * 2

    def big_slot(full):
        return lambda k, h: full.at[pl.ds(h * tall, early), pl.ds(k * wide, wide)]

    mats = [
        (lambda h: small_slot(qkv)(0, h), small_slot(qkv)),
        (lambda h: wo_own.at[pl.ds(h * half, half)], small_slot(wo)),
    ] + [
        (lambda h, own=own: own.at[pl.ds(h * tall, early)], big_slot(full))
        for own, full in ((gate_own, gate), (up_own, up), (down_own, down))
    ]

    def move(m, i):
        own, slot = mats[m]
        src, dst, way = (
            (own(0), slot(1, 0), 1), (own(1), slot(2, 1), 2), (own(0), slot(2, 0), 2), (own(1), slot(1, 1), 1),
            (slot(1, 0), slot(3, 0), 2), (slot(2, 1), slot(3, 1), 1),
        )[i]
        return remote(src, dst, w_send.at[m, i], w_recv.at[m, i], to[way, 0])

    def begin(m):
        for i in range(4):
            move(m, i).start()

    def pass_on(m):
        for i in (0, 1):
            move(m, i).wait_recv()
            move(m, 4 + i).start()

    def arrived(m):
        for i in (2, 3, 4, 5):
            move(m, i).wait_recv()

    def core_move(m, k):
        full = (qkv, wo)[m]
        block = full.at[pl.ds(pl.multiple_of((k * 2 + c) * piece, piece), piece)]
        return remote(block, block, core_send.at[m, k], core_recv.at[m, k], to[0, 1])

    def gain_move(j):
        kd, kc = others[j]
        return remote(gains_own, gains.at[kd, c], g_send.at[j], g_recv.at[j], to[kd, kc])

    own_rows = pl.ds(pl.multiple_of(c * piece, piece), piece)
    own_qkv = [
        pltpu.make_async_copy(own, qkv.at[own_rows, pl.ds(col, own.shape[1])], own_sem.at[5 + i])
        for i, (own, col) in enumerate(((q_own, 0), (k_own, q_cols), (v_own, q_cols + k_cols)))
    ]
    own_copies = [
        None,
        pltpu.make_async_copy(wo_own, wo.at[pl.ds(pl.multiple_of(c * piece, piece), piece)], own_sem.at[1]),
    ]

    for x in own_qkv + [own_copies[1]] + fetch:
        x.start()
    for k in range(4):
        cot_away(k).start()
    gains_own[...] = gains_in[...]
    shift = (lax.axis_index("dp") * 2 + c) * (128 // 8)
    gains_own[4:6] = pltpu.roll(gains_in[...], shift, 1)[4:6]
    for x in own_qkv:
        x.wait()
    begin(0)
    for j in range(len(others)):
        gain_move(j).start()
    gains[pl.ds(0, 1), pl.ds(c, 1)] = gains_own[...].reshape(1, 1, 8, 128)
    core_move(0, 0).start()
    expert = lax.broadcasted_iota(jnp.int32, (128, rows), 0)
    routes = jnp.zeros((128, rows), f32)
    for j in range(ids.shape[0]):
        routes += jnp.where(expert == ids[j : j + 1], weight[j : j + 1], 0.0)
    table[0:rows] = routes.T
    table_away().start()
    for k in range(4):
        fetch[k].wait()
    own_copies[1].wait()
    core_move(1, 0).start()
    for j in range(len(others)):
        gain_move(j).wait_recv()
    for kd in range(4):
        for kc in range(2):
            g = gains[kd, kc]
            for j in range(2):
                col = (kd * 2 + kc) * 256 + j * 128
                gain_rows[0:1, col : col + 128] = g[j : j + 1]
                gain_rows[1:2, col : col + 128] = g[2 + j : 3 + j]
    heads = jnp.sum(gains[...].reshape(8, 8, 128), axis=0)
    gain_query, gain_key = heads[4:5], heads[5:6]

    def hidden_one(i):
        r = pl.ds(pl.multiple_of(i * 64, 64), 64)
        x = tokens[r].astype(f32)
        scale = lax.rsqrt(jnp.mean(x * x, axis=-1, keepdims=True) + epsilon)
        h1[r] = (x * scale * gain_rows[0:1]).astype(bf16)

    over(rows // 64, hidden_one)

    pass_on(0)
    begin(1)
    for k, waits in ((1, (3,)), (2, (2,)), (3, (4, 5))):
        for i in waits:
            move(0, i).wait_recv()
        core_move(0, k).start()
    pass_on(1)
    for m in (2, 3, 4):
        begin(m)
    for k in range(4):
        core_move(0, k).wait_recv()
    save_qkv = pltpu.make_async_copy(qkv, qkv_out, out_sem.at[0])
    save_qkv.start()

    def project(j):
        col = pl.ds(pl.multiple_of(j * 256, 256), 256)
        raw[:, col] = nn(h1[...], qkv[:, col])

    over(qkv.shape[1] // 256, project)

    def spin(u):
        return u * cos[...] + pltpu.roll(u, 64, 1) * sin[...]

    def unit(u):
        return u * lax.rsqrt(jnp.mean(u * u, axis=-1, keepdims=True) + epsilon)

    krot[...] = spin(unit(raw[:, pl.ds(q_cols, 128)]) * gain_key).astype(bf16)
    value[...] = raw[:, pl.ds(q_cols + 128, 128)].astype(bf16)
    block = rows // 2
    length = lengths[0]

    def head(h):
        col = pl.ds(pl.multiple_of(h * 128, 128), 128)
        qrot[:, col] = spin(unit(raw[:, col]) * gain_query).astype(bf16)
        for i in range(2):
            r, n = slice(i * block, (i + 1) * block), (i + 1) * block
            s = nt(qrot[r, col], krot[0:n]) * 128 ** (-0.5)
            row = lax.broadcasted_iota(jnp.int32, (block, n), 0) + i * block
            key = lax.broadcasted_iota(jnp.int32, (block, n), 1)
            s = jnp.where((key <= row) & (key < length), s, -1e30)
            e = jnp.exp(s - jnp.max(s, axis=-1, keepdims=True))
            p = (e / jnp.sum(e, axis=-1, keepdims=True)).astype(bf16)
            probs[h, r, 0:n] = p
            att[r, col] = nn(p, value[0:n]).astype(bf16)
        probs[h, 0:block, block:] = jnp.zeros((block, block), bf16)

    over(q_cols // 128, head)
    for k, waits in ((1, (3,)), (2, (2,)), (3, (4, 5))):
        for i in waits:
            move(1, i).wait_recv()
        core_move(1, k).start()
    for k in range(4):
        core_move(1, k).wait_recv()
    save_wo = pltpu.make_async_copy(wo, wo_out, out_sem.at[1])
    save_wo.start()

    def out_project(j):
        r = pl.ds(pl.multiple_of(j * 256, 256), 256)
        proj[:, r] = nt(att[...], wo[r]).astype(bf16)

    over(width // 256, out_project)
    pass_on(2)

    def give(i):
        n = rows // CHUNKS
        src = h2.at[pl.ds(pl.multiple_of(i * n, n), n)]
        dst = h2.at[pl.ds(pl.multiple_of(rows + i * n, n), n)]
        return remote(src, dst, h_send.at[i], h_recv.at[i], to[0, 1])

    def finish(r, i):
        mixed = tokens[r].astype(f32) + summed[r].astype(f32)
        x2[r] = mixed
        scale = lax.rsqrt(jnp.mean(mixed * mixed, axis=-1, keepdims=True) + epsilon)
        h2[r] = (mixed * scale * gain_rows[1:2]).astype(bf16)
        give(i).start()

    line_sum_steps(proj, in_buf, mid_buf, part, summed, line, "tensor", finish)
    pass_on(3)
    pass_on(4)
    over(CHUNKS, lambda i: give(i).wait())
    for m in (2, 3, 4):
        arrived(m)
    save_qkv.wait()
    save_wo.wait()
    for k in range(4):
        cot_away(k).wait()
    table_away().wait()
    for m in range(5):
        for i in range(6):
            move(m, i).wait_send()
    for m in range(2):
        for k in range(4):
            core_move(m, k).wait_send()
    for j in range(len(others)):
        gain_move(j).wait_send()


def forward_call(tokens, cot, ids, weight, lengths, q_own, k_own, v_own, wo_own, gate_own, up_own, down_own, gains, cos, sin):
    rows, width = tokens.shape
    q_cols = q_own.shape[1]
    qkv_cols = q_cols + k_own.shape[1] + v_own.shape[1]
    tall = gate_own.shape[0]
    vmem, anyspace = pl.BlockSpec(memory_space=pltpu.VMEM), pl.BlockSpec(memory_space=pl.ANY)
    shape = jax.ShapeDtypeStruct
    outs = [
        (shape((rows, width), bf16), vmem),
        (shape((rows, width), bf16), anyspace),
        (shape((2 * rows, 128), f32), vmem),
        (shape((rows, width), f32), vmem),
        (shape((2 * rows, width), bf16), vmem),
        (shape((rows, q_cols), bf16), vmem),
        (shape((rows, q_cols), bf16), vmem),
        (shape((rows, 128), bf16), vmem),
        (shape((rows, 128), bf16), vmem),
        (shape((rows, qkv_cols), f32), vmem),
        (shape((q_cols // 128, rows, rows), bf16), vmem),
        (shape((4, 2, 8, 128), f32), vmem),
        (shape((tall, width), bf16), anyspace),
        (shape((tall, width), bf16), anyspace),
        (shape((tall, width), bf16), anyspace),
        (shape((width, qkv_cols), bf16), anyspace),
        (shape((width, q_cols), bf16), anyspace),
    ]
    dma = pltpu.SemaphoreType.DMA
    big = pltpu.VMEM((rows, width), bf16)
    return pl.pallas_call(
        forward_kernel,
        out_shape=[o[0] for o in outs],
        in_specs=[anyspace] * 2
        + [vmem] * 2
        + [pl.BlockSpec(memory_space=pltpu.SMEM)]
        + [anyspace] * 7
        + [vmem] * 3,
        out_specs=[o[1] for o in outs],
        scratch_shapes=[
            pltpu.VMEM((width, qkv_cols), bf16),
            pltpu.VMEM((width, q_cols), bf16),
            big, big, big, big, big, big,
            pltpu.VMEM((2, width), f32),
            pltpu.VMEM((8, 128), f32),
            dma((5, 6)), dma((5, 6)), dma((2, 4)), dma((2, 4)), dma((7,)), dma((7,)),
            dma((CHUNKS,)), dma((CHUNKS,)), dma((8,)), dma((2,)), dma((5,)), dma((5,)), dma((4,)),
        ] + line_sems(),
        compiler_params=pltpu.CompilerParams(
            collective_id=1, has_side_effects=True, vmem_limit_bytes=60 * 2**20
        ),
        cost_estimate=pl.CostEstimate(flops=8 * 10**9, bytes_accessed=60 * 10**6, transcendentals=2 * 10**6),
        name="forward_to_experts",
    )(tokens, cot, ids, weight, lengths, q_own, k_own, v_own, wo_own, gate_own, up_own, down_own, gains, cos, sin)


def turn(i):
    return i // 2 + 3 * (i % 2)


def tile(t):
    return pl.ds(pl.multiple_of(t * 256, 256), 256)


def by_half(t, f):
    for first in (1, 2):

        @pl.when(t // 3 == first - 1)
        def _(first=first):
            f(first)


def first_exchange(m, t, j, first, grad, came, send, recv, to, wide):
    return remote(
        grad.at[m, tile(t), pl.ds((3 if j else first) * wide, wide)], came(t, pl.ds(j * wide, wide)), send, recv,
        to[first, 0],
    )


def second_exchange(count, grad_at, came_at, dst_at, load_a, load_b, on_buf, l_sem, s_send, s_recv, to, wide):
    def loads(u, first):
        slot = u % 2
        return (
            pltpu.make_async_copy(grad_at(u, pl.ds((3 - first) * wide, wide)), load_a.at[slot], l_sem.at[slot, 0]),
            pltpu.make_async_copy(came_at(u, pl.ds(wide, wide)), load_b.at[slot], l_sem.at[slot, 1]),
        )

    def pass_on(u, first):
        return remote(on_buf.at[u], dst_at(u), s_send.at[u], s_recv.at[u], to[3 - first, 0])

    def start(u):
        by_half(turn(u % 6), lambda first: [x.start() for x in loads(u, first)])

    def step(u):
        def f(first):
            for x in loads(u, first):
                x.wait()
            on_buf[u] = (load_a[u % 2].astype(f32) + load_b[u % 2].astype(f32)).astype(bf16)
            pass_on(u, first).start()

        by_half(turn(u % 6), f)

        @pl.when(u + 2 < count)
        def _():
            start(u + 2)

    def finish():
        over(count, lambda u: by_half(turn(u % 6), lambda first: pass_on(u, first).wait()))

    return start, step, finish


def expert_kernel(
    h2, g_own, g_other, mine, gate_own, up_own, down_own, gate_in, up_in, down_in,
    grad_h2, out, out_other, grads, got,
    g, g_sem, gate, up, down, acts, drow, rbuf, in_buf, mid_buf, stage,
    load_sem, rest_sem, w_send, w_recv, x_send, x_recv, s_send, s_recv, keep_sem, out_sem, *line,
):
    to = plane_partners()
    side, mid, inner = line_roles("tensor")
    barrier = pltpu.get_barrier_semaphore()
    near = [(1, 0), (2, 0), (0, 1)]
    for k in near:
        pl.semaphore_signal(barrier, inc=1, device_id=to[k], device_id_type=MESH)
    pl.semaphore_signal(barrier, inc=1, device_id={"tensor": side}, device_id_type=MESH)

    @pl.when(inner)
    def _():
        pl.semaphore_signal(barrier, inc=1, device_id={"tensor": mid}, device_id_type=MESH)
        pl.semaphore_wait(barrier, len(near) + 2)

    @pl.when(jnp.logical_not(inner))
    def _():
        pl.semaphore_wait(barrier, len(near) + 1)

    tall, width = down.shape
    rows = drow.shape[0] // 2
    first_expert = 8 * lax.axis_index("expert")
    wide = width // 4
    units = tall // 8
    late = 4 * 256
    mats = ((gate_own, gate_in, gate), (up_own, up_in, up), (down_own, down_in, down))

    def shard_move(j, n):
        shard, _, full = mats[j]
        own = lambda i: shard.at[tile(turn(i))]
        slot = lambda k, i: full.at[tile(i), pl.ds(k * wide, wide)]
        a, b = 4, 5
        src, dst, way = (
            (own(a), slot(1, a), 1), (own(b), slot(2, b), 2), (own(a), slot(2, a), 2), (own(b), slot(1, b), 1),
            (slot(1, a), slot(3, a), 2), (slot(2, b), slot(3, b), 1),
        )[n]
        return remote(src, dst, w_send.at[j, n], w_recv.at[j, n], to[way, 0])

    for j in range(3):
        for n in range(4):
            shard_move(j, n).start()

    def load_own(i, j):
        return pltpu.make_async_copy(
            mats[j][0].at[tile(turn(i))], mats[j][2].at[tile(i), pl.ds(0, wide)], load_sem.at[i, j]
        )

    def load_rest(i, j):
        cols = pl.ds(wide, 3 * wide)
        return pltpu.make_async_copy(
            mats[j][1].at[tile(turn(i)), cols], mats[j][2].at[tile(i), cols], rest_sem.at[i, j]
        )

    load_g = lane_copies(g_own, g.at[pl.ds(0, rows)], [g_sem.at[k] for k in range(4)], to) + [
        pltpu.make_async_copy(g_other, g.at[pl.ds(rows, rows)], g_sem.at[4])
    ]
    for x in load_g:
        x.start()
    over(4, lambda i: [x(i, j).start() for x in (load_own, load_rest) for j in range(3)])
    for i in (4, 5):
        for j in range(3):
            load_own(i, j).start()
    for x in load_g:
        x.wait()

    def hidden_tile(i):
        t = turn(i)
        first = (t * 256) // units
        edge = (first + 1) * units - t * 256
        lanes = lax.broadcasted_iota(jnp.int32, mine.shape, 1)
        pick = lambda e: jnp.sum(jnp.where(lanes == e + first_expert, mine[...], 0.0), axis=1, keepdims=True)
        column = lax.broadcasted_iota(jnp.int32, (2 * rows, 256), 1)
        scale = jnp.where(column < edge, pick(first), pick(first + 1))
        gate_value = nt(h2[...], gate[tile(i)])
        up_value = nt(h2[...], up[tile(i)])
        grad_act = nt(g[...], down[tile(i)]) * scale
        sig = jax.nn.sigmoid(gate_value)
        silu = gate_value * sig
        acts[0, :, tile(i)] = (silu * up_value * scale).astype(bf16)
        acts[2, :, tile(i)] = (grad_act * silu).astype(bf16)
        acts[1, :, tile(i)] = (grad_act * up_value * sig * (1.0 + gate_value * (1.0 - sig))).astype(bf16)

    early_unit = lambda e: (e // 4, (e % 4) // 2, 1 - e % 2, e)
    last_unit = lambda e: (e // 2, 2, 1 - e % 2, 8 + e)
    up_unit = lambda e: (2, e // 2, 1 - e % 2, 12 + e)

    def keep(unit, ab):
        m, q, s, n = unit
        cols = pl.ds(pl.multiple_of(s * 2 * wide, 2 * wide), 2 * wide)
        return pltpu.make_async_copy(
            stage.at[n % 2, pl.ds(ab * 256, 256)], grads.at[m, tile(q + 3 * ab), cols], keep_sem.at[n % 2, ab]
        )

    def send(m, t, j, first):
        came = lambda t, cols: got.at[m, tile(t), cols]
        return first_exchange(m, t, j, first, grads, came, s_send.at[m, t, j], s_recv.at[m, t, j], to, wide)

    def flush(unit, goes=True):
        m, q, s, n = unit
        for ab in range(2):
            keep(unit, ab).wait()

        @pl.when(goes & (s == 1))
        def _():
            send(m, q, 1, 1).start()
            send(m, q + 3, 0, 2).start()
            send(m, q + 3, 1, 2).start()

        @pl.when(goes & (s == 0))
        def _():
            send(m, q, 0, 1).start()

    def grad_unit(unit, rhs):
        m, q, s, n = unit
        low = acts[m, :, pl.ds(pl.multiple_of(q * 512, 512), 512)]
        for b in range(2):
            cols = pl.ds(pl.multiple_of((2 * s + b) * wide, wide), wide)
            stage[n % 2, :, b * wide : (b + 1) * wide] = tn(low, rhs[:, cols]).astype(bf16)
        for ab in range(2):
            keep(unit, ab).start()

    def early_grads(rhs):
        def one(e):
            grad_unit(early_unit(e), rhs)

            @pl.when(e > 0)
            def _():
                flush(early_unit(e - 1))

        return one

    def early_tile(i):
        for x in (load_own, load_rest):
            for j in range(3):
                x(i, j).wait()
        hidden_tile(i)

    over(4, early_tile)

    def early_rows(j):
        col = pl.ds(pl.multiple_of(j * 256, 256), 256)
        drow[:, col] = (nn(acts[1, :, 0:late], gate[0:late, col]) + nn(acts[2, :, 0:late], up[0:late, col])).astype(bf16)

    over(width // 256, early_rows)
    over(2, early_grads(g))
    for j in range(3):
        for n in (0, 1):
            shard_move(j, n).wait_recv()
            shard_move(j, 4 + n).start()
    over(4, early_grads(g), 2)
    over(8, early_grads(h2), 4)
    flush(early_unit(7))
    for i in (4, 5):
        for j in range(3):
            load_own(i, j).wait()
    for j in range(3):
        for n in (2, 3, 4, 5):
            shard_move(j, n).wait_recv()
    over(6, hidden_tile, 4)

    step = rows // CHUNKS

    def give(i):
        src = drow.at[pl.ds(pl.multiple_of(rows + i * step, step), step)]
        dst = rbuf.at[pl.ds(pl.multiple_of(i * step, step), step)]
        return remote(src, dst, x_send.at[i], x_recv.at[i], to[0, 1])

    for some in (slice(rows, 2 * rows), slice(0, rows)):

        def late_rows(j, some=some):
            col = pl.ds(pl.multiple_of(j * 256, 256), 256)
            more = nn(acts[1, some, late:], gate[late:, col]) + nn(acts[2, some, late:], up[late:, col])
            drow[some, col] = (drow[some, col].astype(f32) + more).astype(bf16)

        over(width // 256, late_rows)
        if some.start:
            over(CHUNKS, lambda i: give(i).start())

    def add_other(c):
        give(c).wait_recv()
        r = pl.ds(pl.multiple_of(c * step, step), step)
        drow[r] = (drow[r].astype(f32) + rbuf[r].astype(f32)).astype(bf16)

    def out_copies(j):
        col = pl.ds(pl.multiple_of(j * 256, 256), 256)
        return (
            pltpu.make_async_copy(gate.at[pl.ds(0, rows), col], out.at[:, col], out_sem.at[0, j]),
            remote(
                gate.at[pl.ds(rows, rows), col], out_other.at[:, col], out_sem.at[1, j], out_sem.at[2, j], to[0, 1]
            ),
        )

    def work(i):
        @pl.when(i < 2)
        def _():
            grad_unit(last_unit(i), g)

        @pl.when((i >= 2) & (i < 4))
        def _():
            grad_unit(last_unit(i), h2)

        @pl.when((i >= 4) & (i < 10))
        def _():
            grad_unit(up_unit(i - 4), h2)

        @pl.when((i >= 1) & (i < 5))
        def _():
            flush(last_unit(i - 1))

        @pl.when((i >= 5) & (i < 11))
        def _():
            flush(up_unit(i - 5), i < 7)

        @pl.when(i >= 10)
        def _():
            j = i - 10
            col = pl.ds(pl.multiple_of(j * 256, 256), 256)
            gate[0 : 2 * rows, col] = nn(acts[0], down[:, col]).astype(bf16)
            for x in out_copies(j):
                x.start()

    line_sum_work(
        drow, in_buf, mid_buf, drow, grad_h2, line, "tensor", rows, add_other, lambda r, c: None, work,
        10 + width // 256,
    )
    over(width // 256, lambda j: [x.wait() for x in out_copies(j)])
    over(CHUNKS, lambda i: give(i).wait_send())
    for j in range(3):
        for n in range(6):
            shard_move(j, n).wait_send()
    for m, t in [(m, t) for m in range(2) for t in range(6)] + [(2, 0), (2, 3)]:
        for j in range(2):
            send(m, t, j, 1 + t // 3).wait()


def line_sum_work(x_ref, in_buf, mid_buf, part, out_ref, sems, axis, n_rows, ready, finish, work, n_work):
    a_send, a_recv, b_send, b_recv, c_send, c_recv = sems
    side, mid, inner = line_roles(axis)
    step = n_rows // CHUNKS
    steps = max(n_work, CHUNKS + 4)

    def rows(c):
        return pl.ds(pl.multiple_of(c * step, step), step)

    def copy(src, dst, c, send, recv, to):
        return pltpu.make_async_remote_copy(
            src.at[rows(c)], dst.at[rows(c)], send.at[c], recv.at[c], device_id={axis: to}, device_id_type=MESH
        )

    to_inner = lambda c: copy(x_ref, in_buf, c, a_send, a_recv, side)
    to_middle = lambda c: copy(part, mid_buf, c, b_send, b_recv, mid)
    to_outer = lambda c: copy(out_ref, out_ref, c, c_send, c_recv, side)

    @pl.when(jnp.logical_not(inner))
    def _():
        def begin(c):
            ready(c)
            to_inner(c).start()

        over(CHUNKS, begin)

        def one(i):
            @pl.when((i >= 4) & (i < CHUNKS + 4))
            def _():
                to_outer(i - 4).wait_recv()
                finish(rows(i - 4), i - 4)

            @pl.when(i < n_work)
            def _():
                work(i)

        over(steps, one)
        over(CHUNKS, lambda c: to_inner(c).wait_send())

    @pl.when(inner)
    def _():
        def first(c):
            ready(c)
            to_inner(c).wait_recv()
            r = rows(c)
            part[r] = (x_ref[r].astype(f32) + in_buf[r].astype(f32)).astype(bf16)
            to_middle(c).start()

        def second(c):
            to_middle(c).wait_recv()
            r = rows(c)
            out_ref[r] = (part[r].astype(f32) + mid_buf[r].astype(f32)).astype(bf16)
            to_outer(c).start()
            finish(r, c)

        def one(i):
            @pl.when(i < CHUNKS)
            def _():
                first(i)

            @pl.when((i >= 2) & (i < CHUNKS + 2))
            def _():
                second(i - 2)

            @pl.when(i < n_work)
            def _():
                work(i)

        over(steps, one)

        def done(c):
            to_middle(c).wait_send()
            to_outer(c).wait_send()

        over(CHUNKS, done)


def expert_call(h2, g_own, g_other, mine, gate_own, up_own, down_own, gate, up, down):
    tall, width = down.shape
    rows = h2.shape[0] // 2
    vmem, anyspace = pl.BlockSpec(memory_space=pltpu.VMEM), pl.BlockSpec(memory_space=pl.ANY)
    shape = jax.ShapeDtypeStruct
    dma = pltpu.SemaphoreType.DMA
    return pl.pallas_call(
        expert_kernel,
        out_shape=[
            shape((rows, width), bf16),
            shape((rows, width), bf16),
            shape((rows, width), bf16),
            shape((3, tall, width), bf16),
            shape((3, tall, width // 2), bf16),
        ],
        in_specs=[vmem, anyspace, anyspace, vmem] + [anyspace] * 6,
        out_specs=[vmem, anyspace, anyspace, anyspace, anyspace],
        scratch_shapes=[pltpu.VMEM((2 * rows, width), bf16), dma((5,))]
        + [pltpu.VMEM((tall, width), bf16)] * 3
        + [
            pltpu.VMEM((3, 2 * rows, tall), bf16),
            pltpu.VMEM((2 * rows, width), bf16),
            pltpu.VMEM((rows, width), bf16),
            pltpu.VMEM((rows, width), bf16),
            pltpu.VMEM((rows, width), bf16),
            pltpu.VMEM((2, 512, width // 2), bf16),
            dma((6, 3)), dma((4, 3)), dma((3, 6)), dma((3, 6)), dma((CHUNKS,)), dma((CHUNKS,)), dma((3, 6, 2)), dma((3, 6, 2)),
            dma((2, 2)), dma((3, width // 256)),
        ]
        + line_sems(),
        compiler_params=pltpu.CompilerParams(
            collective_id=2, has_side_effects=True, vmem_limit_bytes=62 * 2**20
        ),
        cost_estimate=pl.CostEstimate(flops=58 * 10**9, bytes_accessed=60 * 10**6, transcendentals=2 * 10**6),
        name="experts",
    )(h2, g_own, g_other, mine, gate_own, up_own, down_own, gate, up, down)


def plane_barrier(to, z_others):
    barrier = pltpu.get_barrier_semaphore()
    others = [k for k in to if k != (0, 0)]
    for k in others:
        pl.semaphore_signal(barrier, inc=1, device_id=to[k], device_id_type=MESH)
    for z in z_others:
        pl.semaphore_signal(barrier, inc=1, device_id={"tensor": z}, device_id_type=MESH)
    pl.semaphore_wait(barrier, len(others) + len(z_others))
    return others


def z_partners():
    p = lax.axis_index("tensor")
    return [p + 1 - 2 * (p % 2), p + 2 - 4 * (p // 2), 3 - p]


def gain_vectors(gains, gain_rows):
    for kd in range(4):
        for kc in range(2):
            g = gains[kd, kc]
            for j in range(2):
                col = (kd * 2 + kc) * 256 + j * 128
                gain_rows[0:1, col : col + 128] = g[j : j + 1]
                gain_rows[1:2, col : col + 128] = g[2 + j : 3 + j]
    heads = jnp.sum(gains[...].reshape(8, 8, 128), axis=0)
    return heads[4:5], heads[5:6]


def attention_back_kernel(
    gains, cos, sin, grad_h2_in, x2_in, cot_in, qrot_in, krot_in, value_in, raw_in, probs, wo_in, qkv_in, out_own, out_other,
    grads, _,
    output, dx2_out, low_out, grad_qkv, grad_h1, gain_grads, got2, got,
    grad_h2, x2, cot, qrot, krot, value, raw, f_sem, dx2, low, wo, qkv, own_out, rbuf, in_buf, mid_buf, summed, datt, pbuf, dk, dv, gain_rows, load_a, load_b, on_buf,
    w_sem, p_sem, l_sem, s_send, s_recv, u_send, u_recv, *line,
):
    to = plane_partners()
    fetch = [
        pltpu.make_async_copy(src, dst, f_sem.at[i])
        for i, (src, dst) in enumerate(
            ((x2_in, x2), (grad_h2_in, grad_h2), (qrot_in, qrot), (krot_in, krot), (value_in, value), (raw_in, raw))
        )
    ]
    early = fetch[:2] + lane_copies(cot_in, cot, [f_sem.at[6 + k] for k in range(4)], to)
    plane_barrier(to, z_partners())
    places = [to[k, 0]["dp"] for k in range(4)]
    rows, width = x2.shape
    wide = width // 4
    q_cols = qrot.shape[1]
    n_heads = q_cols // 128
    step = rows // CHUNKS
    rate = 128 ** (-0.5)

    weights = [
        pltpu.make_async_copy(wo_in, wo, w_sem.at[0]),
        pltpu.make_async_copy(qkv_in, qkv, w_sem.at[1]),
        pltpu.make_async_copy(out_own, own_out, w_sem.at[2]),
        pltpu.make_async_copy(out_other, rbuf, w_sem.at[3]),
    ]
    flushes = [
        pltpu.make_async_copy(dx2, dx2_out, w_sem.at[4]),
        pltpu.make_async_copy(low, low_out, w_sem.at[5]),
    ]
    for w in weights[2:] + early + [weights[0]] + fetch[2:] + [weights[1]]:
        w.start()

    def load_probs(h):
        return pltpu.make_async_copy(probs.at[h], pbuf.at[h % 2], p_sem.at[h % 2])

    def up_move(t, j, first):
        came = lambda t, cols: got.at[2, tile(t), cols]
        return first_exchange(2, t, j, first, grads, came, u_send.at[t, j], u_recv.at[t, j], to, wide)

    def up_moves(i, f):
        t = turn(i)
        by_half(t, lambda first: [f(up_move(t, j, first)) for j in range(2)])

    over(6, lambda i: up_moves(i, lambda x: x.start()), 2)
    at = lambda ref: lambda u, cols=pl.ds(0, wide): ref.at[u // 6, tile(turn(u % 6)), cols]
    start, second_tile, second_done = second_exchange(
        12, at(grads), at(got), at(got2), load_a, load_b, on_buf, l_sem, s_send, s_recv, to, wide
    )
    start(0)
    start(1)
    load_probs(0).start()
    gain_query, gain_key = gain_vectors(gains, gain_rows)
    gain_grads[...] = jnp.zeros_like(gain_grads)
    dk[...] = jnp.zeros_like(dk)
    dv[...] = jnp.zeros_like(dv)

    def mixed_rows(i):
        r = pl.ds(pl.multiple_of(i * 64, 64), 64)
        x = x2[r]
        scale = lax.rsqrt(jnp.mean(x * x, axis=-1, keepdims=True) + epsilon)
        normed = x * scale
        grad = grad_h2[r].astype(f32)
        gain_grads[0:1, :] += jnp.sum(grad * normed, axis=0, keepdims=True)
        n = grad * gain_rows[1:2]
        d = cot[r].astype(f32) + scale * (n - normed * jnp.mean(n * normed, axis=-1, keepdims=True))
        dx2[r] = d
        low[r] = d.astype(bf16)

    def att_grads(j):
        col = pl.ds(pl.multiple_of(j * 256, 256), 256)
        datt[:, col] = nn(low[...], wo[:, col]).astype(bf16)

    def unspin(u):
        return u * cos[...] - pltpu.roll(u, 64, 1) * sin[...]

    def norm_grads(x, rotated, gain, row):
        scale = lax.rsqrt(jnp.mean(x * x, axis=-1, keepdims=True) + epsilon)
        normed = x * scale
        du = unspin(rotated)
        gain_grads[row : row + 1, 0:128] += jnp.sum(du * normed, axis=0, keepdims=True)
        n = du * gain
        return (scale * (n - normed * jnp.mean(n * normed, axis=-1, keepdims=True))).astype(bf16)

    block = rows // 2

    def head(h):
        load_probs(h).wait()

        @pl.when(h + 1 < n_heads)
        def _():
            load_probs(h + 1).start()

        col = pl.ds(pl.multiple_of(h * 128, 128), 128)
        dq = []
        for i in range(2):
            r, n = slice(i * block, (i + 1) * block), (i + 1) * block
            p_low = pbuf[h % 2, r, 0:n]
            p = p_low.astype(f32)
            dp = nt(datt[r, col], value[0:n])
            ds = (p * (dp - jnp.sum(p * dp, axis=-1, keepdims=True))).astype(bf16)
            dq.append(nn(ds, krot[0:n]) * rate)
            dk[0:n] += tn(ds, qrot[r, col])
            dv[0:n] += tn(p_low, datt[r, col])
        grad_qkv[:, col] = norm_grads(raw[:, col], jnp.concatenate(dq, 0), gain_query, 1)

    def key_value():
        grad_qkv[:, pl.ds(q_cols, 128)] = norm_grads(raw[:, pl.ds(q_cols, 128)], dk[...] * rate, gain_key, 2)
        grad_qkv[:, pl.ds(q_cols + 128, 128)] = dv[...].astype(bf16)

    def input_grads(j):
        r = pl.ds(pl.multiple_of(j * 256, 256), 256)
        grad_h1[:, r] = nt(grad_qkv[...], qkv[r]).astype(bf16)

    def work(i):
        @pl.when(i < 12)
        def _():
            second_tile(i)

        @pl.when(i == 0)
        def _():
            for x in early:
                x.wait()

        @pl.when(i < 4)
        def _():
            mixed_rows(2 * i)
            mixed_rows(2 * i + 1)

        @pl.when(i == 4)
        def _():
            weights[0].wait()
            for x in flushes:
                x.start()
            for x in fetch[2:]:
                x.wait()

        @pl.when((i >= 4) & (i < 6))
        def _():
            att_grads(2 * (i - 4))
            att_grads(2 * (i - 4) + 1)

        @pl.when((i >= 6) & (i < 6 + n_heads))
        def _():
            head(i - 6)

        @pl.when(i == 6 + n_heads)
        def _():
            key_value()
            weights[1].wait()

        @pl.when((i > 6 + n_heads) & (i <= 10 + n_heads))
        def _():
            j = 2 * (i - 7 - n_heads)
            input_grads(j)
            input_grads(j + 1)

    def ready(c):
        @pl.when(c == 0)
        def _():
            weights[2].wait()
            weights[3].wait()

        r = pl.ds(pl.multiple_of(c * step, step), step)
        own_out[r] = (own_out[r].astype(f32) + rbuf[r].astype(f32)).astype(bf16)

    def finish(r, c):
        done = (x2[r] + summed[r].astype(f32)).astype(bf16)
        for k in range(4):
            output[r, pl.ds(pl.multiple_of(places[k] * wide, wide), wide)] = done[:, k * wide : (k + 1) * wide]

    line_sum_work(
        own_out, in_buf, mid_buf, own_out, summed, line, "tensor", rows, ready, finish, work, 11 + n_heads
    )
    for x in flushes:
        x.wait()
    second_done()
    over(6, lambda i: up_moves(i, lambda x: x.wait()), 2)


def attention_back_call(grad_h2, x2, cot, qrot, krot, value, raw, gains, cos, sin, probs, wo, qkv, out_own, out_other, grads, got):
    rows, width = x2.shape
    q_cols, qkv_cols = wo.shape[1], qkv.shape[1]
    tall = grads.shape[1]
    wide = width // 4
    vmem, anyspace = pl.BlockSpec(memory_space=pltpu.VMEM), pl.BlockSpec(memory_space=pl.ANY)
    shape = jax.ShapeDtypeStruct
    dma = pltpu.SemaphoreType.DMA
    big = pltpu.VMEM((rows, width), bf16)
    return pl.pallas_call(
        attention_back_kernel,
        out_shape=[
            shape((rows, width), bf16),
            shape((rows, width), f32),
            shape((rows, width), bf16),
            shape((rows, qkv_cols), bf16),
            shape((rows, width), bf16),
            shape((8, width), f32),
            shape((2, tall, wide), bf16),
            shape(got.shape, bf16),
        ],
        in_specs=[vmem] * 3 + [anyspace] * 14,
        out_specs=[vmem, anyspace, anyspace] + [vmem] * 3 + [anyspace] * 2,
        scratch_shapes=[
            big,
            pltpu.VMEM((rows, width), f32),
            big,
            pltpu.VMEM((rows, q_cols), bf16),
            pltpu.VMEM((rows, 128), bf16),
            pltpu.VMEM((rows, 128), bf16),
            pltpu.VMEM((rows, qkv_cols), f32),
            dma((10,)),
            pltpu.VMEM((rows, width), f32),
            big,
            pltpu.VMEM((width, q_cols), bf16),
            pltpu.VMEM((width, qkv_cols), bf16),
            big, big, big, big, big,
            pltpu.VMEM((rows, q_cols), bf16),
            pltpu.VMEM((2, rows, rows), bf16),
            pltpu.VMEM((rows, 128), f32),
            pltpu.VMEM((rows, 128), f32),
            pltpu.VMEM((2, width), f32),
            pltpu.VMEM((2, 256, wide), bf16),
            pltpu.VMEM((2, 256, wide), bf16),
            pltpu.VMEM((12, 256, wide), bf16),
            dma((6,)), dma((2,)), dma((2, 2)), dma((12,)), dma((12,)),
            dma((6, 2)), dma((6, 2)),
        ]
        + line_sems(),
        input_output_aliases={16: 7},
        compiler_params=pltpu.CompilerParams(
            collective_id=3, has_side_effects=True, vmem_limit_bytes=62 * 2**20
        ),
        cost_estimate=pl.CostEstimate(flops=9 * 10**9, bytes_accessed=60 * 10**6, transcendentals=10**5),
        name="attention_backward",
    )(gains, cos, sin, grad_h2, x2, cot, qrot, krot, value, raw, probs, wo, qkv, out_own, out_other, grads, got)


def last_kernel(
    gains, gain_grads, part_in, dx2_in, tokens_in, grad_qkv_in, low_in, att_in, grads, got,
    tokens_grad_out, q_shard, k_shard, v_shard, wo_shard, gain_sum, got2_up,
    tokens_grad, d_sem, part, dx2, tokens, grad_qkv, low, att, f_sem, h1, in_buf, mid_buf, half_sum, summed, gain_rows, wo_all, qkv_all, wo_core, qkv_core, wo_one, qkv_one, wo_two, qkv_two,
    ga, z_got, g_out, g_got, load_a, load_b, on_buf, l_sem, s_send, s_recv,
    z_send, z_recv, c_send, c_recv, f_send, f_recv, t_send, t_recv, g_send, g_recv, *line,
):
    fetch = [
        pltpu.make_async_copy(src, dst, f_sem.at[i])
        for i, (src, dst) in enumerate(
            (
                (part_in, part), (tokens_in, tokens), (low_in, low), (att_in, att), (grad_qkv_in, grad_qkv),
                (dx2_in, dx2),
            )
        )
    ]
    for x in fetch:
        x.start()
    c = lax.axis_index("expert")
    to = plane_partners()
    zs = z_partners()
    others = plane_barrier(to, zs)
    places = [to[k, 0]["dp"] for k in range(4)]
    rows, width = tokens.shape
    wide = width // 4
    piece = wide // 2
    half = piece // 2

    def z_move(j):
        return remote(gain_grads.at[pl.ds(0, 8), pl.ds(0, 128)], z_got.at[j], z_send.at[j], z_recv.at[j], {"tensor": zs[j]})

    for j in range(3):
        z_move(j).start()
    up_at = lambda ref: lambda u, cols: ref.at[2, tile(turn(u)), cols]
    start, second_tile, second_done = second_exchange(
        6, up_at(grads), up_at(got), lambda u: got2_up.at[tile(turn(u))],
        load_a, load_b, on_buf, l_sem, s_send, s_recv, to, wide,
    )
    start(0)
    start(1)
    gain_vectors(gains, gain_rows)
    ga[...] = jnp.zeros_like(ga)

    def unit_rows(r):
        x = tokens[r].astype(f32)
        scale = lax.rsqrt(jnp.mean(x * x, axis=-1, keepdims=True) + epsilon)
        return x * scale, scale

    def hidden_one(i):
        r = pl.ds(pl.multiple_of(i * 64, 64), 64)
        h1[r] = (unit_rows(r)[0] * gain_rows[0:1]).astype(bf16)

    mats = [
        (low, att, wo_all, wo_core, wo_one, wo_two),
        (h1, grad_qkv, qkv_all, qkv_core, qkv_one, qkv_two),
    ]

    def block(k, core):
        return pl.ds(pl.multiple_of((k * 2 + core) * piece, piece), piece)

    def core_move(m, k):
        return remote(mats[m][2].at[block(k, 1 - c)], mats[m][3].at[k], c_send.at[m, k], c_recv.at[m, k], to[0, 1])

    def product(m, k, core):
        left, right, full = mats[m][:3]
        full[block(k, core)] = tn(left[:, block(k, core)], right[...]).astype(bf16)

    def away(m, k):
        product(m, k, 1 - c)
        core_move(m, k).start()

    def home(m, k):
        product(m, k, c)
        full, came = mats[m][2:4]
        core_move(m, k).wait_recv()
        full[block(k, c)] = (full[block(k, c)].astype(f32) + came[k].astype(f32)).astype(bf16)

    def slot(m, k, h):
        return mats[m][2].at[pl.ds(pl.multiple_of((k * 2 + c) * piece + h * half, half), half)]

    def first_move(m, h, j):
        way = 1 + h
        src = slot(m, 3 if j else way, h)
        return remote(src, mats[m][4].at[h, j], f_send.at[m, h, j], f_recv.at[m, h, j], to[way, 0])

    def second_move(m, h):
        return remote(slot(m, 2 - h, h), mats[m][5].at[h], t_send.at[m, h], t_recv.at[m, h], to[2 - h, 0])

    def add_first(m, h, j, k):
        full, one = mats[m][2], mats[m][4]
        r = pl.ds(pl.multiple_of((k * 2 + c) * piece + h * half, half), half)
        first_move(m, h, j).wait_recv()
        full[r] = (full[r].astype(f32) + one[h, j].astype(f32)).astype(bf16)

    def work(i):
        @pl.when(i == 0)
        def _():
            for x in fetch[1:]:
                x.wait()
            over(rows // 64, hidden_one)

        @pl.when(i < 6)
        def _():
            second_tile(i)

        for m in range(2):
            for n, ks in enumerate(((3, 1), (2, 0))):

                @pl.when(i == 1 + 4 * m + n)
                def _(m=m, ks=ks):
                    for k in ks:
                        away(m, k)

                @pl.when(i == 3 + 4 * m + n)
                def _(m=m, n=n, ks=ks):
                    for k in ks:
                        home(m, k)
                    for j in range(2):
                        first_move(m, n, j).start()

            @pl.when(i == SECOND[m])
            def _(m=m):
                for h in range(2):
                    add_first(m, h, 1, 2 - h)
                    second_move(m, h).start()

    def give_back(i):
        r = pl.ds(pl.multiple_of(i * (rows // CHUNKS), rows // CHUNKS), rows // CHUNKS)
        return pltpu.make_async_copy(tokens_grad.at[r], tokens_grad_out.at[r], d_sem.at[i])

    def finish(r, i):
        grad = summed[r].astype(f32)
        normed, scale = unit_rows(r)
        ga[0:1, :] += jnp.sum(grad * normed, axis=0, keepdims=True)
        n = grad * gain_rows[0:1]
        d = dx2[r] + scale * (n - normed * jnp.mean(n * normed, axis=-1, keepdims=True))
        for k in range(4):
            tokens_grad[r, pl.ds(pl.multiple_of(places[k] * wide, wide), wide)] = d[:, k * wide : (k + 1) * wide]
        give_back(i).start()

    fetch[0].wait()
    line_sum_work(part, in_buf, mid_buf, half_sum, summed, line, "tensor", rows, lambda k: None, finish, work, 20)

    head_rows = gain_grads[1:3, 0:128]
    for j in range(3):
        z_move(j).wait()
        head_rows += z_got[j, 1:3]
    for kd in range(4):
        for kc in range(2):
            for j in range(2):
                col = slice((kd * 2 + kc) * piece + j * 128, (kd * 2 + kc) * piece + (j + 1) * 128)
                g_out[kd, kc, j : j + 1] = ga[0:1, col]
                g_out[kd, kc, 2 + j : 3 + j] = gain_grads[0:1, col]
            g_out[kd, kc, 4:6] = head_rows

    def gain_move(j):
        kd, kc = others[j]
        core = c if kc == 0 else 1 - c
        return remote(g_out.at[kd, core], g_got.at[j], g_send.at[j], g_recv.at[j], to[kd, kc])

    for j in range(len(others)):
        gain_move(j).start()
    q_cols, k_cols = q_shard.shape[1], k_shard.shape[1]
    shards = (
        ((wo_shard, 0),),
        ((q_shard, 0), (k_shard, q_cols), (v_shard, q_cols + k_cols)),
    )
    for m in range(2):
        full, two = mats[m][2], mats[m][5]
        for h in range(2):
            add_first(m, h, 0, 0)
            second_move(m, h).wait_recv()
            r = pl.ds(pl.multiple_of(c * piece + h * half, half), half)
            for shard, col in shards[m]:
                cols = pl.ds(col, shard.shape[1])
                shard[h * half : (h + 1) * half] = full[r, cols].astype(f32) + two[h, :, cols].astype(f32)
    total = g_out[0, pl.ds(c, 1)].reshape(8, 128)
    for j in range(len(others)):
        gain_move(j).wait_recv()
        total += g_got[j]
    gain_sum[...] = total
    second_done()
    over(CHUNKS, lambda i: give_back(i).wait())
    for m in range(2):
        for k in range(4):
            core_move(m, k).wait_send()
        for h in range(2):
            for j in range(2):
                first_move(m, h, j).wait_send()
            second_move(m, h).wait_send()
    for j in range(len(others)):
        gain_move(j).wait_send()


def last_call(part, dx2, tokens, grad_qkv, low, att, gains, gain_grads, grads, got):
    rows, width = tokens.shape
    q_cols, qkv_cols = att.shape[1], grad_qkv.shape[1]
    piece = width // 8
    vmem = pl.BlockSpec(memory_space=pltpu.VMEM)
    shape = jax.ShapeDtypeStruct
    dma = pltpu.SemaphoreType.DMA
    big = pltpu.VMEM((rows, width), bf16)
    both = lambda *lead: [pltpu.VMEM(lead + (n,), bf16) for n in (q_cols, qkv_cols)]
    return pl.pallas_call(
        last_kernel,
        out_shape=[
            shape((rows, width), f32),
            shape((piece, q_cols), f32),
            shape((piece, (qkv_cols - q_cols) // 2), f32),
            shape((piece, (qkv_cols - q_cols) // 2), f32),
            shape((piece, q_cols), f32),
            shape((8, 128), f32),
            shape((got.shape[1], width // 4), bf16),
        ],
        in_specs=[vmem] * 2 + [pl.BlockSpec(memory_space=pl.ANY)] * 8,
        out_specs=[pl.BlockSpec(memory_space=pl.ANY)] + [vmem] * 5 + [pl.BlockSpec(memory_space=pl.ANY)],
        scratch_shapes=[
            pltpu.VMEM((rows, width), f32),
            dma((CHUNKS,)),
            big,
            pltpu.VMEM((rows, width), f32),
            big,
            pltpu.VMEM((rows, qkv_cols), bf16),
            big,
            pltpu.VMEM((rows, q_cols), bf16),
            dma((6,)),
        ]
        + [big, big, big, big, big, pltpu.VMEM((2, width), f32)]
        + both(width)
        + both(4, piece)
        + both(2, 2, piece // 2)
        + both(2, piece // 2)
        + [
            pltpu.VMEM((8, width), f32),
            pltpu.VMEM((3, 8, 128), f32),
            pltpu.VMEM((4, 2, 8, 128), f32),
            pltpu.VMEM((7, 8, 128), f32),
            pltpu.VMEM((2, 256, width // 4), bf16),
            pltpu.VMEM((2, 256, width // 4), bf16),
            pltpu.VMEM((6, 256, width // 4), bf16),
            dma((2, 2)), dma((6,)), dma((6,)),
            dma((3,)), dma((3,)), dma((2, 4)), dma((2, 4)), dma((2, 2, 2)), dma((2, 2, 2)), dma((2, 2)), dma((2, 2)),
            dma((7,)), dma((7,)),
        ]
        + line_sems(),
        compiler_params=pltpu.CompilerParams(
            collective_id=4, has_side_effects=True, vmem_limit_bytes=62 * 2**20
        ),
        cost_estimate=pl.CostEstimate(flops=5 * 10**9, bytes_accessed=40 * 10**6, transcendentals=10**5),
        name="input_gradients",
    )(gains, gain_grads, part, dx2, tokens, grad_qkv, low, att, grads, got)


def local_fast(
    tokens,
    cotangent,
    route_ids,
    route_weight,
    lengths,
    attention_norm,
    query_weight,
    key_matrix,
    value_matrix,
    output_weight,
    query_norm,
    key_norm,
    experts_norm,
    gate_weight,
    up_weight,
    down_weight,
):
    n_dp = lax.axis_size("dp")
    n_ex = lax.axis_size("expert")
    me_dp = lax.axis_index("dp")
    me_ex = lax.axis_index("expert")
    rows, width = tokens.shape
    group, hidden, part = gate_weight.shape
    length = lengths[0]
    lane = lambda x, axis=-1: lane_order(x, axis, n_dp, me_dp)

    flat = group * hidden
    na, nq = attention_norm.shape[0], query_norm.shape[0]
    q_cols, k_cols = query_weight.shape[1], key_matrix.shape[1]
    heads_query, heads_key = q_cols // HEAD_SIZE, k_cols // HEAD_SIZE
    per_group = heads_query // heads_key
    own_place = (me_dp * n_ex + me_ex) * nq
    fill = jnp.zeros((128 - nq,), bf16)
    gains_own = jnp.concatenate(
        [attention_norm, experts_norm, query_norm, fill, key_norm, fill, jnp.zeros((256,), bf16)]
    )
    gains_own = gains_own.reshape(8, 128).astype(f32)
    cos2, sin2 = rope_lanes(rows)
    own_experts = [w.reshape(flat, part) for w in (gate_weight, up_weight, down_weight)]
    (
        inputs_low, upstream_other, table, mixed_rows, hidden_all, attended_low, rotated_query, key_rot, value_low, raw,
        prob_low, gains, gate_full, up_full, down_full, full_qkv, full_output,
    ) = forward_call(
        tokens,
        cotangent,
        route_ids.T,
        route_weight.T,
        lengths,
        query_weight,
        key_matrix,
        value_matrix,
        output_weight,
        *own_experts,
        gains_own,
        cos2,
        sin2,
    )
    grad_hidden_two, out_own, out_other, grads, got = expert_call(
        hidden_all, cotangent, upstream_other, table, *own_experts, gate_full, up_full, down_full
    )
    output, grad_mixed, grad_proj_low, grad_qkv_low, grad_hidden_one, gain_grads, got2, got = attention_back_call(
        grad_hidden_two, mixed_rows, cotangent, rotated_query, key_rot, value_low, raw, gains, cos2, sin2,
        prob_low, full_output, full_qkv, out_own, out_other, grads, got,
    )
    tokens_grad, query_shard, key_shard, value_shard, output_shard, gain_sum, got2_up = last_call(
        grad_hidden_one, grad_mixed, inputs_low, grad_qkv_low, grad_proj_low, attended_low, gains, gain_grads,
        grads, got,
    )
    down_shard, gate_shard, up_shard = (
        (grads[m, :, :part].astype(f32) + got[m, :, :part].astype(f32) + last.astype(f32)).reshape(group, hidden, part)
        for m, last in enumerate((got2[0], got2[1], got2_up))
    )
    own_head = lambda row: lax.dynamic_slice_in_dim(gain_sum[row], own_place, nq, 0)
    return (
        output,
        tokens_grad,
        gain_sum[0:2].reshape(-1),
        query_shard,
        key_shard,
        value_shard,
        output_shard,
        own_head(4),
        own_head(5),
        gain_sum[2:4].reshape(-1),
        gate_shard,
        up_shard,
        down_shard,
    )


def local(*args):
    sizes = [lax.axis_size(a) for a in ("dp", "expert", "tensor")]
    return local_fast(*args) if sizes == [4, 2, 4] else local_plain(*args)


def solution(mesh):
    both = ("dp", "expert")
    rows2, rows1, mats = P(both, None), P(both), P(both, "tensor")
    experts = P("expert", "tensor", "dp")
    return jax.shard_map(
        local,
        mesh=mesh,
        in_specs=(rows2, rows2, rows2, rows2, rows1, rows1, mats, mats, mats, mats, rows1, rows1, rows1)
        + (experts,) * 3,
        out_specs=(rows2, rows2, rows1, mats, mats, mats, mats, rows1, rows1, rows1) + (experts,) * 3,
        check_vma=False,
    )
```

```python
import jax
import jax.numpy as jnp
import numpy as np
from jax import lax
from jax.experimental import pallas as pl
from jax.experimental.pallas import tpu as pltpu
from jax.sharding import PartitionSpec as P

HEAD_SIZE = 128
TOP = 8
epsilon = 1e-06
f32 = jnp.float32
bf16 = jnp.bfloat16
MESH = pl.DeviceIdType.MESH


def rms_scale(values):
    return lax.rsqrt(jnp.mean(values * values, axis=-1, keepdims=True) + epsilon)


def rope_lanes(rows):
    half = HEAD_SIZE // 2
    frequency = np.power(np.float32(1000000.0), -(np.arange(half, dtype=np.float32) * np.float32(2.0 / HEAD_SIZE)))
    angles = np.arange(rows, dtype=np.float32)[:, None] * frequency[None, :]
    cos, sin = np.cos(angles), np.sin(angles)
    return np.concatenate([cos, cos], 1), np.concatenate([-sin, sin], 1)


def rope_tables(rows):
    half_dim = HEAD_SIZE // 2
    frequency = jnp.power(f32(1000000.0), -(jnp.arange(half_dim, dtype=f32) * (2.0 / HEAD_SIZE)))
    angles = jnp.arange(rows, dtype=f32)[:, None] * frequency[None, :]
    return (jnp.cos(angles)[:, None, :], jnp.sin(angles)[:, None, :])


def rotate(values, cosine_table, sine_table):
    half_dim = values.shape[-1] // 2
    first_half = values[..., :half_dim]
    second_half = values[..., half_dim:]
    return jnp.concatenate(
        [
            first_half * cosine_table - second_half * sine_table,
            second_half * cosine_table + first_half * sine_table,
        ],
        axis=-1,
    )


def norm_back(grad_hidden, normed, scales, gains):
    grad_normed = grad_hidden * gains
    return scales * (grad_normed - normed * jnp.mean(grad_normed * normed, axis=-1, keepdims=True))


def flip(x, axis, bit):
    n = lax.axis_size(axis)
    return lax.ppermute(x, axis, [(i, i ^ bit) for i in range(n)])


def bits_of(n):
    return [1 << b for b in range(n.bit_length() - 1)]


def xor_gather(x, axis):
    pieces = [x]
    for bit in bits_of(lax.axis_size(axis)):
        pieces = pieces + [flip(p, axis, bit) for p in pieces]
    return pieces


def xor_scatter(parts, axis):
    for bit in reversed(bits_of(lax.axis_size(axis))):
        got = [flip(p, axis, bit) for p in parts[bit:]]
        parts = [
            (a.astype(f32) + r.astype(f32)).astype(a.dtype) for a, r in zip(parts[:bit], got)
        ]
    return parts[0]


def dp_scatter(blocks, axis="dp"):
    n = len(blocks)
    if n != 4:
        return xor_scatter(blocks, axis).astype(f32)
    h = blocks[0].shape[0] // 2
    add = lambda p, q: p.astype(f32) + q.astype(f32)
    done = []
    for rows, first, second in ((slice(0, h), 1, 2), (slice(h, 2 * h), 2, 1)):
        b = [x[rows] for x in blocks]
        got = flip(jnp.concatenate([b[first], b[3]], 0), axis, first)
        on = add(b[second], got[h:]).astype(bf16)
        done.append(add(b[0], got[:h]) + flip(on, axis, second).astype(f32))
    return jnp.concatenate(done, 0)


def all_pieces(x, axis, me):
    got = jnp.stack(xor_gather(x, axis), 0)
    return lane_order(got, 0, got.shape[0], me)


def dp_gather(x, axis="dp"):
    n = lax.axis_size(axis)
    if n != 4:
        return xor_gather(x, axis)
    h = x.shape[0] // 2
    a, b = x[:h], x[h:]
    a1, b2 = flip(a, axis, 1), flip(b, axis, 2)
    a2, b1 = flip(a, axis, 2), flip(b, axis, 1)
    a3, b3 = flip(a1, axis, 2), flip(b2, axis, 1)
    cat = lambda p, q: jnp.concatenate([p, q], 0)
    return [cat(a, b), cat(a1, b1), cat(a2, b2), cat(a3, b3)]


def lane_block(x, axis, n, me, k):
    axis = axis % x.ndim
    size = x.shape[axis] // n
    return lax.dynamic_slice_in_dim(x, (me ^ k) * size, size, axis)


def lane_order(x, axis, n, me):
    return jnp.concatenate([lane_block(x, axis, n, me, k) for k in range(n)], axis)


def block_scores(query_block, key_rot, length):
    query_pos = jnp.arange(query_block.shape[0], dtype=jnp.int32)
    key_pos = jnp.arange(key_rot.shape[0], dtype=jnp.int32)
    allowed = (key_pos[None, :] <= query_pos[:, None]) & (key_pos[None, :] < length)
    scores = jnp.einsum(
        "qkgd,skd->kgqs", query_block, key_rot, preferred_element_type=f32
    ) * HEAD_SIZE ** (-0.5)
    return jnp.where(allowed, scores, -1e30)


def core_rows(pieces, axis="expert"):
    n = lax.axis_size(axis)
    own = jnp.stack(pieces, 0)
    if n == 2:
        other = flip(own, axis, 1)
        first = lax.axis_index(axis) == 0
        both = jnp.stack([jnp.where(first, own, other), jnp.where(first, other, own)], 1)
    else:
        both = lax.all_gather(own, axis, axis=1, tiled=False)
    return both.reshape((-1,) + own.shape[2:])


def dotf(a, b, dims):
    return lax.dot_general(a, b, (dims, ((), ())), preferred_element_type=f32)


def local_plain(
    tokens,
    cotangent,
    route_ids,
    route_weight,
    lengths,
    attention_norm,
    query_weight,
    key_matrix,
    value_matrix,
    output_weight,
    query_norm,
    key_norm,
    experts_norm,
    gate_weight,
    up_weight,
    down_weight,
):
    n_dp = lax.axis_size("dp")
    n_ex = lax.axis_size("expert")
    me_dp = lax.axis_index("dp")
    me_ex = lax.axis_index("expert")
    rows, width = tokens.shape
    group, hidden, part = gate_weight.shape
    length = lengths[0]
    lane = lambda x, axis=-1: lane_order(x, axis, n_dp, me_dp)

    qkv_own = jnp.concatenate([query_weight, key_matrix, value_matrix], 1)
    qkv_pieces = dp_gather(qkv_own)
    wo_own, qkv_pieces = lax.optimization_barrier((output_weight, qkv_pieces))
    wo_pieces = dp_gather(wo_own)
    (gw, uw, dw), wo_pieces = lax.optimization_barrier(
        ((gate_weight, up_weight, down_weight), wo_pieces)
    )
    flat = group * hidden
    gate_up_own = jnp.concatenate([gw.reshape(flat, part), uw.reshape(flat, part)], 0)
    gate_up_pieces = dp_gather(gate_up_own)
    down_own, gate_up_pieces = lax.optimization_barrier((dw.reshape(flat, part), gate_up_pieces))
    down_pieces = dp_gather(down_own)

    na, nq = attention_norm.shape[0], query_norm.shape[0]
    gains = jnp.concatenate([attention_norm, experts_norm, query_norm, key_norm])
    gains = jnp.pad(gains, (0, -gains.size % 128)).reshape(-1, 128)
    gains = all_pieces(all_pieces(gains, "expert", me_ex), "dp", me_dp)
    gains = gains.reshape(n_dp, n_ex, -1).astype(f32)
    gain_attention = lane(gains[:, :, :na].reshape(-1))
    gain_experts = lane(gains[:, :, na : 2 * na].reshape(-1))
    gain_query = gains[:, :, 2 * na : 2 * na + nq].reshape(-1)
    gain_key = gains[:, :, 2 * na + nq : 2 * na + 2 * nq].reshape(-1)

    experts = jnp.arange(group * n_ex, dtype=jnp.int32)
    table = jnp.zeros((rows, group * n_ex), f32)
    for c in range(route_ids.shape[1]):
        table = table + jnp.where(
            route_ids[:, c, None] == experts[None, :], route_weight[:, c, None], 0.0
        )
    table = jnp.concatenate(xor_gather(table, "expert"), 0)
    mine = lax.dynamic_slice_in_dim(table, me_ex * group, group, 1)
    unit_expert = jnp.arange(flat, dtype=jnp.int32) // hidden
    route_scale = jnp.zeros((table.shape[0], flat), f32)
    for j in range(group):
        route_scale = route_scale + jnp.where(unit_expert[None, :] == j, mine[:, j, None], 0.0)

    cosine_table, sine_table = rope_tables(rows)
    inputs = lane(tokens.astype(f32))
    scale_one = rms_scale(inputs)
    normed_one = inputs * scale_one
    first_hidden = (normed_one * gain_attention).astype(bf16)
    upstream_low = lane(cotangent)
    upstream_all = jnp.concatenate(xor_gather(upstream_low, "expert"), 0)

    full_qkv = core_rows(qkv_pieces)
    qkv = jnp.dot(first_hidden, full_qkv, preferred_element_type=f32)
    q_cols, k_cols = query_weight.shape[1], key_matrix.shape[1]
    heads_query, heads_key = q_cols // HEAD_SIZE, k_cols // HEAD_SIZE
    per_group = heads_query // heads_key
    query_raw = qkv[:, :q_cols].reshape(rows, heads_query, HEAD_SIZE)
    key_raw = qkv[:, q_cols : q_cols + k_cols].reshape(rows, heads_key, HEAD_SIZE)
    value_low = qkv[:, q_cols + k_cols :].astype(bf16).reshape(rows, heads_key, HEAD_SIZE)
    scale_query = rms_scale(query_raw)
    normed_query = query_raw * scale_query
    rotated_query = (
        rotate(normed_query * gain_query, cosine_table, sine_table)
        .astype(bf16)
        .reshape(rows, heads_key, per_group, HEAD_SIZE)
    )
    scale_key = rms_scale(key_raw)
    normed_key = key_raw * scale_key
    key_rot = rotate(normed_key * gain_key, cosine_table, sine_table).astype(bf16)
    scores = block_scores(rotated_query, key_rot, length)
    row_peak = jnp.max(scores, axis=-1, keepdims=True)
    shifted = jnp.exp(scores - row_peak)
    totals = jnp.sum(shifted, axis=-1, keepdims=True)
    probs = shifted / totals
    prob_low = probs.astype(bf16)
    attended_low = (
        jnp.einsum("kgqs,skd->qkgd", prob_low, value_low, preferred_element_type=f32)
        .reshape(rows, q_cols)
        .astype(bf16)
    )
    full_output = core_rows(wo_pieces)
    projected = dotf(attended_low, full_output, ((1,), (1,)))
    mixed_rows = inputs + lax.psum(projected.astype(bf16), "tensor").astype(f32)
    scale_two = rms_scale(mixed_rows)
    normed_two = mixed_rows * scale_two
    hidden_two = (normed_two * gain_experts).astype(bf16)

    hidden_all = jnp.concatenate(xor_gather(hidden_two, "expert"), 0)
    gate_up_full = jnp.concatenate(gate_up_pieces, 1)
    down_full = jnp.concatenate(down_pieces, 1)
    gate_up = dotf(hidden_all, gate_up_full, ((1,), (1,)))
    gate_value, up_value = gate_up[:, :flat], gate_up[:, flat:]
    grad_act = lax.optimization_barrier(dotf(upstream_all, down_full, ((1,), (1,)))) * route_scale
    sigmoid_gate = jax.nn.sigmoid(gate_value)
    scaled_act = (gate_value * sigmoid_gate * up_value * route_scale).astype(bf16)
    grad_up_low = (grad_act * gate_value * sigmoid_gate).astype(bf16)
    grad_gate_low = (
        grad_act * up_value * sigmoid_gate * (1.0 + gate_value * (1.0 - sigmoid_gate))
    ).astype(bf16)
    grad_gate_up = jnp.concatenate([grad_gate_low, grad_up_low], 1)
    grad_rows = jnp.dot(grad_gate_up, gate_up_full, preferred_element_type=f32).astype(bf16)
    grad_hidden_two = xor_scatter(jnp.split(grad_rows, n_ex, 0), "expert")
    grad_hidden_two = lax.psum(grad_hidden_two, "tensor")

    expert_out = jnp.dot(scaled_act, down_full, preferred_element_type=f32).astype(bf16)
    combined = xor_scatter(jnp.split(expert_out, n_ex, 0), "expert")
    def expert_grad(low, acts):
        return dotf(low, acts, ((0,), (0,))).astype(bf16)

    grads = [
        expert_grad(scaled_act, upstream_all),
        expert_grad(grad_gate_low, hidden_all),
        expert_grad(grad_up_low, hidden_all),
    ]
    grad_hidden_two, grads = lax.optimization_barrier((grad_hidden_two, grads))
    down_shard, gate_shard, up_shard = (
        dp_scatter(jnp.split(g, n_dp, 1)).reshape(group, hidden, part) for g in grads
    )
    combined, grad_hidden_two = lax.optimization_barrier((combined, grad_hidden_two))
    combined = lax.psum(combined, "tensor")
    output = lane((mixed_rows + combined.astype(f32)).astype(bf16))
    grad_hidden_two = grad_hidden_two.astype(f32)

    def attention_scatter(grad):
        grad = grad.reshape(n_dp, n_ex, width // (n_dp * n_ex), grad.shape[1])
        if n_ex == 2:
            away = lax.dynamic_index_in_dim(grad, 1 - me_ex, 1, keepdims=False)
            own = lax.dynamic_index_in_dim(grad, me_ex, 1, keepdims=False)
            grad = (own.astype(f32) + flip(away, "expert", 1).astype(f32)).astype(bf16)
        else:
            grad = lax.psum_scatter(grad, "expert", scatter_dimension=1, tiled=False)
        return dp_scatter(list(grad))

    upstream = upstream_low.astype(f32)
    experts_gain_grad = jnp.sum(grad_hidden_two * normed_two, axis=0)
    grad_mixed = upstream + norm_back(grad_hidden_two, normed_two, scale_two, gain_experts)
    grad_proj_low = grad_mixed.astype(bf16)
    grad_att_low = (
        jnp.dot(grad_proj_low, full_output, preferred_element_type=f32)
        .astype(bf16)
        .reshape(rows, heads_key, per_group, HEAD_SIZE)
    )
    output_grad = dotf(grad_proj_low, attended_low, ((0,), (0,))).astype(bf16)
    output_shard = attention_scatter(output_grad)
    grad_probs = jnp.einsum("qkgd,skd->kgqs", grad_att_low, value_low, preferred_element_type=f32)
    row_dot = jnp.sum(probs * grad_probs, axis=-1, keepdims=True)
    grad_scores = (probs * (grad_probs - row_dot)).astype(bf16)
    grad_value = jnp.einsum("kgqs,qkgd->skd", prob_low, grad_att_low, preferred_element_type=f32)
    grad_qrot = jnp.einsum(
        "kgqs,skd->qkgd", grad_scores, key_rot, preferred_element_type=f32
    ) * HEAD_SIZE ** (-0.5)
    grad_krot = jnp.einsum(
        "kgqs,qkgd->skd", grad_scores, rotated_query, preferred_element_type=f32
    ) * HEAD_SIZE ** (-0.5)
    grad_qrot = grad_qrot.reshape(rows, heads_query, HEAD_SIZE)
    grad_query_normed = rotate(grad_qrot, cosine_table, -sine_table)
    query_gain_grad = jnp.sum(grad_query_normed * normed_query, axis=(0, 1))
    grad_query_low = (
        norm_back(grad_query_normed, normed_query, scale_query, gain_query)
        .astype(bf16)
        .reshape(rows, q_cols)
    )
    grad_key_normed = rotate(grad_krot, cosine_table, -sine_table)
    key_gain_grad = jnp.sum(grad_key_normed * normed_key, axis=(0, 1))
    grad_key_low = (
        norm_back(grad_key_normed, normed_key, scale_key, gain_key).astype(bf16).reshape(rows, k_cols)
    )
    grad_value_low = grad_value.astype(bf16).reshape(rows, k_cols)
    grad_qkv_low = jnp.concatenate([grad_query_low, grad_key_low, grad_value_low], 1)
    grad_hidden_one = dotf(grad_qkv_low, full_qkv, ((1,), (1,)))
    head_gain_grads = jnp.stack([query_gain_grad, key_gain_grad]).astype(bf16)
    grad_hidden_one, head_gain_grads, _ = lax.optimization_barrier(
        (grad_hidden_one.astype(bf16), head_gain_grads, combined)
    )
    grad_hidden_one, head_gain_grads = lax.psum((grad_hidden_one, head_gain_grads), "tensor")
    grad_hidden_one = grad_hidden_one.astype(f32)
    qkv_grad = dotf(first_hidden, grad_qkv_low, ((0,), (0,))).astype(bf16)
    qkv_shard = attention_scatter(qkv_grad)
    attention_gain_grad = jnp.sum(grad_hidden_one * normed_one, axis=0)
    tokens_grad = grad_mixed + norm_back(grad_hidden_one, normed_one, scale_one, gain_attention)
    tokens_grad = lane(tokens_grad)

    blocks = lambda v: v.reshape(n_dp, n_ex, -1)
    gain_grads = jnp.concatenate(
        [
            blocks(attention_gain_grad),
            blocks(experts_gain_grad),
            lane(blocks(head_gain_grads[0].astype(f32)), 0),
            lane(blocks(head_gain_grads[1].astype(f32)), 0),
        ],
        2,
    )
    gain_grads = lane_order(gain_grads, 1, n_ex, me_ex)
    gain_grads = jnp.pad(gain_grads, ((0, 0), (0, 0), (0, -gain_grads.shape[2] % 128)))
    gain_grads = gain_grads.reshape(n_dp, n_ex, -1, 128)
    gain_grads = xor_scatter([gain_grads[:, k] for k in range(n_ex)], "expert")
    gain_grads = xor_scatter([gain_grads[k] for k in range(n_dp)], "dp").reshape(-1)
    take = lambda start, size: gain_grads[start : start + size]
    return (
        output,
        tokens_grad,
        take(0, na),
        qkv_shard[:, :q_cols],
        qkv_shard[:, q_cols : q_cols + k_cols],
        qkv_shard[:, q_cols + k_cols :],
        output_shard,
        take(2 * na, nq),
        take(2 * na + nq, nq),
        take(na, na),
        gate_shard,
        up_shard,
        down_shard,
    )


CHUNKS = 16
SECOND = (12, 18)


def line_roles(axis):
    p = lax.axis_index(axis)
    return p + 1 - 2 * (p % 2), 3 - p, (p + 1) // 2 == 1


def over(n, f, start=0):
    lax.fori_loop(start, n, lambda c, t: (f(c), t)[1], 0)


def line_sum_steps(x_ref, in_buf, mid_buf, part, out_ref, sems, axis, finish, lag=2):
    a_send, a_recv, b_send, b_recv, c_send, c_recv = sems
    side, mid, inner = line_roles(axis)
    step = x_ref.shape[0] // CHUNKS

    def rows(c):
        return pl.ds(pl.multiple_of(c * step, step), step)

    def copy(src, dst, c, send, recv, to):
        return pltpu.make_async_remote_copy(
            src.at[rows(c)], dst.at[rows(c)], send.at[c], recv.at[c], device_id={axis: to}, device_id_type=MESH
        )

    to_inner = lambda c: copy(x_ref, in_buf, c, a_send, a_recv, side)
    to_middle = lambda c: copy(part, mid_buf, c, b_send, b_recv, mid)
    to_outer = lambda c: copy(out_ref, out_ref, c, c_send, c_recv, side)

    @pl.when(jnp.logical_not(inner))
    def _():
        over(CHUNKS, lambda c: to_inner(c).start())

        def done(c):
            to_outer(c).wait_recv()
            finish(rows(c), c)
            to_inner(c).wait_send()

        over(CHUNKS, done)

    @pl.when(inner)
    def _():
        def first(c):
            to_inner(c).wait_recv()
            r = rows(c)
            part[r] = (x_ref[r].astype(f32) + in_buf[r].astype(f32)).astype(bf16)
            to_middle(c).start()

        def second(c):
            to_middle(c).wait_recv()
            r = rows(c)
            out_ref[r] = (part[r].astype(f32) + mid_buf[r].astype(f32)).astype(bf16)
            to_outer(c).start()
            finish(r, c)

        over(lag, first)
        over(CHUNKS - lag, lambda c: (first(c + lag), second(c))[0])
        over(CHUNKS, second, CHUNKS - lag)

        def done(c):
            to_middle(c).wait_send()
            to_outer(c).wait_send()

        over(CHUNKS, done)


def line_sems():
    return [pltpu.SemaphoreType.DMA((CHUNKS,))] * 6


def plane_partners():
    d, c = lax.axis_index("dp"), lax.axis_index("expert")
    ds = {0: d, 1: d + 1 - 2 * (d % 2), 2: d + 2 - 4 * (d // 2), 3: 3 - d}
    cs = {0: c, 1: 1 - c}
    return {(kd, kc): {"dp": ds[kd], "expert": cs[kc]} for kd in ds for kc in cs}


def lane_copies(src, dst, sems, to):
    wide = src.shape[1] // 4
    places = [to[k, 0]["dp"] for k in range(4)]
    return [
        pltpu.make_async_copy(
            src.at[:, pl.ds(pl.multiple_of(places[k] * wide, wide), wide)], dst.at[:, pl.ds(k * wide, wide)], sems[k]
        )
        for k in range(4)
    ]


def remote(src, dst, send, recv, to):
    return pltpu.make_async_remote_copy(src, dst, send, recv, device_id=to, device_id_type=MESH)


def nt(a, b):
    return lax.dot_general(a, b, (((1,), (1,)), ((), ())), preferred_element_type=f32)


def nn(a, b):
    return lax.dot_general(a, b, (((1,), (0,)), ((), ())), preferred_element_type=f32)


def tn(a, b):
    return lax.dot_general(a, b, (((0,), (0,)), ((), ())), preferred_element_type=f32)


def forward_kernel(
    tokens_in, cot_in, ids, weight, lengths, q_own, k_own, v_own, wo_own, gate_own, up_own, down_own, gains_in, cos, sin,
    tokens_out, cot, table, x2_out, h2_out, att_out, qrot_out, krot_out, value_out, raw_out, probs_out, gains, gate, up,
    down, qkv_out, wo_out,
    tokens, x2, h2, att, qrot, krot, value, raw, probs, save_sem, qkv, wo, h1, proj, in_buf, mid_buf, part, summed, gain_rows, gains_own,
    w_send, w_recv, core_send, core_recv, g_send, g_recv, h_send, h_recv, own_sem, out_sem, r_send, r_recv, t_sem, *line,
):
    c = lax.axis_index("expert")
    to = plane_partners()
    side, mid, inner = line_roles("tensor")
    barrier = pltpu.get_barrier_semaphore()
    others = [k for k in to if k != (0, 0)]
    for k in others:
        pl.semaphore_signal(barrier, inc=1, device_id=to[k], device_id_type=MESH)
    pl.semaphore_signal(barrier, inc=1, device_id={"tensor": side}, device_id_type=MESH)

    @pl.when(inner)
    def _():
        pl.semaphore_signal(barrier, inc=1, device_id={"tensor": mid}, device_id_type=MESH)
        pl.semaphore_wait(barrier, len(others) + 2)

    @pl.when(jnp.logical_not(inner))
    def _():
        pl.semaphore_wait(barrier, len(others) + 1)

    saves = [
        pltpu.make_async_copy(src, dst, save_sem.at[i])
        for i, (src, dst) in enumerate(
            (
                (tokens, tokens_out), (qrot, qrot_out), (krot, krot_out), (value, value_out), (raw, raw_out),
                (probs, probs_out), (att, att_out), (x2, x2_out), (h2, h2_out),
            )
        )
    ]
    rows, width = tokens.shape
    piece = wo_own.shape[0]
    half = piece // 2
    tall = gate_own.shape[0] // 2
    wide = gate_own.shape[1]
    q_cols, k_cols = q_own.shape[1], k_own.shape[1]
    places = [to[k, 0]["dp"] for k in range(4)]

    def lanes(k):
        return pl.ds(pl.multiple_of(places[k] * wide, wide), wide)

    fetch = lane_copies(tokens_in, tokens, [t_sem.at[k] for k in range(4)], to)

    def cot_away(k):
        dst = cot.at[:, pl.ds(k * wide, wide)]
        return remote(cot_in.at[:, lanes(k)], dst, r_send.at[k], r_recv.at[k], to[0, 1])

    def table_away():
        return remote(
            table.at[pl.ds(0, rows)], table.at[pl.ds(rows, rows)], r_send.at[4], r_recv.at[4], to[0, 1]
        )

    def small_slot(full):
        return lambda k, h: full.at[pl.ds(pl.multiple_of((k * 2 + c) * piece + h * half, half), half)]

    early = tall // 3 * 2

    def big_slot(full):
        return lambda k, h: full.at[pl.ds(h * tall, early), pl.ds(k * wide, wide)]

    mats = [
        (lambda h: small_slot(qkv)(0, h), small_slot(qkv)),
        (lambda h: wo_own.at[pl.ds(h * half, half)], small_slot(wo)),
    ] + [
        (lambda h, own=own: own.at[pl.ds(h * tall, early)], big_slot(full))
        for own, full in ((gate_own, gate), (up_own, up), (down_own, down))
    ]

    def move(m, i):
        own, slot = mats[m]
        src, dst, way = (
            (own(0), slot(1, 0), 1), (own(1), slot(2, 1), 2), (own(0), slot(2, 0), 2), (own(1), slot(1, 1), 1),
            (slot(1, 0), slot(3, 0), 2), (slot(2, 1), slot(3, 1), 1),
        )[i]
        return remote(src, dst, w_send.at[m, i], w_recv.at[m, i], to[way, 0])

    def begin(m):
        for i in range(4):
            move(m, i).start()

    def pass_on(m):
        for i in (0, 1):
            move(m, i).wait_recv()
            move(m, 4 + i).start()

    def arrived(m):
        for i in (2, 3, 4, 5):
            move(m, i).wait_recv()

    def core_move(m, k):
        full = (qkv, wo)[m]
        block = full.at[pl.ds(pl.multiple_of((k * 2 + c) * piece, piece), piece)]
        return remote(block, block, core_send.at[m, k], core_recv.at[m, k], to[0, 1])

    def gain_move(j):
        kd, kc = others[j]
        return remote(gains_own, gains.at[kd, c], g_send.at[j], g_recv.at[j], to[kd, kc])

    own_rows = pl.ds(pl.multiple_of(c * piece, piece), piece)
    own_qkv = [
        pltpu.make_async_copy(own, qkv.at[own_rows, pl.ds(col, own.shape[1])], own_sem.at[5 + i])
        for i, (own, col) in enumerate(((q_own, 0), (k_own, q_cols), (v_own, q_cols + k_cols)))
    ]
    own_copies = [
        None,
        pltpu.make_async_copy(wo_own, wo.at[pl.ds(pl.multiple_of(c * piece, piece), piece)], own_sem.at[1]),
    ]

    for x in own_qkv + [own_copies[1]] + fetch:
        x.start()
    for k in range(4):
        cot_away(k).start()
    gains_own[...] = gains_in[...]
    shift = (lax.axis_index("dp") * 2 + c) * (128 // 8)
    gains_own[4:6] = pltpu.roll(gains_in[...], shift, 1)[4:6]
    for x in own_qkv:
        x.wait()
    begin(0)
    for j in range(len(others)):
        gain_move(j).start()
    gains[pl.ds(0, 1), pl.ds(c, 1)] = gains_own[...].reshape(1, 1, 8, 128)
    core_move(0, 0).start()
    expert = lax.broadcasted_iota(jnp.int32, (128, rows), 0)
    routes = jnp.zeros((128, rows), f32)
    for j in range(ids.shape[0]):
        routes += jnp.where(expert == ids[j : j + 1], weight[j : j + 1], 0.0)
    table[0:rows] = routes.T
    table_away().start()
    for k in range(4):
        fetch[k].wait()
    own_copies[1].wait()
    core_move(1, 0).start()
    for j in range(len(others)):
        gain_move(j).wait_recv()
    for kd in range(4):
        for kc in range(2):
            g = gains[kd, kc]
            for j in range(2):
                col = (kd * 2 + kc) * 256 + j * 128
                gain_rows[0:1, col : col + 128] = g[j : j + 1]
                gain_rows[1:2, col : col + 128] = g[2 + j : 3 + j]
    heads = jnp.sum(gains[...].reshape(8, 8, 128), axis=0)
    gain_query, gain_key = heads[4:5], heads[5:6]

    def hidden_one(i):
        r = pl.ds(pl.multiple_of(i * 64, 64), 64)
        x = tokens[r].astype(f32)
        scale = lax.rsqrt(jnp.mean(x * x, axis=-1, keepdims=True) + epsilon)
        h1[r] = (x * scale * gain_rows[0:1]).astype(bf16)

    over(rows // 64, hidden_one)

    pass_on(0)
    begin(1)
    for k, waits in ((1, (3,)), (2, (2,)), (3, (4, 5))):
        for i in waits:
            move(0, i).wait_recv()
        core_move(0, k).start()
    pass_on(1)
    for m in (2, 3, 4):
        begin(m)
    for k in range(4):
        core_move(0, k).wait_recv()
    save_qkv = pltpu.make_async_copy(qkv, qkv_out, out_sem.at[0])
    save_qkv.start()

    def project(j):
        col = pl.ds(pl.multiple_of(j * 256, 256), 256)
        raw[:, col] = nn(h1[...], qkv[:, col])

    over(qkv.shape[1] // 256, project)

    def spin(u):
        return u * cos[...] + pltpu.roll(u, 64, 1) * sin[...]

    def unit(u):
        return u * lax.rsqrt(jnp.mean(u * u, axis=-1, keepdims=True) + epsilon)

    krot[...] = spin(unit(raw[:, pl.ds(q_cols, 128)]) * gain_key).astype(bf16)
    value[...] = raw[:, pl.ds(q_cols + 128, 128)].astype(bf16)
    block = rows // 2
    length = lengths[0]

    def head(h):
        col = pl.ds(pl.multiple_of(h * 128, 128), 128)
        qrot[:, col] = spin(unit(raw[:, col]) * gain_query).astype(bf16)
        for i in range(2):
            r, n = slice(i * block, (i + 1) * block), (i + 1) * block
            s = nt(qrot[r, col], krot[0:n]) * 128 ** (-0.5)
            row = lax.broadcasted_iota(jnp.int32, (block, n), 0) + i * block
            key = lax.broadcasted_iota(jnp.int32, (block, n), 1)
            s = jnp.where((key <= row) & (key < length), s, -1e30)
            e = jnp.exp(s - jnp.max(s, axis=-1, keepdims=True))
            p = (e / jnp.sum(e, axis=-1, keepdims=True)).astype(bf16)
            probs[h, r, 0:n] = p
            att[r, col] = nn(p, value[0:n]).astype(bf16)
        probs[h, 0:block, block:] = jnp.zeros((block, block), bf16)

    over(q_cols // 128, head)
    for x in saves[:7]:
        x.start()
    for k, waits in ((1, (3,)), (2, (2,)), (3, (4, 5))):
        for i in waits:
            move(1, i).wait_recv()
        core_move(1, k).start()
    for k in range(4):
        core_move(1, k).wait_recv()
    save_wo = pltpu.make_async_copy(wo, wo_out, out_sem.at[1])
    save_wo.start()

    def out_project(j):
        r = pl.ds(pl.multiple_of(j * 256, 256), 256)
        proj[:, r] = nt(att[...], wo[r]).astype(bf16)

    over(width // 256, out_project)
    pass_on(2)

    def give(i):
        n = rows // CHUNKS
        src = h2.at[pl.ds(pl.multiple_of(i * n, n), n)]
        dst = h2.at[pl.ds(pl.multiple_of(rows + i * n, n), n)]
        return remote(src, dst, h_send.at[i], h_recv.at[i], to[0, 1])

    def finish(r, i):
        mixed = tokens[r].astype(f32) + summed[r].astype(f32)
        x2[r] = mixed
        scale = lax.rsqrt(jnp.mean(mixed * mixed, axis=-1, keepdims=True) + epsilon)
        h2[r] = (mixed * scale * gain_rows[1:2]).astype(bf16)
        give(i).start()

    line_sum_steps(proj, in_buf, mid_buf, part, summed, line, "tensor", finish)
    pass_on(3)
    pass_on(4)
    saves[7].start()
    over(CHUNKS, lambda i: give(i).wait())
    saves[8].start()
    for m in (2, 3, 4):
        arrived(m)
    save_qkv.wait()
    save_wo.wait()
    for x in saves:
        x.wait()
    for k in range(4):
        cot_away(k).wait()
    table_away().wait()
    for m in range(5):
        for i in range(6):
            move(m, i).wait_send()
    for m in range(2):
        for k in range(4):
            core_move(m, k).wait_send()
    for j in range(len(others)):
        gain_move(j).wait_send()


def forward_call(tokens, cot, ids, weight, lengths, q_own, k_own, v_own, wo_own, gate_own, up_own, down_own, gains, cos, sin):
    rows, width = tokens.shape
    q_cols = q_own.shape[1]
    qkv_cols = q_cols + k_own.shape[1] + v_own.shape[1]
    tall = gate_own.shape[0]
    vmem, anyspace = pl.BlockSpec(memory_space=pltpu.VMEM), pl.BlockSpec(memory_space=pl.ANY)
    shape = jax.ShapeDtypeStruct
    tokens_shape, x2_shape, h2_shape = ((rows, width), bf16), ((rows, width), f32), ((2 * rows, width), bf16)
    att_shape, head_shape = ((rows, q_cols), bf16), ((rows, 128), bf16)
    raw_shape, probs_shape = ((rows, qkv_cols), f32), ((q_cols // 128, rows, rows), bf16)
    kept = [tokens_shape, x2_shape, h2_shape, att_shape, att_shape, head_shape, head_shape, raw_shape, probs_shape]
    outs = [
        (shape(*tokens_shape), anyspace),
        (shape((rows, width), bf16), anyspace),
        (shape((2 * rows, 128), f32), vmem),
        *[(shape(*k), anyspace) for k in kept[1:]],
        (shape((4, 2, 8, 128), f32), vmem),
        *[(shape((tall, width), bf16), anyspace)] * 3,
        (shape((width, qkv_cols), bf16), anyspace),
        (shape((width, q_cols), bf16), anyspace),
    ]
    dma = pltpu.SemaphoreType.DMA
    big = pltpu.VMEM((rows, width), bf16)
    return pl.pallas_call(
        forward_kernel,
        out_shape=[o[0] for o in outs],
        in_specs=[anyspace] * 2
        + [vmem] * 2
        + [pl.BlockSpec(memory_space=pltpu.SMEM)]
        + [anyspace] * 7
        + [vmem] * 3,
        out_specs=[o[1] for o in outs],
        scratch_shapes=[pltpu.VMEM(*k) for k in kept]
        + [
            dma((9,)),
            pltpu.VMEM((width, qkv_cols), bf16),
            pltpu.VMEM((width, q_cols), bf16),
            big, big, big, big, big, big,
            pltpu.VMEM((2, width), f32),
            pltpu.VMEM((8, 128), f32),
            dma((5, 6)), dma((5, 6)), dma((2, 4)), dma((2, 4)), dma((7,)), dma((7,)),
            dma((CHUNKS,)), dma((CHUNKS,)), dma((8,)), dma((2,)), dma((5,)), dma((5,)), dma((4,)),
        ] + line_sems(),
        compiler_params=pltpu.CompilerParams(
            collective_id=1, has_side_effects=True, vmem_limit_bytes=60 * 2**20
        ),
        cost_estimate=pl.CostEstimate(flops=8 * 10**9, bytes_accessed=60 * 10**6, transcendentals=2 * 10**6),
        name="forward_to_experts",
    )(tokens, cot, ids, weight, lengths, q_own, k_own, v_own, wo_own, gate_own, up_own, down_own, gains, cos, sin)


def turn(i):
    return i // 2 + 3 * (i % 2)


def tile(t):
    return pl.ds(pl.multiple_of(t * 256, 256), 256)


def by_half(t, f):
    for first in (1, 2):

        @pl.when(t // 3 == first - 1)
        def _(first=first):
            f(first)


def first_exchange(m, t, j, first, grad, came, send, recv, to, wide):
    return remote(
        grad.at[m, tile(t), pl.ds((3 if j else first) * wide, wide)], came(t, pl.ds(j * wide, wide)), send, recv,
        to[first, 0],
    )


def second_exchange(count, grad_at, came_at, dst_at, load_a, load_b, on_buf, l_sem, s_send, s_recv, to, wide):
    def loads(u, first):
        slot = u % 2
        return (
            pltpu.make_async_copy(grad_at(u, pl.ds((3 - first) * wide, wide)), load_a.at[slot], l_sem.at[slot, 0]),
            pltpu.make_async_copy(came_at(u, pl.ds(wide, wide)), load_b.at[slot], l_sem.at[slot, 1]),
        )

    def pass_on(u, first):
        return remote(on_buf.at[u], dst_at(u), s_send.at[u], s_recv.at[u], to[3 - first, 0])

    def start(u):
        by_half(turn(u % 6), lambda first: [x.start() for x in loads(u, first)])

    def step(u):
        def f(first):
            for x in loads(u, first):
                x.wait()
            on_buf[u] = (load_a[u % 2].astype(f32) + load_b[u % 2].astype(f32)).astype(bf16)
            pass_on(u, first).start()

        by_half(turn(u % 6), f)

        @pl.when(u + 2 < count)
        def _():
            start(u + 2)

    def finish():
        over(count, lambda u: by_half(turn(u % 6), lambda first: pass_on(u, first).wait()))

    return start, step, finish


def expert_kernel(
    h2_in, g_own, g_other, mine_in, gate_own, up_own, down_own, gate_in, up_in, down_in,
    grad_h2, out, out_other, grads, got,
    g, g_sem, h2, mine, gate, up, down, acts, drow, rbuf, in_buf, mid_buf, stage, late_gate, late_up,
    load_sem, rest_sem, w_send, w_recv, x_send, x_recv, s_send, s_recv, keep_sem, out_sem, *line,
):
    to = plane_partners()
    side, mid, inner = line_roles("tensor")
    barrier = pltpu.get_barrier_semaphore()
    near = [(1, 0), (2, 0), (0, 1)]
    for k in near:
        pl.semaphore_signal(barrier, inc=1, device_id=to[k], device_id_type=MESH)
    pl.semaphore_signal(barrier, inc=1, device_id={"tensor": side}, device_id_type=MESH)

    @pl.when(inner)
    def _():
        pl.semaphore_signal(barrier, inc=1, device_id={"tensor": mid}, device_id_type=MESH)
        pl.semaphore_wait(barrier, len(near) + 2)

    @pl.when(jnp.logical_not(inner))
    def _():
        pl.semaphore_wait(barrier, len(near) + 1)

    tall, width = down.shape
    rows = drow.shape[0] // 2
    first_expert = 8 * lax.axis_index("expert")
    wide = width // 4
    units = tall // 8
    late = 4 * 256
    mats = ((gate_own, gate_in, gate), (up_own, up_in, up), (down_own, down_in, down))

    def shard_move(j, n):
        shard, _, full = mats[j]
        own = lambda i: shard.at[tile(turn(i))]
        slot = lambda k, i: full.at[tile(i), pl.ds(k * wide, wide)]
        a, b = 4, 5
        src, dst, way = (
            (own(a), slot(1, a), 1), (own(b), slot(2, b), 2), (own(a), slot(2, a), 2), (own(b), slot(1, b), 1),
            (slot(1, a), slot(3, a), 2), (slot(2, b), slot(3, b), 1),
        )[n]
        return remote(src, dst, w_send.at[j, n], w_recv.at[j, n], to[way, 0])

    for j in range(3):
        for n in range(4):
            shard_move(j, n).start()

    def load_own(i, j):
        return pltpu.make_async_copy(
            mats[j][0].at[tile(turn(i))], mats[j][2].at[tile(i), pl.ds(0, wide)], load_sem.at[i, j]
        )

    def load_rest(i, j):
        cols = pl.ds(wide, 3 * wide)
        return pltpu.make_async_copy(
            mats[j][1].at[tile(turn(i)), cols], mats[j][2].at[tile(i), cols], rest_sem.at[i, j]
        )

    load_g = lane_copies(g_own, g.at[pl.ds(0, rows)], [g_sem.at[k] for k in range(4)], to) + [
        pltpu.make_async_copy(g_other, g.at[pl.ds(rows, rows)], g_sem.at[4]),
        pltpu.make_async_copy(h2_in, h2, g_sem.at[5]),
        pltpu.make_async_copy(mine_in, mine, g_sem.at[6]),
    ]
    for x in load_g:
        x.start()
    over(4, lambda i: [x(i, j).start() for x in (load_own, load_rest) for j in range(3)])
    for i in (4, 5):
        for j in range(3):
            load_own(i, j).start()
    for x in load_g:
        x.wait()

    def gate_up(i):
        return nt(h2[...], gate[tile(i)]), nt(h2[...], up[tile(i)])

    def hidden_tile(i, gate_value, up_value):
        t = turn(i)
        first = (t * 256) // units
        edge = (first + 1) * units - t * 256
        lanes = lax.broadcasted_iota(jnp.int32, mine.shape, 1)
        pick = lambda e: jnp.sum(jnp.where(lanes == e + first_expert, mine[...], 0.0), axis=1, keepdims=True)
        column = lax.broadcasted_iota(jnp.int32, (2 * rows, 256), 1)
        scale = jnp.where(column < edge, pick(first), pick(first + 1))
        grad_act = nt(g[...], down[tile(i)]) * scale
        sig = jax.nn.sigmoid(gate_value)
        silu = gate_value * sig
        acts[0, :, tile(i)] = (silu * up_value * scale).astype(bf16)
        acts[2, :, tile(i)] = (grad_act * silu).astype(bf16)
        acts[1, :, tile(i)] = (grad_act * up_value * sig * (1.0 + gate_value * (1.0 - sig))).astype(bf16)

    early_unit = lambda e: (e // 4, (e % 4) // 2, 1 - e % 2, e)
    last_unit = lambda e: (e // 2, 2, 1 - e % 2, 8 + e)
    up_unit = lambda e: (2, e // 2, 1 - e % 2, 12 + e)

    def keep(unit, ab):
        m, q, s, n = unit
        cols = pl.ds(pl.multiple_of(s * 2 * wide, 2 * wide), 2 * wide)
        return pltpu.make_async_copy(
            stage.at[n % 2, pl.ds(ab * 256, 256)], grads.at[m, tile(q + 3 * ab), cols], keep_sem.at[n % 2, ab]
        )

    def send(m, t, j, first):
        came = lambda t, cols: got.at[m, tile(t), cols]
        return first_exchange(m, t, j, first, grads, came, s_send.at[m, t, j], s_recv.at[m, t, j], to, wide)

    def flush(unit, goes=True):
        m, q, s, n = unit
        for ab in range(2):
            keep(unit, ab).wait()

        @pl.when(goes & (s == 1))
        def _():
            send(m, q, 1, 1).start()
            send(m, q + 3, 0, 2).start()
            send(m, q + 3, 1, 2).start()

        @pl.when(goes & (s == 0))
        def _():
            send(m, q, 0, 1).start()

    def grad_unit(unit, rhs):
        m, q, s, n = unit
        low = acts[m, :, pl.ds(pl.multiple_of(q * 512, 512), 512)]
        for b in range(2):
            cols = pl.ds(pl.multiple_of((2 * s + b) * wide, wide), wide)
            stage[n % 2, :, b * wide : (b + 1) * wide] = tn(low, rhs[:, cols]).astype(bf16)
        for ab in range(2):
            keep(unit, ab).start()

    def early_grads(rhs):
        def one(e):
            grad_unit(early_unit(e), rhs)

            @pl.when(e > 0)
            def _():
                flush(early_unit(e - 1))

        return one

    def early_tile(i):
        for x in (load_own, load_rest):
            for j in range(3):
                x(i, j).wait()
        hidden_tile(i, *gate_up(i))

    over(4, early_tile)

    def early_rows(j):
        col = pl.ds(pl.multiple_of(j * 256, 256), 256)
        drow[:, col] = (nn(acts[1, :, 0:late], gate[0:late, col]) + nn(acts[2, :, 0:late], up[0:late, col])).astype(bf16)

    over(width // 256, early_rows)
    over(2, early_grads(g))
    for j in range(3):
        for n in (0, 1):
            shard_move(j, n).wait_recv()
            shard_move(j, 4 + n).start()
    over(4, early_grads(g), 2)
    over(8, early_grads(h2), 4)
    flush(early_unit(7))
    for i in (4, 5):
        for j in range(3):
            load_own(i, j).wait()
    for j in (0, 1):
        for n in (2, 3, 4, 5):
            shard_move(j, n).wait_recv()

    def late_gate_up(i):
        late_gate[i - 4], late_up[i - 4] = gate_up(i)

    over(6, late_gate_up, 4)
    for n in (2, 3, 4, 5):
        shard_move(2, n).wait_recv()
    over(6, lambda i: hidden_tile(i, late_gate[i - 4], late_up[i - 4]), 4)

    step = rows // CHUNKS

    def give(i):
        src = drow.at[pl.ds(pl.multiple_of(rows + i * step, step), step)]
        dst = rbuf.at[pl.ds(pl.multiple_of(i * step, step), step)]
        return remote(src, dst, x_send.at[i], x_recv.at[i], to[0, 1])

    for some in (slice(rows, 2 * rows), slice(0, rows)):

        def late_rows(j, some=some):
            col = pl.ds(pl.multiple_of(j * 256, 256), 256)
            more = nn(acts[1, some, late:], gate[late:, col]) + nn(acts[2, some, late:], up[late:, col])
            drow[some, col] = (drow[some, col].astype(f32) + more).astype(bf16)

        over(width // 256, late_rows)
        if some.start:
            over(CHUNKS, lambda i: give(i).start())

    def add_other(c):
        give(c).wait_recv()
        r = pl.ds(pl.multiple_of(c * step, step), step)
        drow[r] = (drow[r].astype(f32) + rbuf[r].astype(f32)).astype(bf16)

    def out_copies(j):
        col = pl.ds(pl.multiple_of(j * 256, 256), 256)
        return (
            pltpu.make_async_copy(gate.at[pl.ds(0, rows), col], out.at[:, col], out_sem.at[0, j]),
            remote(
                gate.at[pl.ds(rows, rows), col], out_other.at[:, col], out_sem.at[1, j], out_sem.at[2, j], to[0, 1]
            ),
        )

    def work(i):
        @pl.when(i < 2)
        def _():
            grad_unit(last_unit(i), g)

        @pl.when((i >= 2) & (i < 4))
        def _():
            grad_unit(last_unit(i), h2)

        @pl.when((i >= 4) & (i < 10))
        def _():
            grad_unit(up_unit(i - 4), h2)

        @pl.when((i >= 1) & (i < 5))
        def _():
            flush(last_unit(i - 1))

        @pl.when((i >= 5) & (i < 11))
        def _():
            flush(up_unit(i - 5), i < 7)

        @pl.when(i >= 10)
        def _():
            j = i - 10
            col = pl.ds(pl.multiple_of(j * 256, 256), 256)
            gate[0 : 2 * rows, col] = nn(acts[0], down[:, col]).astype(bf16)
            for x in out_copies(j):
                x.start()

    line_sum_work(
        drow, in_buf, mid_buf, drow, grad_h2, line, "tensor", rows, add_other, lambda r, c: None, work,
        10 + width // 256,
    )
    over(width // 256, lambda j: [x.wait() for x in out_copies(j)])
    over(CHUNKS, lambda i: give(i).wait_send())
    for j in range(3):
        for n in range(6):
            shard_move(j, n).wait_send()
    for m, t in [(m, t) for m in range(2) for t in range(6)] + [(2, 0), (2, 3)]:
        for j in range(2):
            send(m, t, j, 1 + t // 3).wait()


def line_sum_work(x_ref, in_buf, mid_buf, part, out_ref, sems, axis, n_rows, ready, finish, work, n_work):
    a_send, a_recv, b_send, b_recv, c_send, c_recv = sems
    side, mid, inner = line_roles(axis)
    step = n_rows // CHUNKS
    steps = max(n_work, CHUNKS + 4)

    def rows(c):
        return pl.ds(pl.multiple_of(c * step, step), step)

    def copy(src, dst, c, send, recv, to):
        return pltpu.make_async_remote_copy(
            src.at[rows(c)], dst.at[rows(c)], send.at[c], recv.at[c], device_id={axis: to}, device_id_type=MESH
        )

    to_inner = lambda c: copy(x_ref, in_buf, c, a_send, a_recv, side)
    to_middle = lambda c: copy(part, mid_buf, c, b_send, b_recv, mid)
    to_outer = lambda c: copy(out_ref, out_ref, c, c_send, c_recv, side)

    @pl.when(jnp.logical_not(inner))
    def _():
        def begin(c):
            ready(c)
            to_inner(c).start()

        over(CHUNKS, begin)

        def one(i):
            @pl.when((i >= 4) & (i < CHUNKS + 4))
            def _():
                to_outer(i - 4).wait_recv()
                finish(rows(i - 4), i - 4)

            @pl.when(i < n_work)
            def _():
                work(i)

        over(steps, one)
        over(CHUNKS, lambda c: to_inner(c).wait_send())

    @pl.when(inner)
    def _():
        def first(c):
            ready(c)
            to_inner(c).wait_recv()
            r = rows(c)
            part[r] = (x_ref[r].astype(f32) + in_buf[r].astype(f32)).astype(bf16)
            to_middle(c).start()

        def second(c):
            to_middle(c).wait_recv()
            r = rows(c)
            out_ref[r] = (part[r].astype(f32) + mid_buf[r].astype(f32)).astype(bf16)
            to_outer(c).start()
            finish(r, c)

        def one(i):
            @pl.when(i < CHUNKS)
            def _():
                first(i)

            @pl.when((i >= 2) & (i < CHUNKS + 2))
            def _():
                second(i - 2)

            @pl.when(i < n_work)
            def _():
                work(i)

        over(steps, one)

        def done(c):
            to_middle(c).wait_send()
            to_outer(c).wait_send()

        over(CHUNKS, done)


def expert_call(h2, g_own, g_other, mine, gate_own, up_own, down_own, gate, up, down):
    tall, width = down.shape
    rows = h2.shape[0] // 2
    vmem, anyspace = pl.BlockSpec(memory_space=pltpu.VMEM), pl.BlockSpec(memory_space=pl.ANY)
    shape = jax.ShapeDtypeStruct
    dma = pltpu.SemaphoreType.DMA
    return pl.pallas_call(
        expert_kernel,
        out_shape=[
            shape((rows, width), bf16),
            shape((rows, width), bf16),
            shape((rows, width), bf16),
            shape((3, tall, width), bf16),
            shape((3, tall, width // 2), bf16),
        ],
        in_specs=[anyspace] * 10,
        out_specs=[vmem, anyspace, anyspace, anyspace, anyspace],
        scratch_shapes=[
            pltpu.VMEM((2 * rows, width), bf16),
            dma((7,)),
            pltpu.VMEM((2 * rows, width), bf16),
            pltpu.VMEM(mine.shape, f32),
        ]
        + [pltpu.VMEM((tall, width), bf16)] * 3
        + [
            pltpu.VMEM((3, 2 * rows, tall), bf16),
            pltpu.VMEM((2 * rows, width), bf16),
            pltpu.VMEM((rows, width), bf16),
            pltpu.VMEM((rows, width), bf16),
            pltpu.VMEM((rows, width), bf16),
            pltpu.VMEM((2, 512, width // 2), bf16),
            pltpu.VMEM((2, 2 * rows, 256), f32),
            pltpu.VMEM((2, 2 * rows, 256), f32),
            dma((6, 3)), dma((4, 3)), dma((3, 6)), dma((3, 6)), dma((CHUNKS,)), dma((CHUNKS,)), dma((3, 6, 2)), dma((3, 6, 2)),
            dma((2, 2)), dma((3, width // 256)),
        ]
        + line_sems(),
        compiler_params=pltpu.CompilerParams(
            collective_id=2, has_side_effects=True, vmem_limit_bytes=62 * 2**20
        ),
        cost_estimate=pl.CostEstimate(flops=58 * 10**9, bytes_accessed=60 * 10**6, transcendentals=2 * 10**6),
        name="experts",
    )(h2, g_own, g_other, mine, gate_own, up_own, down_own, gate, up, down)


def plane_barrier(to, z_others):
    barrier = pltpu.get_barrier_semaphore()
    others = [k for k in to if k != (0, 0)]
    for k in others:
        pl.semaphore_signal(barrier, inc=1, device_id=to[k], device_id_type=MESH)
    for z in z_others:
        pl.semaphore_signal(barrier, inc=1, device_id={"tensor": z}, device_id_type=MESH)
    pl.semaphore_wait(barrier, len(others) + len(z_others))
    return others


def z_partners():
    p = lax.axis_index("tensor")
    return [p + 1 - 2 * (p % 2), p + 2 - 4 * (p // 2), 3 - p]


def gain_vectors(gains, gain_rows):
    for kd in range(4):
        for kc in range(2):
            g = gains[kd, kc]
            for j in range(2):
                col = (kd * 2 + kc) * 256 + j * 128
                gain_rows[0:1, col : col + 128] = g[j : j + 1]
                gain_rows[1:2, col : col + 128] = g[2 + j : 3 + j]
    heads = jnp.sum(gains[...].reshape(8, 8, 128), axis=0)
    return heads[4:5], heads[5:6]


def attention_back_kernel(
    gains, cos, sin, grad_h2_in, x2_in, cot_in, qrot_in, krot_in, value_in, raw_in, probs, wo_in, qkv_in, out_own, out_other,
    grads, _,
    output, dx2_out, low_out, grad_qkv, grad_h1, gain_grads, got2, got,
    grad_h2, x2, cot, qrot, krot, value, raw, f_sem, dx2, low, wo, qkv, own_out, rbuf, in_buf, mid_buf, summed, datt, pbuf, dk, dv, gain_rows, load_a, load_b, on_buf,
    w_sem, p_sem, l_sem, s_send, s_recv, u_send, u_recv, *line,
):
    to = plane_partners()
    fetch = [
        pltpu.make_async_copy(src, dst, f_sem.at[i])
        for i, (src, dst) in enumerate(
            ((x2_in, x2), (grad_h2_in, grad_h2), (qrot_in, qrot), (krot_in, krot), (value_in, value), (raw_in, raw))
        )
    ]
    early = fetch[:2] + lane_copies(cot_in, cot, [f_sem.at[6 + k] for k in range(4)], to)
    plane_barrier(to, z_partners())
    places = [to[k, 0]["dp"] for k in range(4)]
    rows, width = x2.shape
    wide = width // 4
    q_cols = qrot.shape[1]
    n_heads = q_cols // 128
    step = rows // CHUNKS
    rate = 128 ** (-0.5)

    weights = [
        pltpu.make_async_copy(wo_in, wo, w_sem.at[0]),
        pltpu.make_async_copy(qkv_in, qkv, w_sem.at[1]),
        pltpu.make_async_copy(out_own, own_out, w_sem.at[2]),
        pltpu.make_async_copy(out_other, rbuf, w_sem.at[3]),
    ]
    flushes = [
        pltpu.make_async_copy(dx2, dx2_out, w_sem.at[4]),
        pltpu.make_async_copy(low, low_out, w_sem.at[5]),
    ]
    for w in weights[2:] + early + [weights[0]] + fetch[2:] + [weights[1]]:
        w.start()

    def load_probs(h):
        return pltpu.make_async_copy(probs.at[h], pbuf.at[h % 2], p_sem.at[h % 2])

    def up_move(t, j, first):
        came = lambda t, cols: got.at[2, tile(t), cols]
        return first_exchange(2, t, j, first, grads, came, u_send.at[t, j], u_recv.at[t, j], to, wide)

    def up_moves(i, f):
        t = turn(i)
        by_half(t, lambda first: [f(up_move(t, j, first)) for j in range(2)])

    over(6, lambda i: up_moves(i, lambda x: x.start()), 2)
    at = lambda ref: lambda u, cols=pl.ds(0, wide): ref.at[u // 6, tile(turn(u % 6)), cols]
    start, second_tile, second_done = second_exchange(
        12, at(grads), at(got), at(got2), load_a, load_b, on_buf, l_sem, s_send, s_recv, to, wide
    )
    start(0)
    start(1)
    load_probs(0).start()
    gain_query, gain_key = gain_vectors(gains, gain_rows)
    gain_grads[...] = jnp.zeros_like(gain_grads)
    dk[...] = jnp.zeros_like(dk)
    dv[...] = jnp.zeros_like(dv)

    def mixed_rows(i):
        r = pl.ds(pl.multiple_of(i * 64, 64), 64)
        x = x2[r]
        scale = lax.rsqrt(jnp.mean(x * x, axis=-1, keepdims=True) + epsilon)
        normed = x * scale
        grad = grad_h2[r].astype(f32)
        gain_grads[0:1, :] += jnp.sum(grad * normed, axis=0, keepdims=True)
        n = grad * gain_rows[1:2]
        d = cot[r].astype(f32) + scale * (n - normed * jnp.mean(n * normed, axis=-1, keepdims=True))
        dx2[r] = d
        low[r] = d.astype(bf16)

    def att_grads(j):
        col = pl.ds(pl.multiple_of(j * 256, 256), 256)
        datt[:, col] = nn(low[...], wo[:, col]).astype(bf16)

    def unspin(u):
        return u * cos[...] - pltpu.roll(u, 64, 1) * sin[...]

    def norm_grads(x, rotated, gain, row):
        scale = lax.rsqrt(jnp.mean(x * x, axis=-1, keepdims=True) + epsilon)
        normed = x * scale
        du = unspin(rotated)
        gain_grads[row : row + 1, 0:128] += jnp.sum(du * normed, axis=0, keepdims=True)
        n = du * gain
        return (scale * (n - normed * jnp.mean(n * normed, axis=-1, keepdims=True))).astype(bf16)

    block = rows // 2

    def head(h):
        load_probs(h).wait()

        @pl.when(h + 1 < n_heads)
        def _():
            load_probs(h + 1).start()

        col = pl.ds(pl.multiple_of(h * 128, 128), 128)
        dq = []
        for i in range(2):
            r, n = slice(i * block, (i + 1) * block), (i + 1) * block
            p_low = pbuf[h % 2, r, 0:n]
            p = p_low.astype(f32)
            dp = nt(datt[r, col], value[0:n])
            ds = (p * (dp - jnp.sum(p * dp, axis=-1, keepdims=True))).astype(bf16)
            dq.append(nn(ds, krot[0:n]) * rate)
            dk[0:n] += tn(ds, qrot[r, col])
            dv[0:n] += tn(p_low, datt[r, col])
        grad_qkv[:, col] = norm_grads(raw[:, col], jnp.concatenate(dq, 0), gain_query, 1)

    def key_value():
        grad_qkv[:, pl.ds(q_cols, 128)] = norm_grads(raw[:, pl.ds(q_cols, 128)], dk[...] * rate, gain_key, 2)
        grad_qkv[:, pl.ds(q_cols + 128, 128)] = dv[...].astype(bf16)

    def input_grads(j):
        r = pl.ds(pl.multiple_of(j * 256, 256), 256)
        grad_h1[:, r] = nt(grad_qkv[...], qkv[r]).astype(bf16)

    def work(i):
        @pl.when(i < 12)
        def _():
            second_tile(i)

        @pl.when(i == 0)
        def _():
            for x in early:
                x.wait()

        @pl.when(i < 4)
        def _():
            mixed_rows(2 * i)
            mixed_rows(2 * i + 1)

        @pl.when(i == 4)
        def _():
            weights[0].wait()
            for x in flushes:
                x.start()
            for x in fetch[2:]:
                x.wait()

        @pl.when((i >= 4) & (i < 6))
        def _():
            att_grads(2 * (i - 4))
            att_grads(2 * (i - 4) + 1)

        @pl.when((i >= 6) & (i < 6 + n_heads))
        def _():
            head(i - 6)

        @pl.when(i == 6 + n_heads)
        def _():
            key_value()
            weights[1].wait()

        @pl.when((i > 6 + n_heads) & (i <= 10 + n_heads))
        def _():
            j = 2 * (i - 7 - n_heads)
            input_grads(j)
            input_grads(j + 1)

    def ready(c):
        @pl.when(c == 0)
        def _():
            weights[2].wait()
            weights[3].wait()

        r = pl.ds(pl.multiple_of(c * step, step), step)
        own_out[r] = (own_out[r].astype(f32) + rbuf[r].astype(f32)).astype(bf16)

    def finish(r, c):
        done = (x2[r] + summed[r].astype(f32)).astype(bf16)
        for k in range(4):
            output[r, pl.ds(pl.multiple_of(places[k] * wide, wide), wide)] = done[:, k * wide : (k + 1) * wide]

    line_sum_work(
        own_out, in_buf, mid_buf, own_out, summed, line, "tensor", rows, ready, finish, work, 11 + n_heads
    )
    for x in flushes:
        x.wait()
    second_done()
    over(6, lambda i: up_moves(i, lambda x: x.wait()), 2)


def attention_back_call(grad_h2, x2, cot, qrot, krot, value, raw, gains, cos, sin, probs, wo, qkv, out_own, out_other, grads, got):
    rows, width = x2.shape
    q_cols, qkv_cols = wo.shape[1], qkv.shape[1]
    tall = grads.shape[1]
    wide = width // 4
    vmem, anyspace = pl.BlockSpec(memory_space=pltpu.VMEM), pl.BlockSpec(memory_space=pl.ANY)
    shape = jax.ShapeDtypeStruct
    dma = pltpu.SemaphoreType.DMA
    big = pltpu.VMEM((rows, width), bf16)
    return pl.pallas_call(
        attention_back_kernel,
        out_shape=[
            shape((rows, width), bf16),
            shape((rows, width), f32),
            shape((rows, width), bf16),
            shape((rows, qkv_cols), bf16),
            shape((rows, width), bf16),
            shape((8, width), f32),
            shape((2, tall, wide), bf16),
            shape(got.shape, bf16),
        ],
        in_specs=[vmem] * 3 + [anyspace] * 14,
        out_specs=[vmem, anyspace, anyspace] + [vmem] * 3 + [anyspace] * 2,
        scratch_shapes=[
            big,
            pltpu.VMEM((rows, width), f32),
            big,
            pltpu.VMEM((rows, q_cols), bf16),
            pltpu.VMEM((rows, 128), bf16),
            pltpu.VMEM((rows, 128), bf16),
            pltpu.VMEM((rows, qkv_cols), f32),
            dma((10,)),
            pltpu.VMEM((rows, width), f32),
            big,
            pltpu.VMEM((width, q_cols), bf16),
            pltpu.VMEM((width, qkv_cols), bf16),
            big, big, big, big, big,
            pltpu.VMEM((rows, q_cols), bf16),
            pltpu.VMEM((2, rows, rows), bf16),
            pltpu.VMEM((rows, 128), f32),
            pltpu.VMEM((rows, 128), f32),
            pltpu.VMEM((2, width), f32),
            pltpu.VMEM((2, 256, wide), bf16),
            pltpu.VMEM((2, 256, wide), bf16),
            pltpu.VMEM((12, 256, wide), bf16),
            dma((6,)), dma((2,)), dma((2, 2)), dma((12,)), dma((12,)),
            dma((6, 2)), dma((6, 2)),
        ]
        + line_sems(),
        input_output_aliases={16: 7},
        compiler_params=pltpu.CompilerParams(
            collective_id=3, has_side_effects=True, vmem_limit_bytes=62 * 2**20
        ),
        cost_estimate=pl.CostEstimate(flops=9 * 10**9, bytes_accessed=60 * 10**6, transcendentals=10**5),
        name="attention_backward",
    )(gains, cos, sin, grad_h2, x2, cot, qrot, krot, value, raw, probs, wo, qkv, out_own, out_other, grads, got)


def last_kernel(
    gains, gain_grads, part_in, dx2_in, tokens_in, grad_qkv_in, low_in, att_in, grads, got,
    tokens_grad_out, q_shard, k_shard, v_shard, wo_shard, gain_sum, got2_up,
    tokens_grad, d_sem, part, dx2, tokens, grad_qkv, low, att, f_sem, h1, in_buf, mid_buf, half_sum, summed, gain_rows, wo_all, qkv_all, wo_core, qkv_core, wo_one, qkv_one, wo_two, qkv_two,
    ga, z_got, g_out, g_got, load_a, load_b, on_buf, l_sem, s_send, s_recv,
    z_send, z_recv, c_send, c_recv, f_send, f_recv, t_send, t_recv, g_send, g_recv, *line,
):
    fetch = [
        pltpu.make_async_copy(src, dst, f_sem.at[i])
        for i, (src, dst) in enumerate(
            (
                (part_in, part), (tokens_in, tokens), (low_in, low), (att_in, att), (grad_qkv_in, grad_qkv),
                (dx2_in, dx2),
            )
        )
    ]
    for x in fetch:
        x.start()
    c = lax.axis_index("expert")
    to = plane_partners()
    zs = z_partners()
    others = plane_barrier(to, zs)
    places = [to[k, 0]["dp"] for k in range(4)]
    rows, width = tokens.shape
    wide = width // 4
    piece = wide // 2
    half = piece // 2

    def z_move(j):
        return remote(gain_grads.at[pl.ds(0, 8), pl.ds(0, 128)], z_got.at[j], z_send.at[j], z_recv.at[j], {"tensor": zs[j]})

    for j in range(3):
        z_move(j).start()
    up_at = lambda ref: lambda u, cols: ref.at[2, tile(turn(u)), cols]
    start, second_tile, second_done = second_exchange(
        6, up_at(grads), up_at(got), lambda u: got2_up.at[tile(turn(u))],
        load_a, load_b, on_buf, l_sem, s_send, s_recv, to, wide,
    )
    start(0)
    start(1)
    gain_vectors(gains, gain_rows)
    ga[...] = jnp.zeros_like(ga)

    def unit_rows(r):
        x = tokens[r].astype(f32)
        scale = lax.rsqrt(jnp.mean(x * x, axis=-1, keepdims=True) + epsilon)
        return x * scale, scale

    def hidden_one(i):
        r = pl.ds(pl.multiple_of(i * 64, 64), 64)
        h1[r] = (unit_rows(r)[0] * gain_rows[0:1]).astype(bf16)

    mats = [
        (low, att, wo_all, wo_core, wo_one, wo_two),
        (h1, grad_qkv, qkv_all, qkv_core, qkv_one, qkv_two),
    ]

    def block(k, core):
        return pl.ds(pl.multiple_of((k * 2 + core) * piece, piece), piece)

    def core_move(m, k):
        return remote(mats[m][2].at[block(k, 1 - c)], mats[m][3].at[k], c_send.at[m, k], c_recv.at[m, k], to[0, 1])

    def product(m, k, core):
        left, right, full = mats[m][:3]
        full[block(k, core)] = tn(left[:, block(k, core)], right[...]).astype(bf16)

    def away(m, k):
        product(m, k, 1 - c)
        core_move(m, k).start()

    def home(m, k):
        product(m, k, c)
        full, came = mats[m][2:4]
        core_move(m, k).wait_recv()
        full[block(k, c)] = (full[block(k, c)].astype(f32) + came[k].astype(f32)).astype(bf16)

    def slot(m, k, h):
        return mats[m][2].at[pl.ds(pl.multiple_of((k * 2 + c) * piece + h * half, half), half)]

    def first_move(m, h, j):
        way = 1 + h
        src = slot(m, 3 if j else way, h)
        return remote(src, mats[m][4].at[h, j], f_send.at[m, h, j], f_recv.at[m, h, j], to[way, 0])

    def second_move(m, h):
        return remote(slot(m, 2 - h, h), mats[m][5].at[h], t_send.at[m, h], t_recv.at[m, h], to[2 - h, 0])

    def add_first(m, h, j, k):
        full, one = mats[m][2], mats[m][4]
        r = pl.ds(pl.multiple_of((k * 2 + c) * piece + h * half, half), half)
        first_move(m, h, j).wait_recv()
        full[r] = (full[r].astype(f32) + one[h, j].astype(f32)).astype(bf16)

    def work(i):
        @pl.when(i == 0)
        def _():
            for x in fetch[1:]:
                x.wait()
            over(rows // 64, hidden_one)

        @pl.when(i < 6)
        def _():
            second_tile(i)

        for m in range(2):
            for n, ks in enumerate(((3, 1), (2, 0))):

                @pl.when(i == 1 + 4 * m + n)
                def _(m=m, ks=ks):
                    for k in ks:
                        away(m, k)

                @pl.when(i == 3 + 4 * m + n)
                def _(m=m, n=n, ks=ks):
                    for k in ks:
                        home(m, k)
                    for j in range(2):
                        first_move(m, n, j).start()

            @pl.when(i == SECOND[m])
            def _(m=m):
                for h in range(2):
                    add_first(m, h, 1, 2 - h)
                    second_move(m, h).start()

    def give_back(i):
        r = pl.ds(pl.multiple_of(i * (rows // CHUNKS), rows // CHUNKS), rows // CHUNKS)
        return pltpu.make_async_copy(tokens_grad.at[r], tokens_grad_out.at[r], d_sem.at[i])

    def finish(r, i):
        grad = summed[r].astype(f32)
        normed, scale = unit_rows(r)
        ga[0:1, :] += jnp.sum(grad * normed, axis=0, keepdims=True)
        n = grad * gain_rows[0:1]
        d = dx2[r] + scale * (n - normed * jnp.mean(n * normed, axis=-1, keepdims=True))
        for k in range(4):
            tokens_grad[r, pl.ds(pl.multiple_of(places[k] * wide, wide), wide)] = d[:, k * wide : (k + 1) * wide]
        give_back(i).start()

    fetch[0].wait()
    line_sum_work(part, in_buf, mid_buf, half_sum, summed, line, "tensor", rows, lambda k: None, finish, work, 20)

    head_rows = gain_grads[1:3, 0:128]
    for j in range(3):
        z_move(j).wait()
        head_rows += z_got[j, 1:3]
    for kd in range(4):
        for kc in range(2):
            for j in range(2):
                col = slice((kd * 2 + kc) * piece + j * 128, (kd * 2 + kc) * piece + (j + 1) * 128)
                g_out[kd, kc, j : j + 1] = ga[0:1, col]
                g_out[kd, kc, 2 + j : 3 + j] = gain_grads[0:1, col]
            g_out[kd, kc, 4:6] = head_rows

    def gain_move(j):
        kd, kc = others[j]
        core = c if kc == 0 else 1 - c
        return remote(g_out.at[kd, core], g_got.at[j], g_send.at[j], g_recv.at[j], to[kd, kc])

    for j in range(len(others)):
        gain_move(j).start()
    q_cols, k_cols = q_shard.shape[1], k_shard.shape[1]
    shards = (
        ((wo_shard, 0),),
        ((q_shard, 0), (k_shard, q_cols), (v_shard, q_cols + k_cols)),
    )
    for m in range(2):
        full, two = mats[m][2], mats[m][5]
        for h in range(2):
            add_first(m, h, 0, 0)
            second_move(m, h).wait_recv()
            r = pl.ds(pl.multiple_of(c * piece + h * half, half), half)
            for shard, col in shards[m]:
                cols = pl.ds(col, shard.shape[1])
                shard[h * half : (h + 1) * half] = full[r, cols].astype(f32) + two[h, :, cols].astype(f32)
    total = g_out[0, pl.ds(c, 1)].reshape(8, 128)
    for j in range(len(others)):
        gain_move(j).wait_recv()
        total += g_got[j]
    gain_sum[...] = total
    second_done()
    over(CHUNKS, lambda i: give_back(i).wait())
    for m in range(2):
        for k in range(4):
            core_move(m, k).wait_send()
        for h in range(2):
            for j in range(2):
                first_move(m, h, j).wait_send()
            second_move(m, h).wait_send()
    for j in range(len(others)):
        gain_move(j).wait_send()


def last_call(part, dx2, tokens, grad_qkv, low, att, gains, gain_grads, grads, got):
    rows, width = tokens.shape
    q_cols, qkv_cols = att.shape[1], grad_qkv.shape[1]
    piece = width // 8
    vmem = pl.BlockSpec(memory_space=pltpu.VMEM)
    shape = jax.ShapeDtypeStruct
    dma = pltpu.SemaphoreType.DMA
    big = pltpu.VMEM((rows, width), bf16)
    both = lambda *lead: [pltpu.VMEM(lead + (n,), bf16) for n in (q_cols, qkv_cols)]
    return pl.pallas_call(
        last_kernel,
        out_shape=[
            shape((rows, width), f32),
            shape((piece, q_cols), f32),
            shape((piece, (qkv_cols - q_cols) // 2), f32),
            shape((piece, (qkv_cols - q_cols) // 2), f32),
            shape((piece, q_cols), f32),
            shape((8, 128), f32),
            shape((got.shape[1], width // 4), bf16),
        ],
        in_specs=[vmem] * 2 + [pl.BlockSpec(memory_space=pl.ANY)] * 8,
        out_specs=[pl.BlockSpec(memory_space=pl.ANY)] + [vmem] * 5 + [pl.BlockSpec(memory_space=pl.ANY)],
        scratch_shapes=[
            pltpu.VMEM((rows, width), f32),
            dma((CHUNKS,)),
            big,
            pltpu.VMEM((rows, width), f32),
            big,
            pltpu.VMEM((rows, qkv_cols), bf16),
            big,
            pltpu.VMEM((rows, q_cols), bf16),
            dma((6,)),
        ]
        + [big, big, big, big, big, pltpu.VMEM((2, width), f32)]
        + both(width)
        + both(4, piece)
        + both(2, 2, piece // 2)
        + both(2, piece // 2)
        + [
            pltpu.VMEM((8, width), f32),
            pltpu.VMEM((3, 8, 128), f32),
            pltpu.VMEM((4, 2, 8, 128), f32),
            pltpu.VMEM((7, 8, 128), f32),
            pltpu.VMEM((2, 256, width // 4), bf16),
            pltpu.VMEM((2, 256, width // 4), bf16),
            pltpu.VMEM((6, 256, width // 4), bf16),
            dma((2, 2)), dma((6,)), dma((6,)),
            dma((3,)), dma((3,)), dma((2, 4)), dma((2, 4)), dma((2, 2, 2)), dma((2, 2, 2)), dma((2, 2)), dma((2, 2)),
            dma((7,)), dma((7,)),
        ]
        + line_sems(),
        compiler_params=pltpu.CompilerParams(
            collective_id=4, has_side_effects=True, vmem_limit_bytes=62 * 2**20
        ),
        cost_estimate=pl.CostEstimate(flops=5 * 10**9, bytes_accessed=40 * 10**6, transcendentals=10**5),
        name="input_gradients",
    )(gains, gain_grads, part, dx2, tokens, grad_qkv, low, att, grads, got)


def local_fast(
    tokens,
    cotangent,
    route_ids,
    route_weight,
    lengths,
    attention_norm,
    query_weight,
    key_matrix,
    value_matrix,
    output_weight,
    query_norm,
    key_norm,
    experts_norm,
    gate_weight,
    up_weight,
    down_weight,
):
    n_dp = lax.axis_size("dp")
    n_ex = lax.axis_size("expert")
    me_dp = lax.axis_index("dp")
    me_ex = lax.axis_index("expert")
    rows, width = tokens.shape
    group, hidden, part = gate_weight.shape
    length = lengths[0]
    lane = lambda x, axis=-1: lane_order(x, axis, n_dp, me_dp)

    flat = group * hidden
    na, nq = attention_norm.shape[0], query_norm.shape[0]
    q_cols, k_cols = query_weight.shape[1], key_matrix.shape[1]
    heads_query, heads_key = q_cols // HEAD_SIZE, k_cols // HEAD_SIZE
    per_group = heads_query // heads_key
    own_place = (me_dp * n_ex + me_ex) * nq
    fill = jnp.zeros((128 - nq,), bf16)
    gains_own = jnp.concatenate(
        [attention_norm, experts_norm, query_norm, fill, key_norm, fill, jnp.zeros((256,), bf16)]
    )
    gains_own = gains_own.reshape(8, 128).astype(f32)
    cos2, sin2 = rope_lanes(rows)
    own_experts = [w.reshape(flat, part) for w in (gate_weight, up_weight, down_weight)]
    (
        inputs_low, upstream_other, table, mixed_rows, hidden_all, attended_low, rotated_query, key_rot, value_low, raw,
        prob_low, gains, gate_full, up_full, down_full, full_qkv, full_output,
    ) = forward_call(
        tokens,
        cotangent,
        route_ids.T,
        route_weight.T,
        lengths,
        query_weight,
        key_matrix,
        value_matrix,
        output_weight,
        *own_experts,
        gains_own,
        cos2,
        sin2,
    )
    grad_hidden_two, out_own, out_other, grads, got = expert_call(
        hidden_all, cotangent, upstream_other, table, *own_experts, gate_full, up_full, down_full
    )
    output, grad_mixed, grad_proj_low, grad_qkv_low, grad_hidden_one, gain_grads, got2, got = attention_back_call(
        grad_hidden_two, mixed_rows, cotangent, rotated_query, key_rot, value_low, raw, gains, cos2, sin2,
        prob_low, full_output, full_qkv, out_own, out_other, grads, got,
    )
    tokens_grad, query_shard, key_shard, value_shard, output_shard, gain_sum, got2_up = last_call(
        grad_hidden_one, grad_mixed, inputs_low, grad_qkv_low, grad_proj_low, attended_low, gains, gain_grads,
        grads, got,
    )
    down_shard, gate_shard, up_shard = (
        (grads[m, :, :part].astype(f32) + got[m, :, :part].astype(f32) + last.astype(f32)).reshape(group, hidden, part)
        for m, last in enumerate((got2[0], got2[1], got2_up))
    )
    own_head = lambda row: lax.dynamic_slice_in_dim(gain_sum[row], own_place, nq, 0)
    return (
        output,
        tokens_grad,
        gain_sum[0:2].reshape(-1),
        query_shard,
        key_shard,
        value_shard,
        output_shard,
        own_head(4),
        own_head(5),
        gain_sum[2:4].reshape(-1),
        gate_shard,
        up_shard,
        down_shard,
    )


def local(*args):
    sizes = [lax.axis_size(a) for a in ("dp", "expert", "tensor")]
    return local_fast(*args) if sizes == [4, 2, 4] else local_plain(*args)


def solution(mesh):
    both = ("dp", "expert")
    rows2, rows1, mats = P(both, None), P(both), P(both, "tensor")
    experts = P("expert", "tensor", "dp")
    return jax.shard_map(
        local,
        mesh=mesh,
        in_specs=(rows2, rows2, rows2, rows2, rows1, rows1, mats, mats, mats, mats, rows1, rows1, rows1)
        + (experts,) * 3,
        out_specs=(rows2, rows2, rows1, mats, mats, mats, mats, rows1, rows1, rows1) + (experts,) * 3,
        check_vma=False,
    )
```

```python
import jax
import jax.numpy as jnp
import numpy as np
from jax import lax
from jax.experimental import pallas as pl
from jax.experimental.pallas import tpu as pltpu
from jax.sharding import PartitionSpec as P

HEAD_SIZE = 128
TOP = 8
epsilon = 1e-06
f32 = jnp.float32
bf16 = jnp.bfloat16
MESH = pl.DeviceIdType.MESH


def rms_scale(values):
    return lax.rsqrt(jnp.mean(values * values, axis=-1, keepdims=True) + epsilon)


def rope_lanes(rows):
    half = HEAD_SIZE // 2
    frequency = np.power(np.float32(1000000.0), -(np.arange(half, dtype=np.float32) * np.float32(2.0 / HEAD_SIZE)))
    angles = np.arange(rows, dtype=np.float32)[:, None] * frequency[None, :]
    cos, sin = np.cos(angles), np.sin(angles)
    return np.concatenate([cos, cos], 1), np.concatenate([-sin, sin], 1)


def rope_tables(rows):
    half_dim = HEAD_SIZE // 2
    frequency = jnp.power(f32(1000000.0), -(jnp.arange(half_dim, dtype=f32) * (2.0 / HEAD_SIZE)))
    angles = jnp.arange(rows, dtype=f32)[:, None] * frequency[None, :]
    return (jnp.cos(angles)[:, None, :], jnp.sin(angles)[:, None, :])


def rotate(values, cosine_table, sine_table):
    half_dim = values.shape[-1] // 2
    first_half = values[..., :half_dim]
    second_half = values[..., half_dim:]
    return jnp.concatenate(
        [
            first_half * cosine_table - second_half * sine_table,
            second_half * cosine_table + first_half * sine_table,
        ],
        axis=-1,
    )


def norm_back(grad_hidden, normed, scales, gains):
    grad_normed = grad_hidden * gains
    return scales * (grad_normed - normed * jnp.mean(grad_normed * normed, axis=-1, keepdims=True))


def flip(x, axis, bit):
    n = lax.axis_size(axis)
    return lax.ppermute(x, axis, [(i, i ^ bit) for i in range(n)])


def bits_of(n):
    return [1 << b for b in range(n.bit_length() - 1)]


def xor_gather(x, axis):
    pieces = [x]
    for bit in bits_of(lax.axis_size(axis)):
        pieces = pieces + [flip(p, axis, bit) for p in pieces]
    return pieces


def xor_scatter(parts, axis):
    for bit in reversed(bits_of(lax.axis_size(axis))):
        got = [flip(p, axis, bit) for p in parts[bit:]]
        parts = [
            (a.astype(f32) + r.astype(f32)).astype(a.dtype) for a, r in zip(parts[:bit], got)
        ]
    return parts[0]


def dp_scatter(blocks, axis="dp"):
    n = len(blocks)
    if n != 4:
        return xor_scatter(blocks, axis).astype(f32)
    h = blocks[0].shape[0] // 2
    add = lambda p, q: p.astype(f32) + q.astype(f32)
    done = []
    for rows, first, second in ((slice(0, h), 1, 2), (slice(h, 2 * h), 2, 1)):
        b = [x[rows] for x in blocks]
        got = flip(jnp.concatenate([b[first], b[3]], 0), axis, first)
        on = add(b[second], got[h:]).astype(bf16)
        done.append(add(b[0], got[:h]) + flip(on, axis, second).astype(f32))
    return jnp.concatenate(done, 0)


def all_pieces(x, axis, me):
    got = jnp.stack(xor_gather(x, axis), 0)
    return lane_order(got, 0, got.shape[0], me)


def dp_gather(x, axis="dp"):
    n = lax.axis_size(axis)
    if n != 4:
        return xor_gather(x, axis)
    h = x.shape[0] // 2
    a, b = x[:h], x[h:]
    a1, b2 = flip(a, axis, 1), flip(b, axis, 2)
    a2, b1 = flip(a, axis, 2), flip(b, axis, 1)
    a3, b3 = flip(a1, axis, 2), flip(b2, axis, 1)
    cat = lambda p, q: jnp.concatenate([p, q], 0)
    return [cat(a, b), cat(a1, b1), cat(a2, b2), cat(a3, b3)]


def lane_block(x, axis, n, me, k):
    axis = axis % x.ndim
    size = x.shape[axis] // n
    return lax.dynamic_slice_in_dim(x, (me ^ k) * size, size, axis)


def lane_order(x, axis, n, me):
    return jnp.concatenate([lane_block(x, axis, n, me, k) for k in range(n)], axis)


def block_scores(query_block, key_rot, length):
    query_pos = jnp.arange(query_block.shape[0], dtype=jnp.int32)
    key_pos = jnp.arange(key_rot.shape[0], dtype=jnp.int32)
    allowed = (key_pos[None, :] <= query_pos[:, None]) & (key_pos[None, :] < length)
    scores = jnp.einsum(
        "qkgd,skd->kgqs", query_block, key_rot, preferred_element_type=f32
    ) * HEAD_SIZE ** (-0.5)
    return jnp.where(allowed, scores, -1e30)


def core_rows(pieces, axis="expert"):
    n = lax.axis_size(axis)
    own = jnp.stack(pieces, 0)
    if n == 2:
        other = flip(own, axis, 1)
        first = lax.axis_index(axis) == 0
        both = jnp.stack([jnp.where(first, own, other), jnp.where(first, other, own)], 1)
    else:
        both = lax.all_gather(own, axis, axis=1, tiled=False)
    return both.reshape((-1,) + own.shape[2:])


def dotf(a, b, dims):
    return lax.dot_general(a, b, (dims, ((), ())), preferred_element_type=f32)


def local_plain(
    tokens,
    cotangent,
    route_ids,
    route_weight,
    lengths,
    attention_norm,
    query_weight,
    key_matrix,
    value_matrix,
    output_weight,
    query_norm,
    key_norm,
    experts_norm,
    gate_weight,
    up_weight,
    down_weight,
):
    n_dp = lax.axis_size("dp")
    n_ex = lax.axis_size("expert")
    me_dp = lax.axis_index("dp")
    me_ex = lax.axis_index("expert")
    rows, width = tokens.shape
    group, hidden, part = gate_weight.shape
    length = lengths[0]
    lane = lambda x, axis=-1: lane_order(x, axis, n_dp, me_dp)

    qkv_own = jnp.concatenate([query_weight, key_matrix, value_matrix], 1)
    qkv_pieces = dp_gather(qkv_own)
    wo_own, qkv_pieces = lax.optimization_barrier((output_weight, qkv_pieces))
    wo_pieces = dp_gather(wo_own)
    (gw, uw, dw), wo_pieces = lax.optimization_barrier(
        ((gate_weight, up_weight, down_weight), wo_pieces)
    )
    flat = group * hidden
    gate_up_own = jnp.concatenate([gw.reshape(flat, part), uw.reshape(flat, part)], 0)
    gate_up_pieces = dp_gather(gate_up_own)
    down_own, gate_up_pieces = lax.optimization_barrier((dw.reshape(flat, part), gate_up_pieces))
    down_pieces = dp_gather(down_own)

    na, nq = attention_norm.shape[0], query_norm.shape[0]
    gains = jnp.concatenate([attention_norm, experts_norm, query_norm, key_norm])
    gains = jnp.pad(gains, (0, -gains.size % 128)).reshape(-1, 128)
    gains = all_pieces(all_pieces(gains, "expert", me_ex), "dp", me_dp)
    gains = gains.reshape(n_dp, n_ex, -1).astype(f32)
    gain_attention = lane(gains[:, :, :na].reshape(-1))
    gain_experts = lane(gains[:, :, na : 2 * na].reshape(-1))
    gain_query = gains[:, :, 2 * na : 2 * na + nq].reshape(-1)
    gain_key = gains[:, :, 2 * na + nq : 2 * na + 2 * nq].reshape(-1)

    experts = jnp.arange(group * n_ex, dtype=jnp.int32)
    table = jnp.zeros((rows, group * n_ex), f32)
    for c in range(route_ids.shape[1]):
        table = table + jnp.where(
            route_ids[:, c, None] == experts[None, :], route_weight[:, c, None], 0.0
        )
    table = jnp.concatenate(xor_gather(table, "expert"), 0)
    mine = lax.dynamic_slice_in_dim(table, me_ex * group, group, 1)
    unit_expert = jnp.arange(flat, dtype=jnp.int32) // hidden
    route_scale = jnp.zeros((table.shape[0], flat), f32)
    for j in range(group):
        route_scale = route_scale + jnp.where(unit_expert[None, :] == j, mine[:, j, None], 0.0)

    cosine_table, sine_table = rope_tables(rows)
    inputs = lane(tokens.astype(f32))
    scale_one = rms_scale(inputs)
    normed_one = inputs * scale_one
    first_hidden = (normed_one * gain_attention).astype(bf16)
    upstream_low = lane(cotangent)
    upstream_all = jnp.concatenate(xor_gather(upstream_low, "expert"), 0)

    full_qkv = core_rows(qkv_pieces)
    qkv = jnp.dot(first_hidden, full_qkv, preferred_element_type=f32)
    q_cols, k_cols = query_weight.shape[1], key_matrix.shape[1]
    heads_query, heads_key = q_cols // HEAD_SIZE, k_cols // HEAD_SIZE
    per_group = heads_query // heads_key
    query_raw = qkv[:, :q_cols].reshape(rows, heads_query, HEAD_SIZE)
    key_raw = qkv[:, q_cols : q_cols + k_cols].reshape(rows, heads_key, HEAD_SIZE)
    value_low = qkv[:, q_cols + k_cols :].astype(bf16).reshape(rows, heads_key, HEAD_SIZE)
    scale_query = rms_scale(query_raw)
    normed_query = query_raw * scale_query
    rotated_query = (
        rotate(normed_query * gain_query, cosine_table, sine_table)
        .astype(bf16)
        .reshape(rows, heads_key, per_group, HEAD_SIZE)
    )
    scale_key = rms_scale(key_raw)
    normed_key = key_raw * scale_key
    key_rot = rotate(normed_key * gain_key, cosine_table, sine_table).astype(bf16)
    scores = block_scores(rotated_query, key_rot, length)
    row_peak = jnp.max(scores, axis=-1, keepdims=True)
    shifted = jnp.exp(scores - row_peak)
    totals = jnp.sum(shifted, axis=-1, keepdims=True)
    probs = shifted / totals
    prob_low = probs.astype(bf16)
    attended_low = (
        jnp.einsum("kgqs,skd->qkgd", prob_low, value_low, preferred_element_type=f32)
        .reshape(rows, q_cols)
        .astype(bf16)
    )
    full_output = core_rows(wo_pieces)
    projected = dotf(attended_low, full_output, ((1,), (1,)))
    mixed_rows = inputs + lax.psum(projected.astype(bf16), "tensor").astype(f32)
    scale_two = rms_scale(mixed_rows)
    normed_two = mixed_rows * scale_two
    hidden_two = (normed_two * gain_experts).astype(bf16)

    hidden_all = jnp.concatenate(xor_gather(hidden_two, "expert"), 0)
    gate_up_full = jnp.concatenate(gate_up_pieces, 1)
    down_full = jnp.concatenate(down_pieces, 1)
    gate_up = dotf(hidden_all, gate_up_full, ((1,), (1,)))
    gate_value, up_value = gate_up[:, :flat], gate_up[:, flat:]
    grad_act = lax.optimization_barrier(dotf(upstream_all, down_full, ((1,), (1,)))) * route_scale
    sigmoid_gate = jax.nn.sigmoid(gate_value)
    scaled_act = (gate_value * sigmoid_gate * up_value * route_scale).astype(bf16)
    grad_up_low = (grad_act * gate_value * sigmoid_gate).astype(bf16)
    grad_gate_low = (
        grad_act * up_value * sigmoid_gate * (1.0 + gate_value * (1.0 - sigmoid_gate))
    ).astype(bf16)
    grad_gate_up = jnp.concatenate([grad_gate_low, grad_up_low], 1)
    grad_rows = jnp.dot(grad_gate_up, gate_up_full, preferred_element_type=f32).astype(bf16)
    grad_hidden_two = xor_scatter(jnp.split(grad_rows, n_ex, 0), "expert")
    grad_hidden_two = lax.psum(grad_hidden_two, "tensor")

    expert_out = jnp.dot(scaled_act, down_full, preferred_element_type=f32).astype(bf16)
    combined = xor_scatter(jnp.split(expert_out, n_ex, 0), "expert")
    def expert_grad(low, acts):
        return dotf(low, acts, ((0,), (0,))).astype(bf16)

    grads = [
        expert_grad(scaled_act, upstream_all),
        expert_grad(grad_gate_low, hidden_all),
        expert_grad(grad_up_low, hidden_all),
    ]
    grad_hidden_two, grads = lax.optimization_barrier((grad_hidden_two, grads))
    down_shard, gate_shard, up_shard = (
        dp_scatter(jnp.split(g, n_dp, 1)).reshape(group, hidden, part) for g in grads
    )
    combined, grad_hidden_two = lax.optimization_barrier((combined, grad_hidden_two))
    combined = lax.psum(combined, "tensor")
    output = lane((mixed_rows + combined.astype(f32)).astype(bf16))
    grad_hidden_two = grad_hidden_two.astype(f32)

    def attention_scatter(grad):
        grad = grad.reshape(n_dp, n_ex, width // (n_dp * n_ex), grad.shape[1])
        if n_ex == 2:
            away = lax.dynamic_index_in_dim(grad, 1 - me_ex, 1, keepdims=False)
            own = lax.dynamic_index_in_dim(grad, me_ex, 1, keepdims=False)
            grad = (own.astype(f32) + flip(away, "expert", 1).astype(f32)).astype(bf16)
        else:
            grad = lax.psum_scatter(grad, "expert", scatter_dimension=1, tiled=False)
        return dp_scatter(list(grad))

    upstream = upstream_low.astype(f32)
    experts_gain_grad = jnp.sum(grad_hidden_two * normed_two, axis=0)
    grad_mixed = upstream + norm_back(grad_hidden_two, normed_two, scale_two, gain_experts)
    grad_proj_low = grad_mixed.astype(bf16)
    grad_att_low = (
        jnp.dot(grad_proj_low, full_output, preferred_element_type=f32)
        .astype(bf16)
        .reshape(rows, heads_key, per_group, HEAD_SIZE)
    )
    output_grad = dotf(grad_proj_low, attended_low, ((0,), (0,))).astype(bf16)
    output_shard = attention_scatter(output_grad)
    grad_probs = jnp.einsum("qkgd,skd->kgqs", grad_att_low, value_low, preferred_element_type=f32)
    row_dot = jnp.sum(probs * grad_probs, axis=-1, keepdims=True)
    grad_scores = (probs * (grad_probs - row_dot)).astype(bf16)
    grad_value = jnp.einsum("kgqs,qkgd->skd", prob_low, grad_att_low, preferred_element_type=f32)
    grad_qrot = jnp.einsum(
        "kgqs,skd->qkgd", grad_scores, key_rot, preferred_element_type=f32
    ) * HEAD_SIZE ** (-0.5)
    grad_krot = jnp.einsum(
        "kgqs,qkgd->skd", grad_scores, rotated_query, preferred_element_type=f32
    ) * HEAD_SIZE ** (-0.5)
    grad_qrot = grad_qrot.reshape(rows, heads_query, HEAD_SIZE)
    grad_query_normed = rotate(grad_qrot, cosine_table, -sine_table)
    query_gain_grad = jnp.sum(grad_query_normed * normed_query, axis=(0, 1))
    grad_query_low = (
        norm_back(grad_query_normed, normed_query, scale_query, gain_query)
        .astype(bf16)
        .reshape(rows, q_cols)
    )
    grad_key_normed = rotate(grad_krot, cosine_table, -sine_table)
    key_gain_grad = jnp.sum(grad_key_normed * normed_key, axis=(0, 1))
    grad_key_low = (
        norm_back(grad_key_normed, normed_key, scale_key, gain_key).astype(bf16).reshape(rows, k_cols)
    )
    grad_value_low = grad_value.astype(bf16).reshape(rows, k_cols)
    grad_qkv_low = jnp.concatenate([grad_query_low, grad_key_low, grad_value_low], 1)
    grad_hidden_one = dotf(grad_qkv_low, full_qkv, ((1,), (1,)))
    head_gain_grads = jnp.stack([query_gain_grad, key_gain_grad]).astype(bf16)
    grad_hidden_one, head_gain_grads, _ = lax.optimization_barrier(
        (grad_hidden_one.astype(bf16), head_gain_grads, combined)
    )
    grad_hidden_one, head_gain_grads = lax.psum((grad_hidden_one, head_gain_grads), "tensor")
    grad_hidden_one = grad_hidden_one.astype(f32)
    qkv_grad = dotf(first_hidden, grad_qkv_low, ((0,), (0,))).astype(bf16)
    qkv_shard = attention_scatter(qkv_grad)
    attention_gain_grad = jnp.sum(grad_hidden_one * normed_one, axis=0)
    tokens_grad = grad_mixed + norm_back(grad_hidden_one, normed_one, scale_one, gain_attention)
    tokens_grad = lane(tokens_grad)

    blocks = lambda v: v.reshape(n_dp, n_ex, -1)
    gain_grads = jnp.concatenate(
        [
            blocks(attention_gain_grad),
            blocks(experts_gain_grad),
            lane(blocks(head_gain_grads[0].astype(f32)), 0),
            lane(blocks(head_gain_grads[1].astype(f32)), 0),
        ],
        2,
    )
    gain_grads = lane_order(gain_grads, 1, n_ex, me_ex)
    gain_grads = jnp.pad(gain_grads, ((0, 0), (0, 0), (0, -gain_grads.shape[2] % 128)))
    gain_grads = gain_grads.reshape(n_dp, n_ex, -1, 128)
    gain_grads = xor_scatter([gain_grads[:, k] for k in range(n_ex)], "expert")
    gain_grads = xor_scatter([gain_grads[k] for k in range(n_dp)], "dp").reshape(-1)
    take = lambda start, size: gain_grads[start : start + size]
    return (
        output,
        tokens_grad,
        take(0, na),
        qkv_shard[:, :q_cols],
        qkv_shard[:, q_cols : q_cols + k_cols],
        qkv_shard[:, q_cols + k_cols :],
        output_shard,
        take(2 * na, nq),
        take(2 * na + nq, nq),
        take(na, na),
        gate_shard,
        up_shard,
        down_shard,
    )


CHUNKS = 16
SECOND = (12, 18)


def line_roles(axis):
    p = lax.axis_index(axis)
    return p + 1 - 2 * (p % 2), 3 - p, (p + 1) // 2 == 1


def over(n, f, start=0):
    lax.fori_loop(start, n, lambda c, t: (f(c), t)[1], 0)


def line_sum_steps(x_ref, in_buf, mid_buf, part, out_ref, sems, axis, finish, lag=2):
    a_send, a_recv, b_send, b_recv, c_send, c_recv = sems
    side, mid, inner = line_roles(axis)
    step = x_ref.shape[0] // CHUNKS

    def rows(c):
        return pl.ds(pl.multiple_of(c * step, step), step)

    def copy(src, dst, c, send, recv, to):
        return pltpu.make_async_remote_copy(
            src.at[rows(c)], dst.at[rows(c)], send.at[c], recv.at[c], device_id={axis: to}, device_id_type=MESH
        )

    to_inner = lambda c: copy(x_ref, in_buf, c, a_send, a_recv, side)
    to_middle = lambda c: copy(part, mid_buf, c, b_send, b_recv, mid)
    to_outer = lambda c: copy(out_ref, out_ref, c, c_send, c_recv, side)

    @pl.when(jnp.logical_not(inner))
    def _():
        over(CHUNKS, lambda c: to_inner(c).start())

        def done(c):
            to_outer(c).wait_recv()
            finish(rows(c), c)
            to_inner(c).wait_send()

        over(CHUNKS, done)

    @pl.when(inner)
    def _():
        def first(c):
            to_inner(c).wait_recv()
            r = rows(c)
            part[r] = (x_ref[r].astype(f32) + in_buf[r].astype(f32)).astype(bf16)
            to_middle(c).start()

        def second(c):
            to_middle(c).wait_recv()
            r = rows(c)
            out_ref[r] = (part[r].astype(f32) + mid_buf[r].astype(f32)).astype(bf16)
            to_outer(c).start()
            finish(r, c)

        over(lag, first)
        over(CHUNKS - lag, lambda c: (first(c + lag), second(c))[0])
        over(CHUNKS, second, CHUNKS - lag)

        def done(c):
            to_middle(c).wait_send()
            to_outer(c).wait_send()

        over(CHUNKS, done)


def line_sems():
    return [pltpu.SemaphoreType.DMA((CHUNKS,))] * 6


def plane_partners():
    d, c = lax.axis_index("dp"), lax.axis_index("expert")
    ds = {0: d, 1: d + 1 - 2 * (d % 2), 2: d + 2 - 4 * (d // 2), 3: 3 - d}
    cs = {0: c, 1: 1 - c}
    return {(kd, kc): {"dp": ds[kd], "expert": cs[kc]} for kd in ds for kc in cs}


def lane_copies(src, dst, sems, to):
    wide = src.shape[1] // 4
    places = [to[k, 0]["dp"] for k in range(4)]
    return [
        pltpu.make_async_copy(
            src.at[:, pl.ds(pl.multiple_of(places[k] * wide, wide), wide)], dst.at[:, pl.ds(k * wide, wide)], sems[k]
        )
        for k in range(4)
    ]


def remote(src, dst, send, recv, to):
    return pltpu.make_async_remote_copy(src, dst, send, recv, device_id=to, device_id_type=MESH)


def nt(a, b):
    return lax.dot_general(a, b, (((1,), (1,)), ((), ())), preferred_element_type=f32)


def nn(a, b):
    return lax.dot_general(a, b, (((1,), (0,)), ((), ())), preferred_element_type=f32)


def tn(a, b):
    return lax.dot_general(a, b, (((0,), (0,)), ((), ())), preferred_element_type=f32)


def forward_kernel(
    tokens_in, cot_in, ids, weight, lengths, q_own, k_own, v_own, wo_own, gate_own, up_own, down_own, gains_in, cos, sin,
    tokens_out, cot, table, x2_out, h2_out, att_out, qrot_out, krot_out, value_out, raw_out, probs_out, gains, gate, up,
    down, qkv_out, wo_out,
    tokens, x2, h2, att, qrot, krot, value, raw, probs, save_sem, qkv, wo, h1, proj, in_buf, mid_buf, part, summed, gain_rows, gains_own,
    w_send, w_recv, core_send, core_recv, g_send, g_recv, h_send, h_recv, own_sem, out_sem, r_send, r_recv, t_sem, *line,
):
    c = lax.axis_index("expert")
    to = plane_partners()
    side, mid, inner = line_roles("tensor")
    barrier = pltpu.get_barrier_semaphore()
    others = [k for k in to if k != (0, 0)]
    for k in others:
        pl.semaphore_signal(barrier, inc=1, device_id=to[k], device_id_type=MESH)
    pl.semaphore_signal(barrier, inc=1, device_id={"tensor": side}, device_id_type=MESH)

    @pl.when(inner)
    def _():
        pl.semaphore_signal(barrier, inc=1, device_id={"tensor": mid}, device_id_type=MESH)
        pl.semaphore_wait(barrier, len(others) + 2)

    @pl.when(jnp.logical_not(inner))
    def _():
        pl.semaphore_wait(barrier, len(others) + 1)

    saves = [
        pltpu.make_async_copy(src, dst, save_sem.at[i])
        for i, (src, dst) in enumerate(
            (
                (tokens, tokens_out), (qrot, qrot_out), (krot, krot_out), (value, value_out), (raw, raw_out),
                (probs, probs_out), (att, att_out), (x2, x2_out), (h2, h2_out),
            )
        )
    ]
    rows, width = tokens.shape
    piece = wo_own.shape[0]
    half = piece // 2
    tall = gate_own.shape[0] // 2
    wide = gate_own.shape[1]
    q_cols, k_cols = q_own.shape[1], k_own.shape[1]
    places = [to[k, 0]["dp"] for k in range(4)]

    def lanes(k):
        return pl.ds(pl.multiple_of(places[k] * wide, wide), wide)

    fetch = lane_copies(tokens_in, tokens, [t_sem.at[k] for k in range(4)], to)

    def cot_away(k):
        dst = cot.at[:, pl.ds(k * wide, wide)]
        return remote(cot_in.at[:, lanes(k)], dst, r_send.at[k], r_recv.at[k], to[0, 1])

    def table_away():
        return remote(
            table.at[pl.ds(0, rows)], table.at[pl.ds(rows, rows)], r_send.at[4], r_recv.at[4], to[0, 1]
        )

    def small_slot(full):
        return lambda k, h: full.at[pl.ds(pl.multiple_of((k * 2 + c) * piece + h * half, half), half)]

    early = tall // 3 * 2

    def big_slot(full):
        return lambda k, h: full.at[pl.ds(h * tall, early), pl.ds(k * wide, wide)]

    mats = [
        (lambda h: small_slot(qkv)(0, h), small_slot(qkv)),
        (lambda h: wo_own.at[pl.ds(h * half, half)], small_slot(wo)),
    ] + [
        (lambda h, own=own: own.at[pl.ds(h * tall, early)], big_slot(full))
        for own, full in ((gate_own, gate), (up_own, up), (down_own, down))
    ]

    def move(m, i):
        own, slot = mats[m]
        src, dst, way = (
            (own(0), slot(1, 0), 1), (own(1), slot(2, 1), 2), (own(0), slot(2, 0), 2), (own(1), slot(1, 1), 1),
            (slot(1, 0), slot(3, 0), 2), (slot(2, 1), slot(3, 1), 1),
        )[i]
        return remote(src, dst, w_send.at[m, i], w_recv.at[m, i], to[way, 0])

    def begin(m):
        for i in range(4):
            move(m, i).start()

    def pass_on(m):
        for i in (0, 1):
            move(m, i).wait_recv()
            move(m, 4 + i).start()

    def arrived(m):
        for i in (2, 3, 4, 5):
            move(m, i).wait_recv()

    def core_move(m, k):
        full = (qkv, wo)[m]
        block = full.at[pl.ds(pl.multiple_of((k * 2 + c) * piece, piece), piece)]
        return remote(block, block, core_send.at[m, k], core_recv.at[m, k], to[0, 1])

    def gain_move(j):
        kd, kc = others[j]
        return remote(gains_own, gains.at[kd, c], g_send.at[j], g_recv.at[j], to[kd, kc])

    own_rows = pl.ds(pl.multiple_of(c * piece, piece), piece)
    own_qkv = [
        pltpu.make_async_copy(own, qkv.at[own_rows, pl.ds(col, own.shape[1])], own_sem.at[5 + i])
        for i, (own, col) in enumerate(((q_own, 0), (k_own, q_cols), (v_own, q_cols + k_cols)))
    ]
    own_copies = [
        None,
        pltpu.make_async_copy(wo_own, wo.at[pl.ds(pl.multiple_of(c * piece, piece), piece)], own_sem.at[1]),
    ]

    for x in own_qkv + [own_copies[1]] + fetch:
        x.start()
    for k in range(4):
        cot_away(k).start()
    gains_own[...] = gains_in[...]
    shift = (lax.axis_index("dp") * 2 + c) * (128 // 8)
    gains_own[4:6] = pltpu.roll(gains_in[...], shift, 1)[4:6]
    for x in own_qkv:
        x.wait()
    begin(0)
    for j in range(len(others)):
        gain_move(j).start()
    gains[pl.ds(0, 1), pl.ds(c, 1)] = gains_own[...].reshape(1, 1, 8, 128)
    core_move(0, 0).start()
    expert = lax.broadcasted_iota(jnp.int32, (128, rows), 0)
    routes = jnp.zeros((128, rows), f32)
    for j in range(ids.shape[0]):
        routes += jnp.where(expert == ids[j : j + 1], weight[j : j + 1], 0.0)
    table[0:rows] = routes.T
    table_away().start()
    for k in range(4):
        fetch[k].wait()
    own_copies[1].wait()
    core_move(1, 0).start()
    for j in range(len(others)):
        gain_move(j).wait_recv()
    for kd in range(4):
        for kc in range(2):
            g = gains[kd, kc]
            for j in range(2):
                col = (kd * 2 + kc) * 256 + j * 128
                gain_rows[0:1, col : col + 128] = g[j : j + 1]
                gain_rows[1:2, col : col + 128] = g[2 + j : 3 + j]
    heads = jnp.sum(gains[...].reshape(8, 8, 128), axis=0)
    gain_query, gain_key = heads[4:5], heads[5:6]

    def hidden_one(i):
        r = pl.ds(pl.multiple_of(i * 64, 64), 64)
        x = tokens[r].astype(f32)
        scale = lax.rsqrt(jnp.mean(x * x, axis=-1, keepdims=True) + epsilon)
        h1[r] = (x * scale * gain_rows[0:1]).astype(bf16)

    over(rows // 64, hidden_one)

    pass_on(0)
    begin(1)
    for k, waits in ((1, (3,)), (2, (2,)), (3, (4, 5))):
        for i in waits:
            move(0, i).wait_recv()
        core_move(0, k).start()
    pass_on(1)
    for m in (2, 3, 4):
        begin(m)
    for k in range(4):
        core_move(0, k).wait_recv()
    save_qkv = pltpu.make_async_copy(qkv, qkv_out, out_sem.at[0])
    save_qkv.start()

    def project(j):
        col = pl.ds(pl.multiple_of(j * 256, 256), 256)
        raw[:, col] = nn(h1[...], qkv[:, col])

    over(qkv.shape[1] // 256, project)

    def spin(u):
        return u * cos[...] + pltpu.roll(u, 64, 1) * sin[...]

    def unit(u):
        return u * lax.rsqrt(jnp.mean(u * u, axis=-1, keepdims=True) + epsilon)

    krot[...] = spin(unit(raw[:, pl.ds(q_cols, 128)]) * gain_key).astype(bf16)
    value[...] = raw[:, pl.ds(q_cols + 128, 128)].astype(bf16)
    block = rows // 2
    length = lengths[0]

    def head(h):
        col = pl.ds(pl.multiple_of(h * 128, 128), 128)
        qrot[:, col] = spin(unit(raw[:, col]) * gain_query).astype(bf16)
        for i in range(2):
            r, n = slice(i * block, (i + 1) * block), (i + 1) * block
            s = nt(qrot[r, col], krot[0:n]) * 128 ** (-0.5)
            row = lax.broadcasted_iota(jnp.int32, (block, n), 0) + i * block
            key = lax.broadcasted_iota(jnp.int32, (block, n), 1)
            s = jnp.where((key <= row) & (key < length), s, -1e30)
            e = jnp.exp(s - jnp.max(s, axis=-1, keepdims=True))
            p = (e / jnp.sum(e, axis=-1, keepdims=True)).astype(bf16)
            probs[h, r, 0:n] = p
            att[r, col] = nn(p, value[0:n]).astype(bf16)
        probs[h, 0:block, block:] = jnp.zeros((block, block), bf16)

    over(q_cols // 128, head)
    for x in saves[:7]:
        x.start()
    for k, waits in ((1, (3,)), (2, (2,)), (3, (4, 5))):
        for i in waits:
            move(1, i).wait_recv()
        core_move(1, k).start()
    for k in range(4):
        core_move(1, k).wait_recv()
    save_wo = pltpu.make_async_copy(wo, wo_out, out_sem.at[1])
    save_wo.start()

    def out_project(j):
        r = pl.ds(pl.multiple_of(j * 256, 256), 256)
        proj[:, r] = nt(att[...], wo[r]).astype(bf16)

    over(width // 256, out_project)
    pass_on(2)

    def give(i):
        n = rows // CHUNKS
        src = h2.at[pl.ds(pl.multiple_of(i * n, n), n)]
        dst = h2.at[pl.ds(pl.multiple_of(rows + i * n, n), n)]
        return remote(src, dst, h_send.at[i], h_recv.at[i], to[0, 1])

    def finish(r, i):
        mixed = tokens[r].astype(f32) + summed[r].astype(f32)
        x2[r] = mixed
        scale = lax.rsqrt(jnp.mean(mixed * mixed, axis=-1, keepdims=True) + epsilon)
        h2[r] = (mixed * scale * gain_rows[1:2]).astype(bf16)
        give(i).start()

    line_sum_steps(proj, in_buf, mid_buf, part, summed, line, "tensor", finish)
    pass_on(3)
    pass_on(4)
    saves[7].start()
    over(CHUNKS, lambda i: give(i).wait())
    saves[8].start()
    for m in (2, 3, 4):
        arrived(m)
    save_qkv.wait()
    save_wo.wait()
    for x in saves:
        x.wait()
    for k in range(4):
        cot_away(k).wait()
    table_away().wait()
    for m in range(5):
        for i in range(6):
            move(m, i).wait_send()
    for m in range(2):
        for k in range(4):
            core_move(m, k).wait_send()
    for j in range(len(others)):
        gain_move(j).wait_send()


def forward_call(tokens, cot, ids, weight, lengths, q_own, k_own, v_own, wo_own, gate_own, up_own, down_own, gains, cos, sin):
    rows, width = tokens.shape
    q_cols = q_own.shape[1]
    qkv_cols = q_cols + k_own.shape[1] + v_own.shape[1]
    tall = gate_own.shape[0]
    vmem, anyspace = pl.BlockSpec(memory_space=pltpu.VMEM), pl.BlockSpec(memory_space=pl.ANY)
    shape = jax.ShapeDtypeStruct
    tokens_shape, x2_shape, h2_shape = ((rows, width), bf16), ((rows, width), f32), ((2 * rows, width), bf16)
    att_shape, head_shape = ((rows, q_cols), bf16), ((rows, 128), bf16)
    raw_shape, probs_shape = ((rows, qkv_cols), f32), ((q_cols // 128, rows, rows), bf16)
    kept = [tokens_shape, x2_shape, h2_shape, att_shape, att_shape, head_shape, head_shape, raw_shape, probs_shape]
    outs = [
        (shape(*tokens_shape), anyspace),
        (shape((rows, width), bf16), anyspace),
        (shape((2 * rows, 128), f32), vmem),
        *[(shape(*k), anyspace) for k in kept[1:]],
        (shape((4, 2, 8, 128), f32), vmem),
        *[(shape((tall, width), bf16), anyspace)] * 3,
        (shape((width, qkv_cols), bf16), anyspace),
        (shape((width, q_cols), bf16), anyspace),
    ]
    dma = pltpu.SemaphoreType.DMA
    big = pltpu.VMEM((rows, width), bf16)
    return pl.pallas_call(
        forward_kernel,
        out_shape=[o[0] for o in outs],
        in_specs=[anyspace] * 2
        + [vmem] * 2
        + [pl.BlockSpec(memory_space=pltpu.SMEM)]
        + [anyspace] * 7
        + [vmem] * 3,
        out_specs=[o[1] for o in outs],
        scratch_shapes=[pltpu.VMEM(*k) for k in kept]
        + [
            dma((9,)),
            pltpu.VMEM((width, qkv_cols), bf16),
            pltpu.VMEM((width, q_cols), bf16),
            big, big, big, big, big, big,
            pltpu.VMEM((2, width), f32),
            pltpu.VMEM((8, 128), f32),
            dma((5, 6)), dma((5, 6)), dma((2, 4)), dma((2, 4)), dma((7,)), dma((7,)),
            dma((CHUNKS,)), dma((CHUNKS,)), dma((8,)), dma((2,)), dma((5,)), dma((5,)), dma((4,)),
        ] + line_sems(),
        compiler_params=pltpu.CompilerParams(
            collective_id=1, has_side_effects=True, vmem_limit_bytes=60 * 2**20
        ),
        cost_estimate=pl.CostEstimate(flops=8 * 10**9, bytes_accessed=60 * 10**6, transcendentals=2 * 10**6),
        name="forward_to_experts",
    )(tokens, cot, ids, weight, lengths, q_own, k_own, v_own, wo_own, gate_own, up_own, down_own, gains, cos, sin)


def turn(i):
    return i // 2 + 3 * (i % 2)


def tile(t):
    return pl.ds(pl.multiple_of(t * 256, 256), 256)


def by_half(t, f):
    for first in (1, 2):

        @pl.when(t // 3 == first - 1)
        def _(first=first):
            f(first)


def first_exchange(m, t, j, first, grad, came, send, recv, to, wide):
    return remote(
        grad.at[m, tile(t), pl.ds((3 if j else first) * wide, wide)], came(t, pl.ds(j * wide, wide)), send, recv,
        to[first, 0],
    )


def second_exchange(count, grad_at, came_at, dst_at, load_a, load_b, on_buf, l_sem, s_send, s_recv, to, wide):
    def loads(u, first):
        slot = u % 2
        return (
            pltpu.make_async_copy(grad_at(u, pl.ds((3 - first) * wide, wide)), load_a.at[slot], l_sem.at[slot, 0]),
            pltpu.make_async_copy(came_at(u, pl.ds(wide, wide)), load_b.at[slot], l_sem.at[slot, 1]),
        )

    def pass_on(u, first):
        return remote(on_buf.at[u], dst_at(u), s_send.at[u], s_recv.at[u], to[3 - first, 0])

    def start(u):
        by_half(turn(u % 6), lambda first: [x.start() for x in loads(u, first)])

    def step(u):
        def f(first):
            for x in loads(u, first):
                x.wait()
            on_buf[u] = (load_a[u % 2].astype(f32) + load_b[u % 2].astype(f32)).astype(bf16)
            pass_on(u, first).start()

        by_half(turn(u % 6), f)

        @pl.when(u + 2 < count)
        def _():
            start(u + 2)

    def finish():
        over(count, lambda u: by_half(turn(u % 6), lambda first: pass_on(u, first).wait()))

    return start, step, finish


def expert_kernel(
    h2_in, g_own, g_other, mine_in, gate_own, up_own, down_own, gate_in, up_in, down_in,
    grad_h2, out, out_other, grads, got,
    g, g_sem, h2, mine, gate, up, down, acts, drow, rbuf, in_buf, mid_buf, stage, late_gate, late_up,
    load_sem, rest_sem, w_send, w_recv, x_send, x_recv, s_send, s_recv, keep_sem, out_sem, *line,
):
    to = plane_partners()
    side, mid, inner = line_roles("tensor")
    barrier = pltpu.get_barrier_semaphore()
    near = [(1, 0), (2, 0), (0, 1)]
    for k in near:
        pl.semaphore_signal(barrier, inc=1, device_id=to[k], device_id_type=MESH)
    pl.semaphore_signal(barrier, inc=1, device_id={"tensor": side}, device_id_type=MESH)

    @pl.when(inner)
    def _():
        pl.semaphore_signal(barrier, inc=1, device_id={"tensor": mid}, device_id_type=MESH)
        pl.semaphore_wait(barrier, len(near) + 2)

    @pl.when(jnp.logical_not(inner))
    def _():
        pl.semaphore_wait(barrier, len(near) + 1)

    tall, width = down.shape
    rows = drow.shape[0] // 2
    first_expert = 8 * lax.axis_index("expert")
    wide = width // 4
    units = tall // 8
    late = 4 * 256
    mats = ((gate_own, gate_in, gate), (up_own, up_in, up), (down_own, down_in, down))

    def shard_move(j, n):
        shard, _, full = mats[j]
        own = lambda i: shard.at[tile(turn(i))]
        slot = lambda k, i: full.at[tile(i), pl.ds(k * wide, wide)]
        a, b = 4, 5
        src, dst, way = (
            (own(a), slot(1, a), 1), (own(b), slot(2, b), 2), (own(a), slot(2, a), 2), (own(b), slot(1, b), 1),
            (slot(1, a), slot(3, a), 2), (slot(2, b), slot(3, b), 1),
        )[n]
        return remote(src, dst, w_send.at[j, n], w_recv.at[j, n], to[way, 0])

    for j in range(3):
        for n in range(4):
            shard_move(j, n).start()

    def load_own(i, j):
        return pltpu.make_async_copy(
            mats[j][0].at[tile(turn(i))], mats[j][2].at[tile(i), pl.ds(0, wide)], load_sem.at[i, j]
        )

    def load_rest(i, j):
        cols = pl.ds(wide, 3 * wide)
        return pltpu.make_async_copy(
            mats[j][1].at[tile(turn(i)), cols], mats[j][2].at[tile(i), cols], rest_sem.at[i, j]
        )

    load_g = lane_copies(g_own, g.at[pl.ds(0, rows)], [g_sem.at[k] for k in range(4)], to) + [
        pltpu.make_async_copy(g_other, g.at[pl.ds(rows, rows)], g_sem.at[4]),
        pltpu.make_async_copy(h2_in, h2, g_sem.at[5]),
        pltpu.make_async_copy(mine_in, mine, g_sem.at[6]),
    ]
    for x in load_g:
        x.start()
    over(4, lambda i: [x(i, j).start() for x in (load_own, load_rest) for j in range(3)])
    for i in (4, 5):
        for j in range(3):
            load_own(i, j).start()
    for x in load_g:
        x.wait()

    def gate_up(i):
        return nt(h2[...], gate[tile(i)]), nt(h2[...], up[tile(i)])

    def hidden_tile(i, gate_value, up_value):
        t = turn(i)
        first = (t * 256) // units
        edge = (first + 1) * units - t * 256
        lanes = lax.broadcasted_iota(jnp.int32, mine.shape, 1)
        pick = lambda e: jnp.sum(jnp.where(lanes == e + first_expert, mine[...], 0.0), axis=1, keepdims=True)
        column = lax.broadcasted_iota(jnp.int32, (2 * rows, 256), 1)
        scale = jnp.where(column < edge, pick(first), pick(first + 1))
        grad_act = nt(g[...], down[tile(i)]) * scale
        sig = jax.nn.sigmoid(gate_value)
        silu = gate_value * sig
        acts[0, :, tile(i)] = (silu * up_value * scale).astype(bf16)
        acts[2, :, tile(i)] = (grad_act * silu).astype(bf16)
        acts[1, :, tile(i)] = (grad_act * up_value * sig * (1.0 + gate_value * (1.0 - sig))).astype(bf16)

    early_unit = lambda e: (e // 4, (e % 4) // 2, 1 - e % 2, e)
    last_unit = lambda e: (e // 2, 2, 1 - e % 2, 8 + e)
    up_unit = lambda e: (2, e // 2, 1 - e % 2, 12 + e)

    def keep(unit, ab):
        m, q, s, n = unit
        cols = pl.ds(pl.multiple_of(s * 2 * wide, 2 * wide), 2 * wide)
        return pltpu.make_async_copy(
            stage.at[n % 2, pl.ds(ab * 256, 256)], grads.at[m, tile(q + 3 * ab), cols], keep_sem.at[n % 2, ab]
        )

    def send(m, t, j, first):
        came = lambda t, cols: got.at[m, tile(t), cols]
        return first_exchange(m, t, j, first, grads, came, s_send.at[m, t, j], s_recv.at[m, t, j], to, wide)

    def flush(unit, goes=True):
        m, q, s, n = unit
        for ab in range(2):
            keep(unit, ab).wait()

        @pl.when(goes & (s == 1))
        def _():
            send(m, q, 1, 1).start()
            send(m, q + 3, 0, 2).start()
            send(m, q + 3, 1, 2).start()

        @pl.when(goes & (s == 0))
        def _():
            send(m, q, 0, 1).start()

    def grad_unit(unit, rhs):
        m, q, s, n = unit
        low = acts[m, :, pl.ds(pl.multiple_of(q * 512, 512), 512)]
        for b in range(2):
            cols = pl.ds(pl.multiple_of((2 * s + b) * wide, wide), wide)
            stage[n % 2, :, b * wide : (b + 1) * wide] = tn(low, rhs[:, cols]).astype(bf16)
        for ab in range(2):
            keep(unit, ab).start()

    def early_grads(rhs):
        def one(e):
            grad_unit(early_unit(e), rhs)

            @pl.when(e > 0)
            def _():
                flush(early_unit(e - 1))

        return one

    def early_tile(i):
        for x in (load_own, load_rest):
            for j in range(3):
                x(i, j).wait()
        hidden_tile(i, *gate_up(i))

    over(4, early_tile)

    def early_rows(j):
        col = pl.ds(pl.multiple_of(j * 256, 256), 256)
        drow[:, col] = (nn(acts[1, :, 0:late], gate[0:late, col]) + nn(acts[2, :, 0:late], up[0:late, col])).astype(bf16)

    over(width // 256, early_rows)
    over(2, early_grads(g))
    for j in range(3):
        for n in (0, 1):
            shard_move(j, n).wait_recv()
            shard_move(j, 4 + n).start()
    over(4, early_grads(g), 2)
    over(8, early_grads(h2), 4)
    flush(early_unit(7))
    for i in (4, 5):
        for j in range(3):
            load_own(i, j).wait()
    for j in (0, 1):
        for n in (2, 3, 4, 5):
            shard_move(j, n).wait_recv()

    def late_gate_up(i):
        late_gate[i - 4], late_up[i - 4] = gate_up(i)

    over(6, late_gate_up, 4)
    for n in (2, 3, 4, 5):
        shard_move(2, n).wait_recv()
    over(6, lambda i: hidden_tile(i, late_gate[i - 4], late_up[i - 4]), 4)

    step = rows // CHUNKS

    def give(i):
        src = drow.at[pl.ds(pl.multiple_of(rows + i * step, step), step)]
        dst = rbuf.at[pl.ds(pl.multiple_of(i * step, step), step)]
        return remote(src, dst, x_send.at[i], x_recv.at[i], to[0, 1])

    for some in (slice(rows, 2 * rows), slice(0, rows)):

        def late_rows(j, some=some):
            col = pl.ds(pl.multiple_of(j * 256, 256), 256)
            more = nn(acts[1, some, late:], gate[late:, col]) + nn(acts[2, some, late:], up[late:, col])
            drow[some, col] = (drow[some, col].astype(f32) + more).astype(bf16)

        over(width // 256, late_rows)
        if some.start:
            over(CHUNKS, lambda i: give(i).start())

    def add_other(c):
        give(c).wait_recv()
        r = pl.ds(pl.multiple_of(c * step, step), step)
        drow[r] = (drow[r].astype(f32) + rbuf[r].astype(f32)).astype(bf16)

    def out_copies(j):
        col = pl.ds(pl.multiple_of(j * 256, 256), 256)
        return (
            pltpu.make_async_copy(gate.at[pl.ds(0, rows), col], out.at[:, col], out_sem.at[0, j]),
            remote(
                gate.at[pl.ds(rows, rows), col], out_other.at[:, col], out_sem.at[1, j], out_sem.at[2, j], to[0, 1]
            ),
        )

    def work(i):
        @pl.when(i < 2)
        def _():
            grad_unit(last_unit(i), g)

        @pl.when((i >= 2) & (i < 4))
        def _():
            grad_unit(last_unit(i), h2)

        @pl.when((i >= 4) & (i < 10))
        def _():
            grad_unit(up_unit(i - 4), h2)

        @pl.when((i >= 1) & (i < 5))
        def _():
            flush(last_unit(i - 1))

        @pl.when((i >= 5) & (i < 11))
        def _():
            flush(up_unit(i - 5), i < 7)

        @pl.when(i >= 10)
        def _():
            j = i - 10
            col = pl.ds(pl.multiple_of(j * 256, 256), 256)
            gate[0 : 2 * rows, col] = nn(acts[0], down[:, col]).astype(bf16)
            for x in out_copies(j):
                x.start()

    line_sum_work(
        drow, in_buf, mid_buf, drow, grad_h2, line, "tensor", rows, add_other, lambda r, c: None, work,
        10 + width // 256,
    )
    over(width // 256, lambda j: [x.wait() for x in out_copies(j)])
    over(CHUNKS, lambda i: give(i).wait_send())
    for j in range(3):
        for n in range(6):
            shard_move(j, n).wait_send()
    for m, t in [(m, t) for m in range(2) for t in range(6)] + [(2, 0), (2, 3)]:
        for j in range(2):
            send(m, t, j, 1 + t // 3).wait()


def line_sum_work(x_ref, in_buf, mid_buf, part, out_ref, sems, axis, n_rows, ready, finish, work, n_work):
    a_send, a_recv, b_send, b_recv, c_send, c_recv = sems
    side, mid, inner = line_roles(axis)
    step = n_rows // CHUNKS
    steps = max(n_work, CHUNKS + 4)

    def rows(c):
        return pl.ds(pl.multiple_of(c * step, step), step)

    def copy(src, dst, c, send, recv, to):
        return pltpu.make_async_remote_copy(
            src.at[rows(c)], dst.at[rows(c)], send.at[c], recv.at[c], device_id={axis: to}, device_id_type=MESH
        )

    to_inner = lambda c: copy(x_ref, in_buf, c, a_send, a_recv, side)
    to_middle = lambda c: copy(part, mid_buf, c, b_send, b_recv, mid)
    to_outer = lambda c: copy(out_ref, out_ref, c, c_send, c_recv, side)

    @pl.when(jnp.logical_not(inner))
    def _():
        def begin(c):
            ready(c)
            to_inner(c).start()

        over(CHUNKS, begin)

        def one(i):
            @pl.when((i >= 4) & (i < CHUNKS + 4))
            def _():
                to_outer(i - 4).wait_recv()
                finish(rows(i - 4), i - 4)

            @pl.when(i < n_work)
            def _():
                work(i)

        over(steps, one)
        over(CHUNKS, lambda c: to_inner(c).wait_send())

    @pl.when(inner)
    def _():
        def first(c):
            ready(c)
            to_inner(c).wait_recv()
            r = rows(c)
            part[r] = (x_ref[r].astype(f32) + in_buf[r].astype(f32)).astype(bf16)
            to_middle(c).start()

        def second(c):
            to_middle(c).wait_recv()
            r = rows(c)
            out_ref[r] = (part[r].astype(f32) + mid_buf[r].astype(f32)).astype(bf16)
            to_outer(c).start()
            finish(r, c)

        def one(i):
            @pl.when(i < CHUNKS)
            def _():
                first(i)

            @pl.when((i >= 2) & (i < CHUNKS + 2))
            def _():
                second(i - 2)

            @pl.when(i < n_work)
            def _():
                work(i)

        over(steps, one)

        def done(c):
            to_middle(c).wait_send()
            to_outer(c).wait_send()

        over(CHUNKS, done)


def expert_call(h2, g_own, g_other, mine, gate_own, up_own, down_own, gate, up, down):
    tall, width = down.shape
    rows = h2.shape[0] // 2
    vmem, anyspace = pl.BlockSpec(memory_space=pltpu.VMEM), pl.BlockSpec(memory_space=pl.ANY)
    shape = jax.ShapeDtypeStruct
    dma = pltpu.SemaphoreType.DMA
    return pl.pallas_call(
        expert_kernel,
        out_shape=[
            shape((rows, width), bf16),
            shape((rows, width), bf16),
            shape((rows, width), bf16),
            shape((3, tall, width), bf16),
            shape((3, tall, width // 2), bf16),
        ],
        in_specs=[anyspace] * 10,
        out_specs=[vmem, anyspace, anyspace, anyspace, anyspace],
        scratch_shapes=[
            pltpu.VMEM((2 * rows, width), bf16),
            dma((7,)),
            pltpu.VMEM((2 * rows, width), bf16),
            pltpu.VMEM(mine.shape, f32),
        ]
        + [pltpu.VMEM((tall, width), bf16)] * 3
        + [
            pltpu.VMEM((3, 2 * rows, tall), bf16),
            pltpu.VMEM((2 * rows, width), bf16),
            pltpu.VMEM((rows, width), bf16),
            pltpu.VMEM((rows, width), bf16),
            pltpu.VMEM((rows, width), bf16),
            pltpu.VMEM((2, 512, width // 2), bf16),
            pltpu.VMEM((2, 2 * rows, 256), f32),
            pltpu.VMEM((2, 2 * rows, 256), f32),
            dma((6, 3)), dma((4, 3)), dma((3, 6)), dma((3, 6)), dma((CHUNKS,)), dma((CHUNKS,)), dma((3, 6, 2)), dma((3, 6, 2)),
            dma((2, 2)), dma((3, width // 256)),
        ]
        + line_sems(),
        compiler_params=pltpu.CompilerParams(
            collective_id=2, has_side_effects=True, vmem_limit_bytes=62 * 2**20
        ),
        cost_estimate=pl.CostEstimate(flops=58 * 10**9, bytes_accessed=60 * 10**6, transcendentals=2 * 10**6),
        name="experts",
    )(h2, g_own, g_other, mine, gate_own, up_own, down_own, gate, up, down)


def plane_barrier(to, z_others):
    barrier = pltpu.get_barrier_semaphore()
    others = [k for k in to if k != (0, 0)]
    for k in others:
        pl.semaphore_signal(barrier, inc=1, device_id=to[k], device_id_type=MESH)
    for z in z_others:
        pl.semaphore_signal(barrier, inc=1, device_id={"tensor": z}, device_id_type=MESH)
    pl.semaphore_wait(barrier, len(others) + len(z_others))
    return others


def z_partners():
    p = lax.axis_index("tensor")
    return [p + 1 - 2 * (p % 2), p + 2 - 4 * (p // 2), 3 - p]


def gain_vectors(gains, gain_rows):
    for kd in range(4):
        for kc in range(2):
            g = gains[kd, kc]
            for j in range(2):
                col = (kd * 2 + kc) * 256 + j * 128
                gain_rows[0:1, col : col + 128] = g[j : j + 1]
                gain_rows[1:2, col : col + 128] = g[2 + j : 3 + j]
    heads = jnp.sum(gains[...].reshape(8, 8, 128), axis=0)
    return heads[4:5], heads[5:6]


def attention_back_kernel(
    gains, cos, sin, grad_h2_in, x2_in, cot_in, qrot_in, krot_in, value_in, raw_in, probs, wo_in, qkv_in, out_own, out_other,
    grads, _,
    output, dx2_out, low_out, grad_qkv, grad_h1, gain_grads, got2, got,
    grad_h2, x2, cot, qrot, krot, value, raw, f_sem, dx2, low, wo, qkv, own_out, rbuf, in_buf, mid_buf, summed, datt, pbuf, dk, dv, gain_rows, load_a, load_b, on_buf,
    w_sem, p_sem, l_sem, s_send, s_recv, u_send, u_recv, *line,
):
    to = plane_partners()
    fetch = [
        pltpu.make_async_copy(src, dst, f_sem.at[i])
        for i, (src, dst) in enumerate(
            ((x2_in, x2), (grad_h2_in, grad_h2), (qrot_in, qrot), (krot_in, krot), (value_in, value), (raw_in, raw))
        )
    ]
    early = fetch[:2] + lane_copies(cot_in, cot, [f_sem.at[6 + k] for k in range(4)], to)
    plane_barrier(to, z_partners())
    places = [to[k, 0]["dp"] for k in range(4)]
    rows, width = x2.shape
    wide = width // 4
    q_cols = qrot.shape[1]
    n_heads = q_cols // 128
    step = rows // CHUNKS
    rate = 128 ** (-0.5)

    weights = [
        pltpu.make_async_copy(wo_in, wo, w_sem.at[0]),
        pltpu.make_async_copy(qkv_in, qkv, w_sem.at[1]),
        pltpu.make_async_copy(out_own, own_out, w_sem.at[2]),
        pltpu.make_async_copy(out_other, rbuf, w_sem.at[3]),
    ]
    flushes = [
        pltpu.make_async_copy(dx2, dx2_out, w_sem.at[4]),
        pltpu.make_async_copy(low, low_out, w_sem.at[5]),
    ]
    for w in weights[2:] + early + [weights[0]] + fetch[2:] + [weights[1]]:
        w.start()

    def load_probs(h):
        return pltpu.make_async_copy(probs.at[h], pbuf.at[h % 2], p_sem.at[h % 2])

    def up_move(t, j, first):
        came = lambda t, cols: got.at[2, tile(t), cols]
        return first_exchange(2, t, j, first, grads, came, u_send.at[t, j], u_recv.at[t, j], to, wide)

    def up_moves(i, f):
        t = turn(i)
        by_half(t, lambda first: [f(up_move(t, j, first)) for j in range(2)])

    over(6, lambda i: up_moves(i, lambda x: x.start()), 2)
    at = lambda ref: lambda u, cols=pl.ds(0, wide): ref.at[u // 6, tile(turn(u % 6)), cols]
    start, second_tile, second_done = second_exchange(
        12, at(grads), at(got), at(got2), load_a, load_b, on_buf, l_sem, s_send, s_recv, to, wide
    )
    start(0)
    start(1)
    load_probs(0).start()
    gain_query, gain_key = gain_vectors(gains, gain_rows)
    gain_grads[...] = jnp.zeros_like(gain_grads)
    dk[...] = jnp.zeros_like(dk)
    dv[...] = jnp.zeros_like(dv)

    def mixed_rows(i):
        r = pl.ds(pl.multiple_of(i * 64, 64), 64)
        x = x2[r]
        scale = lax.rsqrt(jnp.mean(x * x, axis=-1, keepdims=True) + epsilon)
        normed = x * scale
        grad = grad_h2[r].astype(f32)
        gain_grads[0:1, :] += jnp.sum(grad * normed, axis=0, keepdims=True)
        n = grad * gain_rows[1:2]
        d = cot[r].astype(f32) + scale * (n - normed * jnp.mean(n * normed, axis=-1, keepdims=True))
        dx2[r] = d
        low[r] = d.astype(bf16)

    def att_grads(j):
        col = pl.ds(pl.multiple_of(j * 256, 256), 256)
        datt[:, col] = nn(low[...], wo[:, col]).astype(bf16)

    def unspin(u):
        return u * cos[...] - pltpu.roll(u, 64, 1) * sin[...]

    def norm_grads(x, rotated, gain, row):
        scale = lax.rsqrt(jnp.mean(x * x, axis=-1, keepdims=True) + epsilon)
        normed = x * scale
        du = unspin(rotated)
        gain_grads[row : row + 1, 0:128] += jnp.sum(du * normed, axis=0, keepdims=True)
        n = du * gain
        return (scale * (n - normed * jnp.mean(n * normed, axis=-1, keepdims=True))).astype(bf16)

    block = rows // 2

    def head(h):
        load_probs(h).wait()

        @pl.when(h + 1 < n_heads)
        def _():
            load_probs(h + 1).start()

        col = pl.ds(pl.multiple_of(h * 128, 128), 128)
        dq = []
        for i in range(2):
            r, n = slice(i * block, (i + 1) * block), (i + 1) * block
            p_low = pbuf[h % 2, r, 0:n]
            p = p_low.astype(f32)
            dp = nt(datt[r, col], value[0:n])
            ds = (p * (dp - jnp.sum(p * dp, axis=-1, keepdims=True))).astype(bf16)
            dq.append(nn(ds, krot[0:n]) * rate)
            dk[0:n] += tn(ds, qrot[r, col])
            dv[0:n] += tn(p_low, datt[r, col])
        grad_qkv[:, col] = norm_grads(raw[:, col], jnp.concatenate(dq, 0), gain_query, 1)

    def key_value():
        grad_qkv[:, pl.ds(q_cols, 128)] = norm_grads(raw[:, pl.ds(q_cols, 128)], dk[...] * rate, gain_key, 2)
        grad_qkv[:, pl.ds(q_cols + 128, 128)] = dv[...].astype(bf16)

    def input_grads(j):
        r = pl.ds(pl.multiple_of(j * 256, 256), 256)
        grad_h1[:, r] = nt(grad_qkv[...], qkv[r]).astype(bf16)

    def work(i):
        @pl.when(i < 12)
        def _():
            second_tile(i)

        @pl.when(i == 0)
        def _():
            for x in early:
                x.wait()

        @pl.when(i < 4)
        def _():
            mixed_rows(2 * i)
            mixed_rows(2 * i + 1)

        @pl.when(i == 4)
        def _():
            weights[0].wait()
            for x in flushes:
                x.start()
            for x in fetch[2:]:
                x.wait()

        @pl.when((i >= 4) & (i < 6))
        def _():
            att_grads(2 * (i - 4))
            att_grads(2 * (i - 4) + 1)

        @pl.when((i >= 6) & (i < 6 + n_heads))
        def _():
            head(i - 6)

        @pl.when(i == 6 + n_heads)
        def _():
            key_value()
            weights[1].wait()

        @pl.when((i > 6 + n_heads) & (i <= 10 + n_heads))
        def _():
            j = 2 * (i - 7 - n_heads)
            input_grads(j)
            input_grads(j + 1)

    def ready(c):
        @pl.when(c == 0)
        def _():
            weights[2].wait()
            weights[3].wait()

        r = pl.ds(pl.multiple_of(c * step, step), step)
        own_out[r] = (own_out[r].astype(f32) + rbuf[r].astype(f32)).astype(bf16)

    def finish(r, c):
        done = (x2[r] + summed[r].astype(f32)).astype(bf16)
        for k in range(4):
            output[r, pl.ds(pl.multiple_of(places[k] * wide, wide), wide)] = done[:, k * wide : (k + 1) * wide]

    line_sum_work(
        own_out, in_buf, mid_buf, own_out, summed, line, "tensor", rows, ready, finish, work, 11 + n_heads
    )
    for x in flushes:
        x.wait()
    second_done()
    over(6, lambda i: up_moves(i, lambda x: x.wait()), 2)


def attention_back_call(grad_h2, x2, cot, qrot, krot, value, raw, gains, cos, sin, probs, wo, qkv, out_own, out_other, grads, got):
    rows, width = x2.shape
    q_cols, qkv_cols = wo.shape[1], qkv.shape[1]
    tall = grads.shape[1]
    wide = width // 4
    vmem, anyspace = pl.BlockSpec(memory_space=pltpu.VMEM), pl.BlockSpec(memory_space=pl.ANY)
    shape = jax.ShapeDtypeStruct
    dma = pltpu.SemaphoreType.DMA
    big = pltpu.VMEM((rows, width), bf16)
    return pl.pallas_call(
        attention_back_kernel,
        out_shape=[
            shape((rows, width), bf16),
            shape((rows, width), f32),
            shape((rows, width), bf16),
            shape((rows, qkv_cols), bf16),
            shape((rows, width), bf16),
            shape((8, width), f32),
            shape((2, tall, wide), bf16),
            shape(got.shape, bf16),
        ],
        in_specs=[vmem] * 3 + [anyspace] * 14,
        out_specs=[vmem, anyspace, anyspace] + [vmem] * 3 + [anyspace] * 2,
        scratch_shapes=[
            big,
            pltpu.VMEM((rows, width), f32),
            big,
            pltpu.VMEM((rows, q_cols), bf16),
            pltpu.VMEM((rows, 128), bf16),
            pltpu.VMEM((rows, 128), bf16),
            pltpu.VMEM((rows, qkv_cols), f32),
            dma((10,)),
            pltpu.VMEM((rows, width), f32),
            big,
            pltpu.VMEM((width, q_cols), bf16),
            pltpu.VMEM((width, qkv_cols), bf16),
            big, big, big, big, big,
            pltpu.VMEM((rows, q_cols), bf16),
            pltpu.VMEM((2, rows, rows), bf16),
            pltpu.VMEM((rows, 128), f32),
            pltpu.VMEM((rows, 128), f32),
            pltpu.VMEM((2, width), f32),
            pltpu.VMEM((2, 256, wide), bf16),
            pltpu.VMEM((2, 256, wide), bf16),
            pltpu.VMEM((12, 256, wide), bf16),
            dma((6,)), dma((2,)), dma((2, 2)), dma((12,)), dma((12,)),
            dma((6, 2)), dma((6, 2)),
        ]
        + line_sems(),
        input_output_aliases={16: 7},
        compiler_params=pltpu.CompilerParams(
            collective_id=3, has_side_effects=True, vmem_limit_bytes=62 * 2**20
        ),
        cost_estimate=pl.CostEstimate(flops=9 * 10**9, bytes_accessed=60 * 10**6, transcendentals=10**5),
        name="attention_backward",
    )(gains, cos, sin, grad_h2, x2, cot, qrot, krot, value, raw, probs, wo, qkv, out_own, out_other, grads, got)


def last_kernel(
    gains, gain_grads, part_in, dx2_in, tokens_in, grad_qkv_in, low_in, att_in, grads, got, got2,
    tokens_grad_out, q_shard, k_shard, v_shard, wo_shard, gain_sum, got2_up, down_shard, gate_shard,
    f_in, f_out, fi_sem, fo_sem, tokens_grad, d_sem, part, dx2, tokens, grad_qkv, low, att, f_sem, h1, in_buf, mid_buf, half_sum, summed, gain_rows, wo_all, qkv_all, wo_core, qkv_core, wo_one, qkv_one, wo_two, qkv_two,
    ga, z_got, g_out, g_got, load_a, load_b, on_buf, l_sem, s_send, s_recv,
    z_send, z_recv, c_send, c_recv, f_send, f_recv, t_send, t_recv, g_send, g_recv, *line,
):
    fetch = [
        pltpu.make_async_copy(src, dst, f_sem.at[i])
        for i, (src, dst) in enumerate(
            (
                (part_in, part), (tokens_in, tokens), (low_in, low), (att_in, att), (grad_qkv_in, grad_qkv),
                (dx2_in, dx2),
            )
        )
    ]
    for x in fetch:
        x.start()
    c = lax.axis_index("expert")
    to = plane_partners()
    zs = z_partners()
    others = plane_barrier(to, zs)
    places = [to[k, 0]["dp"] for k in range(4)]
    rows, width = tokens.shape
    wide = width // 4
    piece = wide // 2
    half = piece // 2

    def z_move(j):
        return remote(gain_grads.at[pl.ds(0, 8), pl.ds(0, 128)], z_got.at[j], z_send.at[j], z_recv.at[j], {"tensor": zs[j]})

    for j in range(3):
        z_move(j).start()
    up_at = lambda ref: lambda u, cols: ref.at[2, tile(turn(u)), cols]
    start, second_tile, second_done = second_exchange(
        6, up_at(grads), up_at(got), lambda u: got2_up.at[tile(turn(u))],
        load_a, load_b, on_buf, l_sem, s_send, s_recv, to, wide,
    )
    start(0)
    start(1)

    def final_loads(u):
        at = (u // 6, tile(u % 6), pl.ds(0, wide))
        return [
            pltpu.make_async_copy(src.at[at], f_in.at[u % 2, j], fi_sem.at[u % 2, j])
            for j, src in enumerate((grads, got, got2))
        ]

    def final_out(u, f):
        for m, shard in enumerate((down_shard, gate_shard)):

            @pl.when(u // 6 == m)
            def _(shard=shard):
                f(pltpu.make_async_copy(f_out.at[u % 2], shard.at[tile(u % 6)], fo_sem.at[u % 2]))

    def final_tile(u):
        for x in final_loads(u):
            x.wait()

        @pl.when(u >= 2)
        def _():
            final_out(u - 2, lambda x: x.wait())

        a, b, c = (f_in[u % 2, j].astype(f32) for j in range(3))
        f_out[u % 2] = a + b + c
        final_out(u, lambda x: x.start())

        @pl.when(u + 2 < 12)
        def _():
            for x in final_loads(u + 2):
                x.start()

    for u in range(2):
        for x in final_loads(u):
            x.start()
    gain_vectors(gains, gain_rows)
    ga[...] = jnp.zeros_like(ga)

    def unit_rows(r):
        x = tokens[r].astype(f32)
        scale = lax.rsqrt(jnp.mean(x * x, axis=-1, keepdims=True) + epsilon)
        return x * scale, scale

    def hidden_one(i):
        r = pl.ds(pl.multiple_of(i * 64, 64), 64)
        h1[r] = (unit_rows(r)[0] * gain_rows[0:1]).astype(bf16)

    mats = [
        (low, att, wo_all, wo_core, wo_one, wo_two),
        (h1, grad_qkv, qkv_all, qkv_core, qkv_one, qkv_two),
    ]

    def block(k, core):
        return pl.ds(pl.multiple_of((k * 2 + core) * piece, piece), piece)

    def core_move(m, k):
        return remote(mats[m][2].at[block(k, 1 - c)], mats[m][3].at[k], c_send.at[m, k], c_recv.at[m, k], to[0, 1])

    def product(m, k, core):
        left, right, full = mats[m][:3]
        full[block(k, core)] = tn(left[:, block(k, core)], right[...]).astype(bf16)

    def away(m, k):
        product(m, k, 1 - c)
        core_move(m, k).start()

    def home(m, k):
        product(m, k, c)
        full, came = mats[m][2:4]
        core_move(m, k).wait_recv()
        full[block(k, c)] = (full[block(k, c)].astype(f32) + came[k].astype(f32)).astype(bf16)

    def slot(m, k, h):
        return mats[m][2].at[pl.ds(pl.multiple_of((k * 2 + c) * piece + h * half, half), half)]

    def first_move(m, h, j):
        way = 1 + h
        src = slot(m, 3 if j else way, h)
        return remote(src, mats[m][4].at[h, j], f_send.at[m, h, j], f_recv.at[m, h, j], to[way, 0])

    def second_move(m, h):
        return remote(slot(m, 2 - h, h), mats[m][5].at[h], t_send.at[m, h], t_recv.at[m, h], to[2 - h, 0])

    def add_first(m, h, j, k):
        full, one = mats[m][2], mats[m][4]
        r = pl.ds(pl.multiple_of((k * 2 + c) * piece + h * half, half), half)
        first_move(m, h, j).wait_recv()
        full[r] = (full[r].astype(f32) + one[h, j].astype(f32)).astype(bf16)

    def work(i):
        @pl.when(i == 0)
        def _():
            for x in fetch[1:]:
                x.wait()
            over(rows // 64, hidden_one)

        @pl.when(i >= 8)
        def _():
            final_tile(i - 8)

        @pl.when(i < 6)
        def _():
            second_tile(i)

        for m in range(2):
            for n, ks in enumerate(((3, 1), (2, 0))):

                @pl.when(i == 1 + 4 * m + n)
                def _(m=m, ks=ks):
                    for k in ks:
                        away(m, k)

                @pl.when(i == 3 + 4 * m + n)
                def _(m=m, n=n, ks=ks):
                    for k in ks:
                        home(m, k)
                    for j in range(2):
                        first_move(m, n, j).start()

            @pl.when(i == SECOND[m])
            def _(m=m):
                for h in range(2):
                    add_first(m, h, 1, 2 - h)
                    second_move(m, h).start()

    def give_back(i):
        r = pl.ds(pl.multiple_of(i * (rows // CHUNKS), rows // CHUNKS), rows // CHUNKS)
        return pltpu.make_async_copy(tokens_grad.at[r], tokens_grad_out.at[r], d_sem.at[i])

    def finish(r, i):
        grad = summed[r].astype(f32)
        normed, scale = unit_rows(r)
        ga[0:1, :] += jnp.sum(grad * normed, axis=0, keepdims=True)
        n = grad * gain_rows[0:1]
        d = dx2[r] + scale * (n - normed * jnp.mean(n * normed, axis=-1, keepdims=True))
        for k in range(4):
            tokens_grad[r, pl.ds(pl.multiple_of(places[k] * wide, wide), wide)] = d[:, k * wide : (k + 1) * wide]
        give_back(i).start()

    fetch[0].wait()
    line_sum_work(part, in_buf, mid_buf, half_sum, summed, line, "tensor", rows, lambda k: None, finish, work, 20)

    head_rows = gain_grads[1:3, 0:128]
    for j in range(3):
        z_move(j).wait()
        head_rows += z_got[j, 1:3]
    for kd in range(4):
        for kc in range(2):
            for j in range(2):
                col = slice((kd * 2 + kc) * piece + j * 128, (kd * 2 + kc) * piece + (j + 1) * 128)
                g_out[kd, kc, j : j + 1] = ga[0:1, col]
                g_out[kd, kc, 2 + j : 3 + j] = gain_grads[0:1, col]
            g_out[kd, kc, 4:6] = head_rows

    def gain_move(j):
        kd, kc = others[j]
        core = c if kc == 0 else 1 - c
        return remote(g_out.at[kd, core], g_got.at[j], g_send.at[j], g_recv.at[j], to[kd, kc])

    for j in range(len(others)):
        gain_move(j).start()
    q_cols, k_cols = q_shard.shape[1], k_shard.shape[1]
    shards = (
        ((wo_shard, 0),),
        ((q_shard, 0), (k_shard, q_cols), (v_shard, q_cols + k_cols)),
    )
    for m in range(2):
        full, two = mats[m][2], mats[m][5]
        for h in range(2):
            add_first(m, h, 0, 0)
            second_move(m, h).wait_recv()
            r = pl.ds(pl.multiple_of(c * piece + h * half, half), half)
            for shard, col in shards[m]:
                cols = pl.ds(col, shard.shape[1])
                shard[h * half : (h + 1) * half] = full[r, cols].astype(f32) + two[h, :, cols].astype(f32)
    total = g_out[0, pl.ds(c, 1)].reshape(8, 128)
    for j in range(len(others)):
        gain_move(j).wait_recv()
        total += g_got[j]
    gain_sum[...] = total
    second_done()
    over(12, lambda u: final_out(u, lambda x: x.wait()), 10)
    over(CHUNKS, lambda i: give_back(i).wait())
    for m in range(2):
        for k in range(4):
            core_move(m, k).wait_send()
        for h in range(2):
            for j in range(2):
                first_move(m, h, j).wait_send()
            second_move(m, h).wait_send()
    for j in range(len(others)):
        gain_move(j).wait_send()


def last_call(part, dx2, tokens, grad_qkv, low, att, gains, gain_grads, grads, got, got2):
    rows, width = tokens.shape
    q_cols, qkv_cols = att.shape[1], grad_qkv.shape[1]
    piece = width // 8
    vmem = pl.BlockSpec(memory_space=pltpu.VMEM)
    shape = jax.ShapeDtypeStruct
    dma = pltpu.SemaphoreType.DMA
    big = pltpu.VMEM((rows, width), bf16)
    both = lambda *lead: [pltpu.VMEM(lead + (n,), bf16) for n in (q_cols, qkv_cols)]
    return pl.pallas_call(
        last_kernel,
        out_shape=[
            shape((rows, width), f32),
            shape((piece, q_cols), f32),
            shape((piece, (qkv_cols - q_cols) // 2), f32),
            shape((piece, (qkv_cols - q_cols) // 2), f32),
            shape((piece, q_cols), f32),
            shape((8, 128), f32),
            shape((got.shape[1], width // 4), bf16),
            shape((got.shape[1], width // 4), f32),
            shape((got.shape[1], width // 4), f32),
        ],
        in_specs=[vmem] * 2 + [pl.BlockSpec(memory_space=pl.ANY)] * 9,
        out_specs=[pl.BlockSpec(memory_space=pl.ANY)] + [vmem] * 5 + [pl.BlockSpec(memory_space=pl.ANY)] * 3,
        scratch_shapes=[
            pltpu.VMEM((2, 3, 256, width // 4), bf16),
            pltpu.VMEM((2, 256, width // 4), f32),
            dma((2, 3)),
            dma((2,)),
            pltpu.VMEM((rows, width), f32),
            dma((CHUNKS,)),
            big,
            pltpu.VMEM((rows, width), f32),
            big,
            pltpu.VMEM((rows, qkv_cols), bf16),
            big,
            pltpu.VMEM((rows, q_cols), bf16),
            dma((6,)),
        ]
        + [big, big, big, big, big, pltpu.VMEM((2, width), f32)]
        + both(width)
        + both(4, piece)
        + both(2, 2, piece // 2)
        + both(2, piece // 2)
        + [
            pltpu.VMEM((8, width), f32),
            pltpu.VMEM((3, 8, 128), f32),
            pltpu.VMEM((4, 2, 8, 128), f32),
            pltpu.VMEM((7, 8, 128), f32),
            pltpu.VMEM((2, 256, width // 4), bf16),
            pltpu.VMEM((2, 256, width // 4), bf16),
            pltpu.VMEM((6, 256, width // 4), bf16),
            dma((2, 2)), dma((6,)), dma((6,)),
            dma((3,)), dma((3,)), dma((2, 4)), dma((2, 4)), dma((2, 2, 2)), dma((2, 2, 2)), dma((2, 2)), dma((2, 2)),
            dma((7,)), dma((7,)),
        ]
        + line_sems(),
        compiler_params=pltpu.CompilerParams(
            collective_id=4, has_side_effects=True, vmem_limit_bytes=62 * 2**20
        ),
        cost_estimate=pl.CostEstimate(flops=5 * 10**9, bytes_accessed=40 * 10**6, transcendentals=10**5),
        name="input_gradients",
    )(gains, gain_grads, part, dx2, tokens, grad_qkv, low, att, grads, got, got2)


def local_fast(
    tokens,
    cotangent,
    route_ids,
    route_weight,
    lengths,
    attention_norm,
    query_weight,
    key_matrix,
    value_matrix,
    output_weight,
    query_norm,
    key_norm,
    experts_norm,
    gate_weight,
    up_weight,
    down_weight,
):
    n_dp = lax.axis_size("dp")
    n_ex = lax.axis_size("expert")
    me_dp = lax.axis_index("dp")
    me_ex = lax.axis_index("expert")
    rows, width = tokens.shape
    group, hidden, part = gate_weight.shape
    length = lengths[0]
    lane = lambda x, axis=-1: lane_order(x, axis, n_dp, me_dp)

    flat = group * hidden
    na, nq = attention_norm.shape[0], query_norm.shape[0]
    q_cols, k_cols = query_weight.shape[1], key_matrix.shape[1]
    heads_query, heads_key = q_cols // HEAD_SIZE, k_cols // HEAD_SIZE
    per_group = heads_query // heads_key
    own_place = (me_dp * n_ex + me_ex) * nq
    fill = jnp.zeros((128 - nq,), bf16)
    gains_own = jnp.concatenate(
        [attention_norm, experts_norm, query_norm, fill, key_norm, fill, jnp.zeros((256,), bf16)]
    )
    gains_own = gains_own.reshape(8, 128).astype(f32)
    cos2, sin2 = rope_lanes(rows)
    own_experts = [w.reshape(flat, part) for w in (gate_weight, up_weight, down_weight)]
    (
        inputs_low, upstream_other, table, mixed_rows, hidden_all, attended_low, rotated_query, key_rot, value_low, raw,
        prob_low, gains, gate_full, up_full, down_full, full_qkv, full_output,
    ) = forward_call(
        tokens,
        cotangent,
        route_ids.T,
        route_weight.T,
        lengths,
        query_weight,
        key_matrix,
        value_matrix,
        output_weight,
        *own_experts,
        gains_own,
        cos2,
        sin2,
    )
    grad_hidden_two, out_own, out_other, grads, got = expert_call(
        hidden_all, cotangent, upstream_other, table, *own_experts, gate_full, up_full, down_full
    )
    output, grad_mixed, grad_proj_low, grad_qkv_low, grad_hidden_one, gain_grads, got2, got = attention_back_call(
        grad_hidden_two, mixed_rows, cotangent, rotated_query, key_rot, value_low, raw, gains, cos2, sin2,
        prob_low, full_output, full_qkv, out_own, out_other, grads, got,
    )
    tokens_grad, query_shard, key_shard, value_shard, output_shard, gain_sum, got2_up, down_shard, gate_shard = last_call(
        grad_hidden_one, grad_mixed, inputs_low, grad_qkv_low, grad_proj_low, attended_low, gains, gain_grads,
        grads, got, got2,
    )
    up_shard = grads[2, :, :part].astype(f32) + got[2, :, :part].astype(f32) + got2_up.astype(f32)
    down_shard, gate_shard, up_shard = (x.reshape(group, hidden, part) for x in (down_shard, gate_shard, up_shard))
    own_head = lambda row: lax.dynamic_slice_in_dim(gain_sum[row], own_place, nq, 0)
    return (
        output,
        tokens_grad,
        gain_sum[0:2].reshape(-1),
        query_shard,
        key_shard,
        value_shard,
        output_shard,
        own_head(4),
        own_head(5),
        gain_sum[2:4].reshape(-1),
        gate_shard,
        up_shard,
        down_shard,
    )


def local(*args):
    sizes = [lax.axis_size(a) for a in ("dp", "expert", "tensor")]
    return local_fast(*args) if sizes == [4, 2, 4] else local_plain(*args)


def solution(mesh):
    both = ("dp", "expert")
    rows2, rows1, mats = P(both, None), P(both), P(both, "tensor")
    experts = P("expert", "tensor", "dp")
    return jax.shard_map(
        local,
        mesh=mesh,
        in_specs=(rows2, rows2, rows2, rows2, rows1, rows1, mats, mats, mats, mats, rows1, rows1, rows1)
        + (experts,) * 3,
        out_specs=(rows2, rows2, rows1, mats, mats, mats, mats, rows1, rows1, rows1) + (experts,) * 3,
        check_vma=False,
    )
```
